32 devices in a mesh: grp: 1, ep: 8 (over z, y), rep: 2 (over x), sub: 2 (over core).
Axes of the slice: x: 2, y: 2, z: 4, core: 2. Of those that a mesh axis runs over, the one named last changes fastest.
Arguments:
- output_gradient: bfloat16 [2048, 4096], P(('grp', 'ep', 'sub'), 'rep'), may hold values from -6 to 6
- hidden: bfloat16 [2048, 8, 1536], P(('grp', 'ep', 'sub'), None, 'rep'), may hold values from -0.29882812 to 0.29882812
- route_expert_index: int32 [2048, 8], P(('grp', 'ep', 'sub')), may hold values from 0 to 15, all different within a row; in each aligned block of 128 rows (0 to 127, 128 to 255, ...) at most 80 rows name the same one
- route_weight: bfloat16 [2048, 8], P(('grp', 'ep', 'sub')), may hold values from 0.019897461 to 0.5
- down_matrix: bfloat16 [16, 1536, 4096], P(('ep', 'sub'), None, 'rep'), may hold values from -0.15625 to 0.15625
- first_adapter_factor: bfloat16 [16, 1536, 32], P(('grp', 'ep', 'sub'), 'rep'), may hold values from -0.15625 to 0.15625
- second_adapter_factor: bfloat16 [16, 32, 4096], P(('grp', 'ep', 'sub'), None, 'rep'), may hold values from -0.09375 to 0.09375
Outputs:
- grad_hidden: bfloat16 [2048, 8, 1536], P(('grp', 'ep', 'sub'), None, 'rep')
- grad_probs: float32 [2048, 8], P(('grp', 'ep', 'sub'))
- first_factor_gradient: float32 [16, 1536, 32], P(('grp', 'ep', 'sub'), 'rep')
- second_factor_gradient: float32 [16, 32, 4096], P(('grp', 'ep', 'sub'), None, 'rep')
The draws below stay inside these ranges and needn't reach their ends.
Inputs may be any that keep to these rules, and one draw needn't show every extreme that they name: `route_expert_index`: each row names 8 different experts; among the rows of one device no expert is named more than 80 times, a bound that some block reaches.
All inputs are finite; a program needn't handle non-finite values.
Results may differ from the reference program's by a relative error of at most 0.0059.
Values may be sent and summed in bfloat16 or wider, within the bound.
No kernel may reach another device: no remote copies, remote signals or barrier semaphores. Data moves between devices by JAX's collectives and lax.ppermute only.
A program may use at most 128 MiB of HBM per device.

```python
import math
import jax
import jax.numpy as jnp
import numpy as np
from jax import lax

MODEL_WIDTH = 4096
HIDDEN_UNITS = 1536
ADAPTER_RANK = 32
TOP = 8
TOK_DEV = 128
EXPERT_COUNT = 16
TOKENS = 2048
CAP = 80
N_EP = 8
N_REP = 2
N_SUB = 2


def block_scale(stream_key, shape, cuts, low, largest):
    loudness = 1.0
    for axis_at, blocks in cuts:
        steps = jax.random.uniform(jax.random.fold_in(jax.random.fold_in(stream_key, 6), axis_at), (blocks,), jnp.float32, low / len(cuts), largest / len(cuts))
        loudness = loudness * jnp.repeat(jnp.exp(steps), shape[axis_at] // blocks).reshape((-1,) + (1,) * (len(shape) - 1 - axis_at))
    return loudness


def deal_out(key, own, number, rows, count, top, limit, slope):
    sequence = jax.random.permutation(key, count)
    crowded, common = shares(count, rows * top, limit, slope, True), shares(count, rows * top, limit, slope, False)
    places = jnp.arange(count)

    def named(sizes, rotation):
        used = int((sizes > 0).sum())
        fixed = max(1, used // 4)
        passed = fixed + (places - fixed + rotation * (used - fixed)) % max(1, count - fixed)
        return jnp.zeros((count,), jnp.int32).at[sequence[jnp.where(places < fixed, places, passed)]].set(jnp.asarray(sizes, jnp.int32))

    sizes = jnp.where(number % 4 == 0, named(crowded, number // 4), named(common, number - number // 4 - 1))
    mixed = jax.random.permutation(jax.random.fold_in(own, 3), count)
    source_of, sink = mixed[0:count // 2 * 2:2], mixed[1:count // 2 * 2:2]
    slack = jnp.minimum(sizes[source_of] - 1, limit - sizes[sink]) // 2
    slack = jnp.where((source_of == sequence[0]) | (sink == sequence[0]) | (sizes[sink] == 0), 0, jnp.maximum(slack, 0))
    passed = jax.random.randint(jax.random.fold_in(own, 4), (count // 2,), 0, 1 << 20) % (slack + 1)
    sizes = sizes.at[source_of].add(-passed).at[sink].add(passed)
    members = jnp.searchsorted(jnp.cumsum(sizes), jnp.arange(rows * top), side="right").astype(jnp.int32)
    listing = members.reshape(top, rows).T
    listing = listing[jax.random.permutation(jax.random.fold_in(own, 1), rows)]
    rotation = jax.random.randint(jax.random.fold_in(own, 2), (rows, 1), 0, top)
    return jnp.take_along_axis(listing, (jnp.arange(top)[None, :] + rotation) % top, axis=1)


def shares(count, total, limit, lean, full):
    portions = [(1 << 20) // math.isqrt(rank ** lean) + 1 for rank in range(1, count + 1)]
    largest = limit if full else min(limit, max(-(-total // count), total * portions[0] // sum(portions)))
    least = 1 if total - largest >= count - 1 else 0
    holding, spare = [largest] + [least] * (count - 1), total - largest - least * (count - 1)
    while spare > 0:
        movable = [i for i in range(1, count) if holding[i] < largest] or [i for i in range(1, count) if holding[i] < limit]
        whole, budget = sum([portions[i] for i in movable]), spare
        for i in movable:
            extra = min(limit - holding[i], max(1, budget * portions[i] // whole), spare)
            holding[i] = holding[i] + extra
            spare = spare - extra
    return np.array(holding)


def centred(stream_key, shape, spread, reach, pieces=(), kind=jnp.bfloat16):
    gain = block_scale(stream_key, shape, pieces, -0.22, 0.18) if pieces else 1.0
    drawn = jax.random.normal(stream_key, shape, jnp.float32) * spread * gain
    return jnp.minimum(jnp.maximum(drawn, -reach), reach).astype(kind)


def setup_inputs(seed: int = 0, part: int = 0) -> dict:
    key_list = jax.random.split(jax.random.key(seed), 8)
    part_splits = jax.random.split(jax.random.fold_in(key_list[7], part), 8)
    output_gradient = centred(part_splits[0], (TOKENS, MODEL_WIDTH), 1.0, 6.0, ((0, 16), (1, 2)))
    hidden = centred(part_splits[1], (TOKENS, TOP, HIDDEN_UNITS), 0.05, 0.29882812, ((0, 16), (2, 2)))
    route_expert_index_keys = jax.random.split(jax.random.fold_in(part_splits[2], 1), TOKENS // TOK_DEV)
    route_expert_index_turns = jax.random.permutation(jax.random.fold_in(part_splits[2], 3), TOKENS // TOK_DEV)
    route_expert_index = jax.vmap(lambda own, number: deal_out(jax.random.fold_in(part_splits[2], 2), own, number, TOK_DEV, EXPERT_COUNT, TOP, CAP, 2))(route_expert_index_keys, route_expert_index_turns).reshape((TOKENS, TOP))
    route_weight = jnp.clip(jnp.exp(math.log(0.5) - 3.224016 * jax.random.uniform(part_splits[3], (TOKENS, TOP), jnp.float32) ** block_scale(part_splits[3], (TOKENS, TOP), ((0, 16),), -0.2, 0.2)), 0.019897461, 0.5).astype(jnp.bfloat16)
    down_matrix = centred(key_list[4], (EXPERT_COUNT, HIDDEN_UNITS, MODEL_WIDTH), HIDDEN_UNITS ** -0.5, 0.15625, ((0, 16), (2, 2)))
    first_adapter_factor = centred(part_splits[5], (EXPERT_COUNT, HIDDEN_UNITS, ADAPTER_RANK), HIDDEN_UNITS ** -0.5, 0.15625, ((0, 16), (1, 2)))
    second_adapter_factor = centred(part_splits[6], (EXPERT_COUNT, ADAPTER_RANK, MODEL_WIDTH), MODEL_WIDTH ** -0.5, 0.09375, ((0, 16), (2, 2)))
    return {"output_gradient": output_gradient, "hidden": hidden, "route_expert_index": route_expert_index, "route_weight": route_weight, "down_matrix": down_matrix, "first_adapter_factor": first_adapter_factor, "second_adapter_factor": second_adapter_factor}


adapter_scale = 2.0


def rounded(value):
    return lax.optimization_barrier(value.astype(jnp.bfloat16)).astype(jnp.float32)


def reference(output_gradient, hidden, route_expert_index, route_weight, down_matrix, first_adapter_factor, second_adapter_factor):
    pair_total = TOKENS * TOP
    max_load = CAP * N_EP * N_SUB
    feat_part = MODEL_WIDTH // N_REP
    unit_portion = HIDDEN_UNITS // N_REP
    exact_precision = lax.Precision.HIGHEST
    flat_ids = route_expert_index.reshape(pair_total).astype(jnp.int32)
    sorted_rows = jnp.argsort(flat_ids, stable=True).astype(jnp.int32)
    counts = jnp.sum((flat_ids[:, None] == jnp.arange(EXPERT_COUNT, dtype=jnp.int32)[None, :]).astype(jnp.int32), axis=0)
    starts = (jnp.cumsum(counts) - counts).astype(jnp.int32)
    hid_flat = hidden.reshape(pair_total, HIDDEN_UNITS)
    prob_flat = route_weight.reshape(pair_total).astype(jnp.float32)

    def expert_step(running, expert_index):
        all_hidden, all_probs = running
        offsets = jnp.arange(max_load, dtype=jnp.int32)
        in_use = offsets < counts[expert_index]
        pair_rows = sorted_rows[jnp.minimum(starts[expert_index] + offsets, pair_total - 1)]
        token_rows = pair_rows // TOP
        gradient_row_block = output_gradient[token_rows].astype(jnp.float32)
        hidden_row_block = hid_flat[pair_rows].astype(jnp.float32)
        prob_rows = jnp.where(in_use, prob_flat[pair_rows], jnp.float32(0.0))
        weight = down_matrix[expert_index].astype(jnp.float32)
        first_factor_local = first_adapter_factor[expert_index].astype(jnp.float32)
        second_factor_local = second_adapter_factor[expert_index].astype(jnp.float32)
        grad_lowrank = jnp.dot(gradient_row_block, second_factor_local.T, precision=exact_precision)
        hid_lowrank = jnp.dot(hidden_row_block, first_factor_local, precision=exact_precision)
        rank_step_body = rounded(grad_lowrank)
        total = jnp.zeros((max_load, HIDDEN_UNITS), jnp.float32)
        for fourth_portion in range(N_REP):
            partial_result = jnp.dot(gradient_row_block[:, fourth_portion * feat_part:(fourth_portion + 1) * feat_part],
                              weight[:, fourth_portion * feat_part:(fourth_portion + 1) * feat_part].T, precision=exact_precision)
            adapter_contrib = adapter_scale * jnp.dot(rank_step_body, first_factor_local[fourth_portion * unit_portion:(fourth_portion + 1) * unit_portion].T, precision=exact_precision)
            partial_result = partial_result.at[:, fourth_portion * unit_portion:(fourth_portion + 1) * unit_portion].add(adapter_contrib)
            total = total + rounded(partial_result)
        hidden_sum = rounded(total)
        out_grad = (prob_rows[:, None] * hidden_sum).astype(jnp.bfloat16)
        out_prob = jnp.sum(hidden_row_block * hidden_sum, axis=1)
        weighted_gradient = rounded(grad_lowrank * prob_rows[:, None])
        weighted_hidden = rounded(hid_lowrank * prob_rows[:, None])
        first_adapter_gradient = adapter_scale * jnp.dot(hidden_row_block.T, weighted_gradient, precision=exact_precision)
        second_adapter_gradient = adapter_scale * jnp.dot(weighted_hidden.T, gradient_row_block, precision=exact_precision)
        landing = jnp.where(in_use, pair_rows, pair_total)
        all_hidden = all_hidden.at[landing].set(out_grad, mode="drop")
        all_probs = all_probs.at[landing].set(out_prob, mode="drop")
        return (all_hidden, all_probs), (first_adapter_gradient, second_adapter_gradient)

    start_state = (jnp.zeros((pair_total, HIDDEN_UNITS), jnp.bfloat16), jnp.zeros((pair_total,), jnp.float32))
    (all_hidden, all_probs), (first_factor_gradient, second_factor_gradient) = lax.scan(expert_step, start_state, jnp.arange(EXPERT_COUNT, dtype=jnp.int32))
    return all_hidden.reshape(TOKENS, TOP, HIDDEN_UNITS), all_probs.reshape(TOKENS, TOP), first_factor_gradient, second_factor_gradient
```

```python
import functools

import jax
import jax.numpy as jnp
from jax import lax
from jax.experimental import pallas as pl
from jax.experimental.pallas import tpu as pltpu
from jax.sharding import PartitionSpec as P

adapter_scale = 2.0
CHUNKS = 3
BF16 = jnp.bfloat16
F32 = jnp.float32
NT = (((1,), (1,)), ((), ()))
TN = (((0,), (0,)), ((), ()))
NN = (((1,), (0,)), ((), ()))


def dot(a, b, dims):
    return lax.dot_general(a, b, dims, preferred_element_type=F32)


def params(mib=48):
    return pltpu.CompilerParams(vmem_limit_bytes=mib * 2**20)


def expert_mask(idx_col, width, rank):
    column = lax.broadcasted_iota(jnp.int32, (idx_col.shape[0], width), 1) // rank
    return column == idx_col


def spread_pairs(dense, top):
    toks, width = dense.shape
    return jnp.broadcast_to(dense[:, None, :], (toks, top, width)).reshape(toks * top, width)


def lowrank_hid_kernel(rank, top, idx_ref, hid_ref, first_ref, out_ref):
    wide = dot(hid_ref[...], first_ref[...], NT)
    wide = jnp.where(expert_mask(idx_ref[...], wide.shape[1], rank), wide, 0.0)
    out_ref[...] = wide.reshape(wide.shape[0] // top, top, wide.shape[1]).sum(axis=1)


def lowrank_hid_call(idx_col, hid, first_all, rank, top):
    pairs, units = hid.shape
    width = first_all.shape[0]
    blk = pairs // 4
    return pl.pallas_call(
        functools.partial(lowrank_hid_kernel, rank, top),
        grid=(4,),
        in_specs=[
            pl.BlockSpec((blk, 1), lambda i: (i, 0)),
            pl.BlockSpec((blk, units), lambda i: (i, 0)),
            pl.BlockSpec((width, units), lambda i: (0, 0)),
        ],
        out_specs=pl.BlockSpec((blk // top, width), lambda i: (i, 0)),
        out_shape=jax.ShapeDtypeStruct((pairs // top, width), F32),
        compiler_params=params(),
        name="lowrank_hid",
    )(idx_col, hid, first_all)


def select_kernel(slots, pos_ref, grad_ref, second_ref, rows_ref, low_ref):
    grad = grad_ref[0]
    slot = lax.broadcasted_iota(jnp.int32, (slots, grad.shape[0]), 0)
    pick = jnp.where(slot == pos_ref[0], 1.0, 0.0).astype(BF16)
    rows_ref[0] = dot(pick, grad, NN).astype(BF16)
    low_ref[0] = dot(second_ref[...], grad, NT).astype(low_ref.dtype)


def select_call(pos, grad_all, second, slots):
    owners, toks, feats = grad_all.shape
    rank = second.shape[0]
    return pl.pallas_call(
        functools.partial(select_kernel, slots),
        grid=(owners,),
        in_specs=[
            pl.BlockSpec((1, 1, toks), lambda i: (i, 0, 0)),
            pl.BlockSpec((1, toks, feats), lambda i: (i, 0, 0)),
            pl.BlockSpec((rank, feats), lambda i: (0, 0)),
        ],
        out_specs=[
            pl.BlockSpec((1, slots, feats), lambda i: (i, 0, 0)),
            pl.BlockSpec((1, rank, toks), lambda i: (i, 0, 0)),
        ],
        out_shape=[
            jax.ShapeDtypeStruct((owners, slots, feats), BF16),
            jax.ShapeDtypeStruct((owners, rank, toks), BF16),
        ],
        compiler_params=params(),
        name="select_rows",
    )(pos, grad_all, second)


def frozen_kernel(shares, rep_ref, rows_ref, *rest):
    rows = rows_ref[...]
    for weight_ref, out_ref in zip(rest[:shares], rest[shares:]):
        out_ref[...] = dot(rows, weight_ref[...], NT).astype(BF16)


def frozen_call(rep_at, rows, down, shares, chunk, chunks):
    count, feats = rows.shape
    units = down.shape[0] // shares // chunks
    blk = 320 if count % 320 == 0 else 256

    def weight_at(offset, i, rep):
        return (lax.rem(rep[0] + offset, shares) * chunks + chunk, 0)

    offsets = [(k + 1) % shares for k in range(shares)]
    return pl.pallas_call(
        functools.partial(frozen_kernel, shares),
        grid_spec=pltpu.PrefetchScalarGridSpec(
            num_scalar_prefetch=1,
            grid=(count // blk,),
            in_specs=[pl.BlockSpec((blk, feats), lambda i, rep: (i, 0))]
            + [pl.BlockSpec((units, feats), functools.partial(weight_at, k)) for k in offsets],
            out_specs=[pl.BlockSpec((blk, units), lambda i, rep: (i, 0))] * shares,
        ),
        out_shape=[jax.ShapeDtypeStruct((count, units), BF16)] * shares,
        compiler_params=params(),
        cost_estimate=pl.CostEstimate(
            flops=2 * shares * count * units * feats,
            bytes_accessed=2 * count * feats,
            transcendentals=0,
        ),
        name="frozen_rows",
    )(rep_at, rows, *[down] * shares)


def second_grad_kernel(scaled_ref, grad_ref, out_ref):
    @pl.when(pl.program_id(0) == 0)
    def _():
        out_ref[...] = jnp.zeros_like(out_ref)

    out_ref[...] += adapter_scale * dot(scaled_ref[0], grad_ref[0], NN)


def second_grad_call(scaled, grad_all):
    owners, rank, toks = scaled.shape
    feats = grad_all.shape[2]
    return pl.pallas_call(
        second_grad_kernel,
        grid=(owners,),
        in_specs=[
            pl.BlockSpec((1, rank, toks), lambda i: (i, 0, 0)),
            pl.BlockSpec((1, toks, feats), lambda i: (i, 0, 0)),
        ],
        out_specs=pl.BlockSpec((rank, feats), lambda i: (0, 0)),
        out_shape=jax.ShapeDtypeStruct((rank, feats), F32),
        compiler_params=params(),
        name="second_grad",
    )(scaled, grad_all)


def first_grad_kernel(rank, top, idx_ref, prob_ref, low_ref, hid_ref, out_ref):
    @pl.when(pl.program_id(0) == 0)
    def _():
        out_ref[...] = jnp.zeros_like(out_ref)

    low = spread_pairs(low_ref[...], top)
    keep = expert_mask(idx_ref[...], low.shape[1], rank)
    scaled = jnp.where(keep, low * prob_ref[...], 0.0).astype(BF16)
    out_ref[...] += adapter_scale * dot(scaled, hid_ref[...], TN)


def first_grad_call(idx_col, prob_col, low, hid, rank, top):
    pairs, units = hid.shape
    width = low.shape[1]
    blk = pairs // 4
    return pl.pallas_call(
        functools.partial(first_grad_kernel, rank, top),
        grid=(4,),
        in_specs=[
            pl.BlockSpec((blk, 1), lambda i: (i, 0)),
            pl.BlockSpec((blk, 1), lambda i: (i, 0)),
            pl.BlockSpec((blk // top, width), lambda i: (i, 0)),
            pl.BlockSpec((blk, units), lambda i: (i, 0)),
        ],
        out_specs=pl.BlockSpec((width, units), lambda i: (0, 0)),
        out_shape=jax.ShapeDtypeStruct((width, units), F32),
        compiler_params=params(),
        name="first_grad",
    )(idx_col, prob_col, low, hid)


def finish_kernel(rank, top, chunks, idx_ref, target_ref, prob_ref, low_ref, hid_ref, first_ref, *rest):
    back, out_ref, sum_ref = rest[:chunks], rest[chunks], rest[chunks + 1]
    slots = back[0].shape[0]
    pairs = hid_ref.shape[0]
    low = spread_pairs(low_ref[...], top)
    keep = expert_mask(idx_ref[...], low.shape[1], rank)
    low = jnp.where(keep, adapter_scale * low.astype(BF16).astype(F32), 0.0).astype(BF16)
    slot = lax.broadcasted_iota(jnp.int32, (pairs, slots), 1)
    pick = jnp.where(slot == target_ref[...], 1.0, 0.0).astype(BF16)
    total = jnp.zeros((pairs, 1), F32)
    units = back[0].shape[1]
    for c in range(chunks):
        at = pl.ds(c * units, units)
        value = dot(pick, back[c][...], NN) + dot(low, first_ref[:, at], NN)
        value = value.astype(BF16).astype(F32)
        out_ref[:, at] = (value * prob_ref[...]).astype(BF16)
        total = total + jnp.sum(value * hid_ref[:, at].astype(F32), axis=1, keepdims=True)
    sum_ref[...] = total


def finish_call(idx_col, target, prob_col, low, hid, first_all, back, rank, top):
    pairs, units = hid.shape
    width = low.shape[1]
    slots, part = back[0].shape
    blk = pairs // 4
    return pl.pallas_call(
        functools.partial(finish_kernel, rank, top, len(back)),
        grid=(4,),
        in_specs=[
            pl.BlockSpec((blk, 1), lambda i: (i, 0)),
            pl.BlockSpec((blk, 1), lambda i: (i, 0)),
            pl.BlockSpec((blk, 1), lambda i: (i, 0)),
            pl.BlockSpec((blk // top, width), lambda i: (i, 0)),
            pl.BlockSpec((blk, units), lambda i: (i, 0)),
            pl.BlockSpec((width, units), lambda i: (0, 0)),
        ]
        + [pl.BlockSpec((slots, part), lambda i: (0, 0))] * len(back),
        out_specs=[
            pl.BlockSpec((blk, units), lambda i: (i, 0)),
            pl.BlockSpec((blk, 1), lambda i: (i, 0)),
        ],
        out_shape=[
            jax.ShapeDtypeStruct((pairs, units), BF16),
            jax.ShapeDtypeStruct((pairs, 1), F32),
        ],
        compiler_params=params(),
        name="finish",
    )(idx_col, target, prob_col, low, hid, first_all, *back)


def body(grad, hidden, index, weight, down, first, second):
    toks, top = index.shape
    exp_local, units_all, feats = down.shape
    assert exp_local == 1
    units, rank = first.shape[1:]
    where = ("ep", "sub")
    owners = lax.axis_size(where)
    cap = min(toks, 5 * toks * top // (4 * owners))
    slots = -(-cap // 16) * 16
    pairs = toks * top
    width = owners * rank
    shares = lax.axis_size("rep")

    def turn(x, offset):
        return lax.ppermute(x, "rep", [(r, (r + offset) % shares) for r in range(shares)])

    def over_rep(x):
        return x + turn(x, 1) if shares == 2 else lax.psum(x, "rep")

    def exchange(x):
        return lax.all_to_all(x, where, split_axis=0, concat_axis=0, tiled=True)

    index_rows = jnp.pad(index.T.astype(BF16), ((0, 0), (0, units - toks)))
    small = jnp.concatenate([first[0].T, index_rows], axis=0)
    small_all = lax.all_gather(small, where)
    grad_all = lax.all_gather(grad, where)

    first_all = small_all[:, :rank].reshape(width, units)
    index_all = small_all[:, rank:, :toks].astype(jnp.int32)
    me = lax.axis_index(where)
    mine = jnp.any(index_all == me, axis=1)
    before = jnp.triu(jnp.ones((toks, toks), BF16), 1)
    pos = jnp.dot(mine.astype(BF16), before, preferred_element_type=F32).astype(jnp.int32)
    pos = jnp.where(mine, pos, -1).reshape(owners, 1, toks)

    hid = hidden.reshape(pairs, units)
    idx_col = index.reshape(pairs, 1)
    prob_col = weight.reshape(pairs, 1).astype(F32)
    hits = index[:, :, None] == jnp.arange(owners, dtype=jnp.int32)
    hit = jnp.any(hits, axis=1)
    place = jnp.dot(before.T, hit.astype(BF16), preferred_element_type=F32).astype(jnp.int32)
    place = place + slots * jnp.arange(owners, dtype=jnp.int32)
    target = jnp.sum(jnp.where(hits, place[:, None, :], 0), axis=2).reshape(pairs, 1)
    prob_dense = jnp.sum(jnp.where(hits, weight[:, :, None].astype(F32), 0.0), axis=1)

    low_hid = over_rep(lowrank_hid_call(idx_col, hid, first_all, rank, top))
    scaled_hid = (low_hid * jnp.repeat(prob_dense, rank, axis=1)).astype(BF16)
    scaled_hid = exchange(scaled_hid.T.reshape(owners, rank, toks))

    rows, low_grad = select_call(pos, grad_all, second[0], slots)
    rows = rows.reshape(owners * slots, feats)
    low_grad = exchange(low_grad).reshape(width, toks).T.astype(F32)
    low_grad = over_rep(low_grad)

    rep_at = lax.axis_index("rep").astype(jnp.int32).reshape(1)
    back = []
    for c in range(CHUNKS):
        *give, keep = frozen_call(rep_at, rows, down[0], shares, c, CHUNKS)
        total = keep.astype(F32)
        for k, share in enumerate(give):
            total = total + turn(share, k + 1).astype(F32)
        total = total.astype(BF16)
        back.append(exchange(total.reshape(owners, slots, -1)).reshape(owners * slots, -1))

    second_grad = second_grad_call(scaled_hid, grad_all)
    first_part = first_grad_call(idx_col, prob_col, low_grad, hid, rank, top)
    first_grad = lax.psum_scatter(
        first_part.reshape(owners, rank, units), where, scatter_dimension=0, tiled=True
    )
    grad_hidden, sums = finish_call(
        idx_col, target, prob_col, low_grad, hid, first_all, back, rank, top
    )
    return (
        grad_hidden.reshape(toks, top, units),
        over_rep(sums.reshape(toks, top)),
        jnp.swapaxes(first_grad, 1, 2),
        second_grad[None],
    )


def solution(mesh):
    return jax.shard_map(
        body,
        mesh=mesh,
        in_specs=(
            P(("grp", "ep", "sub"), "rep"),
            P(("grp", "ep", "sub"), None, "rep"),
            P(("grp", "ep", "sub"), None),
            P(("grp", "ep", "sub"), None),
            P(("ep", "sub"), None, "rep"),
            P(("grp", "ep", "sub"), "rep", None),
            P(("grp", "ep", "sub"), None, "rep"),
        ),
        out_specs=(
            P(("grp", "ep", "sub"), None, "rep"),
            P(("grp", "ep", "sub"), None),
            P(("grp", "ep", "sub"), "rep", None),
            P(("grp", "ep", "sub"), None, "rep"),
        ),
        check_vma=False,
    )
```

```python
import functools

import jax
import jax.numpy as jnp
from jax import lax
from jax.experimental import pallas as pl
from jax.experimental.pallas import tpu as pltpu
from jax.sharding import PartitionSpec as P

adapter_scale = 2.0
BF16 = jnp.bfloat16
F32 = jnp.float32
NT = (((1,), (1,)), ((), ()))
TN = (((0,), (0,)), ((), ()))
NN = (((1,), (0,)), ((), ()))


def dot(a, b, dims):
    return lax.dot_general(a, b, dims, preferred_element_type=F32)


def params(mib=48):
    return pltpu.CompilerParams(vmem_limit_bytes=mib * 2**20)


def whole(shape):
    return pl.BlockSpec(shape, lambda *_: (0,) * len(shape))


def expert_mask(idx_col, width, rank):
    column = lax.broadcasted_iota(jnp.int32, (idx_col.shape[0], width), 1) // rank
    return column == idx_col


def spread_pairs(dense, top):
    toks, width = dense.shape
    return jnp.broadcast_to(dense[:, None, :], (toks, top, width)).reshape(toks * top, width)


def lowrank_hid_kernel(rank, top, idx_ref, hid_ref, first_ref, out_ref):
    wide = dot(hid_ref[...], first_ref[...], NT)
    wide = jnp.where(expert_mask(idx_ref[...], wide.shape[1], rank), wide, 0.0)
    out_ref[...] = wide.reshape(wide.shape[0] // top, top, wide.shape[1]).sum(axis=1)


def lowrank_hid_call(idx_col, hid, first_all, rank, top):
    pairs, units = hid.shape
    width = first_all.shape[0]
    blk = pairs // 4
    return pl.pallas_call(
        functools.partial(lowrank_hid_kernel, rank, top),
        grid=(4,),
        in_specs=[
            pl.BlockSpec((blk, 1), lambda i: (i, 0)),
            pl.BlockSpec((blk, units), lambda i: (i, 0)),
            whole((width, units)),
        ],
        out_specs=pl.BlockSpec((blk // top, width), lambda i: (i, 0)),
        out_shape=jax.ShapeDtypeStruct((pairs // top, width), F32),
        compiler_params=params(),
        cost_estimate=pl.CostEstimate(
            flops=4 * pairs * width * units, bytes_accessed=2 * pairs * units, transcendentals=0
        ),
        name="lowrank_hid",
    )(idx_col, hid, first_all)


def expert_rows_kernel(slots, tiles, shares, batch, rep_ref, *rest):
    pos_ref, grads = rest[0], rest[1 : 1 + batch]
    second_ref, weight_ref = rest[1 + batch], rest[2 + batch]
    outs, low_ref, rows_ref = rest[3 + batch : -2], rest[-2], rest[-1]
    step = pl.program_id(0)

    @pl.when(step == 0)
    def _():
        for k, grad_ref in enumerate(grads):
            grad = grad_ref[...]
            slot = lax.broadcasted_iota(jnp.int32, (slots, grad.shape[0]), 0)
            pick = jnp.where(slot == pos_ref[k], 1.0, 0.0).astype(BF16)
            rows_ref[pl.ds(k * slots, slots), :] = dot(pick, grad, NN).astype(BF16)
            low_ref[k] = dot(second_ref[...], grad, NT).astype(BF16)

    value = dot(rows_ref[...], weight_ref[...], NT).astype(BF16)
    for k, out_ref in enumerate(outs):

        @pl.when(step // tiles == k)
        def _():
            out_ref[...] = value


def expert_rows_call(rep_at, pos, grads, second, down, shares, slots):
    batch, (toks, feats) = len(grads), grads[0].shape
    rank = second.shape[0]
    units = down.shape[0] // shares
    tiles = 3
    tile = units // tiles
    rows = batch * slots

    def weight_at(i, rep):
        return (lax.rem(rep[0] + i // tiles + 1, shares) * tiles + lax.rem(i, tiles), 0)

    def out_at(k, i, rep):
        return (0, jnp.clip(i - k * tiles, 0, tiles - 1))

    return pl.pallas_call(
        functools.partial(expert_rows_kernel, slots, tiles, shares, batch),
        grid_spec=pltpu.PrefetchScalarGridSpec(
            num_scalar_prefetch=1,
            grid=(shares * tiles,),
            in_specs=[whole((batch, 1, toks))]
            + [whole((toks, feats))] * batch
            + [whole((rank, feats)), pl.BlockSpec((tile, feats), weight_at)],
            out_specs=[
                pl.BlockSpec((rows, tile), functools.partial(out_at, k)) for k in range(shares)
            ]
            + [whole((batch, rank, toks))],
            scratch_shapes=[pltpu.VMEM((rows, feats), BF16)],
        ),
        out_shape=[jax.ShapeDtypeStruct((rows, units), BF16)] * shares
        + [jax.ShapeDtypeStruct((batch, rank, toks), BF16)],
        compiler_params=params(),
        cost_estimate=pl.CostEstimate(
            flops=2 * rows * down.shape[0] * feats,
            bytes_accessed=2 * down.shape[0] * feats,
            transcendentals=0,
        ),
        name="expert_rows",
    )(rep_at, pos, *grads, second, down)


def share_sum_kernel(parts, *refs):
    outs = refs[parts:]
    slots = outs[0].shape[0]
    for k, out_ref in enumerate(outs):
        at = pl.ds(k * slots, slots)
        total = refs[0][at, :].astype(F32)
        for part in refs[1:parts]:
            total = total + part[at, :].astype(F32)
        out_ref[...] = total.astype(BF16)


def share_sum_call(parts, batch):
    rows, units = parts[0].shape
    return pl.pallas_call(
        functools.partial(share_sum_kernel, len(parts)),
        out_shape=[jax.ShapeDtypeStruct((rows // batch, units), BF16)] * batch,
        compiler_params=params(),
        name="share_sum",
    )(*parts)


def place_kernel(me_ref, *refs):
    out_ref, at = refs[-1], 0
    for ref in refs[:-1]:
        for k in range(ref.shape[0]):
            out_ref[lax.bitwise_xor(me_ref[0], at)] = ref[k]
            at += 1


def place_call(me_at, blocks):
    count = sum(b.shape[0] for b in blocks)
    shape = (count,) + blocks[0].shape[1:]
    return pl.pallas_call(
        place_kernel,
        grid_spec=pltpu.PrefetchScalarGridSpec(
            num_scalar_prefetch=1,
            grid=(1,),
            in_specs=[whole(b.shape) for b in blocks],
            out_specs=whole(shape),
        ),
        out_shape=jax.ShapeDtypeStruct(shape, blocks[0].dtype),
        compiler_params=params(),
        name="place_blocks",
    )(me_at, *blocks)


def second_grad_kernel(me_ref, scaled_ref, *refs):
    out_ref = refs[-1]
    total = jnp.zeros(out_ref.shape, F32)
    for r, grad_ref in enumerate(refs[:-1]):
        total = total + dot(scaled_ref[lax.bitwise_xor(me_ref[0], r)], grad_ref[...], NN)
    out_ref[...] = adapter_scale * total


def second_grad_call(me_at, scaled, grads):
    owners, rank, toks = scaled.shape
    feats = grads[0].shape[1]
    steps = 4
    tile = feats // steps
    return pl.pallas_call(
        second_grad_kernel,
        grid_spec=pltpu.PrefetchScalarGridSpec(
            num_scalar_prefetch=1,
            grid=(steps,),
            in_specs=[whole((owners, rank, toks))]
            + [pl.BlockSpec((toks, tile), lambda i, me: (0, i))] * owners,
            out_specs=pl.BlockSpec((rank, tile), lambda i, me: (0, i)),
        ),
        out_shape=jax.ShapeDtypeStruct((rank, feats), F32),
        compiler_params=params(),
        cost_estimate=pl.CostEstimate(
            flops=2 * rank * feats * toks * owners,
            bytes_accessed=2 * owners * toks * feats,
            transcendentals=0,
        ),
        name="second_grad",
    )(me_at, scaled, *grads)


def first_grad_kernel(rank, top, steps, cores, sub_ref, idx_ref, prob_ref, low_ref, hid_ref, *rest):
    outs, sum_ref = rest[:cores], rest[cores]
    step = pl.program_id(0)
    low = spread_pairs(low_ref[...], top)
    keep = expert_mask(idx_ref[...], low.shape[1], rank)
    scaled = jnp.where(keep, low * prob_ref[...], 0.0).astype(BF16)
    part = adapter_scale * dot(scaled, hid_ref[...], TN)
    part = part.reshape(sum_ref.shape)

    @pl.when(step == 0)
    def _():
        sum_ref[...] = part

    @pl.when(step > 0)
    def _():
        sum_ref[...] += part

    @pl.when(step == steps - 1)
    def _():
        for k, out_ref in enumerate(outs):
            out_ref[...] = sum_ref[:, lax.rem(sub_ref[0] + k, cores)].astype(out_ref.dtype)


def first_grad_call(sub_at, idx_col, prob_col, low, hid, rank, top, cores):
    pairs, units = hid.shape
    width = low.shape[1]
    steps = 4
    blk = pairs // steps
    shape = (width // rank // cores, rank, units)
    return pl.pallas_call(
        functools.partial(first_grad_kernel, rank, top, steps, cores),
        grid_spec=pltpu.PrefetchScalarGridSpec(
            num_scalar_prefetch=1,
            grid=(steps,),
            in_specs=[
                pl.BlockSpec((blk, 1), lambda i, s: (i, 0)),
                pl.BlockSpec((blk, 1), lambda i, s: (i, 0)),
                pl.BlockSpec((blk // top, width), lambda i, s: (i, 0)),
                pl.BlockSpec((blk, units), lambda i, s: (i, 0)),
            ],
            out_specs=[whole(shape)] * cores,
            scratch_shapes=[pltpu.VMEM((shape[0], cores) + shape[1:], F32)],
        ),
        out_shape=[jax.ShapeDtypeStruct(shape, F32)]
        + [jax.ShapeDtypeStruct(shape, BF16)] * (cores - 1),
        compiler_params=params(),
        name="first_grad",
    )(sub_at, idx_col, prob_col, low, hid)


def finish_kernel(rank, top, count, idx_ref, target_ref, prob_ref, low_ref, hid_ref, first_ref, *rest):
    back, out_ref, sum_ref, all_ref = rest[:count], rest[count], rest[count + 1], rest[count + 2]
    slots = back[0].shape[0]
    pairs = hid_ref.shape[0]

    @pl.when(pl.program_id(0) == 0)
    def _():
        for r, ref in enumerate(back):
            all_ref[pl.ds(r * slots, slots), :] = ref[...]

    low = spread_pairs(low_ref[...], top)
    keep = expert_mask(idx_ref[...], low.shape[1], rank)
    low = jnp.where(keep, adapter_scale * low.astype(BF16).astype(F32), 0.0).astype(BF16)
    slot = lax.broadcasted_iota(jnp.int32, (pairs, count * slots), 1)
    pick = jnp.where(slot == target_ref[...], 1.0, 0.0).astype(BF16)
    value = dot(pick, all_ref[...], NN) + dot(low, first_ref[...], NN)
    value = value.astype(BF16).astype(F32)
    out_ref[...] = (value * prob_ref[...]).astype(BF16)
    sum_ref[...] = jnp.sum(value * hid_ref[...].astype(F32), axis=1, keepdims=True)


def finish_call(idx_col, target, prob_col, low, hid, first_all, back, rank, top):
    pairs, units = hid.shape
    width = low.shape[1]
    slots, part = back[0].shape
    blk = pairs // 4
    return pl.pallas_call(
        functools.partial(finish_kernel, rank, top, len(back)),
        grid=(4,),
        in_specs=[
            pl.BlockSpec((blk, 1), lambda i: (i, 0)),
            pl.BlockSpec((blk, 1), lambda i: (i, 0)),
            pl.BlockSpec((blk, 1), lambda i: (i, 0)),
            pl.BlockSpec((blk // top, width), lambda i: (i, 0)),
            pl.BlockSpec((blk, units), lambda i: (i, 0)),
            whole((width, units)),
        ]
        + [whole((slots, part))] * len(back),
        out_specs=[
            pl.BlockSpec((blk, units), lambda i: (i, 0)),
            pl.BlockSpec((blk, 1), lambda i: (i, 0)),
        ],
        out_shape=[
            jax.ShapeDtypeStruct((pairs, units), BF16),
            jax.ShapeDtypeStruct((pairs, 1), F32),
        ],
        scratch_shapes=[pltpu.VMEM((len(back) * slots, units), BF16)],
        compiler_params=params(),
        name="finish",
    )(idx_col, target, prob_col, low, hid, first_all, *back)


def body(grad, hidden, index, weight, down, first, second):
    toks, top = index.shape
    exp_local, units_all, feats = down.shape
    assert exp_local == 1
    units, rank = first.shape[1:]
    where = ("ep", "sub")
    groups, cores, shares = lax.axis_size("ep"), lax.axis_size("sub"), lax.axis_size("rep")
    owners = groups * cores
    assert cores == 2 and groups & (groups - 1) == 0
    cap = min(toks, 5 * toks * top // (4 * owners))
    slots = -(-cap // 16) * 16
    pairs = toks * top
    width = owners * rank
    me = lax.axis_index(where).astype(jnp.int32)
    me_at = me.reshape(1)
    rep_at = lax.axis_index("rep").astype(jnp.int32).reshape(1)
    sub_at = lax.axis_index("sub").astype(jnp.int32).reshape(1)

    def turn(x, offset):
        return lax.ppermute(x, "rep", [(r, (r + offset) % shares) for r in range(shares)])

    def over_rep(x):
        return x + turn(x, 1) if shares == 2 else lax.psum(x, "rep")

    def flip(x, mask, axis="ep"):
        size = groups if axis == "ep" else cores if axis == "sub" else owners
        return lax.ppermute(x, axis, [(i, i ^ mask) for i in range(size)])

    def gather_relative(x):
        known, mask = [0], groups // 2
        held = x[None]
        while mask:
            held = jnp.concatenate([held, flip(held, mask)])
            known = known + [o ^ mask for o in known]
            mask //= 2
        held = jnp.concatenate([held, flip(held, 1, "sub")])
        known = [2 * o for o in known] + [2 * o + 1 for o in known]
        return jnp.stack([held[known.index(r)] for r in range(owners)])

    def exchange(x, axes=where):
        return lax.all_to_all(x, axes, split_axis=0, concat_axis=0, tiled=True)

    index_all = gather_relative(jnp.pad(index.T.astype(BF16), ((0, 16 - top), (0, 0))))[:, :top]
    blocks = {0: grad}
    for o in sorted(range(1, groups), key=lambda o: (o.bit_count(), o)):
        last = o & -o
        blocks[o] = flip(blocks[o ^ last], last)
    first_all = gather_relative(first[0].T)

    mine = jnp.any(index_all.astype(jnp.int32) == me, axis=1)
    before = jnp.triu(jnp.ones((toks, toks), BF16), 1)
    pos = jnp.dot(mine.astype(BF16), before, preferred_element_type=F32).astype(jnp.int32)
    pos = jnp.where(mine, pos, -1).reshape(owners, 1, toks)

    back, grads, low_parts = [], [], []
    for o in range(0, groups, 2):
        batch = [blocks[o], flip(blocks[o], 1, "sub"), blocks[o + 1], flip(blocks[o + 1], 1, "sub")]
        *give, keep, low = expert_rows_call(
            rep_at, pos[2 * o : 2 * o + 4], batch, second[0], down[0], shares, slots
        )
        parts = [keep] + [turn(x, k + 1) for k, x in enumerate(give)]
        for k, rows in enumerate(share_sum_call(parts, 4)):
            r = 2 * o + k
            back.append(flip(rows, r, where) if r else rows)
        grads += batch
        low_parts.append(low)

    hid = hidden.reshape(pairs, units)
    idx_col = index.reshape(pairs, 1)
    prob_col = weight.reshape(pairs, 1).astype(F32)
    hits = index[:, :, None] == jnp.arange(owners, dtype=jnp.int32)
    hit = jnp.any(hits, axis=1)
    place = jnp.dot(before.T, hit.astype(BF16), preferred_element_type=F32).astype(jnp.int32)
    place = place + slots * lax.bitwise_xor(me, jnp.arange(owners, dtype=jnp.int32))
    target = jnp.sum(jnp.where(hits, place[:, None, :], 0), axis=2).reshape(pairs, 1)
    prob_dense = jnp.sum(jnp.where(hits, weight[:, :, None].astype(F32), 0.0), axis=1)

    first_all = place_call(me_at, [first_all]).reshape(width, units)
    low_hid = over_rep(lowrank_hid_call(idx_col, hid, first_all, rank, top))
    scaled_hid = (low_hid * jnp.repeat(prob_dense, rank, axis=1)).astype(BF16)
    scaled_hid = exchange(scaled_hid.T.reshape(owners, rank, toks))
    second_grad = second_grad_call(me_at, scaled_hid, grads)

    low_grad = exchange(place_call(me_at, low_parts))
    low_grad = over_rep(low_grad.reshape(width, toks).T.astype(F32))

    keep, give = first_grad_call(sub_at, idx_col, prob_col, low_grad, hid, rank, top, cores)
    first_part = (keep + flip(give, 1, "sub").astype(F32)).astype(BF16)
    first_grad = jnp.sum(exchange(first_part, "ep").astype(F32), axis=0)

    grad_hidden, sums = finish_call(
        idx_col, target, prob_col, low_grad, hid, first_all, back, rank, top
    )
    return (
        grad_hidden.reshape(toks, top, units),
        over_rep(sums.reshape(toks, top)),
        first_grad.T[None],
        second_grad[None],
    )


def solution(mesh):
    return jax.shard_map(
        body,
        mesh=mesh,
        in_specs=(
            P(("grp", "ep", "sub"), "rep"),
            P(("grp", "ep", "sub"), None, "rep"),
            P(("grp", "ep", "sub"), None),
            P(("grp", "ep", "sub"), None),
            P(("ep", "sub"), None, "rep"),
            P(("grp", "ep", "sub"), "rep", None),
            P(("grp", "ep", "sub"), None, "rep"),
        ),
        out_specs=(
            P(("grp", "ep", "sub"), None, "rep"),
            P(("grp", "ep", "sub"), None),
            P(("grp", "ep", "sub"), "rep", None),
            P(("grp", "ep", "sub"), None, "rep"),
        ),
        check_vma=False,
    )
```

```python
import functools

import jax
import jax.numpy as jnp
from jax import lax
from jax.experimental import pallas as pl
from jax.experimental.pallas import tpu as pltpu
from jax.sharding import PartitionSpec as P

adapter_scale = 2.0
BF16 = jnp.bfloat16
F32 = jnp.float32
NT = (((1,), (1,)), ((), ()))
TN = (((0,), (0,)), ((), ()))
NN = (((1,), (0,)), ((), ()))


def dot(a, b, dims):
    return lax.dot_general(a, b, dims, preferred_element_type=F32)


def params(mib=16):
    return pltpu.CompilerParams(vmem_limit_bytes=mib * 2**20)


SMALL = pl.CostEstimate(flops=1, bytes_accessed=1, transcendentals=0)


def whole(shape):
    return pl.BlockSpec(shape, lambda *_: (0,) * len(shape))


def expert_mask(idx_col, width, rank):
    column = lax.broadcasted_iota(jnp.int32, (idx_col.shape[0], width), 1) // rank
    return column == idx_col


def spread_pairs(dense, top):
    toks, width = dense.shape
    return jnp.broadcast_to(dense[:, None, :], (toks, top, width)).reshape(toks * top, width)


def lowrank_hid_kernel(rank, top, idx_ref, hid_ref, first_ref, out_ref):
    wide = dot(hid_ref[...], first_ref[...], NT)
    wide = jnp.where(expert_mask(idx_ref[...], wide.shape[1], rank), wide, 0.0)
    out_ref[...] = wide.reshape(wide.shape[0] // top, top, wide.shape[1]).sum(axis=1)


def lowrank_hid_call(idx_col, hid, first_all, rank, top):
    pairs, units = hid.shape
    width = first_all.shape[0]
    blk = pairs // 4
    return pl.pallas_call(
        functools.partial(lowrank_hid_kernel, rank, top),
        grid=(4,),
        in_specs=[
            pl.BlockSpec((blk, 1), lambda i: (i, 0)),
            pl.BlockSpec((blk, units), lambda i: (i, 0)),
            whole((width, units)),
        ],
        out_specs=pl.BlockSpec((blk // top, width), lambda i: (i, 0)),
        out_shape=jax.ShapeDtypeStruct((pairs // top, width), F32),
        compiler_params=params(),
        cost_estimate=SMALL,
        name="lowrank_hid",
    )(idx_col, hid, first_all)


def expert_rows_kernel(slots, tiles, shares, batch, feats, route_row, at_ref, *rest):
    grads, second_ref, weight_ref = rest[:batch], rest[batch], rest[batch + 1]
    outs, low_ref, rows_ref = rest[-2 - shares : -2], rest[-2], rest[-1]
    step = pl.program_id(0)

    @pl.when(step == 0)
    def _():
        toks = grads[0].shape[0]
        before = lax.broadcasted_iota(jnp.int32, (toks, toks), 0) < lax.broadcasted_iota(
            jnp.int32, (toks, toks), 1
        )
        before = jnp.where(before, 1.0, 0.0).astype(BF16)
        slot = lax.broadcasted_iota(jnp.int32, (slots, toks), 0).astype(F32)
        for k, grad_ref in enumerate(grads):
            routes = grad_ref[pl.ds(route_row, 16), pl.ds(feats, toks)].astype(F32)
            hits = jnp.where(routes == at_ref[1].astype(F32), 1.0, 0.0)
            mine = jnp.max(hits, axis=0, keepdims=True)
            pos = dot(jnp.broadcast_to(mine, (16, toks)).astype(BF16), before, NN)[:1]
            pick = jnp.where((slot == pos) & (mine > 0.0), 1.0, 0.0).astype(BF16)
            grad = grad_ref[:, pl.ds(0, feats)]
            rows_ref[pl.ds(k * slots, slots), :] = dot(pick, grad, NN).astype(BF16)
            low_ref[k] = dot(second_ref[...], grad, NT).astype(BF16)

    value = dot(rows_ref[...], weight_ref[...], NT).astype(BF16)
    for k, out_ref in enumerate(outs):

        @pl.when(step // tiles == k)
        def _():
            out_ref[...] = value


def expert_rows_call(at, grads, second, down, shares, slots, after):
    batch, (toks, wide) = len(grads), grads[0].shape
    rank, feats = second.shape
    units = down.shape[0] // shares
    tiles = 3
    tile = units // tiles
    rows = batch * slots

    def weight_at(i, at):
        return (lax.rem(at[0] + i // tiles + 1, shares) * tiles + lax.rem(i, tiles), 0)

    def out_at(k, i, at):
        return (0, jnp.clip(i - k * tiles, 0, tiles - 1))

    return pl.pallas_call(
        functools.partial(expert_rows_kernel, slots, tiles, shares, batch, feats, 3 * rank),
        grid_spec=pltpu.PrefetchScalarGridSpec(
            num_scalar_prefetch=1,
            grid=(shares * tiles,),
            in_specs=[whole((toks, wide))] * batch
            + [whole((rank, feats)), pl.BlockSpec((tile, feats), weight_at)]
            + [pl.BlockSpec(memory_space=pl.ANY)] * len(after),
            out_specs=[
                pl.BlockSpec((rows, tile), functools.partial(out_at, k)) for k in range(shares)
            ]
            + [whole((batch, rank, toks))],
            scratch_shapes=[pltpu.VMEM((rows, feats), BF16)],
        ),
        out_shape=[jax.ShapeDtypeStruct((rows, units), BF16)] * shares
        + [jax.ShapeDtypeStruct((batch, rank, toks), BF16)],
        compiler_params=params(),
        cost_estimate=SMALL,
        name="expert_rows",
    )(at, *grads, second, down, *after)


def share_sum_kernel(parts, *refs):
    outs = refs[parts:]
    slots = outs[0].shape[0]
    for k, out_ref in enumerate(outs):
        at = pl.ds(k * slots, slots)
        total = refs[0][at, :].astype(F32)
        for part in refs[1:parts]:
            total = total + part[at, :].astype(F32)
        out_ref[...] = total.astype(BF16)


def share_sum_call(parts, batch):
    rows, units = parts[0].shape
    return pl.pallas_call(
        functools.partial(share_sum_kernel, len(parts)),
        out_shape=[jax.ShapeDtypeStruct((rows // batch, units), BF16)] * batch,
        compiler_params=params(),
        cost_estimate=SMALL,
        name="share_sum",
    )(*parts)


def collect_kernel(parts, me_ref, *refs):
    low_ref, first_ref = refs[-2:]
    rank = first_ref.shape[1]
    at = 0
    for ref in refs[:parts]:
        for k in range(ref.shape[0]):
            low_ref[lax.bitwise_xor(me_ref[0], at)] = ref[k]
            at += 1
    for r, ref in enumerate(refs[parts:-2]):
        wide = ref.shape[1]
        for k in range(3):
            first_ref[lax.bitwise_xor(me_ref[0], r), :, pl.ds(k * wide, wide)] = ref[
                pl.ds(k * rank, rank), :
            ]


def collect_call(me_at, lows, grads, feats):
    owners, (toks, wide) = len(grads), grads[0].shape
    rank = lows[0].shape[1]
    extra = wide - feats
    low_shape, first_shape = (owners, rank, toks), (owners, rank, 3 * extra)
    return pl.pallas_call(
        functools.partial(collect_kernel, len(lows)),
        grid_spec=pltpu.PrefetchScalarGridSpec(
            num_scalar_prefetch=1,
            grid=(1,),
            in_specs=[whole(b.shape) for b in lows]
            + [pl.BlockSpec((toks, extra), lambda i, me: (0, feats // extra))] * owners,
            out_specs=[whole(low_shape), whole(first_shape)],
        ),
        out_shape=[
            jax.ShapeDtypeStruct(low_shape, BF16),
            jax.ShapeDtypeStruct(first_shape, BF16),
        ],
        compiler_params=params(),
        cost_estimate=SMALL,
        name="collect_blocks",
    )(me_at, *lows, *grads)


def second_grad_kernel(me_ref, scaled_ref, *refs):
    out_ref = refs[-1]
    total = jnp.zeros(out_ref.shape, F32)
    for r, grad_ref in enumerate(refs[:-1]):
        total = total + dot(scaled_ref[lax.bitwise_xor(me_ref[0], r)], grad_ref[...], NN)
    out_ref[...] = adapter_scale * total


def second_grad_call(me_at, scaled, grads, feats):
    owners, rank, toks = scaled.shape
    steps = 4
    tile = feats // steps
    return pl.pallas_call(
        second_grad_kernel,
        grid_spec=pltpu.PrefetchScalarGridSpec(
            num_scalar_prefetch=1,
            grid=(steps,),
            in_specs=[whole((owners, rank, toks))]
            + [pl.BlockSpec((toks, tile), lambda i, me: (0, i))] * owners,
            out_specs=pl.BlockSpec((rank, tile), lambda i, me: (0, i)),
        ),
        out_shape=jax.ShapeDtypeStruct((rank, feats), F32),
        compiler_params=params(),
        cost_estimate=SMALL,
        name="second_grad",
    )(me_at, scaled, *grads)


def first_grad_kernel(rank, top, steps, cores, sub_ref, idx_ref, prob_ref, low_ref, hid_ref, *rest):
    outs, sum_ref = rest[:cores], rest[cores]
    step = pl.program_id(0)
    low = spread_pairs(low_ref[...], top)
    keep = expert_mask(idx_ref[...], low.shape[1], rank)
    scaled = jnp.where(keep, low * prob_ref[...], 0.0).astype(BF16)
    part = adapter_scale * dot(scaled, hid_ref[...], TN)
    part = part.reshape(sum_ref.shape)

    @pl.when(step == 0)
    def _():
        sum_ref[...] = part

    @pl.when(step > 0)
    def _():
        sum_ref[...] += part

    @pl.when(step == steps - 1)
    def _():
        for k, out_ref in enumerate(outs):
            out_ref[...] = sum_ref[:, lax.rem(sub_ref[0] + k, cores)].astype(out_ref.dtype)


def first_grad_call(sub_at, idx_col, prob_col, low, hid, rank, top, cores):
    pairs, units = hid.shape
    width = low.shape[1]
    steps = 4
    blk = pairs // steps
    shape = (width // rank // cores, rank, units)
    return pl.pallas_call(
        functools.partial(first_grad_kernel, rank, top, steps, cores),
        grid_spec=pltpu.PrefetchScalarGridSpec(
            num_scalar_prefetch=1,
            grid=(steps,),
            in_specs=[
                pl.BlockSpec((blk, 1), lambda i, s: (i, 0)),
                pl.BlockSpec((blk, 1), lambda i, s: (i, 0)),
                pl.BlockSpec((blk // top, width), lambda i, s: (i, 0)),
                pl.BlockSpec((blk, units), lambda i, s: (i, 0)),
            ],
            out_specs=[whole(shape)] * cores,
            scratch_shapes=[pltpu.VMEM((shape[0], cores) + shape[1:], F32)],
        ),
        out_shape=[jax.ShapeDtypeStruct(shape, F32)]
        + [jax.ShapeDtypeStruct(shape, BF16)] * (cores - 1),
        compiler_params=params(),
        cost_estimate=SMALL,
        name="first_grad",
    )(sub_at, idx_col, prob_col, low, hid)


def finish_kernel(rank, top, count, idx_ref, target_ref, prob_ref, low_ref, hid_ref, first_ref, *rest):
    back, out_ref, sum_ref, all_ref = rest[:count], rest[count], rest[count + 1], rest[count + 2]
    slots = back[0].shape[0]
    pairs = hid_ref.shape[0]

    @pl.when(pl.program_id(0) == 0)
    def _():
        for r, ref in enumerate(back):
            all_ref[pl.ds(r * slots, slots), :] = ref[...]

    low = spread_pairs(low_ref[...], top)
    keep = expert_mask(idx_ref[...], low.shape[1], rank)
    low = jnp.where(keep, adapter_scale * low.astype(BF16).astype(F32), 0.0).astype(BF16)
    slot = lax.broadcasted_iota(jnp.int32, (pairs, count * slots), 1)
    pick = jnp.where(slot == target_ref[...], 1.0, 0.0).astype(BF16)
    value = dot(pick, all_ref[...], NN) + dot(low, first_ref[...], NN)
    value = value.astype(BF16).astype(F32)
    out_ref[...] = (value * prob_ref[...]).astype(BF16)
    sum_ref[...] = jnp.sum(value * hid_ref[...].astype(F32), axis=1, keepdims=True)


def finish_call(idx_col, target, prob_col, low, hid, first_all, back, rank, top):
    pairs, units = hid.shape
    width = low.shape[1]
    slots, part = back[0].shape
    blk = pairs // 4
    return pl.pallas_call(
        functools.partial(finish_kernel, rank, top, len(back)),
        grid=(4,),
        in_specs=[
            pl.BlockSpec((blk, 1), lambda i: (i, 0)),
            pl.BlockSpec((blk, 1), lambda i: (i, 0)),
            pl.BlockSpec((blk, 1), lambda i: (i, 0)),
            pl.BlockSpec((blk // top, width), lambda i: (i, 0)),
            pl.BlockSpec((blk, units), lambda i: (i, 0)),
            whole((width, units)),
        ]
        + [whole((slots, part))] * len(back),
        out_specs=[
            pl.BlockSpec((blk, units), lambda i: (i, 0)),
            pl.BlockSpec((blk, 1), lambda i: (i, 0)),
        ],
        out_shape=[
            jax.ShapeDtypeStruct((pairs, units), BF16),
            jax.ShapeDtypeStruct((pairs, 1), F32),
        ],
        scratch_shapes=[pltpu.VMEM((len(back) * slots, units), BF16)],
        compiler_params=params(),
        cost_estimate=SMALL,
        name="finish",
    )(idx_col, target, prob_col, low, hid, first_all, *back)


def body(grad, hidden, index, weight, down, first, second):
    toks, top = index.shape
    exp_local, units_all, feats = down.shape
    assert exp_local == 1
    units, rank = first.shape[1:]
    where = ("ep", "sub")
    groups, cores, shares = lax.axis_size("ep"), lax.axis_size("sub"), lax.axis_size("rep")
    owners = groups * cores
    assert cores == 2 and groups & (groups - 1) == 0
    cap = min(toks, 5 * toks * top // (4 * owners))
    slots = -(-cap // 16) * 16
    pairs = toks * top
    width = owners * rank
    me = lax.axis_index(where).astype(jnp.int32)
    me_at = me.reshape(1)
    sub_at = lax.axis_index("sub").astype(jnp.int32).reshape(1)

    def turn(x, offset):
        return lax.ppermute(x, "rep", [(r, (r + offset) % shares) for r in range(shares)])

    def over_rep(x):
        return x + turn(x, 1) if shares == 2 else lax.psum(x, "rep")

    def flip(x, mask, axis="ep"):
        size = groups if axis == "ep" else cores if axis == "sub" else owners
        return lax.ppermute(x, axis, [(i, i ^ mask) for i in range(size)])

    def exchange(x, axes=where):
        return lax.all_to_all(x, axes, split_axis=0, concat_axis=0, tiled=True)

    extra = units // 3
    factor = first[0].T
    routes = jnp.pad(
        index.T.astype(BF16),
        ((0, toks - 3 * rank - top), (0, extra - toks)),
        constant_values=-1,
    )
    columns = jnp.concatenate([factor[:, k * extra : (k + 1) * extra] for k in range(3)] + [routes])
    blocks = {0: jnp.concatenate([grad, columns], axis=1)}
    for o in sorted(range(1, groups), key=lambda o: (o.bit_count(), o)):
        last = o & -o
        blocks[o] = flip(blocks[o ^ last], last)

    at = jnp.stack([lax.axis_index("rep").astype(jnp.int32), me])
    back, grads, low_parts, after = [], [], [], [[], []]
    for o in range(0, groups, 2):
        batch = [blocks[o], flip(blocks[o], 1, "sub"), blocks[o + 1], flip(blocks[o + 1], 1, "sub")]
        *give, keep, low = expert_rows_call(
            at, batch, second[0], down[0], shares, slots, after[-2]
        )
        parts = [keep] + [turn(x, k + 1) for k, x in enumerate(give)]
        sums = share_sum_call(parts, 4)
        for k, rows in enumerate(sums):
            r = 2 * o + k
            back.append(flip(rows, r, where) if r else rows)
        grads += batch
        low_parts.append(low)
        after.append(sums[:1])

    hid = hidden.reshape(pairs, units)
    idx_col = index.reshape(pairs, 1)
    prob_col = weight.reshape(pairs, 1).astype(F32)
    hits = index[:, :, None] == jnp.arange(owners, dtype=jnp.int32)
    hit = jnp.any(hits, axis=1)
    before = jnp.tril(jnp.ones((toks, toks), BF16), -1)
    place = jnp.dot(before, hit.astype(BF16), preferred_element_type=F32).astype(jnp.int32)
    place = place + slots * lax.bitwise_xor(me, jnp.arange(owners, dtype=jnp.int32))
    target = jnp.sum(jnp.where(hits, place[:, None, :], 0), axis=2).reshape(pairs, 1)
    prob_dense = jnp.sum(jnp.where(hits, weight[:, :, None].astype(F32), 0.0), axis=1)

    low_grad, first_all = collect_call(me_at, low_parts, grads, feats)
    first_all = first_all.reshape(width, units)
    low_hid = over_rep(lowrank_hid_call(idx_col, hid, first_all, rank, top))
    scaled_hid = (low_hid * jnp.repeat(prob_dense, rank, axis=1)).astype(BF16)
    scaled_hid = exchange(scaled_hid.T.reshape(owners, rank, toks))
    second_grad = second_grad_call(me_at, scaled_hid, grads, feats)

    low_grad = exchange(low_grad)
    low_grad = over_rep(low_grad.reshape(width, toks).T.astype(F32))

    keep, give = first_grad_call(sub_at, idx_col, prob_col, low_grad, hid, rank, top, cores)
    first_part = (keep + flip(give, 1, "sub").astype(F32)).astype(BF16)
    first_grad = jnp.sum(exchange(first_part, "ep").astype(F32), axis=0)

    grad_hidden, sums = finish_call(
        idx_col, target, prob_col, low_grad, hid, first_all, back, rank, top
    )
    return (
        grad_hidden.reshape(toks, top, units),
        over_rep(sums.reshape(toks, top)),
        first_grad.T[None],
        second_grad[None],
    )


def solution(mesh):
    return jax.shard_map(
        body,
        mesh=mesh,
        in_specs=(
            P(("grp", "ep", "sub"), "rep"),
            P(("grp", "ep", "sub"), None, "rep"),
            P(("grp", "ep", "sub"), None),
            P(("grp", "ep", "sub"), None),
            P(("ep", "sub"), None, "rep"),
            P(("grp", "ep", "sub"), "rep", None),
            P(("grp", "ep", "sub"), None, "rep"),
        ),
        out_specs=(
            P(("grp", "ep", "sub"), None, "rep"),
            P(("grp", "ep", "sub"), None),
            P(("grp", "ep", "sub"), "rep", None),
            P(("grp", "ep", "sub"), None, "rep"),
        ),
        check_vma=False,
    )
```

```python
import functools

import jax
import jax.numpy as jnp
from jax import lax
from jax.experimental import pallas as pl
from jax.experimental.pallas import tpu as pltpu
from jax.sharding import PartitionSpec as P

adapter_scale = 2.0
BF16 = jnp.bfloat16
F32 = jnp.float32
NT = (((1,), (1,)), ((), ()))
TN = (((0,), (0,)), ((), ()))
NN = (((1,), (0,)), ((), ()))
PARAMS = pltpu.CompilerParams(vmem_limit_bytes=20 * 2**20)
SMALL = pl.CostEstimate(flops=1, bytes_accessed=1, transcendentals=0)
ANY = pl.BlockSpec(memory_space=pl.ANY)


def dot(a, b, dims):
    return lax.dot_general(a, b, dims, preferred_element_type=F32)


def iota(shape, axis):
    return lax.broadcasted_iota(jnp.int32, shape, axis)


def whole(shape):
    return pl.BlockSpec(shape, lambda *_: (0,) * len(shape))


def call(kernel, name, at, arrays, in_specs, outs, out_specs, grid=(1,), scratch=()):
    return pl.pallas_call(
        kernel,
        grid_spec=pltpu.PrefetchScalarGridSpec(
            num_scalar_prefetch=1,
            grid=grid,
            in_specs=in_specs,
            out_specs=out_specs,
            scratch_shapes=scratch,
        ),
        out_shape=[jax.ShapeDtypeStruct(*o) for o in outs],
        compiler_params=PARAMS,
        cost_estimate=SMALL,
        name=name,
    )(at, *arrays)


def relative(at_ref, index, groups):
    o = lax.bitwise_xor(lax.shift_right_logical(index, 1), at_ref[1])
    q = lax.bitwise_xor(lax.bitwise_and(index, 1), at_ref[2])
    return q * groups + o


def spread_pairs(dense, top):
    toks, width = dense.shape
    return jnp.broadcast_to(dense[:, None, :], (toks, top, width)).reshape(toks * top, width)


def diagonal(pairs, top):
    return iota((pairs, top), 1) == lax.bitwise_and(iota((pairs, top), 0), top - 1)


def pair_column(table):
    toks, top = table.shape
    wide = spread_pairs(table, top)
    return jnp.sum(jnp.where(diagonal(toks * top, top), wide, 0.0), axis=1, keepdims=True)


def expert_mask(column, width, rank):
    return iota((column.shape[0], width), 1) // rank == column.astype(jnp.int32)


def pack_kernel(rank, at_ref, grad_ref, first_ref, index_ref, out_ref):
    toks, feats = grad_ref.shape
    extra = out_ref.shape[1] - feats
    out_ref[:, pl.ds(0, feats)] = grad_ref[...]
    same = jnp.where(iota((rank, rank), 0) == iota((rank, rank), 1), 1.0, 0.0).astype(BF16)
    factor = dot(same, first_ref[...], NT).astype(BF16)
    for k in range(3):
        piece = factor[:, k * extra : (k + 1) * extra]
        out_ref[pl.ds(k * rank, rank), pl.ds(feats, extra)] = piece
    top = index_ref.shape[1]
    out_ref[pl.ds(3 * rank, toks - 3 * rank), pl.ds(feats, extra)] = jnp.full(
        (toks - 3 * rank, extra), -1.0, BF16
    )
    turn = jnp.where(iota((16, top), 0) == iota((16, top), 1), 1.0, 0.0).astype(BF16)
    routes = dot(turn, index_ref[...].astype(F32).astype(BF16), NT)
    routes = jnp.where(iota((16, toks), 0) < top, routes, -1.0)
    out_ref[pl.ds(3 * rank, 16), pl.ds(feats, toks)] = routes.astype(BF16)


def pack_call(at, grad, first, index):
    (toks, feats), (units, rank) = grad.shape, first.shape
    extra = units // 3
    shape = (toks, feats + extra)
    return call(
        functools.partial(pack_kernel, rank),
        "pack_block",
        at,
        [grad, first, index],
        [whole(grad.shape), whole(first.shape), whole(index.shape)],
        [(shape, BF16)],
        [whole(shape)],
    )[0]


def expert_rows_kernel(slots, tiles, shares, batch, feats, route_row, at_ref, *rest):
    grads, seconds, weights = rest[:batch], rest[batch : batch + 2], rest[batch + 2 : batch + 4]
    outs, low_ref, rows_ref = rest[-2 - shares : -2], rest[-2], rest[-1]
    step = pl.program_id(0)

    @pl.when(step == 0)
    def _():
        toks = grads[0].shape[0]
        before = jnp.where(iota((toks, toks), 0) < iota((toks, toks), 1), 1.0, 0.0).astype(BF16)
        slot = iota((slots, toks), 0).astype(F32)
        second = jnp.concatenate([ref[...] for ref in seconds], axis=0)
        for k, grad_ref in enumerate(grads):
            routes = grad_ref[pl.ds(route_row, 16), pl.ds(feats, toks)].astype(F32)
            picks = []
            for q in range(2):
                expert = at_ref[1] * 2 + lax.bitwise_xor(at_ref[2], q)
                hits = jnp.where(routes == expert.astype(F32), 1.0, 0.0)
                mine = jnp.max(hits, axis=0, keepdims=True)
                pos = dot(jnp.broadcast_to(mine, (16, toks)).astype(BF16), before, NN)[:1]
                picks.append(jnp.where((slot == pos) & (mine > 0.0), 1.0, 0.0).astype(BF16))
            grad = grad_ref[:, pl.ds(0, feats)]
            rows = dot(jnp.concatenate(picks, axis=0), grad, NN).astype(BF16)
            for q in range(2):
                rows_ref[q, pl.ds(k * slots, slots), :] = rows[q * slots : (q + 1) * slots]
            low_ref[k] = dot(second, grad, NT).astype(BF16)

    turn = step // tiles
    tile = weights[0].shape[0]
    column = pl.ds(pl.multiple_of(lax.rem(step, tiles) * tile, 128), tile)
    for q in range(2):

        @pl.when(lax.rem(turn, 2) == q)
        def _():
            value = dot(rows_ref[q], weights[q][...], NT).astype(BF16)
            for k, out_ref in enumerate(outs):

                @pl.when(turn // 2 == k)
                def _():
                    out_ref[pl.ds(q * batch * slots, batch * slots), column] = value


def expert_rows_call(at, grads, seconds, downs, shares, slots, after):
    batch, (toks, wide) = len(grads), grads[0].shape
    rank, feats = seconds[0].shape
    units = downs[0].shape[0] // shares
    tiles = 3
    tile = units // tiles
    rows = 2 * batch * slots

    def weight_at(q, i, at):
        share = lax.rem(at[0] + i // (2 * tiles) + 1, shares)
        turn = lax.rem(i // tiles, 2)
        idle = (tiles - 1) * (1 - q)
        return (share * tiles + jnp.where(turn == q, lax.rem(i, tiles), idle), 0)

    return call(
        functools.partial(expert_rows_kernel, slots, tiles, shares, batch, feats, 3 * rank),
        "expert_rows",
        at,
        [*grads, *seconds, *downs, *after],
        [whole((toks, wide))] * batch
        + [whole((rank, feats))] * 2
        + [pl.BlockSpec((tile, feats), functools.partial(weight_at, q)) for q in range(2)]
        + [ANY] * len(after),
        [((rows, units), BF16)] * shares + [((batch, 2 * rank, toks), BF16)],
        [whole((rows, units))] * shares + [whole((batch, 2 * rank, toks))],
        grid=(shares * 2 * tiles,),
        scratch=[pltpu.VMEM((2, batch * slots, feats), BF16)],
    )


def share_sum_kernel(parts, slots, at_ref, *refs):
    outs = refs[parts:]
    for k, out_ref in enumerate(outs):
        for q in range(2):
            at = pl.ds((q * len(outs) + k) * slots, slots)
            total = refs[0][at, :].astype(F32)
            for part in refs[1:parts]:
                total = total + part[at, :].astype(F32)
            out_ref[pl.ds(q * slots, slots), :] = total.astype(BF16)


def share_sum_call(at, parts, batch, slots):
    rows, units = parts[0].shape
    shape = (2 * slots, units)
    return call(
        functools.partial(share_sum_kernel, len(parts), slots),
        "share_sum",
        at,
        parts,
        [whole((rows, units))] * len(parts),
        [(shape, BF16)] * batch,
        [whole(shape)] * batch,
    )


def collect_kernel(parts, at_ref, *refs):
    low_ref, first_ref = refs[-2:]
    rank = first_ref.shape[1]
    o = 0
    for ref in refs[:parts]:
        for k in range(ref.shape[0]):
            low_ref[lax.bitwise_xor(at_ref[1], o)] = ref[k]
            o += 1
    for o, ref in enumerate(refs[parts:-2]):
        wide = ref.shape[1]
        for k in range(3):
            first_ref[o, :, pl.ds(k * wide, wide)] = ref[pl.ds(k * rank, rank), :]


def collect_call(at, lows, grads, feats):
    groups, (toks, wide) = len(grads), grads[0].shape
    rank = lows[0].shape[1] // 2
    extra = wide - feats
    low_shape, first_shape = (groups, 2 * rank, toks), (groups, rank, 3 * extra)
    return call(
        functools.partial(collect_kernel, len(lows)),
        "collect_blocks",
        at,
        [*lows, *grads],
        [whole(b.shape) for b in lows]
        + [pl.BlockSpec((toks, extra), lambda i, at: (0, feats // extra))] * groups,
        [(low_shape, BF16), (first_shape, BF16)],
        [whole(low_shape), whole(first_shape)],
    )


def low_dense_kernel(at_ref, *refs):
    out_ref, sum_ref = refs[-2:]
    groups, both, _ = refs[0].shape
    rank = both // 2
    for o in range(groups):
        total = refs[0][lax.bitwise_xor(at_ref[1], o)].astype(F32)
        for ref in refs[1:-2]:
            total = total + ref[lax.bitwise_xor(at_ref[1], o)].astype(F32)
        for q in range(2):
            at = pl.ds((q * groups + o) * rank, rank)
            sum_ref[at, :] = total[q * rank : (q + 1) * rank]
    out_ref[...] = sum_ref[...].T


def low_dense_call(at, parts):
    groups, both, toks = parts[0].shape
    shape = (toks, groups * both)
    return call(
        low_dense_kernel,
        "low_dense",
        at,
        parts,
        [whole(parts[0].shape)] * len(parts),
        [(shape, F32)],
        [whole(shape)],
        scratch=[pltpu.VMEM((groups * both, toks), F32)],
    )[0]


def lowrank_hid_kernel(groups, at_ref, index_ref, hid_ref, *rest):
    firsts, out_ref = rest[:2], rest[2]
    top = index_ref.shape[1]
    rank = firsts[0].shape[0] // groups
    wide = jnp.concatenate([dot(hid_ref[...], ref[...], NT) for ref in firsts], axis=1)
    column = pair_column(relative(at_ref, index_ref[...], groups).astype(F32))
    wide = jnp.where(expert_mask(column, wide.shape[1], rank), wide, 0.0)
    out_ref[...] = wide.reshape(wide.shape[0] // top, top, wide.shape[1]).sum(axis=1)


def lowrank_hid_call(at, index, hid, firsts, groups):
    (toks, top), (pairs, units) = index.shape, hid.shape
    half = firsts[0].shape[0]
    steps = 4
    return call(
        functools.partial(lowrank_hid_kernel, groups),
        "lowrank_hid",
        at,
        [index, hid, *firsts],
        [
            pl.BlockSpec((toks // steps, top), lambda i, at: (i, 0)),
            pl.BlockSpec((pairs // steps, units), lambda i, at: (i, 0)),
        ]
        + [whole((half, units))] * 2,
        [((toks, 2 * half), F32)],
        [pl.BlockSpec((toks // steps, 2 * half), lambda i, at: (i, 0))],
        grid=(steps,),
    )[0]


def scaled_hid_kernel(groups, rank, at_ref, index_ref, prob_ref, *refs):
    out_ref = refs[-1]
    total = refs[0][...]
    for ref in refs[1:-1]:
        total = total + ref[...]
    place = relative(at_ref, index_ref[...], groups)
    prob = prob_ref[...].astype(F32)
    expert = iota(total.shape, 1) // rank
    scale = jnp.zeros(total.shape, F32)
    for k in range(place.shape[1]):
        scale = jnp.where(expert == place[:, k : k + 1], prob[:, k : k + 1], scale)
    scaled = (total * scale).T.astype(BF16)
    for o in range(groups):
        for q in range(2):
            at = (q * groups + o) * rank
            out_ref[lax.bitwise_xor(at_ref[1], o), pl.ds(q * rank, rank), :] = scaled[at : at + rank]


def scaled_hid_call(at, index, prob, parts, groups):
    toks, width = parts[0].shape
    rank = width // groups // 2
    shape = (groups, 2 * rank, toks)
    return call(
        functools.partial(scaled_hid_kernel, groups, rank),
        "scaled_hid",
        at,
        [index, prob, *parts],
        [whole(index.shape), whole(prob.shape)] + [whole((toks, width))] * len(parts),
        [(shape, BF16)],
        [whole(shape)],
    )[0]


def second_grad_kernel(at_ref, scaled_ref, *refs):
    grads, outs = refs[:-2], refs[-2:]
    rank, tile = outs[0].shape
    total = jnp.zeros((2 * rank, tile), F32)
    for o, grad_ref in enumerate(grads):
        total = total + dot(scaled_ref[lax.bitwise_xor(at_ref[1], o)], grad_ref[...], NN)
    for q, out_ref in enumerate(outs):
        out_ref[...] = adapter_scale * total[q * rank : (q + 1) * rank]


def second_grad_call(at, scaled, grads, feats):
    groups, both, toks = scaled.shape
    steps = 4
    tile = feats // steps
    block = pl.BlockSpec((both // 2, tile), lambda i, at: (0, i))
    return call(
        second_grad_kernel,
        "second_grad",
        at,
        [scaled, *grads],
        [whole(scaled.shape)] + [pl.BlockSpec((toks, tile), lambda i, at: (0, i))] * groups,
        [((both // 2, feats), F32)] * 2,
        [block] * 2,
        grid=(steps,),
    )


def first_grad_kernel(groups, steps, at_ref, index_ref, prob_ref, low_ref, hid_ref, *rest):
    keep_ref, give_ref, sum_ref = rest
    step = pl.program_id(0)
    top = index_ref.shape[1]
    rank = keep_ref.shape[1]
    low = spread_pairs(low_ref[...], top)
    column = pair_column(relative(at_ref, index_ref[...], groups).astype(F32))
    keep = expert_mask(column, low.shape[1], rank)
    scaled = jnp.where(keep, low * pair_column(prob_ref[...].astype(F32)), 0.0).astype(BF16)
    part = adapter_scale * dot(scaled, hid_ref[...], TN)

    @pl.when(step == 0)
    def _():
        sum_ref[...] = part

    @pl.when(step > 0)
    def _():
        sum_ref[...] += part

    @pl.when(step == steps - 1)
    def _():
        for q, out_ref in enumerate((keep_ref, give_ref)):
            half = sum_ref[pl.ds(q * groups * rank, groups * rank), :]
            out_ref[...] = half.reshape(out_ref.shape).astype(out_ref.dtype)


def first_grad_call(at, index, prob, low, hid, groups):
    (toks, top), (pairs, units) = index.shape, hid.shape
    width = low.shape[1]
    steps = 4
    shape = (groups, width // groups // 2, units)
    return call(
        functools.partial(first_grad_kernel, groups, steps),
        "first_grad",
        at,
        [index, prob, low, hid],
        [
            pl.BlockSpec((toks // steps, top), lambda i, at: (i, 0)),
            pl.BlockSpec((toks // steps, top), lambda i, at: (i, 0)),
            pl.BlockSpec((toks // steps, width), lambda i, at: (i, 0)),
            pl.BlockSpec((pairs // steps, units), lambda i, at: (i, 0)),
        ],
        [(shape, F32), (shape, BF16)],
        [whole(shape)] * 2,
        grid=(steps,),
        scratch=[pltpu.VMEM((width, units), F32)],
    )


def first_sum_kernel(at_ref, keep_ref, got_ref, out_ref):
    for o in range(keep_ref.shape[0]):
        total = keep_ref[o] + got_ref[o].astype(F32)
        out_ref[lax.bitwise_xor(at_ref[1], o)] = total.astype(BF16)


def first_sum_call(at, keep, got):
    shape = keep.shape
    return call(
        first_sum_kernel,
        "first_sum",
        at,
        [keep, got],
        [whole(shape)] * 2,
        [(shape, BF16)],
        [whole(shape)],
    )[0]


def finish_kernel(count, slots, at_ref, index_all_ref, index_ref, prob_ref, low_ref, hid_ref, *rest):
    firsts, back = rest[:2], rest[2 : 2 + count]
    out_ref, sum_ref, all_ref, place_ref = rest[2 + count :]
    top = index_ref.shape[1]
    toks = index_all_ref.shape[0]
    experts = 2 * count

    @pl.when(pl.program_id(0) == 0)
    def _():
        for o, ref in enumerate(back):
            for q in range(2):
                all_ref[pl.ds((q * count + o) * slots, slots), :] = ref[pl.ds(q * slots, slots), :]
        experts_all = relative(at_ref, index_all_ref[...], count)
        hit = jnp.zeros((toks, experts), F32)
        for k in range(top):
            hit = jnp.where(iota((toks, experts), 1) == experts_all[:, k : k + 1], 1.0, hit)
        before = jnp.where(iota((toks, toks), 0) > iota((toks, toks), 1), 1.0, 0.0).astype(BF16)
        place_ref[...] = dot(before, hit.astype(BF16), NN)

    pairs = hid_ref.shape[0]
    some = index_ref.shape[0]
    column = pair_column(relative(at_ref, index_ref[...], count).astype(F32))
    place = spread_pairs(place_ref[pl.ds(pl.program_id(0) * some, some), :], top)
    mine = iota((pairs, experts), 1) == column.astype(jnp.int32)
    target = column * slots + jnp.sum(jnp.where(mine, place, 0.0), axis=1, keepdims=True)
    low = spread_pairs(low_ref[...], top)
    keep = expert_mask(column, low.shape[1], low.shape[1] // experts)
    low = jnp.where(keep, adapter_scale * low.astype(BF16).astype(F32), 0.0).astype(BF16)
    slot = iota((pairs, experts * slots), 1)
    pick = jnp.where(slot == target.astype(jnp.int32), 1.0, 0.0).astype(BF16)
    half = low.shape[1] // 2
    value = dot(pick, all_ref[...], NN)
    value = value + dot(low[:, :half], firsts[0][...], NN) + dot(low[:, half:], firsts[1][...], NN)
    value = value.astype(BF16).astype(F32)
    out_ref[...] = (value * pair_column(prob_ref[...].astype(F32))).astype(BF16)
    sums = jnp.sum(value * hid_ref[...].astype(F32), axis=1, keepdims=True)
    sums = jnp.where(diagonal(pairs, top), sums, 0.0)
    sum_ref[...] = sums.reshape(some, top, top).sum(axis=1)


def finish_call(at, index, prob, low, hid, firsts, back):
    (toks, top), (pairs, units) = index.shape, hid.shape
    width = low.shape[1]
    both = back[0].shape[0]
    steps = 4
    count = len(back)

    def rows(n, columns):
        return pl.BlockSpec((n // steps, columns), lambda i, at: (i, 0))

    return call(
        functools.partial(finish_kernel, count, both // 2),
        "finish",
        at,
        [index, index, prob, low, hid, *firsts, *back],
        [whole(index.shape), rows(toks, top), rows(toks, top), rows(toks, width), rows(pairs, units)]
        + [whole(firsts[0].shape)] * 2
        + [whole((both, units))] * count,
        [((pairs, units), BF16), ((toks, top), F32)],
        [rows(pairs, units), rows(toks, top)],
        grid=(steps,),
        scratch=[pltpu.VMEM((count * both, units), BF16), pltpu.VMEM((toks, 2 * count), F32)],
    )


def body(grad, hidden, index, weight, down, first, second):
    toks, top = index.shape
    exp_local, units_all, feats = down.shape
    units, rank = first.shape[1:]
    groups, cores, shares = lax.axis_size("ep"), lax.axis_size("sub"), lax.axis_size("rep")
    assert exp_local == 1 and cores == 2 and groups & (groups - 1) == 0
    cap = min(toks, 5 * toks * top // (4 * groups * cores))
    slots = -(-cap // 16) * 16
    pairs = toks * top
    at = jnp.stack([lax.axis_index(name).astype(jnp.int32) for name in ("rep", "ep", "sub")])

    def turn(x, offset):
        return lax.ppermute(x, "rep", [(r, (r + offset) % shares) for r in range(shares)])

    def all_shares(x):
        return [x] + [turn(x, k) for k in range(1, shares)]

    def flip(x, mask):
        return lax.ppermute(x, "ep", [(i, i ^ mask) for i in range(groups)])

    def swap(x):
        return lax.ppermute(x, "sub", [(0, 1), (1, 0)])

    def exchange(x):
        return lax.all_to_all(x, "ep", split_axis=0, concat_axis=0, tiled=True)

    blocks = [pack_call(at, grad, first[0], index)]
    for o in range(1, groups):
        last = o & -o
        blocks.append(flip(blocks[o ^ last], last))
        if last == o and o >= 4:
            blocks[o], blocks[o - 1] = lax.optimization_barrier((blocks[o], blocks[o - 1]))
    downs = [pltpu.with_memory_space_constraint(down[0], pltpu.HBM), swap(down[0])]
    seconds = [second[0], swap(second[0])]

    back, lows, after = [], [], [[], []]
    for o in range(0, groups, 2):
        *give, keep, low = expert_rows_call(
            at, blocks[o : o + 2], seconds, downs, shares, slots, after[-2]
        )
        parts = [keep] + [turn(x, k + 1) for k, x in enumerate(give)]
        sums = share_sum_call(at, parts, 2, slots)
        back += [flip(rows, o + k) if o + k else rows for k, rows in enumerate(sums)]
        lows.append(low)
        after.append(sums[:1])

    hid = hidden.reshape(pairs, units)
    low_grad, first_own = collect_call(at, lows, blocks, feats)
    firsts = [x.reshape(groups * rank, units) for x in (first_own, swap(first_own))]

    low_hid = all_shares(lowrank_hid_call(at, index, hid, firsts, groups))
    scaled_hid = exchange(scaled_hid_call(at, index, weight, low_hid, groups))
    second_keep, second_give = second_grad_call(at, scaled_hid, blocks, feats)
    second_grad = second_keep + swap(second_give)

    low_grad = low_dense_call(at, all_shares(exchange(low_grad)))
    first_keep, first_give = first_grad_call(at, index, weight, low_grad, hid, groups)
    first_part = exchange(first_sum_call(at, first_keep, swap(first_give)))
    first_grad = jnp.sum(first_part.astype(F32), axis=0)

    grad_hidden, sums = finish_call(at, index, weight, low_grad, hid, firsts, back)
    sums = sums + turn(sums, 1) if shares == 2 else lax.psum(sums, "rep")
    return (
        grad_hidden.reshape(toks, top, units),
        sums,
        first_grad.T[None],
        second_grad[None],
    )


def solution(mesh):
    return jax.shard_map(
        body,
        mesh=mesh,
        in_specs=(
            P(("grp", "ep", "sub"), "rep"),
            P(("grp", "ep", "sub"), None, "rep"),
            P(("grp", "ep", "sub"), None),
            P(("grp", "ep", "sub"), None),
            P(("ep", "sub"), None, "rep"),
            P(("grp", "ep", "sub"), "rep", None),
            P(("grp", "ep", "sub"), None, "rep"),
        ),
        out_specs=(
            P(("grp", "ep", "sub"), None, "rep"),
            P(("grp", "ep", "sub"), None),
            P(("grp", "ep", "sub"), "rep", None),
            P(("grp", "ep", "sub"), None, "rep"),
        ),
        check_vma=False,
    )
```

```python
import functools

import jax
import jax.numpy as jnp
from jax import lax
from jax.experimental import pallas as pl
from jax.experimental.pallas import tpu as pltpu
from jax.sharding import PartitionSpec as P

adapter_scale = 2.0
CHUNKS = 3
BF16 = jnp.bfloat16
F32 = jnp.float32
NT = (((1,), (1,)), ((), ()))
TN = (((0,), (0,)), ((), ()))
NN = (((1,), (0,)), ((), ()))
PARAMS = pltpu.CompilerParams(vmem_limit_bytes=40 * 2**20)
SMALL = pl.CostEstimate(flops=1, bytes_accessed=1, transcendentals=0)
ANY = pl.BlockSpec(memory_space=pl.ANY)


def dot(a, b, dims):
    return lax.dot_general(a, b, dims, preferred_element_type=F32)


def in_hbm(x):
    return pltpu.with_memory_space_constraint(x, pltpu.HBM)


def iota(shape, axis):
    return lax.broadcasted_iota(jnp.int32, shape, axis)


def whole(shape):
    return pl.BlockSpec(shape, lambda *_: (0,) * len(shape))


def call(kernel, name, at, arrays, in_specs, outs, out_specs, grid=(1,), scratch=()):
    return pl.pallas_call(
        kernel,
        grid_spec=pltpu.PrefetchScalarGridSpec(
            num_scalar_prefetch=1,
            grid=grid,
            in_specs=in_specs,
            out_specs=out_specs,
            scratch_shapes=scratch,
        ),
        out_shape=[jax.ShapeDtypeStruct(*o) for o in outs],
        compiler_params=PARAMS,
        cost_estimate=SMALL,
        name=name,
    )(at, *arrays)


def relative(at_ref, index, groups):
    o = lax.shift_right_logical(index, 1)
    q = lax.bitwise_xor(lax.bitwise_and(index, 1), at_ref[2])
    return q * groups + o


def spread_pairs(dense, top):
    toks, width = dense.shape
    return jnp.broadcast_to(dense[:, None, :], (toks, top, width)).reshape(toks * top, width)


def diagonal(pairs, top):
    return iota((pairs, top), 1) == lax.bitwise_and(iota((pairs, top), 0), top - 1)


def pair_column(table):
    toks, top = table.shape
    wide = spread_pairs(table, top)
    return jnp.sum(jnp.where(diagonal(toks * top, top), wide, 0.0), axis=1, keepdims=True)


def expert_mask(column, width, rank):
    return iota((column.shape[0], width), 1) // rank == column.astype(jnp.int32)


def pack_kernel(rank, at_ref, grad_ref, first_ref, index_ref, out_ref):
    toks, feats = grad_ref.shape
    extra = out_ref.shape[1] - feats
    out_ref[:, pl.ds(0, feats)] = grad_ref[...]
    same = jnp.where(iota((rank, rank), 0) == iota((rank, rank), 1), 1.0, 0.0).astype(BF16)
    factor = dot(same, first_ref[...], NT).astype(BF16)
    for k in range(3):
        piece = factor[:, k * extra : (k + 1) * extra]
        out_ref[pl.ds(k * rank, rank), pl.ds(feats, extra)] = piece
    top = index_ref.shape[1]
    out_ref[pl.ds(3 * rank, toks - 3 * rank), pl.ds(feats, extra)] = jnp.full(
        (toks - 3 * rank, extra), -1.0, BF16
    )
    turn = jnp.where(iota((16, top), 0) == iota((16, top), 1), 1.0, 0.0).astype(BF16)
    routes = dot(turn, index_ref[...].astype(F32).astype(BF16), NT)
    routes = jnp.where(iota((16, toks), 0) < top, routes, -1.0)
    out_ref[pl.ds(3 * rank, 16), pl.ds(feats, toks)] = routes.astype(BF16)


def pack_call(at, grad, first, index):
    (toks, feats), (units, rank) = grad.shape, first.shape
    extra = units // 3
    shape = (toks, feats + extra)
    return call(
        functools.partial(pack_kernel, rank),
        "pack_block",
        at,
        [grad, first, index],
        [whole(grad.shape), whole(first.shape), whole(index.shape)],
        [(shape, BF16)],
        [whole(shape)],
    )[0]


def weight_copies(chunk, chunks, at_ref, downs, tiles_ref, sems):
    _, shares, units, _ = tiles_ref.shape
    copies = []
    for q in range(2):
        for k in range(shares):
            share = lax.rem(at_ref[0] + k + 1, shares)
            row = pl.multiple_of((share * chunks + chunk) * units, units)
            copies.append(
                pltpu.make_async_copy(
                    downs[q].at[pl.ds(row, units), :], tiles_ref.at[q, k], sems.at[q * shares + k]
                )
            )
    return copies


def chunk_product(copies, rows_ref, tiles_ref, outs):
    shares = len(outs)
    groups, both, units = outs[0].shape
    slots = both // 2
    for q in range(2):
        for k in range(shares):
            copies[q * shares + k].wait()
            value = dot(rows_ref[q], tiles_ref[q, k], NT).astype(BF16)
            outs[k][:, pl.ds(q * slots, slots), :] = value.reshape(groups, slots, units)


def first_chunk_kernel(chunks, route_row, at_ref, grad_ref, *rest):
    seconds, downs = rest[:2], rest[2:4]
    *outs, rows_ref, low_ref, block_ref, tiles_ref, block_sems, sems = rest[4:]
    groups, toks, wide = grad_ref.shape
    slots = outs[0].shape[1] // 2
    feats = rows_ref.shape[2]
    copies = weight_copies(0, chunks, at_ref, downs, tiles_ref, sems)
    blocks = [
        pltpu.make_async_copy(grad_ref.at[j], block_ref.at[j], block_sems.at[j])
        for j in range(groups)
    ]
    for copy in blocks + copies:
        copy.start()
    before = jnp.where(iota((toks, toks), 0) < iota((toks, toks), 1), 1.0, 0.0).astype(BF16)
    slot = iota((slots, toks), 0).astype(F32)
    second = jnp.concatenate([ref[...] for ref in seconds], axis=0)
    for j in range(groups):
        blocks[j].wait()
        routes = block_ref[j, pl.ds(route_row, 16), pl.ds(feats, toks)].astype(F32)
        picks = []
        for q in range(2):
            expert = at_ref[1] * 2 + lax.bitwise_xor(at_ref[2], q)
            hits = jnp.where(routes == expert.astype(F32), 1.0, 0.0)
            mine = jnp.max(hits, axis=0, keepdims=True)
            pos = dot(jnp.broadcast_to(mine, (16, toks)).astype(BF16), before, NN)[:1]
            picks.append(jnp.where((slot == pos) & (mine > 0.0), 1.0, 0.0).astype(BF16))
        grad = block_ref[j, :, pl.ds(0, feats)]
        rows = dot(jnp.concatenate(picks, axis=0), grad, NN).astype(BF16)
        for q in range(2):
            rows_ref[q, pl.ds(j * slots, slots), :] = rows[q * slots : (q + 1) * slots]
        low_ref[j] = dot(second, grad, NT).astype(BF16)
    chunk_product(copies, rows_ref, tiles_ref, outs)


def next_chunk_kernel(chunk, chunks, at_ref, rows_ref, *rest):
    downs = rest[:2]
    *outs, tiles_ref, sems = rest[2:]
    copies = weight_copies(chunk, chunks, at_ref, downs, tiles_ref, sems)
    for copy in copies:
        copy.start()
    chunk_product(copies, rows_ref, tiles_ref, outs)


SMEM = pl.BlockSpec(memory_space=pltpu.SMEM)
VMEM = pl.BlockSpec(memory_space=pltpu.VMEM)


def chunk_call(at, chunk, chunks, source, seconds, downs, shares, slots):
    rank, feats = seconds[0].shape
    units = downs[0].shape[0] // shares // chunks
    if chunk == 0:
        groups, toks, wide = source.shape
        kernel = functools.partial(first_chunk_kernel, chunks, 3 * rank)
        arrays = [at, in_hbm(source), *seconds, in_hbm(downs[0]), downs[1]]
        in_specs = [SMEM, ANY, VMEM, VMEM, ANY, ANY]
        extra_outs = [
            jax.ShapeDtypeStruct((2, groups * slots, feats), BF16),
            jax.ShapeDtypeStruct((groups, 2 * rank, toks), BF16),
        ]
        extra_scratch = [pltpu.VMEM((groups, toks, wide), BF16)]
        extra_sems = [pltpu.SemaphoreType.DMA((groups,))]
    else:
        groups = source.shape[1] // slots
        kernel = functools.partial(next_chunk_kernel, chunk, chunks)
        arrays = [at, source, in_hbm(downs[0]), downs[1]]
        in_specs = [SMEM, VMEM, ANY, ANY]
        extra_outs, extra_scratch, extra_sems = [], [], []
    outs = [jax.ShapeDtypeStruct((groups, 2 * slots, units), BF16)] * shares + extra_outs
    return pl.pallas_call(
        kernel,
        in_specs=in_specs,
        out_specs=[VMEM] * len(outs),
        out_shape=outs,
        scratch_shapes=extra_scratch
        + [pltpu.VMEM((2, shares, units, feats), BF16)]
        + extra_sems
        + [pltpu.SemaphoreType.DMA((2 * shares,))],
        compiler_params=PARAMS,
        cost_estimate=SMALL,
        name="chunk_product",
    )(*arrays)


def collect_kernel(at_ref, extra_ref, *rest):
    first_ref = rest[-1]
    groups, rank, units = first_ref.shape
    wide = units // 3
    for o in range(groups):
        for k in range(3):
            first_ref[o, :, pl.ds(k * wide, wide)] = extra_ref[o, pl.ds(k * rank, rank), :]


def collect_call(at, grads, rank, feats, after):
    groups, toks, wide = grads.shape
    extra = wide - feats
    shape = (groups, rank, 3 * extra)
    return call(
        collect_kernel,
        "collect_first",
        at,
        [in_hbm(grads), *after],
        [pl.BlockSpec((groups, toks, extra), lambda i, at: (0, 0, feats // extra))]
        + [ANY] * len(after),
        [(shape, BF16)],
        [whole(shape)],
    )[0]


def low_dense_kernel(at_ref, *refs):
    out_ref, sum_ref = refs[-2:]
    groups, both, _ = refs[0].shape
    rank = both // 2
    for o in range(groups):
        total = refs[0][o].astype(F32)
        for ref in refs[1:-2]:
            total = total + ref[o].astype(F32)
        for q in range(2):
            at = pl.ds((q * groups + o) * rank, rank)
            sum_ref[at, :] = total[q * rank : (q + 1) * rank]
    out_ref[...] = sum_ref[...].T


def low_dense_call(at, parts):
    groups, both, toks = parts[0].shape
    shape = (toks, groups * both)
    return call(
        low_dense_kernel,
        "low_dense",
        at,
        parts,
        [whole(parts[0].shape)] * len(parts),
        [(shape, F32)],
        [whole(shape)],
        scratch=[pltpu.VMEM((groups * both, toks), F32)],
    )[0]


def lowrank_hid_kernel(groups, at_ref, index_ref, hid_ref, *rest):
    firsts, out_ref = rest[:2], rest[2]
    top = index_ref.shape[1]
    rank = firsts[0].shape[0] // groups
    wide = jnp.concatenate([dot(hid_ref[...], ref[...], NT) for ref in firsts], axis=1)
    column = pair_column(relative(at_ref, index_ref[...], groups).astype(F32))
    wide = jnp.where(expert_mask(column, wide.shape[1], rank), wide, 0.0)
    out_ref[...] = wide.reshape(wide.shape[0] // top, top, wide.shape[1]).sum(axis=1)


def lowrank_hid_call(at, index, hid, firsts, groups):
    (toks, top), (pairs, units) = index.shape, hid.shape
    half = firsts[0].shape[0]
    steps = 4
    return call(
        functools.partial(lowrank_hid_kernel, groups),
        "lowrank_hid",
        at,
        [index, in_hbm(hid), *firsts],
        [
            pl.BlockSpec((toks // steps, top), lambda i, at: (i, 0)),
            pl.BlockSpec((pairs // steps, units), lambda i, at: (i, 0)),
        ]
        + [whole((half, units))] * 2,
        [((toks, 2 * half), F32)],
        [pl.BlockSpec((toks // steps, 2 * half), lambda i, at: (i, 0))],
        grid=(steps,),
    )[0]


def scaled_hid_kernel(groups, rank, at_ref, index_ref, prob_ref, *refs):
    out_ref = refs[-1]
    total = refs[0][...]
    for ref in refs[1:-1]:
        total = total + ref[...]
    place = relative(at_ref, index_ref[...], groups)
    prob = prob_ref[...].astype(F32)
    expert = iota(total.shape, 1) // rank
    scale = jnp.zeros(total.shape, F32)
    for k in range(place.shape[1]):
        scale = jnp.where(expert == place[:, k : k + 1], prob[:, k : k + 1], scale)
    scaled = (total * scale).T.astype(BF16)
    for o in range(groups):
        for q in range(2):
            at = (q * groups + o) * rank
            out_ref[o, pl.ds(q * rank, rank), :] = scaled[at : at + rank]


def scaled_hid_call(at, index, prob, parts, groups):
    toks, width = parts[0].shape
    rank = width // groups // 2
    shape = (groups, 2 * rank, toks)
    return call(
        functools.partial(scaled_hid_kernel, groups, rank),
        "scaled_hid",
        at,
        [index, prob, *parts],
        [whole(index.shape), whole(prob.shape)] + [whole((toks, width))] * len(parts),
        [(shape, BF16)],
        [whole(shape)],
    )[0]


def second_grad_kernel(at_ref, scaled_ref, grad_ref, *outs):
    rank, tile = outs[0].shape
    total = jnp.zeros((2 * rank, tile), F32)
    for o in range(scaled_ref.shape[0]):
        total = total + dot(scaled_ref[o], grad_ref[o], NN)
    for q, out_ref in enumerate(outs):
        out_ref[...] = adapter_scale * total[q * rank : (q + 1) * rank]


def second_grad_call(at, scaled, grads, feats):
    groups, both, toks = scaled.shape
    steps = 4
    tile = feats // steps
    block = pl.BlockSpec((both // 2, tile), lambda i, at: (0, i))
    return call(
        second_grad_kernel,
        "second_grad",
        at,
        [scaled, in_hbm(grads)],
        [whole(scaled.shape), pl.BlockSpec((groups, toks, tile), lambda i, at: (0, 0, i))],
        [((both // 2, feats), F32)] * 2,
        [block] * 2,
        grid=(steps,),
    )


def first_grad_kernel(groups, steps, at_ref, index_ref, prob_ref, low_ref, hid_ref, *rest):
    keep_ref, give_ref, sum_ref = rest
    step = pl.program_id(0)
    top = index_ref.shape[1]
    rank = keep_ref.shape[1]
    low = spread_pairs(low_ref[...], top)
    column = pair_column(relative(at_ref, index_ref[...], groups).astype(F32))
    keep = expert_mask(column, low.shape[1], rank)
    scaled = jnp.where(keep, low * pair_column(prob_ref[...].astype(F32)), 0.0).astype(BF16)
    part = adapter_scale * dot(scaled, hid_ref[...], TN)

    @pl.when(step == 0)
    def _():
        sum_ref[...] = part

    @pl.when(step > 0)
    def _():
        sum_ref[...] += part

    @pl.when(step == steps - 1)
    def _():
        for q, out_ref in enumerate((keep_ref, give_ref)):
            half = sum_ref[pl.ds(q * groups * rank, groups * rank), :]
            out_ref[...] = half.reshape(out_ref.shape).astype(out_ref.dtype)


def first_grad_call(at, index, prob, low, hid, groups):
    (toks, top), (pairs, units) = index.shape, hid.shape
    width = low.shape[1]
    steps = 4
    shape = (groups, width // groups // 2, units)
    return call(
        functools.partial(first_grad_kernel, groups, steps),
        "first_grad",
        at,
        [index, prob, low, in_hbm(hid)],
        [
            pl.BlockSpec((toks // steps, top), lambda i, at: (i, 0)),
            pl.BlockSpec((toks // steps, top), lambda i, at: (i, 0)),
            pl.BlockSpec((toks // steps, width), lambda i, at: (i, 0)),
            pl.BlockSpec((pairs // steps, units), lambda i, at: (i, 0)),
        ],
        [(shape, F32), (shape, BF16)],
        [whole(shape)] * 2,
        grid=(steps,),
        scratch=[pltpu.VMEM((width, units), F32)],
    )


def first_sum_kernel(at_ref, keep_ref, got_ref, out_ref):
    for o in range(keep_ref.shape[0]):
        total = keep_ref[o] + got_ref[o].astype(F32)
        out_ref[o] = total.astype(BF16)


def first_sum_call(at, keep, got):
    shape = keep.shape
    return call(
        first_sum_kernel,
        "first_sum",
        at,
        [keep, got],
        [whole(shape)] * 2,
        [(shape, BF16)],
        [whole(shape)],
    )[0]


def finish_kernel(chunks, at_ref, index_all_ref, index_ref, prob_ref, low_ref, hid_ref, *rest):
    firsts, back = rest[:2], rest[2 : 2 + chunks]
    out_ref, sum_ref, all_ref, place_ref = rest[2 + chunks :]
    top = index_ref.shape[1]
    toks = index_all_ref.shape[0]
    groups, both, units = back[0].shape
    slots = both // 2
    experts = 2 * groups

    @pl.when(pl.program_id(0) == 0)
    def _():
        for c, ref in enumerate(back):
            for o in range(groups):
                for q in range(2):
                    all_ref[pl.ds((q * groups + o) * slots, slots), pl.ds(c * units, units)] = ref[
                        o, pl.ds(q * slots, slots), :
                    ]
        experts_all = relative(at_ref, index_all_ref[...], groups)
        hit = jnp.zeros((toks, experts), F32)
        for k in range(top):
            hit = jnp.where(iota((toks, experts), 1) == experts_all[:, k : k + 1], 1.0, hit)
        before = jnp.where(iota((toks, toks), 0) > iota((toks, toks), 1), 1.0, 0.0).astype(BF16)
        place_ref[...] = dot(before, hit.astype(BF16), NN)

    pairs = hid_ref.shape[0]
    some = index_ref.shape[0]
    column = pair_column(relative(at_ref, index_ref[...], groups).astype(F32))
    place = spread_pairs(place_ref[pl.ds(pl.program_id(0) * some, some), :], top)
    mine = iota((pairs, experts), 1) == column.astype(jnp.int32)
    target = column * slots + jnp.sum(jnp.where(mine, place, 0.0), axis=1, keepdims=True)
    low = spread_pairs(low_ref[...], top)
    keep = expert_mask(column, low.shape[1], low.shape[1] // experts)
    low = jnp.where(keep, adapter_scale * low.astype(BF16).astype(F32), 0.0).astype(BF16)
    slot = iota((pairs, experts * slots), 1)
    pick = jnp.where(slot == target.astype(jnp.int32), 1.0, 0.0).astype(BF16)
    half = low.shape[1] // 2
    value = dot(pick, all_ref[...], NN)
    value = value + dot(low[:, :half], firsts[0][...], NN) + dot(low[:, half:], firsts[1][...], NN)
    value = value.astype(BF16).astype(F32)
    out_ref[...] = (value * pair_column(prob_ref[...].astype(F32))).astype(BF16)
    sums = jnp.sum(value * hid_ref[...].astype(F32), axis=1, keepdims=True)
    sums = jnp.where(diagonal(pairs, top), sums, 0.0)
    sum_ref[...] = sums.reshape(some, top, top).sum(axis=1)


def finish_call(at, index, prob, low, hid, firsts, back):
    (toks, top), (pairs, units) = index.shape, hid.shape
    width = low.shape[1]
    groups, both, _ = back[0].shape
    steps = 4

    def rows(n, columns):
        return pl.BlockSpec((n // steps, columns), lambda i, at: (i, 0))

    return call(
        functools.partial(finish_kernel, len(back)),
        "finish",
        at,
        [index, index, prob, low, in_hbm(hid), *firsts, *back],
        [whole(index.shape), rows(toks, top), rows(toks, top), rows(toks, width), rows(pairs, units)]
        + [whole(firsts[0].shape)] * 2
        + [whole(back[0].shape)] * len(back),
        [((pairs, units), BF16), ((toks, top), F32)],
        [rows(pairs, units), rows(toks, top)],
        grid=(steps,),
        scratch=[pltpu.VMEM((groups * both, units), BF16), pltpu.VMEM((toks, 2 * groups), F32)],
    )


def body(grad, hidden, index, weight, down, first, second):
    toks, top = index.shape
    exp_local, units_all, feats = down.shape
    units, rank = first.shape[1:]
    groups, cores, shares = lax.axis_size("ep"), lax.axis_size("sub"), lax.axis_size("rep")
    assert exp_local == 1 and cores == 2 and groups & (groups - 1) == 0
    cap = min(toks, 5 * toks * top // (4 * groups * cores))
    slots = -(-cap // 16) * 16
    pairs = toks * top
    at = jnp.stack([lax.axis_index(name).astype(jnp.int32) for name in ("rep", "ep", "sub")])

    def turn(x, offset):
        return lax.ppermute(x, "rep", [(r, (r + offset) % shares) for r in range(shares)])

    def all_shares(x):
        return [x] + [turn(x, k) for k in range(1, shares)]

    def swap(x):
        return lax.ppermute(x, "sub", [(0, 1), (1, 0)])

    def exchange(x):
        return lax.all_to_all(x, "ep", split_axis=0, concat_axis=0, tiled=True)

    grads = lax.all_gather(pack_call(at, grad, first[0], index), "ep")
    downs = [down[0], swap(down[0])]
    seconds = [second[0], swap(second[0])]

    back = []
    for c in range(CHUNKS):
        *give, keep = chunk_call(
            at, c, CHUNKS, rows if c else grads, seconds, downs, shares, slots
        )
        if c == 0:
            rows, low_grad = give[-1], keep
            *give, keep = give[:-1]
        total = keep.astype(F32)
        for k, x in enumerate(give):
            total = total + turn(x, k + 1).astype(F32)
        back.append(exchange(total.astype(BF16)))

    hid = hidden.reshape(pairs, units)
    first_own = collect_call(at, grads, rank, feats, [low_grad])
    firsts = [x.reshape(groups * rank, units) for x in (first_own, swap(first_own))]

    low_hid = all_shares(lowrank_hid_call(at, index, hid, firsts, groups))
    scaled_hid = exchange(scaled_hid_call(at, index, weight, low_hid, groups))
    second_keep, second_give = second_grad_call(at, scaled_hid, grads, feats)
    second_grad = second_keep + swap(second_give)

    low_grad = low_dense_call(at, all_shares(exchange(low_grad)))
    first_keep, first_give = first_grad_call(at, index, weight, low_grad, hid, groups)
    first_part = exchange(first_sum_call(at, first_keep, swap(first_give)))
    first_grad = jnp.sum(first_part.astype(F32), axis=0)

    grad_hidden, sums = finish_call(at, index, weight, low_grad, hid, firsts, back)
    sums = sums + turn(sums, 1) if shares == 2 else lax.psum(sums, "rep")
    return (
        grad_hidden.reshape(toks, top, units),
        sums,
        first_grad.T[None],
        second_grad[None],
    )


def solution(mesh):
    return jax.shard_map(
        body,
        mesh=mesh,
        in_specs=(
            P(("grp", "ep", "sub"), "rep"),
            P(("grp", "ep", "sub"), None, "rep"),
            P(("grp", "ep", "sub"), None),
            P(("grp", "ep", "sub"), None),
            P(("ep", "sub"), None, "rep"),
            P(("grp", "ep", "sub"), "rep", None),
            P(("grp", "ep", "sub"), None, "rep"),
        ),
        out_specs=(
            P(("grp", "ep", "sub"), None, "rep"),
            P(("grp", "ep", "sub"), None),
            P(("grp", "ep", "sub"), "rep", None),
            P(("grp", "ep", "sub"), None, "rep"),
        ),
        check_vma=False,
    )
```

```python
import functools

import jax
import jax.numpy as jnp
from jax import lax
from jax.experimental import pallas as pl
from jax.experimental.pallas import tpu as pltpu
from jax.sharding import PartitionSpec as P

adapter_scale = 2.0
BF16 = jnp.bfloat16
F32 = jnp.float32
NT = (((1,), (1,)), ((), ()))
TN = (((0,), (0,)), ((), ()))
NN = (((1,), (0,)), ((), ()))
SMALL = pl.CostEstimate(flops=1, bytes_accessed=1, transcendentals=0)
LONG = pl.CostEstimate(flops=1, bytes_accessed=2 * 10**7, transcendentals=0)
ANY = pl.BlockSpec(memory_space=pl.ANY)
SMEM = pl.BlockSpec(memory_space=pltpu.SMEM)


def dot(a, b, dims):
    return lax.dot_general(a, b, dims, preferred_element_type=F32)


def iota(shape, axis):
    return lax.broadcasted_iota(jnp.int32, shape, axis)


def whole(shape):
    return pl.BlockSpec(shape, lambda *_: (0,) * len(shape))


def in_hbm(x):
    return pltpu.with_memory_space_constraint(x, pltpu.HBM)


class Order:
    def __init__(self, at):
        self.at, self.last = at, []

    def wait(self, arrays):
        self.last = self.last + list(arrays)

    def call(self, kernel, name, arrays, in_specs, outs, out_specs, grid=(1,), scratch=(), mib=16, cost=SMALL, **more):
        count, last = 1 + len(arrays), len(self.last)

        def ordered(*refs):
            here = count + last + len(outs)
            kernel(*refs[:count], *refs[count + last : here], *refs[here + 1 :])

        *result, token = pl.pallas_call(
            ordered,
            grid=grid,
            in_specs=[SMEM, *in_specs] + [ANY] * last,
            out_specs=[*out_specs, ANY],
            scratch_shapes=scratch,
            out_shape=[jax.ShapeDtypeStruct(*o) if isinstance(o, tuple) else o for o in outs]
            + [pltpu.HBM((8, 128), F32)],
            compiler_params=pltpu.CompilerParams(vmem_limit_bytes=mib * 2**20),
            cost_estimate=cost,
            name=name,
            **more,
        )(self.at, *arrays, *self.last)
        self.last = [in_hbm(token)]
        return result


def relative(at_ref, index, groups):
    o = lax.bitwise_xor(lax.shift_right_logical(index, 1), at_ref[1])
    q = lax.bitwise_xor(lax.bitwise_and(index, 1), at_ref[2])
    return q * groups + o


def spread_pairs(dense, top):
    toks, width = dense.shape
    return jnp.broadcast_to(dense[:, None, :], (toks, top, width)).reshape(toks * top, width)


def diagonal(pairs, top):
    return iota((pairs, top), 1) == lax.bitwise_and(iota((pairs, top), 0), top - 1)


def pair_column(table):
    toks, top = table.shape
    wide = spread_pairs(table, top)
    return jnp.sum(jnp.where(diagonal(toks * top, top), wide, 0.0), axis=1, keepdims=True)


def expert_mask(column, width, rank):
    return iota((column.shape[0], width), 1) // rank == column.astype(jnp.int32)


def pack_kernel(rank, at_ref, grad_ref, first_ref, index_ref, out_ref):
    toks, feats = grad_ref.shape
    extra = out_ref.shape[1] - feats
    out_ref[:, pl.ds(0, feats)] = grad_ref[...]
    same = jnp.where(iota((rank, rank), 0) == iota((rank, rank), 1), 1.0, 0.0).astype(BF16)
    factor = dot(same, first_ref[...], NT).astype(BF16)
    for k in range(3):
        piece = factor[:, k * extra : (k + 1) * extra]
        out_ref[pl.ds(k * rank, rank), pl.ds(feats, extra)] = piece
    top = index_ref.shape[1]
    out_ref[pl.ds(3 * rank, toks - 3 * rank), pl.ds(feats, extra)] = jnp.full(
        (toks - 3 * rank, extra), -1.0, BF16
    )
    turn = jnp.where(iota((16, top), 0) == iota((16, top), 1), 1.0, 0.0).astype(BF16)
    routes = dot(turn, index_ref[...].astype(F32).astype(BF16), NT)
    routes = jnp.where(iota((16, toks), 0) < top, routes, -1.0)
    out_ref[pl.ds(3 * rank, 16), pl.ds(feats, toks)] = routes.astype(BF16)


def pack_call(order, grad, first, index):
    (toks, feats), (units, rank) = grad.shape, first.shape
    extra = units // 3
    shape = (toks, feats + extra)
    return order.call(
        functools.partial(pack_kernel, rank),
        "pack_block",
        [grad, first, index],
        [whole(grad.shape), whole(first.shape), whole(index.shape)],
        [(shape, BF16)],
        [whole(shape)],
    )[0]


def expert_rows_kernel(slots, tiles, shares, batch, route_row, at_ref, *rest):
    grads, seconds, downs = rest[:batch], rest[batch : batch + 2], rest[batch + 2 : batch + 4]
    *outs, low_ref = rest[batch + 4 : batch + 5 + shares]
    block_ref, rows_ref, tiles_ref, block_sems, sems = rest[batch + 5 + shares :]
    tile = tiles_ref.shape[1]
    feats = rows_ref.shape[2]
    toks = block_ref.shape[1]
    blocks = [
        pltpu.make_async_copy(ref, block_ref.at[k], block_sems.at[k]) for k, ref in enumerate(grads)
    ]
    parts = [(k, q, t) for k in range(shares) for q in range(2) for t in range(tiles)]
    weights = []
    for n, (k, q, t) in enumerate(parts):
        share = lax.rem(at_ref[0] + k + 1, shares)
        row = pl.multiple_of((share * tiles + t) * tile, tile)
        weights.append(
            pltpu.make_async_copy(downs[q].at[pl.ds(row, tile), :], tiles_ref.at[n], sems.at[n])
        )
    for copy in blocks + weights:
        copy.start()

    before = jnp.where(iota((toks, toks), 0) < iota((toks, toks), 1), 1.0, 0.0).astype(BF16)
    slot = iota((slots, toks), 0).astype(F32)
    second = jnp.concatenate([ref[...] for ref in seconds], axis=0)
    for k in range(batch):
        blocks[k].wait()
        routes = block_ref[k, pl.ds(route_row, 16), pl.ds(feats, toks)].astype(F32)
        picks = []
        for q in range(2):
            expert = at_ref[1] * 2 + lax.bitwise_xor(at_ref[2], q)
            hits = jnp.where(routes == expert.astype(F32), 1.0, 0.0)
            mine = jnp.max(hits, axis=0, keepdims=True)
            pos = dot(jnp.broadcast_to(mine, (16, toks)).astype(BF16), before, NN)[:1]
            picks.append(jnp.where((slot == pos) & (mine > 0.0), 1.0, 0.0).astype(BF16))
        grad = block_ref[k, :, pl.ds(0, feats)]
        rows = dot(jnp.concatenate(picks, axis=0), grad, NN).astype(BF16)
        for q in range(2):
            rows_ref[q, pl.ds(k * slots, slots), :] = rows[q * slots : (q + 1) * slots]
        low_ref[k] = dot(second, grad, NT).astype(BF16)

    for n, (k, q, t) in enumerate(parts):
        weights[n].wait()
        value = dot(rows_ref[q], tiles_ref[n], NT).astype(BF16)
        outs[k][pl.ds(q * batch * slots, batch * slots), pl.ds(t * tile, tile)] = value


def expert_rows_call(order, grads, seconds, downs, shares, slots):
    batch, (toks, wide) = len(grads), grads[0].shape
    rank, feats = seconds[0].shape
    units = downs[0].shape[0] // shares
    tiles = 3
    tile = units // tiles
    rows = 2 * batch * slots
    count = shares * 2 * tiles
    low_shape = (batch, 2 * rank, toks)
    return order.call(
        functools.partial(expert_rows_kernel, slots, tiles, shares, batch, 3 * rank),
        "expert_rows",
        [*grads, *seconds, *[in_hbm(x) for x in downs]],
        [ANY] * batch + [whole((rank, feats))] * 2 + [ANY] * 2,
        [((rows, units), BF16)] * (shares - 1)
        + [pltpu.HBM((rows, units), BF16), pltpu.HBM(low_shape, BF16)],
        [whole((rows, units))] * shares + [whole(low_shape)],
        scratch=[
            pltpu.VMEM((batch, toks, wide), BF16),
            pltpu.VMEM((2, batch * slots, feats), BF16),
            pltpu.VMEM((count, tile, feats), BF16),
            pltpu.SemaphoreType.DMA((batch,)),
            pltpu.SemaphoreType.DMA((count,)),
        ],
        mib=28,
    )


def gate_kernel(at_ref, block_ref, out_ref):
    pass


def gate_call(order, block):
    return order.call(
        gate_kernel,
        "gate",
        [block],
        [ANY],
        [(block.shape, block.dtype)],
        [ANY],
        input_output_aliases={1: 0},
    )[0]


def share_sum_kernel(parts, slots, at_ref, *refs):
    outs = refs[parts:]
    for k, out_ref in enumerate(outs):
        for q in range(2):
            at = pl.ds((q * len(outs) + k) * slots, slots)
            total = refs[0][at, :].astype(F32)
            for part in refs[1:parts]:
                total = total + part[at, :].astype(F32)
            out_ref[pl.ds(q * slots, slots), :] = total.astype(BF16)


def share_sum_call(order, parts, batch, slots):
    rows, units = parts[0].shape
    shape = (2 * slots, units)
    return order.call(
        functools.partial(share_sum_kernel, len(parts), slots),
        "share_sum",
        parts,
        [whole((rows, units))] * len(parts),
        [(shape, BF16)] * batch,
        [whole(shape)] * batch,
    )


def collect_kernel(places, at_ref, *refs):
    low_ref, first_ref = refs[-2:]
    rank = first_ref.shape[1]
    at = 0
    lows = len(refs) - 2 - len(places)
    for ref in refs[:lows]:
        for k in range(ref.shape[0]):
            low_ref[lax.bitwise_xor(at_ref[1], places[at])] = ref[k]
            at += 1
    for o, ref in zip(places, refs[lows:-2]):
        wide = ref.shape[1]
        for k in range(3):
            first_ref[o, :, pl.ds(k * wide, wide)] = ref[pl.ds(k * rank, rank), :]


def collect_call(order, places, lows, grads, feats):
    groups, (toks, wide) = len(grads), grads[0].shape
    rank = lows[0].shape[1] // 2
    extra = wide - feats
    low_shape, first_shape = (groups, 2 * rank, toks), (groups, rank, 3 * extra)
    return order.call(
        functools.partial(collect_kernel, places),
        "collect_blocks",
        [*lows, *[in_hbm(x) for x in grads]],
        [whole(b.shape) for b in lows]
        + [pl.BlockSpec((toks, extra), lambda i: (0, feats // extra))] * groups,
        [(low_shape, BF16), (first_shape, BF16)],
        [whole(low_shape), whole(first_shape)],
    )


def low_dense_kernel(at_ref, *refs):
    out_ref, sum_ref = refs[-2:]
    groups, both, _ = refs[0].shape
    rank = both // 2
    for o in range(groups):
        total = refs[0][lax.bitwise_xor(at_ref[1], o)].astype(F32)
        for ref in refs[1:-2]:
            total = total + ref[lax.bitwise_xor(at_ref[1], o)].astype(F32)
        for q in range(2):
            at = pl.ds((q * groups + o) * rank, rank)
            sum_ref[at, :] = total[q * rank : (q + 1) * rank]
    out_ref[...] = sum_ref[...].T


def low_dense_call(order, parts):
    groups, both, toks = parts[0].shape
    shape = (toks, groups * both)
    return order.call(
        low_dense_kernel,
        "low_dense",
        parts,
        [whole(parts[0].shape)] * len(parts),
        [(shape, F32)],
        [whole(shape)],
        scratch=[pltpu.VMEM((groups * both, toks), F32)],
    )[0]


def lowrank_hid_kernel(groups, at_ref, index_ref, hid_ref, *rest):
    firsts, out_ref = rest[:2], rest[2]
    top = index_ref.shape[1]
    rank = firsts[0].shape[0] // groups
    wide = jnp.concatenate([dot(hid_ref[...], ref[...], NT) for ref in firsts], axis=1)
    column = pair_column(relative(at_ref, index_ref[...], groups).astype(F32))
    wide = jnp.where(expert_mask(column, wide.shape[1], rank), wide, 0.0)
    out_ref[...] = wide.reshape(wide.shape[0] // top, top, wide.shape[1]).sum(axis=1)


def lowrank_hid_call(order, index, hid, firsts, groups):
    (toks, top), (pairs, units) = index.shape, hid.shape
    half = firsts[0].shape[0]
    steps = 4
    return order.call(
        functools.partial(lowrank_hid_kernel, groups),
        "lowrank_hid",
        [index, in_hbm(hid), *firsts],
        [
            pl.BlockSpec((toks // steps, top), lambda i: (i, 0)),
            pl.BlockSpec((pairs // steps, units), lambda i: (i, 0)),
        ]
        + [whole((half, units))] * 2,
        [((toks, 2 * half), F32)],
        [pl.BlockSpec((toks // steps, 2 * half), lambda i: (i, 0))],
        grid=(steps,),
    )[0]


def scaled_hid_kernel(groups, rank, at_ref, index_ref, prob_ref, *refs):
    out_ref = refs[-1]
    total = refs[0][...]
    for ref in refs[1:-1]:
        total = total + ref[...]
    place = relative(at_ref, index_ref[...], groups)
    prob = prob_ref[...].astype(F32)
    expert = iota(total.shape, 1) // rank
    scale = jnp.zeros(total.shape, F32)
    for k in range(place.shape[1]):
        scale = jnp.where(expert == place[:, k : k + 1], prob[:, k : k + 1], scale)
    scaled = (total * scale).T.astype(BF16)
    for o in range(groups):
        for q in range(2):
            at = (q * groups + o) * rank
            out_ref[lax.bitwise_xor(at_ref[1], o), pl.ds(q * rank, rank), :] = scaled[at : at + rank]


def scaled_hid_call(order, index, prob, parts, groups):
    toks, width = parts[0].shape
    rank = width // groups // 2
    shape = (groups, 2 * rank, toks)
    return order.call(
        functools.partial(scaled_hid_kernel, groups, rank),
        "scaled_hid",
        [index, prob, *parts],
        [whole(index.shape), whole(prob.shape)] + [whole((toks, width))] * len(parts),
        [(shape, BF16)],
        [whole(shape)],
    )[0]


def second_grad_kernel(places, at_ref, scaled_ref, *refs):
    grads, outs = refs[:-2], refs[-2:]
    rank, tile = outs[0].shape
    total = jnp.zeros((2 * rank, tile), F32)
    for o, grad_ref in zip(places, grads):
        total = total + dot(scaled_ref[lax.bitwise_xor(at_ref[1], o)], grad_ref[...], NN)
    for q, out_ref in enumerate(outs):
        out_ref[...] = adapter_scale * total[q * rank : (q + 1) * rank]


def second_grad_call(order, places, scaled, grads, feats):
    groups, both, toks = scaled.shape
    steps = 4
    tile = feats // steps
    block = pl.BlockSpec((both // 2, tile), lambda i: (0, i))
    return order.call(
        functools.partial(second_grad_kernel, places),
        "second_grad",
        [scaled, *[in_hbm(x) for x in grads]],
        [whole(scaled.shape)] + [pl.BlockSpec((toks, tile), lambda i: (0, i))] * groups,
        [((both // 2, feats), F32)] * 2,
        [block] * 2,
        grid=(steps,),
        cost=LONG,
    )


def first_grad_kernel(groups, steps, at_ref, index_ref, prob_ref, low_ref, hid_ref, *rest):
    keep_ref, give_ref, sum_ref = rest
    step = pl.program_id(0)
    top = index_ref.shape[1]
    rank = keep_ref.shape[1]
    low = spread_pairs(low_ref[...], top)
    column = pair_column(relative(at_ref, index_ref[...], groups).astype(F32))
    keep = expert_mask(column, low.shape[1], rank)
    scaled = jnp.where(keep, low * pair_column(prob_ref[...].astype(F32)), 0.0).astype(BF16)
    part = adapter_scale * dot(scaled, hid_ref[...], TN)

    @pl.when(step == 0)
    def _():
        sum_ref[...] = part

    @pl.when(step > 0)
    def _():
        sum_ref[...] += part

    @pl.when(step == steps - 1)
    def _():
        for q, out_ref in enumerate((keep_ref, give_ref)):
            half = sum_ref[pl.ds(q * groups * rank, groups * rank), :]
            out_ref[...] = half.reshape(out_ref.shape).astype(out_ref.dtype)


def first_grad_call(order, index, prob, low, hid, groups):
    (toks, top), (pairs, units) = index.shape, hid.shape
    width = low.shape[1]
    steps = 4
    shape = (groups, width // groups // 2, units)
    return order.call(
        functools.partial(first_grad_kernel, groups, steps),
        "first_grad",
        [index, prob, low, in_hbm(hid)],
        [
            pl.BlockSpec((toks // steps, top), lambda i: (i, 0)),
            pl.BlockSpec((toks // steps, top), lambda i: (i, 0)),
            pl.BlockSpec((toks // steps, width), lambda i: (i, 0)),
            pl.BlockSpec((pairs // steps, units), lambda i: (i, 0)),
        ],
        [(shape, F32), (shape, BF16)],
        [whole(shape)] * 2,
        grid=(steps,),
        scratch=[pltpu.VMEM((width, units), F32)],
    )


def first_sum_kernel(at_ref, keep_ref, got_ref, out_ref):
    for o in range(keep_ref.shape[0]):
        total = keep_ref[o] + got_ref[o].astype(F32)
        out_ref[lax.bitwise_xor(at_ref[1], o)] = total.astype(BF16)


def first_sum_call(order, keep, got):
    shape = keep.shape
    return order.call(
        first_sum_kernel,
        "first_sum",
        [keep, got],
        [whole(shape)] * 2,
        [(shape, BF16)],
        [whole(shape)],
    )[0]


def finish_kernel(count, slots, at_ref, index_all_ref, index_ref, prob_ref, low_ref, hid_ref, *rest):
    firsts, back = rest[:2], rest[2 : 2 + count]
    out_ref, sum_ref, all_ref, place_ref = rest[2 + count :]
    top = index_ref.shape[1]
    toks = index_all_ref.shape[0]
    experts = 2 * count

    @pl.when(pl.program_id(0) == 0)
    def _():
        for o, ref in enumerate(back):
            for q in range(2):
                all_ref[pl.ds((q * count + o) * slots, slots), :] = ref[pl.ds(q * slots, slots), :]
        experts_all = relative(at_ref, index_all_ref[...], count)
        hit = jnp.zeros((toks, experts), F32)
        for k in range(top):
            hit = jnp.where(iota((toks, experts), 1) == experts_all[:, k : k + 1], 1.0, hit)
        before = jnp.where(iota((toks, toks), 0) > iota((toks, toks), 1), 1.0, 0.0).astype(BF16)
        place_ref[...] = dot(before, hit.astype(BF16), NN)

    pairs = hid_ref.shape[0]
    some = index_ref.shape[0]
    column = pair_column(relative(at_ref, index_ref[...], count).astype(F32))
    place = spread_pairs(place_ref[pl.ds(pl.program_id(0) * some, some), :], top)
    mine = iota((pairs, experts), 1) == column.astype(jnp.int32)
    target = column * slots + jnp.sum(jnp.where(mine, place, 0.0), axis=1, keepdims=True)
    low = spread_pairs(low_ref[...], top)
    keep = expert_mask(column, low.shape[1], low.shape[1] // experts)
    low = jnp.where(keep, adapter_scale * low.astype(BF16).astype(F32), 0.0).astype(BF16)
    slot = iota((pairs, experts * slots), 1)
    pick = jnp.where(slot == target.astype(jnp.int32), 1.0, 0.0).astype(BF16)
    half = low.shape[1] // 2
    value = dot(pick, all_ref[...], NN)
    value = value + dot(low[:, :half], firsts[0][...], NN) + dot(low[:, half:], firsts[1][...], NN)
    value = value.astype(BF16).astype(F32)
    out_ref[...] = (value * pair_column(prob_ref[...].astype(F32))).astype(BF16)
    sums = jnp.sum(value * hid_ref[...].astype(F32), axis=1, keepdims=True)
    sums = jnp.where(diagonal(pairs, top), sums, 0.0)
    sum_ref[...] = sums.reshape(some, top, top).sum(axis=1)


def finish_call(order, index, prob, low, hid, firsts, back):
    (toks, top), (pairs, units) = index.shape, hid.shape
    width = low.shape[1]
    both = back[0].shape[0]
    steps = 4
    count = len(back)

    def rows(n, columns):
        return pl.BlockSpec((n // steps, columns), lambda i: (i, 0))

    return order.call(
        functools.partial(finish_kernel, count, both // 2),
        "finish",
        [index, index, prob, low, in_hbm(hid), *firsts, *[in_hbm(x) for x in back]],
        [whole(index.shape), rows(toks, top), rows(toks, top), rows(toks, width), rows(pairs, units)]
        + [whole(firsts[0].shape)] * 2
        + [whole((both, units))] * count,
        [((pairs, units), BF16), ((toks, top), F32)],
        [rows(pairs, units), rows(toks, top)],
        grid=(steps,),
        scratch=[pltpu.VMEM((count * both, units), BF16), pltpu.VMEM((toks, 2 * count), F32)],
    )


def body(grad, hidden, index, weight, down, first, second):
    toks, top = index.shape
    exp_local, units_all, feats = down.shape
    units, rank = first.shape[1:]
    groups, cores, shares = lax.axis_size("ep"), lax.axis_size("sub"), lax.axis_size("rep")
    assert exp_local == 1 and cores == 2 and groups & (groups - 1) == 0
    cap = min(toks, 5 * toks * top // (4 * groups * cores))
    slots = -(-cap // 16) * 16
    pairs = toks * top
    at = jnp.stack([lax.axis_index(name).astype(jnp.int32) for name in ("rep", "ep", "sub")])
    order = Order(at)

    def turn(x, offset):
        return lax.ppermute(x, "rep", [(r, (r + offset) % shares) for r in range(shares)])

    def all_shares(x):
        return [x] + [turn(x, k) for k in range(1, shares)]

    def flip(x, mask):
        return lax.ppermute(x, "ep", [(i, i ^ mask) for i in range(groups)])

    def swap(x):
        return lax.ppermute(x, "sub", [(0, 1), (1, 0)])

    def exchange(x):
        return lax.all_to_all(x, "ep", split_axis=0, concat_axis=0, tiled=True)

    blocks = {0: pack_call(order, grad, first[0], index)}

    def fetch(o):
        if o not in blocks:
            last = o & -o
            blocks[o] = flip(fetch(o ^ last), last)
        return blocks[o]

    downs = [down[0], swap(down[0])]
    seconds = [second[0], swap(second[0])]

    if groups == 8:
        batches, gates = [(0, 2), (1, 4), (3, 6), (5, 7)], {1: 4, 2: 6}
    else:
        batches, gates = [(o, o + 1) for o in range(0, groups, 2)], {}
    places = [o for batch in batches for o in batch]
    back, lows, waiting = {}, [], []

    def arrived(i):
        order.wait([back[o] for o in batches[i] if o])

    def send_back(batch, parts):
        for o, rows in zip(batch, share_sum_call(order, parts, 2, slots)):
            back[o] = flip(rows, o) if o else rows

    for i, batch in enumerate(batches):
        if i in gates:
            blocks[gates[i]] = gate_call(order, fetch(gates[i]))
        *give, keep, low = expert_rows_call(
            order, [fetch(o) for o in batch], seconds, downs, shares, slots
        )
        lows.append(low)
        if i > 1:
            arrived(i - 2)
        if i > 0:
            send_back(*waiting)
        waiting = (batch, [keep] + [turn(x, k + 1) for k, x in enumerate(give)])

    hid = hidden.reshape(pairs, units)
    grads = [blocks[o] for o in places]

    low_grad, first_own = collect_call(order, places, lows, grads, feats)
    firsts = [x.reshape(groups * rank, units) for x in (first_own, swap(first_own))]
    low_hid = all_shares(lowrank_hid_call(order, index, hid, firsts, groups))
    low_grad = all_shares(exchange(low_grad))
    send_back(*waiting)

    arrived(len(batches) - 2)
    scaled_hid = exchange(scaled_hid_call(order, index, weight, low_hid, groups))

    low_grad = low_dense_call(order, low_grad)
    first_keep, first_give = first_grad_call(order, index, weight, low_grad, hid, groups)
    first_part = exchange(first_sum_call(order, first_keep, swap(first_give)))
    first_grad = jnp.sum(first_part.astype(F32), axis=0)
    order.wait([back[batches[-1][0]]])
    second_keep, second_give = second_grad_call(order, places, scaled_hid, grads, feats)
    second_grad = second_keep + swap(second_give)

    order.wait([first_part])
    back = [back[o] for o in range(groups)]
    grad_hidden, sums = finish_call(order, index, weight, low_grad, hid, firsts, back)
    sums = sums + turn(sums, 1) if shares == 2 else lax.psum(sums, "rep")
    return (
        grad_hidden.reshape(toks, top, units),
        sums,
        first_grad.T[None],
        second_grad[None],
    )


def solution(mesh):
    return jax.shard_map(
        body,
        mesh=mesh,
        in_specs=(
            P(("grp", "ep", "sub"), "rep"),
            P(("grp", "ep", "sub"), None, "rep"),
            P(("grp", "ep", "sub"), None),
            P(("grp", "ep", "sub"), None),
            P(("ep", "sub"), None, "rep"),
            P(("grp", "ep", "sub"), "rep", None),
            P(("grp", "ep", "sub"), None, "rep"),
        ),
        out_specs=(
            P(("grp", "ep", "sub"), None, "rep"),
            P(("grp", "ep", "sub"), None),
            P(("grp", "ep", "sub"), "rep", None),
            P(("grp", "ep", "sub"), None, "rep"),
        ),
        check_vma=False,
    )
```

```python
import functools

import jax
import jax.numpy as jnp
from jax import lax
from jax.experimental import pallas as pl
from jax.experimental.pallas import tpu as pltpu
from jax.sharding import PartitionSpec as P

adapter_scale = 2.0
BF16 = jnp.bfloat16
F32 = jnp.float32
NT = (((1,), (1,)), ((), ()))
TN = (((0,), (0,)), ((), ()))
NN = (((1,), (0,)), ((), ()))
SMALL = pl.CostEstimate(flops=1, bytes_accessed=1, transcendentals=0)
ANY = pl.BlockSpec(memory_space=pl.ANY)
SMEM = pl.BlockSpec(memory_space=pltpu.SMEM)


def dot(a, b, dims):
    return lax.dot_general(a, b, dims, preferred_element_type=F32)


def iota(shape, axis):
    return lax.broadcasted_iota(jnp.int32, shape, axis)


def whole(shape):
    return pl.BlockSpec(shape, lambda *_: (0,) * len(shape))


def in_hbm(x):
    return pltpu.with_memory_space_constraint(x, pltpu.HBM)


class Order:
    def __init__(self, at):
        self.at, self.last = at, []

    def wait(self, arrays):
        self.last = self.last + list(arrays)

    def call(self, kernel, name, arrays, in_specs, outs, out_specs, grid=(1,), scratch=(), mib=16, cost=SMALL, **more):
        count, last = 1 + len(arrays), len(self.last)

        def ordered(*refs):
            here = count + last + len(outs)
            kernel(*refs[:count], *refs[count + last : here], *refs[here + 1 :])

        *result, token = pl.pallas_call(
            ordered,
            grid=grid,
            in_specs=[SMEM, *in_specs] + [ANY] * last,
            out_specs=[*out_specs, ANY],
            scratch_shapes=scratch,
            out_shape=[jax.ShapeDtypeStruct(*o) if isinstance(o, tuple) else o for o in outs]
            + [pltpu.HBM((8, 128), F32)],
            compiler_params=pltpu.CompilerParams(vmem_limit_bytes=mib * 2**20),
            cost_estimate=cost,
            name=name,
            **more,
        )(self.at, *arrays, *self.last)
        self.last = [in_hbm(token)]
        return result


def relative(at_ref, index, groups):
    o = lax.bitwise_xor(lax.shift_right_logical(index, 1), at_ref[1])
    q = lax.bitwise_xor(lax.bitwise_and(index, 1), at_ref[2])
    return q * groups + o


def spread_pairs(dense, top):
    toks, width = dense.shape
    return jnp.broadcast_to(dense[:, None, :], (toks, top, width)).reshape(toks * top, width)


def diagonal(pairs, top):
    return iota((pairs, top), 1) == lax.bitwise_and(iota((pairs, top), 0), top - 1)


def pair_column(table):
    toks, top = table.shape
    wide = spread_pairs(table, top)
    return jnp.sum(jnp.where(diagonal(toks * top, top), wide, 0.0), axis=1, keepdims=True)


def expert_mask(column, width, rank):
    return iota((column.shape[0], width), 1) // rank == column.astype(jnp.int32)


def pack_kernel(rank, at_ref, grad_ref, first_ref, index_ref, out_ref):
    toks, feats = grad_ref.shape
    extra = out_ref.shape[1] - feats
    out_ref[:, pl.ds(0, feats)] = grad_ref[...]
    same = jnp.where(iota((rank, rank), 0) == iota((rank, rank), 1), 1.0, 0.0).astype(BF16)
    factor = dot(same, first_ref[...], NT).astype(BF16)
    for k in range(3):
        piece = factor[:, k * extra : (k + 1) * extra]
        out_ref[pl.ds(k * rank, rank), pl.ds(feats, extra)] = piece
    top = index_ref.shape[1]
    out_ref[pl.ds(3 * rank, toks - 3 * rank), pl.ds(feats, extra)] = jnp.full(
        (toks - 3 * rank, extra), -1.0, BF16
    )
    turn = jnp.where(iota((16, top), 0) == iota((16, top), 1), 1.0, 0.0).astype(BF16)
    routes = dot(turn, index_ref[...].astype(F32).astype(BF16), NT)
    routes = jnp.where(iota((16, toks), 0) < top, routes, -1.0)
    out_ref[pl.ds(3 * rank, 16), pl.ds(feats, toks)] = routes.astype(BF16)


def pack_call(order, grad, first, index):
    (toks, feats), (units, rank) = grad.shape, first.shape
    extra = units // 3
    shape = (toks, feats + extra)
    return order.call(
        functools.partial(pack_kernel, rank),
        "pack_block",
        [grad, first, index],
        [whole(grad.shape), whole(first.shape), whole(index.shape)],
        [(shape, BF16)],
        [whole(shape)],
    )[0]


def expert_rows_kernel(slots, tiles, shares, batch, route_row, at_ref, *rest):
    grads, seconds, downs = rest[:batch], rest[batch : batch + 2], rest[batch + 2 : batch + 4]
    *outs, low_ref = rest[batch + 4 : batch + 5 + shares]
    block_ref, turned_ref, tiles_ref, block_sems, sems = rest[batch + 5 + shares :]
    tile = tiles_ref.shape[1]
    feats = turned_ref.shape[1]
    toks = block_ref.shape[1]
    blocks = [
        pltpu.make_async_copy(ref, block_ref.at[k], block_sems.at[k]) for k, ref in enumerate(grads)
    ]
    parts = [(k, q, t) for k in range(shares) for q in range(2) for t in range(tiles)]
    weights = []
    for n, (k, q, t) in enumerate(parts):
        share = lax.rem(at_ref[0] + k + 1, shares)
        row = pl.multiple_of((share * tiles + t) * tile, tile)
        weights.append(
            pltpu.make_async_copy(downs[q].at[pl.ds(row, tile), :], tiles_ref.at[n], sems.at[n])
        )
    for copy in blocks + weights:
        copy.start()

    before = jnp.where(iota((toks, toks), 0) < iota((toks, toks), 1), 1.0, 0.0).astype(BF16)
    columns = turned_ref.shape[2]
    slot = iota((columns, batch * toks), 0).astype(F32)
    second = jnp.concatenate([ref[...] for ref in seconds], axis=0)
    routes = []
    for k in range(batch):
        blocks[k].wait()
        routes.append(block_ref[k, pl.ds(route_row, 16), pl.ds(feats, toks)].astype(F32))
    grad = block_ref[:, :, pl.ds(0, feats)].reshape(batch * toks, feats)
    for q in range(2):
        expert = at_ref[1] * 2 + lax.bitwise_xor(at_ref[2], q)
        targets = []
        for k in range(batch):
            hits = jnp.where(routes[k] == expert.astype(F32), 1.0, 0.0)
            mine = jnp.max(hits, axis=0, keepdims=True)
            pos = dot(jnp.broadcast_to(mine, (16, toks)).astype(BF16), before, NN)[:1]
            targets.append(jnp.where(mine > 0.0, pos + float(k * slots), -1.0))
        pick = jnp.where(slot == jnp.concatenate(targets, axis=1), 1.0, 0.0)
        turned_ref[q] = dot(grad, pick.T.astype(BF16), TN).astype(BF16)
    low = dot(second, grad, NT).astype(BF16)
    for k in range(batch):
        low_ref[k] = low[:, k * toks : (k + 1) * toks]

    rows = batch * slots
    for n, (k, q, t) in enumerate(parts):
        weights[n].wait()
        value = dot(tiles_ref[n], turned_ref[q], NN)
        outs[k][pl.ds(q * rows, rows), pl.ds(t * tile, tile)] = value.T[:rows].astype(BF16)


def expert_rows_call(order, grads, seconds, downs, shares, slots):
    batch, (toks, wide) = len(grads), grads[0].shape
    rank, feats = seconds[0].shape
    units = downs[0].shape[0] // shares
    tiles = 3
    tile = units // tiles
    rows = 2 * batch * slots
    count = shares * 2 * tiles
    low_shape = (batch, 2 * rank, toks)
    return order.call(
        functools.partial(expert_rows_kernel, slots, tiles, shares, batch, 3 * rank),
        "expert_rows",
        [*grads, *seconds, *[in_hbm(x) for x in downs]],
        [ANY] * batch + [whole((rank, feats))] * 2 + [ANY] * 2,
        [((rows, units), BF16)] * (shares - 1)
        + [pltpu.HBM((rows, units), BF16), pltpu.HBM(low_shape, BF16)],
        [whole((rows, units))] * shares + [whole(low_shape)],
        scratch=[
            pltpu.VMEM((batch, toks, wide), BF16),
            pltpu.VMEM((2, feats, -(-batch * slots // 128) * 128), BF16),
            pltpu.VMEM((count, tile, feats), BF16),
            pltpu.SemaphoreType.DMA((batch,)),
            pltpu.SemaphoreType.DMA((count,)),
        ],
        mib=28,
    )


def share_sum_kernel(parts, slots, at_ref, *refs):
    outs = refs[parts:]
    for k, out_ref in enumerate(outs):
        for q in range(2):
            at = pl.ds((q * len(outs) + k) * slots, slots)
            total = refs[0][at, :].astype(F32)
            for part in refs[1:parts]:
                total = total + part[at, :].astype(F32)
            out_ref[pl.ds(q * slots, slots), :] = total.astype(BF16)


def share_sum_call(order, parts, batch, slots):
    rows, units = parts[0].shape
    shape = (2 * slots, units)
    return order.call(
        functools.partial(share_sum_kernel, len(parts), slots),
        "share_sum",
        parts,
        [whole((rows, units))] * len(parts),
        [(shape, BF16)] * batch,
        [whole(shape)] * batch,
    )


def collect_kernel(places, at_ref, *refs):
    low_ref, first_ref = refs[-2:]
    rank = first_ref.shape[1]
    at = 0
    lows = len(refs) - 2 - len(places)
    for ref in refs[:lows]:
        for k in range(ref.shape[0]):
            low_ref[lax.bitwise_xor(at_ref[1], places[at])] = ref[k]
            at += 1
    for o, ref in zip(places, refs[lows:-2]):
        wide = ref.shape[1]
        for k in range(3):
            first_ref[o, :, pl.ds(k * wide, wide)] = ref[pl.ds(k * rank, rank), :]


def collect_call(order, places, lows, grads, feats):
    groups, (toks, wide) = len(grads), grads[0].shape
    rank = lows[0].shape[1] // 2
    extra = wide - feats
    low_shape, first_shape = (groups, 2 * rank, toks), (groups, rank, 3 * extra)
    return order.call(
        functools.partial(collect_kernel, places),
        "collect_blocks",
        [*lows, *[in_hbm(x) for x in grads]],
        [whole(b.shape) for b in lows]
        + [pl.BlockSpec((toks, extra), lambda i: (0, feats // extra))] * groups,
        [(low_shape, BF16), (first_shape, BF16)],
        [whole(low_shape), whole(first_shape)],
    )


def low_dense_kernel(at_ref, *refs):
    out_ref, sum_ref = refs[-2:]
    groups, both, _ = refs[0].shape
    rank = both // 2
    for o in range(groups):
        total = refs[0][lax.bitwise_xor(at_ref[1], o)].astype(F32)
        for ref in refs[1:-2]:
            total = total + ref[lax.bitwise_xor(at_ref[1], o)].astype(F32)
        for q in range(2):
            at = pl.ds((q * groups + o) * rank, rank)
            sum_ref[at, :] = total[q * rank : (q + 1) * rank]
    out_ref[...] = sum_ref[...].T


def low_dense_call(order, parts):
    groups, both, toks = parts[0].shape
    shape = (toks, groups * both)
    return order.call(
        low_dense_kernel,
        "low_dense",
        parts,
        [whole(parts[0].shape)] * len(parts),
        [(shape, F32)],
        [whole(shape)],
        scratch=[pltpu.VMEM((groups * both, toks), F32)],
    )[0]


def lowrank_hid_kernel(groups, at_ref, index_ref, hid_ref, *rest):
    firsts, out_ref = rest[:2], rest[2]
    top = index_ref.shape[1]
    rank = firsts[0].shape[0] // groups
    wide = jnp.concatenate([dot(hid_ref[...], ref[...], NT) for ref in firsts], axis=1)
    column = pair_column(relative(at_ref, index_ref[...], groups).astype(F32))
    wide = jnp.where(expert_mask(column, wide.shape[1], rank), wide, 0.0)
    out_ref[...] = wide.reshape(wide.shape[0] // top, top, wide.shape[1]).sum(axis=1)


def lowrank_hid_call(order, index, hid, firsts, groups):
    (toks, top), (pairs, units) = index.shape, hid.shape
    half = firsts[0].shape[0]
    steps = 4
    return order.call(
        functools.partial(lowrank_hid_kernel, groups),
        "lowrank_hid",
        [index, in_hbm(hid), *firsts],
        [
            pl.BlockSpec((toks // steps, top), lambda i: (i, 0)),
            pl.BlockSpec((pairs // steps, units), lambda i: (i, 0)),
        ]
        + [whole((half, units))] * 2,
        [((toks, 2 * half), F32)],
        [pl.BlockSpec((toks // steps, 2 * half), lambda i: (i, 0))],
        grid=(steps,),
    )[0]


def scaled_hid_kernel(groups, rank, at_ref, index_ref, prob_ref, *refs):
    out_ref = refs[-1]
    total = refs[0][...]
    for ref in refs[1:-1]:
        total = total + ref[...]
    place = relative(at_ref, index_ref[...], groups)
    prob = prob_ref[...].astype(F32)
    expert = iota(total.shape, 1) // rank
    scale = jnp.zeros(total.shape, F32)
    for k in range(place.shape[1]):
        scale = jnp.where(expert == place[:, k : k + 1], prob[:, k : k + 1], scale)
    scaled = (total * scale).T.astype(BF16)
    for o in range(groups):
        for q in range(2):
            at = (q * groups + o) * rank
            out_ref[lax.bitwise_xor(at_ref[1], o), pl.ds(q * rank, rank), :] = scaled[at : at + rank]


def scaled_hid_call(order, index, prob, parts, groups):
    toks, width = parts[0].shape
    rank = width // groups // 2
    shape = (groups, 2 * rank, toks)
    return order.call(
        functools.partial(scaled_hid_kernel, groups, rank),
        "scaled_hid",
        [index, prob, *parts],
        [whole(index.shape), whole(prob.shape)] + [whole((toks, width))] * len(parts),
        [(shape, BF16)],
        [whole(shape)],
    )[0]


def second_grad_kernel(places, at_ref, scaled_ref, *refs):
    grads, outs = refs[:-2], refs[-2:]
    rank, tile = outs[0].shape
    total = jnp.zeros((2 * rank, tile), F32)
    for o, grad_ref in zip(places, grads):
        total = total + dot(scaled_ref[lax.bitwise_xor(at_ref[1], o)], grad_ref[...], NN)
    for q, out_ref in enumerate(outs):
        out_ref[...] = adapter_scale * total[q * rank : (q + 1) * rank]


def second_grad_call(order, places, scaled, grads, feats):
    groups, both, toks = scaled.shape
    steps = 4
    tile = feats // steps
    block = pl.BlockSpec((both // 2, tile), lambda i: (0, i))
    return order.call(
        functools.partial(second_grad_kernel, places),
        "second_grad",
        [scaled, *[in_hbm(x) for x in grads]],
        [whole(scaled.shape)] + [pl.BlockSpec((toks, tile), lambda i: (0, i))] * groups,
        [((both // 2, feats), F32)] * 2,
        [block] * 2,
        grid=(steps,),
    )


def first_grad_kernel(groups, steps, at_ref, index_ref, prob_ref, low_ref, hid_ref, *rest):
    out_ref, sum_ref = rest
    step = pl.program_id(0)
    top = index_ref.shape[1]
    rank = out_ref.shape[1]
    low = spread_pairs(low_ref[...], top)
    column = pair_column(relative(at_ref, index_ref[...], groups).astype(F32))
    keep = expert_mask(column, low.shape[1], rank)
    scaled = jnp.where(keep, low * pair_column(prob_ref[...].astype(F32)), 0.0).astype(BF16)
    part = adapter_scale * dot(scaled, hid_ref[...], TN)

    @pl.when(step == 0)
    def _():
        sum_ref[...] = part

    @pl.when(step > 0)
    def _():
        sum_ref[...] += part

    @pl.when(step == steps - 1)
    def _():
        for o in range(groups):
            for q in range(2):
                expert = 2 * lax.bitwise_xor(at_ref[1], o) + lax.bitwise_xor(at_ref[2], q)
                rows = sum_ref[pl.ds((q * groups + o) * rank, rank), :]
                out_ref[expert] = rows.astype(BF16)


def first_grad_call(order, index, prob, low, hid, groups):
    (toks, top), (pairs, units) = index.shape, hid.shape
    width = low.shape[1]
    steps = 4
    shape = (2 * groups, width // groups // 2, units)
    return order.call(
        functools.partial(first_grad_kernel, groups, steps),
        "first_grad",
        [index, prob, low, in_hbm(hid)],
        [
            pl.BlockSpec((toks // steps, top), lambda i: (i, 0)),
            pl.BlockSpec((toks // steps, top), lambda i: (i, 0)),
            pl.BlockSpec((toks // steps, width), lambda i: (i, 0)),
            pl.BlockSpec((pairs // steps, units), lambda i: (i, 0)),
        ],
        [(shape, BF16)],
        [whole(shape)],
        grid=(steps,),
        scratch=[pltpu.VMEM((width, units), F32)],
    )[0]


def finish_kernel(count, slots, at_ref, index_all_ref, index_ref, prob_ref, low_ref, hid_ref, *rest):
    firsts, back = rest[:2], rest[2 : 2 + count]
    out_ref, sum_ref, all_ref, place_ref = rest[2 + count :]
    top = index_ref.shape[1]
    toks = index_all_ref.shape[0]
    experts = 2 * count

    @pl.when(pl.program_id(0) == 0)
    def _():
        for o, ref in enumerate(back):
            for q in range(2):
                all_ref[pl.ds((q * count + o) * slots, slots), :] = ref[pl.ds(q * slots, slots), :]
        experts_all = relative(at_ref, index_all_ref[...], count)
        hit = jnp.zeros((toks, experts), F32)
        for k in range(top):
            hit = jnp.where(iota((toks, experts), 1) == experts_all[:, k : k + 1], 1.0, hit)
        before = jnp.where(iota((toks, toks), 0) > iota((toks, toks), 1), 1.0, 0.0).astype(BF16)
        place_ref[...] = dot(before, hit.astype(BF16), NN)

    pairs = hid_ref.shape[0]
    some = index_ref.shape[0]
    column = pair_column(relative(at_ref, index_ref[...], count).astype(F32))
    place = spread_pairs(place_ref[pl.ds(pl.program_id(0) * some, some), :], top)
    mine = iota((pairs, experts), 1) == column.astype(jnp.int32)
    target = column * slots + jnp.sum(jnp.where(mine, place, 0.0), axis=1, keepdims=True)
    low = spread_pairs(low_ref[...], top)
    keep = expert_mask(column, low.shape[1], low.shape[1] // experts)
    low = jnp.where(keep, adapter_scale * low.astype(BF16).astype(F32), 0.0).astype(BF16)
    slot = iota((pairs, experts * slots), 1)
    pick = jnp.where(slot == target.astype(jnp.int32), 1.0, 0.0).astype(BF16)
    half = low.shape[1] // 2
    value = dot(pick, all_ref[...], NN)
    value = value + dot(low[:, :half], firsts[0][...], NN) + dot(low[:, half:], firsts[1][...], NN)
    value = value.astype(BF16).astype(F32)
    out_ref[...] = (value * pair_column(prob_ref[...].astype(F32))).astype(BF16)
    sums = jnp.sum(value * hid_ref[...].astype(F32), axis=1, keepdims=True)
    sums = jnp.where(diagonal(pairs, top), sums, 0.0)
    sum_ref[...] = sums.reshape(some, top, top).sum(axis=1)


def finish_call(order, index, prob, low, hid, firsts, back):
    (toks, top), (pairs, units) = index.shape, hid.shape
    width = low.shape[1]
    both = back[0].shape[0]
    steps = 4
    count = len(back)

    def rows(n, columns):
        return pl.BlockSpec((n // steps, columns), lambda i: (i, 0))

    return order.call(
        functools.partial(finish_kernel, count, both // 2),
        "finish",
        [index, index, prob, low, in_hbm(hid), *firsts, *[in_hbm(x) for x in back]],
        [whole(index.shape), rows(toks, top), rows(toks, top), rows(toks, width), rows(pairs, units)]
        + [whole(firsts[0].shape)] * 2
        + [whole((both, units))] * count,
        [((pairs, units), BF16), ((toks, top), F32)],
        [rows(pairs, units), rows(toks, top)],
        grid=(steps,),
        scratch=[pltpu.VMEM((count * both, units), BF16), pltpu.VMEM((toks, 2 * count), F32)],
    )


def body(grad, hidden, index, weight, down, first, second):
    toks, top = index.shape
    exp_local, units_all, feats = down.shape
    units, rank = first.shape[1:]
    groups, cores, shares = lax.axis_size("ep"), lax.axis_size("sub"), lax.axis_size("rep")
    assert exp_local == 1 and cores == 2 and groups & (groups - 1) == 0
    cap = min(toks, 5 * toks * top // (4 * groups * cores))
    slots = -(-cap // 16) * 16
    pairs = toks * top
    at = jnp.stack([lax.axis_index(name).astype(jnp.int32) for name in ("rep", "ep", "sub")])
    order = Order(at)

    def turn(x, offset):
        return lax.ppermute(x, "rep", [(r, (r + offset) % shares) for r in range(shares)])

    def all_shares(x):
        return [x] + [turn(x, k) for k in range(1, shares)]

    def flip(x, mask):
        return lax.ppermute(x, "ep", [(i, i ^ mask) for i in range(groups)])

    def swap(x):
        return lax.ppermute(x, "sub", [(0, 1), (1, 0)])

    def exchange(x, axes="ep"):
        return lax.all_to_all(x, axes, split_axis=0, concat_axis=0, tiled=True)

    blocks = {0: pack_call(order, grad, first[0], index)}

    def fetch(o):
        if o not in blocks:
            last = o & -o
            blocks[o] = flip(fetch(o ^ last), last)
        return blocks[o]

    downs = [down[0], swap(down[0])]
    seconds = [second[0], swap(second[0])]

    if groups == 8:
        batches = [(0, 1), (2, 4), (3, 6), (5, 7)]
    else:
        batches = [(o, o + 1) for o in range(0, groups, 2)]
    places = [o for batch in batches for o in batch]
    back, lows, waiting = {}, [], []

    def arrived(i):
        order.wait([back[o] for o in batches[i] if o])

    def send_back(batch, parts):
        for o, rows in zip(batch, share_sum_call(order, parts, 2, slots)):
            back[o] = flip(rows, o) if o else rows

    for i, batch in enumerate(batches):
        *give, keep, low = expert_rows_call(
            order, [fetch(o) for o in batch], seconds, downs, shares, slots
        )
        lows.append(low)
        if 1 < i < len(batches) - 1:
            arrived(i - 2)
        if i > 0:
            send_back(*waiting)
        waiting = (batch, [keep] + [turn(x, k + 1) for k, x in enumerate(give)])

    hid = hidden.reshape(pairs, units)
    grads = [blocks[o] for o in places]

    low_grad, first_own = collect_call(order, places, lows, grads, feats)
    firsts = [x.reshape(groups * rank, units) for x in (first_own, swap(first_own))]
    low_grad = all_shares(exchange(low_grad))
    low_hid = all_shares(lowrank_hid_call(order, index, hid, firsts, groups))
    send_back(*waiting)

    arrived(len(batches) - 3)
    arrived(len(batches) - 2)
    scaled_hid = exchange(scaled_hid_call(order, index, weight, low_hid, groups))

    low_grad = low_dense_call(order, low_grad)
    first_part = first_grad_call(order, index, weight, low_grad, hid, groups)
    first_grad = jnp.sum(exchange(first_part, ("ep", "sub")).astype(F32), axis=0)
    second_keep, second_give = second_grad_call(order, places, scaled_hid, grads, feats)
    second_grad = second_keep + swap(second_give)

    back = [back[o] for o in range(groups)]
    grad_hidden, sums = finish_call(order, index, weight, low_grad, hid, firsts, back)
    sums = sums + turn(sums, 1) if shares == 2 else lax.psum(sums, "rep")
    return (
        grad_hidden.reshape(toks, top, units),
        sums,
        first_grad.T[None],
        second_grad[None],
    )


def solution(mesh):
    return jax.shard_map(
        body,
        mesh=mesh,
        in_specs=(
            P(("grp", "ep", "sub"), "rep"),
            P(("grp", "ep", "sub"), None, "rep"),
            P(("grp", "ep", "sub"), None),
            P(("grp", "ep", "sub"), None),
            P(("ep", "sub"), None, "rep"),
            P(("grp", "ep", "sub"), "rep", None),
            P(("grp", "ep", "sub"), None, "rep"),
        ),
        out_specs=(
            P(("grp", "ep", "sub"), None, "rep"),
            P(("grp", "ep", "sub"), None),
            P(("grp", "ep", "sub"), "rep", None),
            P(("grp", "ep", "sub"), None, "rep"),
        ),
        check_vma=False,
    )
```

```python
import functools

import jax
import jax.numpy as jnp
from jax import lax
from jax.experimental import pallas as pl
from jax.experimental.pallas import tpu as pltpu
from jax.sharding import PartitionSpec as P

adapter_scale = 2.0
BF16 = jnp.bfloat16
F32 = jnp.float32
NT = (((1,), (1,)), ((), ()))
TN = (((0,), (0,)), ((), ()))
NN = (((1,), (0,)), ((), ()))
SMALL = pl.CostEstimate(flops=1, bytes_accessed=1, transcendentals=0)
ANY = pl.BlockSpec(memory_space=pl.ANY)
SMEM = pl.BlockSpec(memory_space=pltpu.SMEM)
VMEM = pl.BlockSpec(memory_space=pltpu.VMEM)


def dot(a, b, dims):
    return lax.dot_general(a, b, dims, preferred_element_type=F32)


def iota(shape, axis):
    return lax.broadcasted_iota(jnp.int32, shape, axis)


def whole(shape):
    return pl.BlockSpec(shape, lambda *_: (0,) * len(shape))


def in_hbm(x):
    return pltpu.with_memory_space_constraint(x, pltpu.HBM)


class Order:
    def __init__(self, at):
        self.at, self.last = at, []

    def wait(self, arrays):
        self.last = self.last + list(arrays)

    def call(self, kernel, name, arrays, in_specs, outs, out_specs, grid=(1,), scratch=(), mib=16, cost=SMALL, **more):
        count, last = 1 + len(arrays), len(self.last)

        def ordered(*refs):
            here = count + last + len(outs)
            kernel(*refs[:count], *refs[count + last : here], *refs[here + 1 :])

        *result, token = pl.pallas_call(
            ordered,
            grid=grid,
            in_specs=[SMEM, *in_specs] + [ANY] * last,
            out_specs=[*out_specs, ANY],
            scratch_shapes=scratch,
            out_shape=[jax.ShapeDtypeStruct(*o) if isinstance(o, tuple) else o for o in outs]
            + [pltpu.HBM((8, 128), F32)],
            compiler_params=pltpu.CompilerParams(vmem_limit_bytes=mib * 2**20),
            cost_estimate=cost,
            name=name,
            **more,
        )(self.at, *arrays, *self.last)
        self.last = [in_hbm(token)]
        return result


def relative(at_ref, index, groups):
    o = lax.bitwise_xor(lax.shift_right_logical(index, 1), at_ref[1])
    q = lax.bitwise_xor(lax.bitwise_and(index, 1), at_ref[2])
    return q * groups + o


def spread_pairs(dense, top):
    toks, width = dense.shape
    return jnp.broadcast_to(dense[:, None, :], (toks, top, width)).reshape(toks * top, width)


def diagonal(pairs, top):
    return iota((pairs, top), 1) == lax.bitwise_and(iota((pairs, top), 0), top - 1)


def pair_column(table):
    toks, top = table.shape
    wide = spread_pairs(table, top)
    return jnp.sum(jnp.where(diagonal(toks * top, top), wide, 0.0), axis=1, keepdims=True)


def expert_mask(column, width, rank):
    return iota((column.shape[0], width), 1) // rank == column.astype(jnp.int32)


def pack_kernel(rank, at_ref, grad_ref, first_ref, index_ref, out_ref):
    toks, feats = grad_ref.shape
    extra = out_ref.shape[1] - feats
    out_ref[:, pl.ds(0, feats)] = grad_ref[...]
    same = jnp.where(iota((rank, rank), 0) == iota((rank, rank), 1), 1.0, 0.0).astype(BF16)
    factor = dot(same, first_ref[...], NT).astype(BF16)
    for k in range(3):
        piece = factor[:, k * extra : (k + 1) * extra]
        out_ref[pl.ds(k * rank, rank), pl.ds(feats, extra)] = piece
    top = index_ref.shape[1]
    out_ref[pl.ds(3 * rank, toks - 3 * rank), pl.ds(feats, extra)] = jnp.full(
        (toks - 3 * rank, extra), -1.0, BF16
    )
    turn = jnp.where(iota((16, top), 0) == iota((16, top), 1), 1.0, 0.0).astype(BF16)
    routes = dot(turn, index_ref[...].astype(F32).astype(BF16), NT)
    routes = jnp.where(iota((16, toks), 0) < top, routes, -1.0)
    out_ref[pl.ds(3 * rank, 16), pl.ds(feats, toks)] = routes.astype(BF16)


def pack_call(order, grad, first, index):
    (toks, feats), (units, rank) = grad.shape, first.shape
    extra = units // 3
    shape = (toks, feats + extra)
    return order.call(
        functools.partial(pack_kernel, rank),
        "pack_block",
        [grad, first, index],
        [whole(grad.shape), whole(first.shape), whole(index.shape)],
        [(shape, BF16)],
        [whole(shape)],
    )[0]


def load_kernel(at_ref, down_ref, out_ref, sems):
    parts = sems.shape[0]
    rows = down_ref.shape[0] // parts
    copies = [
        pltpu.make_async_copy(
            down_ref.at[pl.ds(k * rows, rows), :], out_ref.at[pl.ds(k * rows, rows), :], sems.at[k]
        )
        for k in range(parts)
    ]
    for copy in copies:
        copy.start()
    for copy in copies:
        copy.wait()


def load_call(order, down):
    return order.call(
        load_kernel,
        "load_matrix",
        [in_hbm(down)],
        [ANY],
        [pltpu.VMEM(down.shape, down.dtype)],
        [VMEM],
        grid=(),
        scratch=[pltpu.SemaphoreType.DMA((4,))],
    )[0]


def expert_rows_kernel(slots, tiles, shares, batch, route_row, at_ref, *rest):
    grads, seconds, downs = rest[:batch], rest[batch : batch + 2], rest[batch + 2 : batch + 4]
    *outs, low_ref = rest[batch + 4 : batch + 5 + shares]
    block_ref, turned_ref, block_sems = rest[batch + 5 + shares :]
    tile = downs[0].shape[0] // shares // tiles
    feats = turned_ref.shape[1]
    toks = block_ref.shape[1]
    blocks = [
        pltpu.make_async_copy(ref, block_ref.at[k], block_sems.at[k]) for k, ref in enumerate(grads)
    ]
    for copy in blocks:
        copy.start()

    before = jnp.where(iota((toks, toks), 0) < iota((toks, toks), 1), 1.0, 0.0).astype(BF16)
    columns = turned_ref.shape[2]
    slot = iota((columns, batch * toks), 0).astype(F32)
    second = jnp.concatenate([ref[...] for ref in seconds], axis=0)
    routes = []
    for k in range(batch):
        blocks[k].wait()
        routes.append(block_ref[k, pl.ds(route_row, 16), pl.ds(feats, toks)].astype(F32))
    grad = block_ref[:, :, pl.ds(0, feats)].reshape(batch * toks, feats)
    for q in range(2):
        expert = at_ref[1] * 2 + lax.bitwise_xor(at_ref[2], q)
        targets = []
        for k in range(batch):
            hits = jnp.where(routes[k] == expert.astype(F32), 1.0, 0.0)
            mine = jnp.max(hits, axis=0, keepdims=True)
            pos = dot(jnp.broadcast_to(mine, (16, toks)).astype(BF16), before, NN)[:1]
            targets.append(jnp.where(mine > 0.0, pos + float(k * slots), -1.0))
        pick = jnp.where(slot == jnp.concatenate(targets, axis=1), 1.0, 0.0)
        turned_ref[q] = dot(grad, pick.T.astype(BF16), TN).astype(BF16)
    low = dot(second, grad, NT).astype(BF16)
    for k in range(batch):
        low_ref[k] = low[:, k * toks : (k + 1) * toks]

    rows = batch * slots
    for k in range(shares):
        share = lax.rem(at_ref[0] + k + 1, shares)
        for q in range(2):
            for t in range(tiles):
                row = pl.multiple_of((share * tiles + t) * tile, tile)
                value = dot(downs[q][pl.ds(row, tile), :], turned_ref[q], NN)
                outs[k][pl.ds(q * rows, rows), pl.ds(t * tile, tile)] = value.T[:rows].astype(BF16)


def expert_rows_call(order, grads, seconds, downs, shares, slots):
    batch, (toks, wide) = len(grads), grads[0].shape
    rank, feats = seconds[0].shape
    units = downs[0].shape[0] // shares
    rows = 2 * batch * slots
    return order.call(
        functools.partial(expert_rows_kernel, slots, 3, shares, batch, 3 * rank),
        "expert_rows",
        [*grads, *seconds, *[pltpu.with_memory_space_constraint(x, pltpu.VMEM) for x in downs]],
        [ANY] * batch + [VMEM] * 4,
        [((rows, units), BF16)] * shares + [((batch, 2 * rank, toks), BF16)],
        [VMEM] * (shares + 1),
        grid=(),
        scratch=[
            pltpu.VMEM((batch, toks, wide), BF16),
            pltpu.VMEM((2, feats, -(-batch * slots // 128) * 128), BF16),
            pltpu.SemaphoreType.DMA((batch,)),
        ],
    )


def share_sum_kernel(parts, slots, at_ref, *refs):
    outs = refs[parts:]
    for k, out_ref in enumerate(outs):
        for q in range(2):
            at = pl.ds((q * len(outs) + k) * slots, slots)
            total = refs[0][at, :].astype(F32)
            for part in refs[1:parts]:
                total = total + part[at, :].astype(F32)
            out_ref[pl.ds(q * slots, slots), :] = total.astype(BF16)


def share_sum_call(order, parts, batch, slots):
    rows, units = parts[0].shape
    shape = (2 * slots, units)
    return order.call(
        functools.partial(share_sum_kernel, len(parts), slots),
        "share_sum",
        parts,
        [whole((rows, units))] * len(parts),
        [(shape, BF16)] * batch,
        [whole(shape)] * batch,
    )


def collect_kernel(places, at_ref, *refs):
    low_ref, first_ref = refs[-2:]
    rank = first_ref.shape[1]
    at = 0
    lows = len(refs) - 2 - len(places)
    for ref in refs[:lows]:
        for k in range(ref.shape[0]):
            low_ref[lax.bitwise_xor(at_ref[1], places[at])] = ref[k]
            at += 1
    for o, ref in zip(places, refs[lows:-2]):
        wide = ref.shape[1]
        for k in range(3):
            first_ref[o, :, pl.ds(k * wide, wide)] = ref[pl.ds(k * rank, rank), :]


def collect_call(order, places, lows, grads, feats):
    groups, (toks, wide) = len(grads), grads[0].shape
    rank = lows[0].shape[1] // 2
    extra = wide - feats
    low_shape, first_shape = (groups, 2 * rank, toks), (groups, rank, 3 * extra)
    return order.call(
        functools.partial(collect_kernel, places),
        "collect_blocks",
        [*lows, *[in_hbm(x) for x in grads]],
        [whole(b.shape) for b in lows]
        + [pl.BlockSpec((toks, extra), lambda i: (0, feats // extra))] * groups,
        [(low_shape, BF16), (first_shape, BF16)],
        [whole(low_shape), whole(first_shape)],
    )


def low_dense_kernel(at_ref, *refs):
    out_ref, sum_ref = refs[-2:]
    groups, both, _ = refs[0].shape
    rank = both // 2
    for o in range(groups):
        total = refs[0][lax.bitwise_xor(at_ref[1], o)].astype(F32)
        for ref in refs[1:-2]:
            total = total + ref[lax.bitwise_xor(at_ref[1], o)].astype(F32)
        for q in range(2):
            at = pl.ds((q * groups + o) * rank, rank)
            sum_ref[at, :] = total[q * rank : (q + 1) * rank]
    out_ref[...] = sum_ref[...].T


def low_dense_call(order, parts):
    groups, both, toks = parts[0].shape
    shape = (toks, groups * both)
    return order.call(
        low_dense_kernel,
        "low_dense",
        parts,
        [whole(parts[0].shape)] * len(parts),
        [(shape, F32)],
        [whole(shape)],
        scratch=[pltpu.VMEM((groups * both, toks), F32)],
    )[0]


def lowrank_hid_kernel(groups, at_ref, index_ref, hid_ref, *rest):
    firsts, out_ref = rest[:2], rest[2]
    top = index_ref.shape[1]
    rank = firsts[0].shape[0] // groups
    wide = jnp.concatenate([dot(hid_ref[...], ref[...], NT) for ref in firsts], axis=1)
    column = pair_column(relative(at_ref, index_ref[...], groups).astype(F32))
    wide = jnp.where(expert_mask(column, wide.shape[1], rank), wide, 0.0)
    out_ref[...] = wide.reshape(wide.shape[0] // top, top, wide.shape[1]).sum(axis=1)


def lowrank_hid_call(order, index, hid, firsts, groups):
    (toks, top), (pairs, units) = index.shape, hid.shape
    half = firsts[0].shape[0]
    steps = 4
    return order.call(
        functools.partial(lowrank_hid_kernel, groups),
        "lowrank_hid",
        [index, in_hbm(hid), *firsts],
        [
            pl.BlockSpec((toks // steps, top), lambda i: (i, 0)),
            pl.BlockSpec((pairs // steps, units), lambda i: (i, 0)),
        ]
        + [whole((half, units))] * 2,
        [((toks, 2 * half), F32)],
        [pl.BlockSpec((toks // steps, 2 * half), lambda i: (i, 0))],
        grid=(steps,),
    )[0]


def scaled_hid_kernel(groups, rank, at_ref, index_ref, prob_ref, *refs):
    out_ref = refs[-1]
    total = refs[0][...]
    for ref in refs[1:-1]:
        total = total + ref[...]
    place = relative(at_ref, index_ref[...], groups)
    prob = prob_ref[...].astype(F32)
    expert = iota(total.shape, 1) // rank
    scale = jnp.zeros(total.shape, F32)
    for k in range(place.shape[1]):
        scale = jnp.where(expert == place[:, k : k + 1], prob[:, k : k + 1], scale)
    scaled = (total * scale).T.astype(BF16)
    for o in range(groups):
        for q in range(2):
            at = (q * groups + o) * rank
            out_ref[lax.bitwise_xor(at_ref[1], o), pl.ds(q * rank, rank), :] = scaled[at : at + rank]


def scaled_hid_call(order, index, prob, parts, groups):
    toks, width = parts[0].shape
    rank = width // groups // 2
    shape = (groups, 2 * rank, toks)
    return order.call(
        functools.partial(scaled_hid_kernel, groups, rank),
        "scaled_hid",
        [index, prob, *parts],
        [whole(index.shape), whole(prob.shape)] + [whole((toks, width))] * len(parts),
        [(shape, BF16)],
        [whole(shape)],
    )[0]


def second_grad_kernel(places, at_ref, scaled_ref, *refs):
    grads, outs = refs[:-2], refs[-2:]
    rank, tile = outs[0].shape
    total = jnp.zeros((2 * rank, tile), F32)
    for o, grad_ref in zip(places, grads):
        total = total + dot(scaled_ref[lax.bitwise_xor(at_ref[1], o)], grad_ref[...], NN)
    for q, out_ref in enumerate(outs):
        out_ref[...] = adapter_scale * total[q * rank : (q + 1) * rank]


def second_grad_call(order, places, scaled, grads, feats):
    groups, both, toks = scaled.shape
    steps = 4
    tile = feats // steps
    block = pl.BlockSpec((both // 2, tile), lambda i: (0, i))
    return order.call(
        functools.partial(second_grad_kernel, places),
        "second_grad",
        [scaled, *[in_hbm(x) for x in grads]],
        [whole(scaled.shape)] + [pl.BlockSpec((toks, tile), lambda i: (0, i))] * groups,
        [((both // 2, feats), F32)] * 2,
        [block] * 2,
        grid=(steps,),
    )


def first_grad_kernel(groups, steps, at_ref, index_ref, prob_ref, low_ref, hid_ref, *rest):
    out_ref, sum_ref = rest
    step = pl.program_id(0)
    top = index_ref.shape[1]
    rank = out_ref.shape[1]
    low = spread_pairs(low_ref[...], top)
    column = pair_column(relative(at_ref, index_ref[...], groups).astype(F32))
    keep = expert_mask(column, low.shape[1], rank)
    scaled = jnp.where(keep, low * pair_column(prob_ref[...].astype(F32)), 0.0).astype(BF16)
    part = adapter_scale * dot(scaled, hid_ref[...], TN)

    @pl.when(step == 0)
    def _():
        sum_ref[...] = part

    @pl.when(step > 0)
    def _():
        sum_ref[...] += part

    @pl.when(step == steps - 1)
    def _():
        for o in range(groups):
            for q in range(2):
                expert = 2 * lax.bitwise_xor(at_ref[1], o) + lax.bitwise_xor(at_ref[2], q)
                rows = sum_ref[pl.ds((q * groups + o) * rank, rank), :]
                out_ref[expert] = rows.astype(BF16)


def first_grad_call(order, index, prob, low, hid, groups):
    (toks, top), (pairs, units) = index.shape, hid.shape
    width = low.shape[1]
    steps = 4
    shape = (2 * groups, width // groups // 2, units)
    return order.call(
        functools.partial(first_grad_kernel, groups, steps),
        "first_grad",
        [index, prob, low, in_hbm(hid)],
        [
            pl.BlockSpec((toks // steps, top), lambda i: (i, 0)),
            pl.BlockSpec((toks // steps, top), lambda i: (i, 0)),
            pl.BlockSpec((toks // steps, width), lambda i: (i, 0)),
            pl.BlockSpec((pairs // steps, units), lambda i: (i, 0)),
        ],
        [(shape, BF16)],
        [whole(shape)],
        grid=(steps,),
        scratch=[pltpu.VMEM((width, units), F32)],
    )[0]


def finish_kernel(count, slots, at_ref, index_all_ref, index_ref, prob_ref, low_ref, hid_ref, *rest):
    firsts, back = rest[:2], rest[2 : 2 + count]
    out_ref, sum_ref, all_ref, place_ref = rest[2 + count :]
    top = index_ref.shape[1]
    toks = index_all_ref.shape[0]
    experts = 2 * count

    @pl.when(pl.program_id(0) == 0)
    def _():
        for o, ref in enumerate(back):
            for q in range(2):
                all_ref[pl.ds((q * count + o) * slots, slots), :] = ref[pl.ds(q * slots, slots), :]
        experts_all = relative(at_ref, index_all_ref[...], count)
        hit = jnp.zeros((toks, experts), F32)
        for k in range(top):
            hit = jnp.where(iota((toks, experts), 1) == experts_all[:, k : k + 1], 1.0, hit)
        before = jnp.where(iota((toks, toks), 0) > iota((toks, toks), 1), 1.0, 0.0).astype(BF16)
        place_ref[...] = dot(before, hit.astype(BF16), NN)

    pairs = hid_ref.shape[0]
    some = index_ref.shape[0]
    column = pair_column(relative(at_ref, index_ref[...], count).astype(F32))
    place = spread_pairs(place_ref[pl.ds(pl.program_id(0) * some, some), :], top)
    mine = iota((pairs, experts), 1) == column.astype(jnp.int32)
    target = column * slots + jnp.sum(jnp.where(mine, place, 0.0), axis=1, keepdims=True)
    low = spread_pairs(low_ref[...], top)
    keep = expert_mask(column, low.shape[1], low.shape[1] // experts)
    low = jnp.where(keep, adapter_scale * low.astype(BF16).astype(F32), 0.0).astype(BF16)
    slot = iota((pairs, experts * slots), 1)
    pick = jnp.where(slot == target.astype(jnp.int32), 1.0, 0.0).astype(BF16)
    half = low.shape[1] // 2
    value = dot(pick, all_ref[...], NN)
    value = value + dot(low[:, :half], firsts[0][...], NN) + dot(low[:, half:], firsts[1][...], NN)
    value = value.astype(BF16).astype(F32)
    out_ref[...] = (value * pair_column(prob_ref[...].astype(F32))).astype(BF16)
    sums = jnp.sum(value * hid_ref[...].astype(F32), axis=1, keepdims=True)
    sums = jnp.where(diagonal(pairs, top), sums, 0.0)
    sum_ref[...] = sums.reshape(some, top, top).sum(axis=1)


def finish_call(order, index, prob, low, hid, firsts, back):
    (toks, top), (pairs, units) = index.shape, hid.shape
    width = low.shape[1]
    both = back[0].shape[0]
    steps = 4
    count = len(back)

    def rows(n, columns):
        return pl.BlockSpec((n // steps, columns), lambda i: (i, 0))

    return order.call(
        functools.partial(finish_kernel, count, both // 2),
        "finish",
        [index, index, prob, low, in_hbm(hid), *firsts, *[in_hbm(x) for x in back]],
        [whole(index.shape), rows(toks, top), rows(toks, top), rows(toks, width), rows(pairs, units)]
        + [whole(firsts[0].shape)] * 2
        + [whole((both, units))] * count,
        [((pairs, units), BF16), ((toks, top), F32)],
        [rows(pairs, units), rows(toks, top)],
        grid=(steps,),
        scratch=[pltpu.VMEM((count * both, units), BF16), pltpu.VMEM((toks, 2 * count), F32)],
    )


def body(grad, hidden, index, weight, down, first, second):
    toks, top = index.shape
    exp_local, units_all, feats = down.shape
    units, rank = first.shape[1:]
    groups, cores, shares = lax.axis_size("ep"), lax.axis_size("sub"), lax.axis_size("rep")
    assert exp_local == 1 and cores == 2 and groups & (groups - 1) == 0
    cap = min(toks, 5 * toks * top // (4 * groups * cores))
    slots = -(-cap // 16) * 16
    pairs = toks * top
    at = jnp.stack([lax.axis_index(name).astype(jnp.int32) for name in ("rep", "ep", "sub")])
    order = Order(at)

    def turn(x, offset):
        return lax.ppermute(x, "rep", [(r, (r + offset) % shares) for r in range(shares)])

    def all_shares(x):
        return [x] + [turn(x, k) for k in range(1, shares)]

    def flip(x, mask):
        return lax.ppermute(x, "ep", [(i, i ^ mask) for i in range(groups)])

    def swap(x):
        return lax.ppermute(x, "sub", [(0, 1), (1, 0)])

    def exchange(x, axes="ep"):
        return lax.all_to_all(x, axes, split_axis=0, concat_axis=0, tiled=True)

    blocks = {0: pack_call(order, grad, first[0], index)}

    def fetch(o):
        if o not in blocks:
            last = o & -o
            blocks[o] = flip(fetch(o ^ last), last)
        return blocks[o]

    downs = [load_call(order, down[0]), swap(down[0])]
    seconds = [second[0], swap(second[0])]

    if groups == 8:
        batches = [(0, 1), (2, 4), (3, 6), (5, 7)]
    else:
        batches = [(o, o + 1) for o in range(0, groups, 2)]
    places = [o for batch in batches for o in batch]
    back, lows, waiting = {}, [], []

    def arrived(i):
        order.wait([back[o] for o in batches[i] if o])

    def send_back(batch, parts):
        for o, rows in zip(batch, share_sum_call(order, parts, 2, slots)):
            back[o] = flip(rows, o) if o else rows

    for i, batch in enumerate(batches):
        *give, keep, low = expert_rows_call(
            order, [fetch(o) for o in batch], seconds, downs, shares, slots
        )
        lows.append(low)
        if i > 1:
            arrived(i - 2)
        if i > 0:
            send_back(*waiting)
        waiting = (batch, [keep] + [turn(x, k + 1) for k, x in enumerate(give)])

    hid = hidden.reshape(pairs, units)
    grads = [blocks[o] for o in places]

    low_grad, first_own = collect_call(order, places, lows, grads, feats)
    firsts = [x.reshape(groups * rank, units) for x in (first_own, swap(first_own))]
    low_grad = all_shares(exchange(low_grad))
    arrived(len(batches) - 2)
    send_back(*waiting)
    low_hid = all_shares(lowrank_hid_call(order, index, hid, firsts, groups))

    low_grad = low_dense_call(order, low_grad)
    first_part = first_grad_call(order, index, weight, low_grad, hid, groups)
    first_part = exchange(first_part, ("ep", "sub"))
    first_grad = jnp.sum(first_part.astype(F32), axis=0)

    scaled_hid = exchange(scaled_hid_call(order, index, weight, low_hid, groups))
    back = [back[o] for o in range(groups)]
    grad_hidden, sums = finish_call(order, index, weight, low_grad, hid, firsts, back)
    sums = sums + turn(sums, 1) if shares == 2 else lax.psum(sums, "rep")
    order.wait([first_part])
    second_keep, second_give = second_grad_call(order, places, scaled_hid, grads, feats)
    second_grad = second_keep + swap(second_give)
    return (
        grad_hidden.reshape(toks, top, units),
        sums,
        first_grad.T[None],
        second_grad[None],
    )


def solution(mesh):
    return jax.shard_map(
        body,
        mesh=mesh,
        in_specs=(
            P(("grp", "ep", "sub"), "rep"),
            P(("grp", "ep", "sub"), None, "rep"),
            P(("grp", "ep", "sub"), None),
            P(("grp", "ep", "sub"), None),
            P(("ep", "sub"), None, "rep"),
            P(("grp", "ep", "sub"), "rep", None),
            P(("grp", "ep", "sub"), None, "rep"),
        ),
        out_specs=(
            P(("grp", "ep", "sub"), None, "rep"),
            P(("grp", "ep", "sub"), None),
            P(("grp", "ep", "sub"), "rep", None),
            P(("grp", "ep", "sub"), None, "rep"),
        ),
        check_vma=False,
    )
```

```python
import functools

import jax
import jax.numpy as jnp
from jax import lax
from jax.experimental import pallas as pl
from jax.experimental.pallas import tpu as pltpu
from jax.sharding import PartitionSpec as P

adapter_scale = 2.0
BF16 = jnp.bfloat16
F32 = jnp.float32
NT = (((1,), (1,)), ((), ()))
TN = (((0,), (0,)), ((), ()))
NN = (((1,), (0,)), ((), ()))
SMALL = pl.CostEstimate(flops=1, bytes_accessed=1, transcendentals=0)
LONG = pl.CostEstimate(flops=1, bytes_accessed=2 * 10**7, transcendentals=0)
ANY = pl.BlockSpec(memory_space=pl.ANY)
SMEM = pl.BlockSpec(memory_space=pltpu.SMEM)
VMEM = pl.BlockSpec(memory_space=pltpu.VMEM)


def dot(a, b, dims):
    return lax.dot_general(a, b, dims, preferred_element_type=F32)


def iota(shape, axis):
    return lax.broadcasted_iota(jnp.int32, shape, axis)


def whole(shape):
    return pl.BlockSpec(shape, lambda *_: (0,) * len(shape))


def in_hbm(x):
    return pltpu.with_memory_space_constraint(x, pltpu.HBM)


class Order:
    def __init__(self, at):
        self.at, self.last = at, []

    def wait(self, arrays):
        self.last = self.last + list(arrays)

    def call(self, kernel, name, arrays, in_specs, outs, out_specs, grid=(1,), scratch=(), mib=16, cost=SMALL, **more):
        count, last = 1 + len(arrays), len(self.last)

        def ordered(*refs):
            here = count + last + len(outs)
            kernel(*refs[:count], *refs[count + last : here], *refs[here + 1 :])

        *result, token = pl.pallas_call(
            ordered,
            grid=grid,
            in_specs=[SMEM, *in_specs] + [ANY] * last,
            out_specs=[*out_specs, ANY],
            scratch_shapes=scratch,
            out_shape=[jax.ShapeDtypeStruct(*o) if isinstance(o, tuple) else o for o in outs]
            + [pltpu.HBM((8, 128), F32)],
            compiler_params=pltpu.CompilerParams(vmem_limit_bytes=mib * 2**20),
            cost_estimate=cost,
            name=name,
            **more,
        )(self.at, *arrays, *self.last)
        self.last = [in_hbm(token)]
        return result


def relative(at_ref, index, groups):
    o = lax.bitwise_xor(lax.shift_right_logical(index, 1), at_ref[1])
    q = lax.bitwise_xor(lax.bitwise_and(index, 1), at_ref[2])
    return q * groups + o


def spread_pairs(dense, top):
    toks, width = dense.shape
    return jnp.broadcast_to(dense[:, None, :], (toks, top, width)).reshape(toks * top, width)


def diagonal(pairs, top):
    return iota((pairs, top), 1) == lax.bitwise_and(iota((pairs, top), 0), top - 1)


def pair_column(table):
    toks, top = table.shape
    wide = spread_pairs(table, top)
    return jnp.sum(jnp.where(diagonal(toks * top, top), wide, 0.0), axis=1, keepdims=True)


def expert_mask(column, width, rank):
    return iota((column.shape[0], width), 1) // rank == column.astype(jnp.int32)


def pack_kernel(at_ref, grad_ref, first_ref, index_ref, out_ref):
    toks, feats = grad_ref.shape
    rank = first_ref.shape[0]
    extra = out_ref.shape[1] - feats
    out_ref[:, pl.ds(0, feats)] = grad_ref[...]
    for k in range(3):
        piece = first_ref[:, pl.ds(k * extra, extra)]
        out_ref[pl.ds(k * rank, rank), pl.ds(feats, extra)] = piece
    top = index_ref.shape[0]
    out_ref[pl.ds(3 * rank, toks - 3 * rank), pl.ds(feats, extra)] = jnp.full(
        (toks - 3 * rank, extra), -1.0, BF16
    )
    routes = index_ref[...].astype(F32)
    routes = jnp.concatenate([routes, jnp.full((16 - top, toks), -1.0, F32)], axis=0)
    out_ref[pl.ds(3 * rank, 16), pl.ds(feats, toks)] = routes.astype(BF16)


def pack_call(order, grad, first, index):
    (toks, feats), (rank, units) = grad.shape, first.shape
    shape = (toks, feats + units // 3)
    return order.call(
        pack_kernel,
        "pack_block",
        [in_hbm(grad), first, index],
        [whole(grad.shape), whole(first.shape), whole(index.shape)],
        [(shape, BF16)],
        [whole(shape)],
    )[0]


def load_kernel(at_ref, down_ref, second_ref, out_ref, same_ref, sems):
    parts = sems.shape[0]
    rows = down_ref.shape[0] // parts
    copies = [
        pltpu.make_async_copy(
            down_ref.at[pl.ds(k * rows, rows), :], out_ref.at[pl.ds(k * rows, rows), :], sems.at[k]
        )
        for k in range(parts)
    ]
    for copy in copies:
        copy.start()
    same_ref[...] = second_ref[...]
    for copy in copies:
        copy.wait()


def load_call(order, down, second):
    return order.call(
        load_kernel,
        "load_matrix",
        [in_hbm(down), second],
        [ANY, VMEM],
        [pltpu.VMEM(down.shape, down.dtype), (second.shape, second.dtype)],
        [VMEM, VMEM],
        grid=(),
        scratch=[pltpu.SemaphoreType.DMA((4,))],
    )


def expert_rows_kernel(slots, tiles, shares, batch, route_row, at_ref, *rest):
    grads, seconds, downs = rest[:batch], rest[batch : batch + 2], rest[batch + 2 : batch + 4]
    *outs, low_ref = rest[batch + 4 : batch + 5 + shares]
    block_ref, turned_ref, block_sems = rest[batch + 5 + shares :]
    tile = downs[0].shape[0] // shares // tiles
    feats = turned_ref.shape[1]
    toks = block_ref.shape[1]
    blocks = [
        pltpu.make_async_copy(ref, block_ref.at[k], block_sems.at[k]) for k, ref in enumerate(grads)
    ]
    for copy in blocks:
        copy.start()

    before = jnp.where(iota((toks, toks), 0) < iota((toks, toks), 1), 1.0, 0.0).astype(BF16)
    columns = turned_ref.shape[2]
    slot = iota((columns, batch * toks), 0).astype(F32)
    second = jnp.concatenate([ref[...] for ref in seconds], axis=0)
    routes = []
    for k in range(batch):
        blocks[k].wait()
        routes.append(block_ref[k, pl.ds(route_row, 16), pl.ds(feats, toks)].astype(F32))
    grad = block_ref[:, :, pl.ds(0, feats)].reshape(batch * toks, feats)
    for q in range(2):
        expert = at_ref[1] * 2 + lax.bitwise_xor(at_ref[2], q)
        targets = []
        for k in range(batch):
            hits = jnp.where(routes[k] == expert.astype(F32), 1.0, 0.0)
            mine = jnp.max(hits, axis=0, keepdims=True)
            pos = dot(jnp.broadcast_to(mine, (16, toks)).astype(BF16), before, NN)[:1]
            targets.append(jnp.where(mine > 0.0, pos + float(k * slots), -1.0))
        pick = jnp.where(slot == jnp.concatenate(targets, axis=1), 1.0, 0.0)
        turned_ref[q] = dot(grad, pick.T.astype(BF16), TN).astype(BF16)
    low = dot(second, grad, NT).astype(BF16)
    for k in range(batch):
        low_ref[k] = low[:, k * toks : (k + 1) * toks]

    rows = batch * slots
    for k in range(shares):
        share = lax.rem(at_ref[0] + k + 1, shares)
        for q in range(2):
            for t in range(tiles):
                row = pl.multiple_of((share * tiles + t) * tile, tile)
                value = dot(downs[q][pl.ds(row, tile), :], turned_ref[q], NN)
                outs[k][pl.ds(q * rows, rows), pl.ds(t * tile, tile)] = value.T[:rows].astype(BF16)


def expert_rows_call(order, grads, seconds, downs, shares, slots):
    batch, (toks, wide) = len(grads), grads[0].shape
    rank, feats = seconds[0].shape
    units = downs[0].shape[0] // shares
    rows = 2 * batch * slots
    return order.call(
        functools.partial(expert_rows_kernel, slots, 3, shares, batch, 3 * rank),
        "expert_rows",
        [*grads, *seconds, *[pltpu.with_memory_space_constraint(x, pltpu.VMEM) for x in downs]],
        [ANY] * batch + [VMEM] * 4,
        [((rows, units), BF16)] * shares + [((batch, 2 * rank, toks), BF16)],
        [VMEM] * (shares + 1),
        grid=(),
        scratch=[
            pltpu.VMEM((batch, toks, wide), BF16),
            pltpu.VMEM((2, feats, -(-batch * slots // 128) * 128), BF16),
            pltpu.SemaphoreType.DMA((batch,)),
        ],
    )


def share_sum_kernel(parts, slots, at_ref, *refs):
    outs = refs[parts:]
    for k, out_ref in enumerate(outs):
        for q in range(2):
            at = pl.ds((q * len(outs) + k) * slots, slots)
            total = refs[0][at, :].astype(F32)
            for part in refs[1:parts]:
                total = total + part[at, :].astype(F32)
            out_ref[pl.ds(q * slots, slots), :] = total.astype(BF16)


def share_sum_call(order, parts, batch, slots):
    rows, units = parts[0].shape
    shape = (2 * slots, units)
    return order.call(
        functools.partial(share_sum_kernel, len(parts), slots),
        "share_sum",
        parts,
        [whole((rows, units))] * len(parts),
        [(shape, BF16)] * batch,
        [whole(shape)] * batch,
    )


def collect_kernel(places, at_ref, *refs):
    low_ref, first_ref = refs[-2:]
    rank = first_ref.shape[1]
    at = 0
    lows = len(refs) - 2 - len(places)
    for ref in refs[:lows]:
        for k in range(ref.shape[0]):
            low_ref[lax.bitwise_xor(at_ref[1], places[at])] = ref[k]
            at += 1
    for o, ref in zip(places, refs[lows:-2]):
        wide = ref.shape[1]
        for k in range(3):
            first_ref[o, :, pl.ds(k * wide, wide)] = ref[pl.ds(k * rank, rank), :]


def collect_call(order, places, lows, grads, feats):
    groups, (toks, wide) = len(grads), grads[0].shape
    rank = lows[0].shape[1] // 2
    extra = wide - feats
    low_shape, first_shape = (groups, 2 * rank, toks), (groups, rank, 3 * extra)
    return order.call(
        functools.partial(collect_kernel, places),
        "collect_blocks",
        [*lows, *[in_hbm(x) for x in grads]],
        [whole(b.shape) for b in lows]
        + [pl.BlockSpec((toks, extra), lambda i: (0, feats // extra))] * groups,
        [(low_shape, BF16), (first_shape, BF16)],
        [whole(low_shape), whole(first_shape)],
    )


def low_dense_kernel(at_ref, *refs):
    out_ref, sum_ref = refs[-2:]
    groups, both, _ = refs[0].shape
    rank = both // 2
    for o in range(groups):
        total = refs[0][lax.bitwise_xor(at_ref[1], o)].astype(F32)
        for ref in refs[1:-2]:
            total = total + ref[lax.bitwise_xor(at_ref[1], o)].astype(F32)
        for q in range(2):
            at = pl.ds((q * groups + o) * rank, rank)
            sum_ref[at, :] = total[q * rank : (q + 1) * rank]
    out_ref[...] = sum_ref[...].T


def low_dense_call(order, parts):
    groups, both, toks = parts[0].shape
    shape = (toks, groups * both)
    return order.call(
        low_dense_kernel,
        "low_dense",
        parts,
        [whole(parts[0].shape)] * len(parts),
        [(shape, F32)],
        [whole(shape)],
        scratch=[pltpu.VMEM((groups * both, toks), F32)],
    )[0]


def lowrank_hid_kernel(groups, at_ref, index_ref, hid_ref, *rest):
    firsts, out_ref = rest[:2], rest[2]
    top = index_ref.shape[1]
    rank = firsts[0].shape[0] // groups
    wide = jnp.concatenate([dot(hid_ref[...], ref[...], NT) for ref in firsts], axis=1)
    column = pair_column(relative(at_ref, index_ref[...], groups).astype(F32))
    wide = jnp.where(expert_mask(column, wide.shape[1], rank), wide, 0.0)
    out_ref[...] = wide.reshape(wide.shape[0] // top, top, wide.shape[1]).sum(axis=1)


def lowrank_hid_call(order, index, hid, firsts, groups):
    (toks, top), (pairs, units) = index.shape, hid.shape
    half = firsts[0].shape[0]
    steps = 4
    return order.call(
        functools.partial(lowrank_hid_kernel, groups),
        "lowrank_hid",
        [index, in_hbm(hid), *firsts],
        [
            pl.BlockSpec((toks // steps, top), lambda i: (i, 0)),
            pl.BlockSpec((pairs // steps, units), lambda i: (i, 0)),
        ]
        + [whole((half, units))] * 2,
        [((toks, 2 * half), F32)],
        [pl.BlockSpec((toks // steps, 2 * half), lambda i: (i, 0))],
        grid=(steps,),
    )[0]


def scaled_hid_kernel(groups, rank, at_ref, index_ref, prob_ref, *refs):
    out_ref = refs[-1]
    total = refs[0][...]
    for ref in refs[1:-1]:
        total = total + ref[...]
    place = relative(at_ref, index_ref[...], groups)
    prob = prob_ref[...].astype(F32)
    expert = iota(total.shape, 1) // rank
    scale = jnp.zeros(total.shape, F32)
    for k in range(place.shape[1]):
        scale = jnp.where(expert == place[:, k : k + 1], prob[:, k : k + 1], scale)
    scaled = (total * scale).T.astype(BF16)
    for o in range(groups):
        for q in range(2):
            at = (q * groups + o) * rank
            out_ref[lax.bitwise_xor(at_ref[1], o), pl.ds(q * rank, rank), :] = scaled[at : at + rank]


def scaled_hid_call(order, index, prob, parts, groups):
    toks, width = parts[0].shape
    rank = width // groups // 2
    shape = (groups, 2 * rank, toks)
    return order.call(
        functools.partial(scaled_hid_kernel, groups, rank),
        "scaled_hid",
        [index, prob, *parts],
        [whole(index.shape), whole(prob.shape)] + [whole((toks, width))] * len(parts),
        [(shape, BF16)],
        [whole(shape)],
    )[0]


def second_grad_kernel(places, at_ref, scaled_ref, *refs):
    grads, outs = refs[:-2], refs[-2:]
    rank, tile = outs[0].shape
    total = jnp.zeros((2 * rank, tile), F32)
    for o, grad_ref in zip(places, grads):
        total = total + dot(scaled_ref[lax.bitwise_xor(at_ref[1], o)], grad_ref[...], NN)
    for q, out_ref in enumerate(outs):
        out_ref[...] = adapter_scale * total[q * rank : (q + 1) * rank]


def second_grad_call(order, places, scaled, grads, feats):
    groups, both, toks = scaled.shape
    steps = 4
    tile = feats // steps
    block = pl.BlockSpec((both // 2, tile), lambda i: (0, i))
    return order.call(
        functools.partial(second_grad_kernel, places),
        "second_grad",
        [scaled, *[in_hbm(x) for x in grads]],
        [whole(scaled.shape)] + [pl.BlockSpec((toks, tile), lambda i: (0, i))] * groups,
        [((both // 2, feats), F32)] * 2,
        [block] * 2,
        grid=(steps,),
    )


def first_grad_kernel(groups, steps, at_ref, index_ref, prob_ref, low_ref, hid_ref, *rest):
    out_ref, sum_ref = rest
    step = pl.program_id(0)
    top = index_ref.shape[1]
    rank = out_ref.shape[1]
    low = spread_pairs(low_ref[...], top)
    column = pair_column(relative(at_ref, index_ref[...], groups).astype(F32))
    keep = expert_mask(column, low.shape[1], rank)
    scaled = jnp.where(keep, low * pair_column(prob_ref[...].astype(F32)), 0.0).astype(BF16)
    part = adapter_scale * dot(scaled, hid_ref[...], TN)

    @pl.when(step == 0)
    def _():
        sum_ref[...] = part

    @pl.when(step > 0)
    def _():
        sum_ref[...] += part

    @pl.when(step == steps - 1)
    def _():
        for o in range(groups):
            for q in range(2):
                expert = 2 * lax.bitwise_xor(at_ref[1], o) + lax.bitwise_xor(at_ref[2], q)
                rows = sum_ref[pl.ds((q * groups + o) * rank, rank), :]
                out_ref[expert] = rows.astype(BF16)


def first_grad_call(order, index, prob, low, hid, groups):
    (toks, top), (pairs, units) = index.shape, hid.shape
    width = low.shape[1]
    steps = 4
    shape = (2 * groups, width // groups // 2, units)
    return order.call(
        functools.partial(first_grad_kernel, groups, steps),
        "first_grad",
        [index, prob, low, in_hbm(hid)],
        [
            pl.BlockSpec((toks // steps, top), lambda i: (i, 0)),
            pl.BlockSpec((toks // steps, top), lambda i: (i, 0)),
            pl.BlockSpec((toks // steps, width), lambda i: (i, 0)),
            pl.BlockSpec((pairs // steps, units), lambda i: (i, 0)),
        ],
        [(shape, BF16)],
        [whole(shape)],
        grid=(steps,),
        scratch=[pltpu.VMEM((width, units), F32)],
    )[0]


def finish_kernel(count, slots, at_ref, index_all_ref, index_ref, prob_ref, low_ref, hid_ref, *rest):
    firsts, back = rest[:2], rest[2 : 2 + count]
    out_ref, sum_ref, all_ref, place_ref = rest[2 + count :]
    top = index_ref.shape[1]
    toks = index_all_ref.shape[0]
    experts = 2 * count

    @pl.when(pl.program_id(0) == 0)
    def _():
        for o, ref in enumerate(back):
            for q in range(2):
                all_ref[pl.ds((q * count + o) * slots, slots), :] = ref[pl.ds(q * slots, slots), :]
        experts_all = relative(at_ref, index_all_ref[...], count)
        hit = jnp.zeros((toks, experts), F32)
        for k in range(top):
            hit = jnp.where(iota((toks, experts), 1) == experts_all[:, k : k + 1], 1.0, hit)
        before = jnp.where(iota((toks, toks), 0) > iota((toks, toks), 1), 1.0, 0.0).astype(BF16)
        place_ref[...] = dot(before, hit.astype(BF16), NN)

    pairs = hid_ref.shape[0]
    some = index_ref.shape[0]
    column = pair_column(relative(at_ref, index_ref[...], count).astype(F32))
    place = spread_pairs(place_ref[pl.ds(pl.program_id(0) * some, some), :], top)
    mine = iota((pairs, experts), 1) == column.astype(jnp.int32)
    target = column * slots + jnp.sum(jnp.where(mine, place, 0.0), axis=1, keepdims=True)
    low = spread_pairs(low_ref[...], top)
    keep = expert_mask(column, low.shape[1], low.shape[1] // experts)
    low = jnp.where(keep, adapter_scale * low.astype(BF16).astype(F32), 0.0).astype(BF16)
    slot = iota((pairs, experts * slots), 1)
    pick = jnp.where(slot == target.astype(jnp.int32), 1.0, 0.0).astype(BF16)
    half = low.shape[1] // 2
    value = dot(pick, all_ref[...], NN)
    value = value + dot(low[:, :half], firsts[0][...], NN) + dot(low[:, half:], firsts[1][...], NN)
    value = value.astype(BF16).astype(F32)
    out_ref[...] = (value * pair_column(prob_ref[...].astype(F32))).astype(BF16)
    sums = jnp.sum(value * hid_ref[...].astype(F32), axis=1, keepdims=True)
    sums = jnp.where(diagonal(pairs, top), sums, 0.0)
    sum_ref[...] = sums.reshape(some, top, top).sum(axis=1)


def finish_call(order, index, prob, low, hid, firsts, back):
    (toks, top), (pairs, units) = index.shape, hid.shape
    width = low.shape[1]
    both = back[0].shape[0]
    steps = 4
    count = len(back)

    def rows(n, columns):
        return pl.BlockSpec((n // steps, columns), lambda i: (i, 0))

    return order.call(
        functools.partial(finish_kernel, count, both // 2),
        "finish",
        [index, index, prob, low, in_hbm(hid), *firsts, *[in_hbm(x) for x in back]],
        [whole(index.shape), rows(toks, top), rows(toks, top), rows(toks, width), rows(pairs, units)]
        + [whole(firsts[0].shape)] * 2
        + [whole((both, units))] * count,
        [((pairs, units), BF16), ((toks, top), F32)],
        [rows(pairs, units), rows(toks, top)],
        grid=(steps,),
        cost=LONG,
        scratch=[pltpu.VMEM((count * both, units), BF16), pltpu.VMEM((toks, 2 * count), F32)],
    )


def body(grad, hidden, index, weight, down, first, second):
    toks, top = index.shape
    exp_local, units_all, feats = down.shape
    units, rank = first.shape[1:]
    groups, cores, shares = lax.axis_size("ep"), lax.axis_size("sub"), lax.axis_size("rep")
    assert exp_local == 1 and cores == 2 and groups & (groups - 1) == 0
    cap = min(toks, 5 * toks * top // (4 * groups * cores))
    slots = -(-cap // 16) * 16
    pairs = toks * top
    at = jnp.stack([lax.axis_index(name).astype(jnp.int32) for name in ("rep", "ep", "sub")])
    order = Order(at)

    def turn(x, offset):
        return lax.ppermute(x, "rep", [(r, (r + offset) % shares) for r in range(shares)])

    def all_shares(x):
        return [x] + [turn(x, k) for k in range(1, shares)]

    def flip(x, mask):
        return lax.ppermute(x, "ep", [(i, i ^ mask) for i in range(groups)])

    def swap(x):
        return lax.ppermute(x, "sub", [(0, 1), (1, 0)])

    def exchange(x, axes="ep"):
        return lax.all_to_all(x, axes, split_axis=0, concat_axis=0, tiled=True)

    blocks = {0: pack_call(order, grad, first[0].T, index.T)}

    def fetch(o):
        if o not in blocks:
            last = o & -o
            blocks[o] = flip(fetch(o ^ last), last)
        return blocks[o]

    own_down, own_second = load_call(order, down[0], second[0])
    downs = [own_down, swap(down[0])]
    seconds = [own_second, swap(own_second)]

    if groups == 8:
        batches = [(0, 1), (2, 4), (6, 5), (3, 7)]
    else:
        batches = [(o, o + 1) for o in range(0, groups, 2)]
    places = [o for batch in batches for o in batch]
    back, lows, waiting = {}, [], []

    def arrived(i):
        order.wait([back[o] for o in batches[i] if o])

    def send_back(batch, parts):
        for o, rows in zip(batch, share_sum_call(order, parts, 2, slots)):
            if batch == batches[-1] and o > 1 and o % 2:
                back[o] = flip(flip(rows, 1), o - 1)
            else:
                back[o] = flip(rows, o) if o else rows

    for i, batch in enumerate(batches):
        *give, keep, low = expert_rows_call(
            order, [fetch(o) for o in batch], seconds, downs, shares, slots
        )
        lows.append(low)
        if i > 1 and i == len(batches) - 1:
            for j in range(i - 1):
                arrived(j)
        if i > 0:
            send_back(*waiting)
        waiting = (batch, [keep] + [turn(x, k + 1) for k, x in enumerate(give)])

    hid = hidden.reshape(pairs, units)
    grads = [blocks[o] for o in places]

    low_grad, first_own = collect_call(order, places, lows, grads, feats)
    firsts = [x.reshape(groups * rank, units) for x in (first_own, swap(first_own))]
    low_grad = all_shares(exchange(low_grad))
    send_back(*waiting)

    low_grad = low_dense_call(order, low_grad)
    arrived(len(batches) - 2)
    low_hid = all_shares(lowrank_hid_call(order, index, hid, firsts, groups))
    first_part = first_grad_call(order, index, weight, low_grad, hid, groups)
    first_part = exchange(first_part, ("ep", "sub"))
    first_grad = jnp.sum(first_part.astype(F32), axis=0)

    scaled_hid = exchange(scaled_hid_call(order, index, weight, low_hid, groups))
    back = [back[o] for o in range(groups)]
    grad_hidden, sums = finish_call(order, index, weight, low_grad, hid, firsts, back)
    sums = sums + turn(sums, 1) if shares == 2 else lax.psum(sums, "rep")
    order.wait([first_part])
    second_keep, second_give = second_grad_call(order, places, scaled_hid, grads, feats)
    second_grad = second_keep + swap(second_give)
    return (
        grad_hidden.reshape(toks, top, units),
        sums,
        first_grad.T[None],
        second_grad[None],
    )


def solution(mesh):
    return jax.shard_map(
        body,
        mesh=mesh,
        in_specs=(
            P(("grp", "ep", "sub"), "rep"),
            P(("grp", "ep", "sub"), None, "rep"),
            P(("grp", "ep", "sub"), None),
            P(("grp", "ep", "sub"), None),
            P(("ep", "sub"), None, "rep"),
            P(("grp", "ep", "sub"), "rep", None),
            P(("grp", "ep", "sub"), None, "rep"),
        ),
        out_specs=(
            P(("grp", "ep", "sub"), None, "rep"),
            P(("grp", "ep", "sub"), None),
            P(("grp", "ep", "sub"), "rep", None),
            P(("grp", "ep", "sub"), None, "rep"),
        ),
        check_vma=False,
    )
```

```python
import functools

import jax
import jax.numpy as jnp
from jax import lax
from jax.experimental import pallas as pl
from jax.experimental.pallas import tpu as pltpu
from jax.sharding import PartitionSpec as P

adapter_scale = 2.0
BF16 = jnp.bfloat16
F32 = jnp.float32
NT = (((1,), (1,)), ((), ()))
TN = (((0,), (0,)), ((), ()))
NN = (((1,), (0,)), ((), ()))
SMALL = pl.CostEstimate(flops=1, bytes_accessed=1, transcendentals=0)
LONG = pl.CostEstimate(flops=1, bytes_accessed=10**9, transcendentals=0)
ANY = pl.BlockSpec(memory_space=pl.ANY)
SMEM = pl.BlockSpec(memory_space=pltpu.SMEM)
VMEM = pl.BlockSpec(memory_space=pltpu.VMEM)


def dot(a, b, dims):
    return lax.dot_general(a, b, dims, preferred_element_type=F32)


def iota(shape, axis):
    return lax.broadcasted_iota(jnp.int32, shape, axis)


def whole(shape):
    return pl.BlockSpec(shape, lambda *_: (0,) * len(shape))


def in_hbm(x):
    return pltpu.with_memory_space_constraint(x, pltpu.HBM)


class Order:
    def __init__(self, at):
        self.at, self.last = at, []

    def wait(self, arrays):
        self.last = self.last + list(arrays)

    def call(self, kernel, name, arrays, in_specs, outs, out_specs, grid=(1,), scratch=(), mib=16, cost=SMALL, **more):
        count, last = 1 + len(arrays), len(self.last)

        def ordered(*refs):
            here = count + last + len(outs)
            kernel(*refs[:count], *refs[count + last : here], *refs[here + 1 :])

        *result, token = pl.pallas_call(
            ordered,
            grid=grid,
            in_specs=[SMEM, *in_specs] + [ANY] * last,
            out_specs=[*out_specs, ANY],
            scratch_shapes=scratch,
            out_shape=[jax.ShapeDtypeStruct(*o) if isinstance(o, tuple) else o for o in outs]
            + [pltpu.HBM((8, 128), F32)],
            compiler_params=pltpu.CompilerParams(vmem_limit_bytes=mib * 2**20),
            cost_estimate=cost,
            name=name,
            **more,
        )(self.at, *arrays, *self.last)
        self.last = [in_hbm(token)]
        return result


def relative(at_ref, index, groups):
    o = lax.bitwise_xor(lax.shift_right_logical(index, 1), at_ref[1])
    q = lax.bitwise_xor(lax.bitwise_and(index, 1), at_ref[2])
    return q * groups + o


def spread_pairs(dense, top):
    toks, width = dense.shape
    return jnp.broadcast_to(dense[:, None, :], (toks, top, width)).reshape(toks * top, width)


def diagonal(pairs, top):
    return iota((pairs, top), 1) == lax.bitwise_and(iota((pairs, top), 0), top - 1)


def pair_column(table):
    toks, top = table.shape
    wide = spread_pairs(table, top)
    return jnp.sum(jnp.where(diagonal(toks * top, top), wide, 0.0), axis=1, keepdims=True)


def expert_mask(column, width, rank):
    return iota((column.shape[0], width), 1) // rank == column.astype(jnp.int32)


def pack_kernel(at_ref, grad_ref, first_ref, index_ref, out_ref):
    toks, feats = grad_ref.shape
    rank = first_ref.shape[0]
    extra = out_ref.shape[1] - feats
    out_ref[:, pl.ds(0, feats)] = grad_ref[...]
    for k in range(3):
        piece = first_ref[:, pl.ds(k * extra, extra)]
        out_ref[pl.ds(k * rank, rank), pl.ds(feats, extra)] = piece
    top = index_ref.shape[0]
    out_ref[pl.ds(3 * rank, toks - 3 * rank), pl.ds(feats, extra)] = jnp.full(
        (toks - 3 * rank, extra), -1.0, BF16
    )
    routes = index_ref[...].astype(F32)
    routes = jnp.concatenate([routes, jnp.full((16 - top, toks), -1.0, F32)], axis=0)
    out_ref[pl.ds(3 * rank, 16), pl.ds(feats, toks)] = routes.astype(BF16)


def pack_call(order, grad, first, index):
    (toks, feats), (rank, units) = grad.shape, first.shape
    shape = (toks, feats + units // 3)
    return order.call(
        pack_kernel,
        "pack_block",
        [in_hbm(grad), first, index],
        [whole(grad.shape), whole(first.shape), whole(index.shape)],
        [(shape, BF16)],
        [whole(shape)],
    )[0]


def load_kernel(at_ref, down_ref, second_ref, out_ref, same_ref, sems):
    parts = sems.shape[0]
    rows = down_ref.shape[0] // parts
    copies = [
        pltpu.make_async_copy(
            down_ref.at[pl.ds(k * rows, rows), :], out_ref.at[pl.ds(k * rows, rows), :], sems.at[k]
        )
        for k in range(parts)
    ]
    for copy in copies:
        copy.start()
    same_ref[...] = second_ref[...]
    for copy in copies:
        copy.wait()


def load_call(order, down, second):
    return order.call(
        load_kernel,
        "load_matrix",
        [in_hbm(down), second],
        [ANY, VMEM],
        [pltpu.VMEM(down.shape, down.dtype), (second.shape, second.dtype)],
        [VMEM, VMEM],
        grid=(),
        scratch=[pltpu.SemaphoreType.DMA((4,))],
    )


def expert_rows_kernel(slots, tiles, shares, batch, route_row, at_ref, *rest):
    grads, seconds, downs = rest[:batch], rest[batch : batch + 2], rest[batch + 2 : batch + 4]
    *outs, low_ref = rest[batch + 4 : batch + 5 + shares]
    block_ref, turned_ref, block_sems = rest[batch + 5 + shares :]
    tile = downs[0].shape[0] // shares // tiles
    feats = turned_ref.shape[1]
    toks = block_ref.shape[1]
    blocks = [
        pltpu.make_async_copy(ref, block_ref.at[k], block_sems.at[k]) for k, ref in enumerate(grads)
    ]
    for copy in blocks:
        copy.start()

    before = jnp.where(iota((toks, toks), 0) < iota((toks, toks), 1), 1.0, 0.0).astype(BF16)
    columns = turned_ref.shape[2]
    slot = iota((columns, batch * toks), 0).astype(F32)
    second = jnp.concatenate([ref[...] for ref in seconds], axis=0)
    routes = []
    for k in range(batch):
        blocks[k].wait()
        routes.append(block_ref[k, pl.ds(route_row, 16), pl.ds(feats, toks)].astype(F32))
    grad = block_ref[:, :, pl.ds(0, feats)].reshape(batch * toks, feats)
    for q in range(2):
        expert = at_ref[1] * 2 + lax.bitwise_xor(at_ref[2], q)
        targets = []
        for k in range(batch):
            hits = jnp.where(routes[k] == expert.astype(F32), 1.0, 0.0)
            mine = jnp.max(hits, axis=0, keepdims=True)
            pos = dot(jnp.broadcast_to(mine, (16, toks)).astype(BF16), before, NN)[:1]
            targets.append(jnp.where(mine > 0.0, pos + float(k * slots), -1.0))
        pick = jnp.where(slot == jnp.concatenate(targets, axis=1), 1.0, 0.0)
        turned_ref[q] = dot(grad, pick.T.astype(BF16), TN).astype(BF16)
    low = dot(second, grad, NT).astype(BF16)
    for k in range(batch):
        low_ref[k] = low[:, k * toks : (k + 1) * toks]

    rows = batch * slots
    for k in range(shares):
        share = lax.rem(at_ref[0] + k + 1, shares)
        for q in range(2):
            for t in range(tiles):
                row = pl.multiple_of((share * tiles + t) * tile, tile)
                value = dot(downs[q][pl.ds(row, tile), :], turned_ref[q], NN)
                outs[k][pl.ds(q * rows, rows), pl.ds(t * tile, tile)] = value.T[:rows].astype(BF16)


def expert_rows_call(order, grads, seconds, downs, shares, slots):
    batch, (toks, wide) = len(grads), grads[0].shape
    rank, feats = seconds[0].shape
    units = downs[0].shape[0] // shares
    rows = 2 * batch * slots
    return order.call(
        functools.partial(expert_rows_kernel, slots, 3, shares, batch, 3 * rank),
        "expert_rows",
        [*grads, *seconds, *[pltpu.with_memory_space_constraint(x, pltpu.VMEM) for x in downs]],
        [ANY] * batch + [VMEM] * 4,
        [((rows, units), BF16)] * shares + [((batch, 2 * rank, toks), BF16)],
        [VMEM] * (shares + 1),
        grid=(),
        scratch=[
            pltpu.VMEM((batch, toks, wide), BF16),
            pltpu.VMEM((2, feats, -(-batch * slots // 128) * 128), BF16),
            pltpu.SemaphoreType.DMA((batch,)),
        ],
    )


def share_sum_kernel(parts, slots, at_ref, *refs):
    outs = refs[parts:]
    for k, out_ref in enumerate(outs):
        for q in range(2):
            at = pl.ds((q * len(outs) + k) * slots, slots)
            total = refs[0][at, :].astype(F32)
            for part in refs[1:parts]:
                total = total + part[at, :].astype(F32)
            out_ref[pl.ds(q * slots, slots), :] = total.astype(BF16)


def share_sum_call(order, parts, batch, slots):
    rows, units = parts[0].shape
    shape = (2 * slots, units)
    return order.call(
        functools.partial(share_sum_kernel, len(parts), slots),
        "share_sum",
        parts,
        [whole((rows, units))] * len(parts),
        [(shape, BF16)] * batch,
        [whole(shape)] * batch,
    )


def collect_kernel(places, at_ref, *refs):
    low_ref, first_ref = refs[-2:]
    rank = first_ref.shape[1]
    at = 0
    lows = len(refs) - 2 - len(places)
    for ref in refs[:lows]:
        for k in range(ref.shape[0]):
            low_ref[lax.bitwise_xor(at_ref[1], places[at])] = ref[k]
            at += 1
    for o, ref in zip(places, refs[lows:-2]):
        wide = ref.shape[1]
        for k in range(3):
            first_ref[o, :, pl.ds(k * wide, wide)] = ref[pl.ds(k * rank, rank), :]


def collect_call(order, places, lows, grads, feats):
    groups, (toks, wide) = len(grads), grads[0].shape
    rank = lows[0].shape[1] // 2
    extra = wide - feats
    low_shape, first_shape = (groups, 2 * rank, toks), (groups, rank, 3 * extra)
    return order.call(
        functools.partial(collect_kernel, places),
        "collect_blocks",
        [*lows, *[in_hbm(x) for x in grads]],
        [whole(b.shape) for b in lows]
        + [pl.BlockSpec((toks, extra), lambda i: (0, feats // extra))] * groups,
        [(low_shape, BF16), (first_shape, BF16)],
        [whole(low_shape), whole(first_shape)],
    )


def low_dense_kernel(at_ref, *refs):
    out_ref, sum_ref = refs[-2:]
    groups, both, _ = refs[0].shape
    rank = both // 2
    for o in range(groups):
        total = refs[0][lax.bitwise_xor(at_ref[1], o)].astype(F32)
        for ref in refs[1:-2]:
            total = total + ref[lax.bitwise_xor(at_ref[1], o)].astype(F32)
        for q in range(2):
            at = pl.ds((q * groups + o) * rank, rank)
            sum_ref[at, :] = total[q * rank : (q + 1) * rank]
    out_ref[...] = sum_ref[...].T


def low_dense_call(order, parts):
    groups, both, toks = parts[0].shape
    shape = (toks, groups * both)
    return order.call(
        low_dense_kernel,
        "low_dense",
        parts,
        [whole(parts[0].shape)] * len(parts),
        [(shape, F32)],
        [whole(shape)],
        scratch=[pltpu.VMEM((groups * both, toks), F32)],
    )[0]


def lowrank_hid_kernel(groups, at_ref, index_ref, hid_ref, *rest):
    firsts, out_ref = rest[:2], rest[2]
    top = index_ref.shape[1]
    rank = firsts[0].shape[0] // groups
    wide = jnp.concatenate([dot(hid_ref[...], ref[...], NT) for ref in firsts], axis=1)
    column = pair_column(relative(at_ref, index_ref[...], groups).astype(F32))
    wide = jnp.where(expert_mask(column, wide.shape[1], rank), wide, 0.0)
    out_ref[...] = wide.reshape(wide.shape[0] // top, top, wide.shape[1]).sum(axis=1)


def lowrank_hid_call(order, index, hid, firsts, groups):
    (toks, top), (pairs, units) = index.shape, hid.shape
    half = firsts[0].shape[0]
    steps = 4
    return order.call(
        functools.partial(lowrank_hid_kernel, groups),
        "lowrank_hid",
        [index, in_hbm(hid), *firsts],
        [
            pl.BlockSpec((toks // steps, top), lambda i: (i, 0)),
            pl.BlockSpec((pairs // steps, units), lambda i: (i, 0)),
        ]
        + [whole((half, units))] * 2,
        [((toks, 2 * half), F32)],
        [pl.BlockSpec((toks // steps, 2 * half), lambda i: (i, 0))],
        grid=(steps,),
    )[0]


def scaled_hid_kernel(groups, rank, at_ref, index_ref, prob_ref, *refs):
    out_ref = refs[-1]
    total = refs[0][...]
    for ref in refs[1:-1]:
        total = total + ref[...]
    place = relative(at_ref, index_ref[...], groups)
    prob = prob_ref[...].astype(F32)
    expert = iota(total.shape, 1) // rank
    scale = jnp.zeros(total.shape, F32)
    for k in range(place.shape[1]):
        scale = jnp.where(expert == place[:, k : k + 1], prob[:, k : k + 1], scale)
    scaled = (total * scale).T.astype(BF16)
    for o in range(groups):
        for q in range(2):
            at = (q * groups + o) * rank
            out_ref[lax.bitwise_xor(at_ref[1], o), pl.ds(q * rank, rank), :] = scaled[at : at + rank]


def scaled_hid_call(order, index, prob, parts, groups):
    toks, width = parts[0].shape
    rank = width // groups // 2
    shape = (groups, 2 * rank, toks)
    return order.call(
        functools.partial(scaled_hid_kernel, groups, rank),
        "scaled_hid",
        [index, prob, *parts],
        [whole(index.shape), whole(prob.shape)] + [whole((toks, width))] * len(parts),
        [(shape, BF16)],
        [whole(shape)],
    )[0]


def second_grad_kernel(places, at_ref, scaled_ref, *refs):
    grads, outs = refs[:-2], refs[-2:]
    rank, tile = outs[0].shape
    total = jnp.zeros((2 * rank, tile), F32)
    for o, grad_ref in zip(places, grads):
        total = total + dot(scaled_ref[lax.bitwise_xor(at_ref[1], o)], grad_ref[...], NN)
    for q, out_ref in enumerate(outs):
        out_ref[...] = adapter_scale * total[q * rank : (q + 1) * rank]


def second_grad_call(order, places, scaled, grads, feats):
    groups, both, toks = scaled.shape
    steps = 4
    tile = feats // steps
    block = pl.BlockSpec((both // 2, tile), lambda i: (0, i))
    return order.call(
        functools.partial(second_grad_kernel, places),
        "second_grad",
        [scaled, *[in_hbm(x) for x in grads]],
        [whole(scaled.shape)] + [pl.BlockSpec((toks, tile), lambda i: (0, i))] * groups,
        [((both // 2, feats), F32)] * 2,
        [block] * 2,
        grid=(steps,),
    )


def first_grad_kernel(groups, steps, at_ref, index_ref, prob_ref, low_ref, hid_ref, *rest):
    out_ref, sum_ref = rest
    step = pl.program_id(0)
    top = index_ref.shape[1]
    rank = out_ref.shape[1]
    low = spread_pairs(low_ref[...], top)
    column = pair_column(relative(at_ref, index_ref[...], groups).astype(F32))
    keep = expert_mask(column, low.shape[1], rank)
    scaled = jnp.where(keep, low * pair_column(prob_ref[...].astype(F32)), 0.0).astype(BF16)
    part = adapter_scale * dot(scaled, hid_ref[...], TN)

    @pl.when(step == 0)
    def _():
        sum_ref[...] = part

    @pl.when(step > 0)
    def _():
        sum_ref[...] += part

    @pl.when(step == steps - 1)
    def _():
        for o in range(groups):
            for q in range(2):
                expert = 2 * lax.bitwise_xor(at_ref[1], o) + lax.bitwise_xor(at_ref[2], q)
                rows = sum_ref[pl.ds((q * groups + o) * rank, rank), :]
                out_ref[expert] = rows.astype(BF16)


def first_grad_call(order, index, prob, low, hid, groups):
    (toks, top), (pairs, units) = index.shape, hid.shape
    width = low.shape[1]
    steps = 4
    shape = (2 * groups, width // groups // 2, units)
    return order.call(
        functools.partial(first_grad_kernel, groups, steps),
        "first_grad",
        [index, prob, low, in_hbm(hid)],
        [
            pl.BlockSpec((toks // steps, top), lambda i: (i, 0)),
            pl.BlockSpec((toks // steps, top), lambda i: (i, 0)),
            pl.BlockSpec((toks // steps, width), lambda i: (i, 0)),
            pl.BlockSpec((pairs // steps, units), lambda i: (i, 0)),
        ],
        [(shape, BF16)],
        [whole(shape)],
        grid=(steps,),
        scratch=[pltpu.VMEM((width, units), F32)],
    )[0]


def finish_kernel(count, slots, at_ref, index_all_ref, index_ref, prob_ref, low_ref, hid_ref, *rest):
    firsts, back = rest[:2], rest[2 : 2 + count]
    out_ref, sum_ref, all_ref, place_ref = rest[2 + count :]
    top = index_ref.shape[1]
    toks = index_all_ref.shape[0]
    experts = 2 * count

    @pl.when(pl.program_id(0) == 0)
    def _():
        for o, ref in enumerate(back):
            for q in range(2):
                all_ref[pl.ds((q * count + o) * slots, slots), :] = ref[pl.ds(q * slots, slots), :]
        experts_all = relative(at_ref, index_all_ref[...], count)
        hit = jnp.zeros((toks, experts), F32)
        for k in range(top):
            hit = jnp.where(iota((toks, experts), 1) == experts_all[:, k : k + 1], 1.0, hit)
        before = jnp.where(iota((toks, toks), 0) > iota((toks, toks), 1), 1.0, 0.0).astype(BF16)
        place_ref[...] = dot(before, hit.astype(BF16), NN)

    pairs = hid_ref.shape[0]
    some = index_ref.shape[0]
    column = pair_column(relative(at_ref, index_ref[...], count).astype(F32))
    place = spread_pairs(place_ref[pl.ds(pl.program_id(0) * some, some), :], top)
    mine = iota((pairs, experts), 1) == column.astype(jnp.int32)
    target = column * slots + jnp.sum(jnp.where(mine, place, 0.0), axis=1, keepdims=True)
    low = spread_pairs(low_ref[...], top)
    keep = expert_mask(column, low.shape[1], low.shape[1] // experts)
    low = jnp.where(keep, adapter_scale * low.astype(BF16).astype(F32), 0.0).astype(BF16)
    slot = iota((pairs, experts * slots), 1)
    pick = jnp.where(slot == target.astype(jnp.int32), 1.0, 0.0).astype(BF16)
    half = low.shape[1] // 2
    value = dot(pick, all_ref[...], NN)
    value = value + dot(low[:, :half], firsts[0][...], NN) + dot(low[:, half:], firsts[1][...], NN)
    value = value.astype(BF16).astype(F32)
    out_ref[...] = (value * pair_column(prob_ref[...].astype(F32))).astype(BF16)
    sums = jnp.sum(value * hid_ref[...].astype(F32), axis=1, keepdims=True)
    sums = jnp.where(diagonal(pairs, top), sums, 0.0)
    sum_ref[...] = sums.reshape(some, top, top).sum(axis=1)


def finish_call(order, index, prob, low, hid, firsts, back):
    (toks, top), (pairs, units) = index.shape, hid.shape
    width = low.shape[1]
    both = back[0].shape[0]
    steps = 4
    count = len(back)

    def rows(n, columns):
        return pl.BlockSpec((n // steps, columns), lambda i: (i, 0))

    return order.call(
        functools.partial(finish_kernel, count, both // 2),
        "finish",
        [index, index, prob, low, in_hbm(hid), *firsts, *[in_hbm(x) for x in back]],
        [whole(index.shape), rows(toks, top), rows(toks, top), rows(toks, width), rows(pairs, units)]
        + [whole(firsts[0].shape)] * 2
        + [whole((both, units))] * count,
        [((pairs, units), BF16), ((toks, top), F32)],
        [rows(pairs, units), rows(toks, top)],
        grid=(steps,),
        cost=LONG,
        scratch=[pltpu.VMEM((count * both, units), BF16), pltpu.VMEM((toks, 2 * count), F32)],
    )


def body(grad, hidden, index, weight, down, first, second):
    toks, top = index.shape
    exp_local, units_all, feats = down.shape
    units, rank = first.shape[1:]
    groups, cores, shares = lax.axis_size("ep"), lax.axis_size("sub"), lax.axis_size("rep")
    assert exp_local == 1 and cores == 2 and groups & (groups - 1) == 0
    cap = min(toks, 5 * toks * top // (4 * groups * cores))
    slots = -(-cap // 16) * 16
    pairs = toks * top
    at = jnp.stack([lax.axis_index(name).astype(jnp.int32) for name in ("rep", "ep", "sub")])
    order = Order(at)

    def turn(x, offset):
        return lax.ppermute(x, "rep", [(r, (r + offset) % shares) for r in range(shares)])

    def all_shares(x):
        return [x] + [turn(x, k) for k in range(1, shares)]

    def flip(x, mask):
        return lax.ppermute(x, "ep", [(i, i ^ mask) for i in range(groups)])

    def swap(x):
        return lax.ppermute(x, "sub", [(0, 1), (1, 0)])

    def exchange(x, axes="ep"):
        return lax.all_to_all(x, axes, split_axis=0, concat_axis=0, tiled=True)

    blocks = {0: pack_call(order, grad, first[0].T, index.T)}

    def fetch(o):
        if o not in blocks:
            last = o & -o
            blocks[o] = flip(fetch(o ^ last), last)
        return blocks[o]

    own_down, own_second = load_call(order, down[0], second[0])
    downs = [own_down, swap(down[0])]
    seconds = [own_second, swap(own_second)]

    if groups == 8:
        batches = [(0, 1), (2, 4), (6, 5), (3, 7)]
    else:
        batches = [(o, o + 1) for o in range(0, groups, 2)]
    places = [o for batch in batches for o in batch]
    back, lows, waiting = {}, [], []

    def arrived(i):
        order.wait([back[o] for o in batches[i] if o])

    def send_back(batch, parts):
        for o, rows in zip(batch, share_sum_call(order, parts, 2, slots)):
            if batch == batches[-1] and o > 1 and o % 2:
                back[o] = flip(flip(rows, 1), o - 1)
            else:
                back[o] = flip(rows, o) if o else rows

    for i, batch in enumerate(batches):
        *give, keep, low = expert_rows_call(
            order, [fetch(o) for o in batch], seconds, downs, shares, slots
        )
        lows.append(low)
        if i > 1 and i == len(batches) - 1:
            for j in range(i - 1):
                arrived(j)
        if i > 0:
            send_back(*waiting)
        waiting = (batch, [keep] + [turn(x, k + 1) for k, x in enumerate(give)])

    hid = hidden.reshape(pairs, units)
    grads = [blocks[o] for o in places]

    low_grad, first_own = collect_call(order, places, lows, grads, feats)
    firsts = [x.reshape(groups * rank, units) for x in (first_own, swap(first_own))]
    low_grad = all_shares(exchange(low_grad))
    send_back(*waiting)

    arrived(len(batches) - 2)
    low_hid = all_shares(lowrank_hid_call(order, index, hid, firsts, groups))
    low_grad = low_dense_call(order, low_grad)
    first_part = first_grad_call(order, index, weight, low_grad, hid, groups)
    first_part = exchange(first_part, ("ep", "sub"))
    first_grad = jnp.sum(first_part.astype(F32), axis=0)

    scaled_hid = exchange(scaled_hid_call(order, index, weight, low_hid, groups))
    back = [back[o] for o in range(groups)]
    grad_hidden, sums = finish_call(order, index, weight, low_grad, hid, firsts, back)
    sums = sums + turn(sums, 1) if shares == 2 else lax.psum(sums, "rep")
    order.wait([first_part])
    second_keep, second_give = second_grad_call(order, places, scaled_hid, grads, feats)
    second_grad = second_keep + swap(second_give)
    return (
        grad_hidden.reshape(toks, top, units),
        sums,
        first_grad.T[None],
        second_grad[None],
    )


def solution(mesh):
    return jax.shard_map(
        body,
        mesh=mesh,
        in_specs=(
            P(("grp", "ep", "sub"), "rep"),
            P(("grp", "ep", "sub"), None, "rep"),
            P(("grp", "ep", "sub"), None),
            P(("grp", "ep", "sub"), None),
            P(("ep", "sub"), None, "rep"),
            P(("grp", "ep", "sub"), "rep", None),
            P(("grp", "ep", "sub"), None, "rep"),
        ),
        out_specs=(
            P(("grp", "ep", "sub"), None, "rep"),
            P(("grp", "ep", "sub"), None),
            P(("grp", "ep", "sub"), "rep", None),
            P(("grp", "ep", "sub"), None, "rep"),
        ),
        check_vma=False,
    )
```

```python
import functools

import jax
import jax.numpy as jnp
from jax import lax
from jax.experimental import pallas as pl
from jax.experimental.pallas import tpu as pltpu
from jax.sharding import PartitionSpec as P

adapter_scale = 2.0
BF16 = jnp.bfloat16
F32 = jnp.float32
NT = (((1,), (1,)), ((), ()))
TN = (((0,), (0,)), ((), ()))
NN = (((1,), (0,)), ((), ()))
SMALL = pl.CostEstimate(flops=1, bytes_accessed=1, transcendentals=0)
LONG = pl.CostEstimate(flops=1, bytes_accessed=2 * 10**7, transcendentals=0)
ANY = pl.BlockSpec(memory_space=pl.ANY)
SMEM = pl.BlockSpec(memory_space=pltpu.SMEM)
VMEM = pl.BlockSpec(memory_space=pltpu.VMEM)


def dot(a, b, dims):
    return lax.dot_general(a, b, dims, preferred_element_type=F32)


def iota(shape, axis):
    return lax.broadcasted_iota(jnp.int32, shape, axis)


def whole(shape):
    return pl.BlockSpec(shape, lambda *_: (0,) * len(shape))


def in_hbm(x):
    return pltpu.with_memory_space_constraint(x, pltpu.HBM)


class Order:
    def __init__(self, at):
        self.at, self.last = at, []

    def wait(self, arrays):
        self.last = self.last + list(arrays)

    def call(self, kernel, name, arrays, in_specs, outs, out_specs, grid=(1,), scratch=(), mib=16, cost=SMALL, **more):
        count, last = 1 + len(arrays), len(self.last)

        def ordered(*refs):
            here = count + last + len(outs)
            kernel(*refs[:count], *refs[count + last : here], *refs[here + 1 :])

        *result, token = pl.pallas_call(
            ordered,
            grid=grid,
            in_specs=[SMEM, *in_specs] + [ANY] * last,
            out_specs=[*out_specs, ANY],
            scratch_shapes=scratch,
            out_shape=[jax.ShapeDtypeStruct(*o) if isinstance(o, tuple) else o for o in outs]
            + [pltpu.HBM((8, 128), F32)],
            compiler_params=pltpu.CompilerParams(vmem_limit_bytes=mib * 2**20),
            cost_estimate=cost,
            name=name,
            **more,
        )(self.at, *arrays, *self.last)
        self.last = [in_hbm(token)]
        return result


def relative(at_ref, index, groups):
    o = lax.bitwise_xor(lax.shift_right_logical(index, 1), at_ref[1])
    q = lax.bitwise_xor(lax.bitwise_and(index, 1), at_ref[2])
    return q * groups + o


def spread_pairs(dense, top):
    toks, width = dense.shape
    return jnp.broadcast_to(dense[:, None, :], (toks, top, width)).reshape(toks * top, width)


def diagonal(pairs, top):
    return iota((pairs, top), 1) == lax.bitwise_and(iota((pairs, top), 0), top - 1)


def pair_column(table):
    toks, top = table.shape
    wide = spread_pairs(table, top)
    return jnp.sum(jnp.where(diagonal(toks * top, top), wide, 0.0), axis=1, keepdims=True)


def expert_mask(column, width, rank):
    return iota((column.shape[0], width), 1) // rank == column.astype(jnp.int32)


def pack_kernel(at_ref, grad_ref, first_ref, index_ref, out_ref):
    toks, feats = grad_ref.shape
    rank = first_ref.shape[0]
    extra = out_ref.shape[1] - feats
    out_ref[:, pl.ds(0, feats)] = grad_ref[...]
    for k in range(3):
        piece = first_ref[:, pl.ds(k * extra, extra)]
        out_ref[pl.ds(k * rank, rank), pl.ds(feats, extra)] = piece
    top = index_ref.shape[0]
    out_ref[pl.ds(3 * rank, toks - 3 * rank), pl.ds(feats, extra)] = jnp.full(
        (toks - 3 * rank, extra), -1.0, BF16
    )
    routes = index_ref[...].astype(F32)
    routes = jnp.concatenate([routes, jnp.full((16 - top, toks), -1.0, F32)], axis=0)
    out_ref[pl.ds(3 * rank, 16), pl.ds(feats, toks)] = routes.astype(BF16)


def pack_call(order, grad, first, index):
    (toks, feats), (rank, units) = grad.shape, first.shape
    shape = (toks, feats + units // 3)
    return order.call(
        pack_kernel,
        "pack_block",
        [in_hbm(grad), first, index],
        [whole(grad.shape), whole(first.shape), whole(index.shape)],
        [(shape, BF16)],
        [whole(shape)],
    )[0]


def gate_kernel(at_ref, *refs):
    pass


def gate_call(order, arrays):
    return order.call(
        gate_kernel,
        "gate",
        arrays,
        [ANY] * len(arrays),
        [(x.shape, x.dtype) for x in arrays],
        [ANY] * len(arrays),
        input_output_aliases={1 + k: k for k in range(len(arrays))},
    )


def load_kernel(at_ref, down_ref, second_ref, out_ref, same_ref, sems):
    parts = sems.shape[0]
    rows = down_ref.shape[0] // parts
    copies = [
        pltpu.make_async_copy(
            down_ref.at[pl.ds(k * rows, rows), :], out_ref.at[pl.ds(k * rows, rows), :], sems.at[k]
        )
        for k in range(parts)
    ]
    for copy in copies:
        copy.start()
    same_ref[...] = second_ref[...]
    for copy in copies:
        copy.wait()


def load_call(order, down, second):
    return order.call(
        load_kernel,
        "load_matrix",
        [in_hbm(down), second],
        [ANY, VMEM],
        [pltpu.VMEM(down.shape, down.dtype), (second.shape, second.dtype)],
        [VMEM, VMEM],
        grid=(),
        scratch=[pltpu.SemaphoreType.DMA((4,))],
    )


def expert_rows_kernel(slots, tiles, shares, batch, route_row, at_ref, *rest):
    grads, seconds, downs = rest[:batch], rest[batch : batch + 2], rest[batch + 2 : batch + 4]
    *outs, low_ref = rest[batch + 4 : batch + 5 + shares]
    block_ref, turned_ref, block_sems = rest[batch + 5 + shares :]
    tile = downs[0].shape[0] // shares // tiles
    feats = turned_ref.shape[1]
    toks = block_ref.shape[1]
    blocks = [
        pltpu.make_async_copy(ref, block_ref.at[k], block_sems.at[k]) for k, ref in enumerate(grads)
    ]
    for copy in blocks:
        copy.start()

    before = jnp.where(iota((toks, toks), 0) < iota((toks, toks), 1), 1.0, 0.0).astype(BF16)
    columns = turned_ref.shape[2]
    slot = iota((columns, batch * toks), 0).astype(F32)
    second = jnp.concatenate([ref[...] for ref in seconds], axis=0)
    routes = []
    for k in range(batch):
        blocks[k].wait()
        routes.append(block_ref[k, pl.ds(route_row, 16), pl.ds(feats, toks)].astype(F32))
    grad = block_ref[:, :, pl.ds(0, feats)].reshape(batch * toks, feats)
    for q in range(2):
        expert = at_ref[1] * 2 + lax.bitwise_xor(at_ref[2], q)
        targets = []
        for k in range(batch):
            hits = jnp.where(routes[k] == expert.astype(F32), 1.0, 0.0)
            mine = jnp.max(hits, axis=0, keepdims=True)
            pos = dot(jnp.broadcast_to(mine, (16, toks)).astype(BF16), before, NN)[:1]
            targets.append(jnp.where(mine > 0.0, pos + float(k * slots), -1.0))
        pick = jnp.where(slot == jnp.concatenate(targets, axis=1), 1.0, 0.0)
        turned_ref[q] = dot(grad, pick.T.astype(BF16), TN).astype(BF16)
    low = dot(second, grad, NT).astype(BF16)
    for k in range(batch):
        low_ref[k] = low[:, k * toks : (k + 1) * toks]

    rows = batch * slots
    for k in range(shares):
        share = lax.rem(at_ref[0] + k + 1, shares)
        for q in range(2):
            for t in range(tiles):
                row = pl.multiple_of((share * tiles + t) * tile, tile)
                value = dot(downs[q][pl.ds(row, tile), :], turned_ref[q], NN)
                outs[k][pl.ds(q * rows, rows), pl.ds(t * tile, tile)] = value.T[:rows].astype(BF16)


def expert_rows_call(order, grads, seconds, downs, shares, slots):
    batch, (toks, wide) = len(grads), grads[0].shape
    rank, feats = seconds[0].shape
    units = downs[0].shape[0] // shares
    rows = 2 * batch * slots
    return order.call(
        functools.partial(expert_rows_kernel, slots, 3, shares, batch, 3 * rank),
        "expert_rows",
        [*grads, *seconds, *[pltpu.with_memory_space_constraint(x, pltpu.VMEM) for x in downs]],
        [ANY] * batch + [VMEM] * 4,
        [((rows, units), BF16)] * shares + [((batch, 2 * rank, toks), BF16)],
        [VMEM] * (shares + 1),
        grid=(),
        scratch=[
            pltpu.VMEM((batch, toks, wide), BF16),
            pltpu.VMEM((2, feats, -(-batch * slots // 128) * 128), BF16),
            pltpu.SemaphoreType.DMA((batch,)),
        ],
    )


def share_sum_kernel(parts, slots, at_ref, *refs):
    outs = refs[parts:]
    for k, out_ref in enumerate(outs):
        for q in range(2):
            at = pl.ds((q * len(outs) + k) * slots, slots)
            total = refs[0][at, :].astype(F32)
            for part in refs[1:parts]:
                total = total + part[at, :].astype(F32)
            out_ref[pl.ds(q * slots, slots), :] = total.astype(BF16)


def share_sum_call(order, parts, batch, slots):
    rows, units = parts[0].shape
    shape = (2 * slots, units)
    return order.call(
        functools.partial(share_sum_kernel, len(parts), slots),
        "share_sum",
        parts,
        [whole((rows, units))] * len(parts),
        [(shape, BF16)] * batch,
        [whole(shape)] * batch,
    )


def collect_kernel(places, at_ref, *refs):
    low_ref, first_ref = refs[-2:]
    rank = first_ref.shape[1]
    at = 0
    lows = len(refs) - 2 - len(places)
    for ref in refs[:lows]:
        for k in range(ref.shape[0]):
            low_ref[lax.bitwise_xor(at_ref[1], places[at])] = ref[k]
            at += 1
    for o, ref in zip(places, refs[lows:-2]):
        wide = ref.shape[1]
        for k in range(3):
            first_ref[o, :, pl.ds(k * wide, wide)] = ref[pl.ds(k * rank, rank), :]


def collect_call(order, places, lows, grads, feats):
    groups, (toks, wide) = len(grads), grads[0].shape
    rank = lows[0].shape[1] // 2
    extra = wide - feats
    low_shape, first_shape = (groups, 2 * rank, toks), (groups, rank, 3 * extra)
    return order.call(
        functools.partial(collect_kernel, places),
        "collect_blocks",
        [*lows, *[in_hbm(x) for x in grads]],
        [whole(b.shape) for b in lows]
        + [pl.BlockSpec((toks, extra), lambda i: (0, feats // extra))] * groups,
        [(low_shape, BF16), (first_shape, BF16)],
        [whole(low_shape), whole(first_shape)],
    )


def low_dense_kernel(at_ref, *refs):
    out_ref, sum_ref = refs[-2:]
    groups, both, _ = refs[0].shape
    rank = both // 2
    for o in range(groups):
        total = refs[0][lax.bitwise_xor(at_ref[1], o)].astype(F32)
        for ref in refs[1:-2]:
            total = total + ref[lax.bitwise_xor(at_ref[1], o)].astype(F32)
        for q in range(2):
            at = pl.ds((q * groups + o) * rank, rank)
            sum_ref[at, :] = total[q * rank : (q + 1) * rank]
    out_ref[...] = sum_ref[...].T


def low_dense_call(order, parts):
    groups, both, toks = parts[0].shape
    shape = (toks, groups * both)
    return order.call(
        low_dense_kernel,
        "low_dense",
        parts,
        [whole(parts[0].shape)] * len(parts),
        [(shape, F32)],
        [whole(shape)],
        scratch=[pltpu.VMEM((groups * both, toks), F32)],
    )[0]


def lowrank_hid_kernel(groups, at_ref, index_ref, hid_ref, *rest):
    firsts, out_ref = rest[:2], rest[2]
    top = index_ref.shape[1]
    rank = firsts[0].shape[0] // groups
    wide = jnp.concatenate([dot(hid_ref[...], ref[...], NT) for ref in firsts], axis=1)
    column = pair_column(relative(at_ref, index_ref[...], groups).astype(F32))
    wide = jnp.where(expert_mask(column, wide.shape[1], rank), wide, 0.0)
    out_ref[...] = wide.reshape(wide.shape[0] // top, top, wide.shape[1]).sum(axis=1)


def lowrank_hid_call(order, index, hid, firsts, groups):
    (toks, top), (pairs, units) = index.shape, hid.shape
    half = firsts[0].shape[0]
    steps = 4
    return order.call(
        functools.partial(lowrank_hid_kernel, groups),
        "lowrank_hid",
        [index, in_hbm(hid), *firsts],
        [
            pl.BlockSpec((toks // steps, top), lambda i: (i, 0)),
            pl.BlockSpec((pairs // steps, units), lambda i: (i, 0)),
        ]
        + [whole((half, units))] * 2,
        [((toks, 2 * half), F32)],
        [pl.BlockSpec((toks // steps, 2 * half), lambda i: (i, 0))],
        grid=(steps,),
    )[0]


def scaled_hid_kernel(groups, rank, at_ref, index_ref, prob_ref, *refs):
    out_ref = refs[-1]
    total = refs[0][...]
    for ref in refs[1:-1]:
        total = total + ref[...]
    place = relative(at_ref, index_ref[...], groups)
    prob = prob_ref[...].astype(F32)
    expert = iota(total.shape, 1) // rank
    scale = jnp.zeros(total.shape, F32)
    for k in range(place.shape[1]):
        scale = jnp.where(expert == place[:, k : k + 1], prob[:, k : k + 1], scale)
    scaled = (total * scale).T.astype(BF16)
    for o in range(groups):
        for q in range(2):
            at = (q * groups + o) * rank
            out_ref[lax.bitwise_xor(at_ref[1], o), pl.ds(q * rank, rank), :] = scaled[at : at + rank]


def scaled_hid_call(order, index, prob, parts, groups):
    toks, width = parts[0].shape
    rank = width // groups // 2
    shape = (groups, 2 * rank, toks)
    return order.call(
        functools.partial(scaled_hid_kernel, groups, rank),
        "scaled_hid",
        [index, prob, *parts],
        [whole(index.shape), whole(prob.shape)] + [whole((toks, width))] * len(parts),
        [(shape, BF16)],
        [whole(shape)],
    )[0]


def second_grad_kernel(places, at_ref, scaled_ref, *refs):
    grads, outs = refs[:-2], refs[-2:]
    rank, tile = outs[0].shape
    total = jnp.zeros((2 * rank, tile), F32)
    for o, grad_ref in zip(places, grads):
        total = total + dot(scaled_ref[lax.bitwise_xor(at_ref[1], o)], grad_ref[...], NN)
    for q, out_ref in enumerate(outs):
        out_ref[...] = adapter_scale * total[q * rank : (q + 1) * rank]


def second_grad_call(order, places, scaled, grads, feats):
    groups, both, toks = scaled.shape
    steps = 4
    tile = feats // steps
    block = pl.BlockSpec((both // 2, tile), lambda i: (0, i))
    return order.call(
        functools.partial(second_grad_kernel, places),
        "second_grad",
        [scaled, *[in_hbm(x) for x in grads]],
        [whole(scaled.shape)] + [pl.BlockSpec((toks, tile), lambda i: (0, i))] * groups,
        [((both // 2, feats), F32)] * 2,
        [block] * 2,
        grid=(steps,),
    )


def first_grad_kernel(groups, steps, at_ref, index_ref, prob_ref, low_ref, hid_ref, *rest):
    out_ref, sum_ref = rest
    step = pl.program_id(0)
    top = index_ref.shape[1]
    rank = out_ref.shape[1]
    low = spread_pairs(low_ref[...], top)
    column = pair_column(relative(at_ref, index_ref[...], groups).astype(F32))
    keep = expert_mask(column, low.shape[1], rank)
    scaled = jnp.where(keep, low * pair_column(prob_ref[...].astype(F32)), 0.0).astype(BF16)
    part = adapter_scale * dot(scaled, hid_ref[...], TN)

    @pl.when(step == 0)
    def _():
        sum_ref[...] = part

    @pl.when(step > 0)
    def _():
        sum_ref[...] += part

    @pl.when(step == steps - 1)
    def _():
        for o in range(groups):
            for q in range(2):
                expert = 2 * lax.bitwise_xor(at_ref[1], o) + lax.bitwise_xor(at_ref[2], q)
                rows = sum_ref[pl.ds((q * groups + o) * rank, rank), :]
                out_ref[expert] = rows.astype(BF16)


def first_grad_call(order, index, prob, low, hid, groups):
    (toks, top), (pairs, units) = index.shape, hid.shape
    width = low.shape[1]
    steps = 4
    shape = (2 * groups, width // groups // 2, units)
    return order.call(
        functools.partial(first_grad_kernel, groups, steps),
        "first_grad",
        [index, prob, low, in_hbm(hid)],
        [
            pl.BlockSpec((toks // steps, top), lambda i: (i, 0)),
            pl.BlockSpec((toks // steps, top), lambda i: (i, 0)),
            pl.BlockSpec((toks // steps, width), lambda i: (i, 0)),
            pl.BlockSpec((pairs // steps, units), lambda i: (i, 0)),
        ],
        [(shape, BF16)],
        [whole(shape)],
        grid=(steps,),
        scratch=[pltpu.VMEM((width, units), F32)],
    )[0]


def finish_kernel(count, slots, at_ref, index_all_ref, index_ref, prob_ref, low_ref, hid_ref, *rest):
    firsts, back = rest[:2], rest[2 : 2 + count]
    out_ref, sum_ref, all_ref, place_ref = rest[2 + count :]
    top = index_ref.shape[1]
    toks = index_all_ref.shape[0]
    experts = 2 * count

    @pl.when(pl.program_id(0) == 0)
    def _():
        for o, ref in enumerate(back):
            for q in range(2):
                all_ref[pl.ds((q * count + o) * slots, slots), :] = ref[pl.ds(q * slots, slots), :]
        experts_all = relative(at_ref, index_all_ref[...], count)
        hit = jnp.zeros((toks, experts), F32)
        for k in range(top):
            hit = jnp.where(iota((toks, experts), 1) == experts_all[:, k : k + 1], 1.0, hit)
        before = jnp.where(iota((toks, toks), 0) > iota((toks, toks), 1), 1.0, 0.0).astype(BF16)
        place_ref[...] = dot(before, hit.astype(BF16), NN)

    pairs = hid_ref.shape[0]
    some = index_ref.shape[0]
    column = pair_column(relative(at_ref, index_ref[...], count).astype(F32))
    place = spread_pairs(place_ref[pl.ds(pl.program_id(0) * some, some), :], top)
    mine = iota((pairs, experts), 1) == column.astype(jnp.int32)
    target = column * slots + jnp.sum(jnp.where(mine, place, 0.0), axis=1, keepdims=True)
    low = spread_pairs(low_ref[...], top)
    keep = expert_mask(column, low.shape[1], low.shape[1] // experts)
    low = jnp.where(keep, adapter_scale * low.astype(BF16).astype(F32), 0.0).astype(BF16)
    slot = iota((pairs, experts * slots), 1)
    pick = jnp.where(slot == target.astype(jnp.int32), 1.0, 0.0).astype(BF16)
    half = low.shape[1] // 2
    value = dot(pick, all_ref[...], NN)
    value = value + dot(low[:, :half], firsts[0][...], NN) + dot(low[:, half:], firsts[1][...], NN)
    value = value.astype(BF16).astype(F32)
    out_ref[...] = (value * pair_column(prob_ref[...].astype(F32))).astype(BF16)
    sums = jnp.sum(value * hid_ref[...].astype(F32), axis=1, keepdims=True)
    sums = jnp.where(diagonal(pairs, top), sums, 0.0)
    sum_ref[...] = sums.reshape(some, top, top).sum(axis=1)


def finish_call(order, index, prob, low, hid, firsts, back):
    (toks, top), (pairs, units) = index.shape, hid.shape
    width = low.shape[1]
    both = back[0].shape[0]
    steps = 4
    count = len(back)

    def rows(n, columns):
        return pl.BlockSpec((n // steps, columns), lambda i: (i, 0))

    return order.call(
        functools.partial(finish_kernel, count, both // 2),
        "finish",
        [index, index, prob, low, in_hbm(hid), *firsts, *[in_hbm(x) for x in back]],
        [whole(index.shape), rows(toks, top), rows(toks, top), rows(toks, width), rows(pairs, units)]
        + [whole(firsts[0].shape)] * 2
        + [whole((both, units))] * count,
        [((pairs, units), BF16), ((toks, top), F32)],
        [rows(pairs, units), rows(toks, top)],
        grid=(steps,),
        cost=LONG,
        scratch=[pltpu.VMEM((count * both, units), BF16), pltpu.VMEM((toks, 2 * count), F32)],
    )


def body(grad, hidden, index, weight, down, first, second):
    toks, top = index.shape
    exp_local, units_all, feats = down.shape
    units, rank = first.shape[1:]
    groups, cores, shares = lax.axis_size("ep"), lax.axis_size("sub"), lax.axis_size("rep")
    assert exp_local == 1 and cores == 2 and groups & (groups - 1) == 0
    cap = min(toks, 5 * toks * top // (4 * groups * cores))
    slots = -(-cap // 16) * 16
    pairs = toks * top
    at = jnp.stack([lax.axis_index(name).astype(jnp.int32) for name in ("rep", "ep", "sub")])
    order = Order(at)

    def turn(x, offset):
        return lax.ppermute(x, "rep", [(r, (r + offset) % shares) for r in range(shares)])

    def all_shares(x):
        return [x] + [turn(x, k) for k in range(1, shares)]

    def flip(x, mask):
        return lax.ppermute(x, "ep", [(i, i ^ mask) for i in range(groups)])

    def swap(x):
        return lax.ppermute(x, "sub", [(0, 1), (1, 0)])

    def exchange(x, axes="ep"):
        return lax.all_to_all(x, axes, split_axis=0, concat_axis=0, tiled=True)

    blocks = {0: pack_call(order, grad, first[0].T, index.T)}

    def fetch(o):
        if o not in blocks:
            last = o & -o
            blocks[o] = flip(fetch(o ^ last), last)
        return blocks[o]

    own_down, own_second = load_call(order, down[0], second[0])
    downs = [own_down, swap(down[0])]
    seconds = [own_second, swap(own_second)]

    if groups == 8:
        batches = [(0, 1), (2, 4), (6, 5), (3, 7)]
    else:
        batches = [(o, o + 1) for o in range(0, groups, 2)]
    places = [o for batch in batches for o in batch]
    back, lows, waiting = {}, [], []

    def arrived(i):
        order.wait([back[o] for o in batches[i] if o])

    def send_back(batch, parts):
        for o, rows in zip(batch, share_sum_call(order, parts, 2, slots)):
            if batch in batches[-2:] and o > 1 and o % 2:
                back[o] = flip(flip(rows, 1), o - 1)
            else:
                back[o] = flip(rows, o) if o else rows

    for i, batch in enumerate(batches):
        *give, keep, low = expert_rows_call(
            order, [fetch(o) for o in batch], seconds, downs, shares, slots
        )
        lows.append(low)
        if i > 1 and i == len(batches) - 1:
            for j in range(i - 1):
                arrived(j)
        if i > 0:
            send_back(*waiting)
        waiting = (batch, [keep] + [turn(x, k + 1) for k, x in enumerate(give)])

    hid = hidden.reshape(pairs, units)
    grads = [blocks[o] for o in places]

    low_grad, first_own = collect_call(order, places, lows, grads, feats)
    firsts = [x.reshape(groups * rank, units) for x in (first_own, swap(first_own))]
    low_grad = all_shares(exchange(low_grad))
    send_back(*waiting)

    order.wait([back[batches[-2][0]]])
    low_hid = all_shares(lowrank_hid_call(order, index, hid, firsts, groups))
    low_grad = low_dense_call(order, low_grad)
    first_part = first_grad_call(order, index, weight, low_grad, hid, groups)

    scaled_hid = scaled_hid_call(order, index, weight, low_hid, groups)

    order.wait([back[batches[-2][1]], back[batches[-1][0]], back[batches[-1][1]]])
    scaled_hid, first_part = gate_call(order, [scaled_hid, first_part])
    scaled_hid = exchange(scaled_hid)
    first_part = exchange(first_part, ("ep", "sub"))
    first_grad = jnp.sum(first_part.astype(F32), axis=0)
    back = [back[o] for o in range(groups)]
    grad_hidden, sums = finish_call(order, index, weight, low_grad, hid, firsts, back)
    sums = sums + turn(sums, 1) if shares == 2 else lax.psum(sums, "rep")
    order.wait([first_part])
    second_keep, second_give = second_grad_call(order, places, scaled_hid, grads, feats)
    second_grad = second_keep + swap(second_give)
    return (
        grad_hidden.reshape(toks, top, units),
        sums,
        first_grad.T[None],
        second_grad[None],
    )


def solution(mesh):
    return jax.shard_map(
        body,
        mesh=mesh,
        in_specs=(
            P(("grp", "ep", "sub"), "rep"),
            P(("grp", "ep", "sub"), None, "rep"),
            P(("grp", "ep", "sub"), None),
            P(("grp", "ep", "sub"), None),
            P(("ep", "sub"), None, "rep"),
            P(("grp", "ep", "sub"), "rep", None),
            P(("grp", "ep", "sub"), None, "rep"),
        ),
        out_specs=(
            P(("grp", "ep", "sub"), None, "rep"),
            P(("grp", "ep", "sub"), None),
            P(("grp", "ep", "sub"), "rep", None),
            P(("grp", "ep", "sub"), None, "rep"),
        ),
        check_vma=False,
    )
```

```python
import functools

import jax
import jax.numpy as jnp
from jax import lax
from jax.experimental import pallas as pl
from jax.experimental.pallas import tpu as pltpu
from jax.sharding import PartitionSpec as P

adapter_scale = 2.0
BF16 = jnp.bfloat16
F32 = jnp.float32
NT = (((1,), (1,)), ((), ()))
TN = (((0,), (0,)), ((), ()))
NN = (((1,), (0,)), ((), ()))
SMALL = pl.CostEstimate(flops=1, bytes_accessed=1, transcendentals=0)
LONG = pl.CostEstimate(flops=1, bytes_accessed=2 * 10**7, transcendentals=0)
ANY = pl.BlockSpec(memory_space=pl.ANY)
SMEM = pl.BlockSpec(memory_space=pltpu.SMEM)
VMEM = pl.BlockSpec(memory_space=pltpu.VMEM)


def dot(a, b, dims):
    return lax.dot_general(a, b, dims, preferred_element_type=F32)


def iota(shape, axis):
    return lax.broadcasted_iota(jnp.int32, shape, axis)


def whole(shape):
    return pl.BlockSpec(shape, lambda *_: (0,) * len(shape))


def in_hbm(x):
    return pltpu.with_memory_space_constraint(x, pltpu.HBM)


class Order:
    def __init__(self, at):
        self.at, self.last = at, []

    def wait(self, arrays):
        self.last = self.last + list(arrays)

    def call(self, kernel, name, arrays, in_specs, outs, out_specs, grid=(1,), scratch=(), mib=16, cost=SMALL, **more):
        count, last = 1 + len(arrays), len(self.last)

        def ordered(*refs):
            here = count + last + len(outs)
            kernel(*refs[:count], *refs[count + last : here], *refs[here + 1 :])

        *result, token = pl.pallas_call(
            ordered,
            grid=grid,
            in_specs=[SMEM, *in_specs] + [ANY] * last,
            out_specs=[*out_specs, ANY],
            scratch_shapes=scratch,
            out_shape=[jax.ShapeDtypeStruct(*o) if isinstance(o, tuple) else o for o in outs]
            + [pltpu.HBM((8, 128), F32)],
            compiler_params=pltpu.CompilerParams(vmem_limit_bytes=mib * 2**20),
            cost_estimate=cost,
            name=name,
            **more,
        )(self.at, *arrays, *self.last)
        self.last = [in_hbm(token)]
        return result


def relative(at_ref, index, groups):
    o = lax.bitwise_xor(lax.shift_right_logical(index, 1), at_ref[1])
    q = lax.bitwise_xor(lax.bitwise_and(index, 1), at_ref[2])
    return q * groups + o


def spread_pairs(dense, top):
    toks, width = dense.shape
    return jnp.broadcast_to(dense[:, None, :], (toks, top, width)).reshape(toks * top, width)


def diagonal(pairs, top):
    return iota((pairs, top), 1) == lax.bitwise_and(iota((pairs, top), 0), top - 1)


def pair_column(table):
    toks, top = table.shape
    wide = spread_pairs(table, top)
    return jnp.sum(jnp.where(diagonal(toks * top, top), wide, 0.0), axis=1, keepdims=True)


def expert_mask(column, width, rank):
    return iota((column.shape[0], width), 1) // rank == column.astype(jnp.int32)


def pack_kernel(at_ref, grad_ref, first_ref, index_ref, out_ref):
    toks, feats = grad_ref.shape
    rank = first_ref.shape[0]
    extra = out_ref.shape[1] - feats
    out_ref[:, pl.ds(0, feats)] = grad_ref[...]
    for k in range(3):
        piece = first_ref[:, pl.ds(k * extra, extra)]
        out_ref[pl.ds(k * rank, rank), pl.ds(feats, extra)] = piece
    top = index_ref.shape[0]
    out_ref[pl.ds(3 * rank, toks - 3 * rank), pl.ds(feats, extra)] = jnp.full(
        (toks - 3 * rank, extra), -1.0, BF16
    )
    routes = index_ref[...].astype(F32)
    routes = jnp.concatenate([routes, jnp.full((16 - top, toks), -1.0, F32)], axis=0)
    out_ref[pl.ds(3 * rank, 16), pl.ds(feats, toks)] = routes.astype(BF16)


def pack_call(order, grad, first, index):
    (toks, feats), (rank, units) = grad.shape, first.shape
    shape = (toks, feats + units // 3)
    return order.call(
        pack_kernel,
        "pack_block",
        [in_hbm(grad), first, index],
        [whole(grad.shape), whole(first.shape), whole(index.shape)],
        [(shape, BF16)],
        [whole(shape)],
    )[0]


def gate_kernel(at_ref, *refs):
    pass


def gate_call(order, arrays):
    return order.call(
        gate_kernel,
        "gate",
        arrays,
        [ANY] * len(arrays),
        [(x.shape, x.dtype) for x in arrays],
        [ANY] * len(arrays),
        input_output_aliases={1 + k: k for k in range(len(arrays))},
    )


def load_kernel(at_ref, down_ref, second_ref, out_ref, same_ref, sems):
    parts = sems.shape[0]
    rows = down_ref.shape[0] // parts
    copies = [
        pltpu.make_async_copy(
            down_ref.at[pl.ds(k * rows, rows), :], out_ref.at[pl.ds(k * rows, rows), :], sems.at[k]
        )
        for k in range(parts)
    ]
    for copy in copies:
        copy.start()
    same_ref[...] = second_ref[...]
    for copy in copies:
        copy.wait()


def load_call(order, down, second):
    return order.call(
        load_kernel,
        "load_matrix",
        [in_hbm(down), second],
        [ANY, VMEM],
        [pltpu.VMEM(down.shape, down.dtype), (second.shape, second.dtype)],
        [VMEM, VMEM],
        grid=(),
        scratch=[pltpu.SemaphoreType.DMA((4,))],
    )


def expert_rows_kernel(slots, tiles, shares, batch, route_row, at_ref, *rest):
    grads, seconds, downs = rest[:batch], rest[batch : batch + 2], rest[batch + 2 : batch + 4]
    *outs, low_ref = rest[batch + 4 : batch + 5 + shares]
    block_ref, turned_ref, block_sems = rest[batch + 5 + shares :]
    tile = downs[0].shape[0] // shares // tiles
    feats = turned_ref.shape[1]
    toks = block_ref.shape[1]
    blocks = [
        pltpu.make_async_copy(ref, block_ref.at[k], block_sems.at[k]) for k, ref in enumerate(grads)
    ]
    for copy in blocks:
        copy.start()

    before = jnp.where(iota((toks, toks), 0) < iota((toks, toks), 1), 1.0, 0.0).astype(BF16)
    columns = turned_ref.shape[2]
    slot = iota((columns, batch * toks), 0).astype(F32)
    second = jnp.concatenate([ref[...] for ref in seconds], axis=0)
    routes = []
    for k in range(batch):
        blocks[k].wait()
        routes.append(block_ref[k, pl.ds(route_row, 16), pl.ds(feats, toks)].astype(F32))
    grad = block_ref[:, :, pl.ds(0, feats)].reshape(batch * toks, feats)
    for q in range(2):
        expert = at_ref[1] * 2 + lax.bitwise_xor(at_ref[2], q)
        targets = []
        for k in range(batch):
            hits = jnp.where(routes[k] == expert.astype(F32), 1.0, 0.0)
            mine = jnp.max(hits, axis=0, keepdims=True)
            pos = dot(jnp.broadcast_to(mine, (16, toks)).astype(BF16), before, NN)[:1]
            targets.append(jnp.where(mine > 0.0, pos + float(k * slots), -1.0))
        pick = jnp.where(slot == jnp.concatenate(targets, axis=1), 1.0, 0.0)
        turned_ref[q] = dot(grad, pick.T.astype(BF16), TN).astype(BF16)
    low = dot(second, grad, NT).astype(BF16)
    for k in range(batch):
        low_ref[k] = low[:, k * toks : (k + 1) * toks]

    rows = batch * slots
    for k in range(shares):
        share = lax.rem(at_ref[0] + k + 1, shares)
        for q in range(2):
            for t in range(tiles):
                row = pl.multiple_of((share * tiles + t) * tile, tile)
                value = dot(downs[q][pl.ds(row, tile), :], turned_ref[q], NN)
                outs[k][pl.ds(q * rows, rows), pl.ds(t * tile, tile)] = value.T[:rows].astype(BF16)


def expert_rows_call(order, grads, seconds, downs, shares, slots):
    batch, (toks, wide) = len(grads), grads[0].shape
    rank, feats = seconds[0].shape
    units = downs[0].shape[0] // shares
    rows = 2 * batch * slots
    return order.call(
        functools.partial(expert_rows_kernel, slots, 3, shares, batch, 3 * rank),
        "expert_rows",
        [*grads, *seconds, *[pltpu.with_memory_space_constraint(x, pltpu.VMEM) for x in downs]],
        [ANY] * batch + [VMEM] * 4,
        [((rows, units), BF16)] * shares + [((batch, 2 * rank, toks), BF16)],
        [VMEM] * (shares + 1),
        grid=(),
        scratch=[
            pltpu.VMEM((batch, toks, wide), BF16),
            pltpu.VMEM((2, feats, -(-batch * slots // 128) * 128), BF16),
            pltpu.SemaphoreType.DMA((batch,)),
        ],
    )


def share_sum_kernel(parts, slots, at_ref, *refs):
    outs = refs[parts:]
    for k, out_ref in enumerate(outs):
        for q in range(2):
            at = pl.ds((q * len(outs) + k) * slots, slots)
            total = refs[0][at, :].astype(F32)
            for part in refs[1:parts]:
                total = total + part[at, :].astype(F32)
            out_ref[pl.ds(q * slots, slots), :] = total.astype(BF16)


def share_sum_call(order, parts, batch, slots):
    rows, units = parts[0].shape
    shape = (2 * slots, units)
    return order.call(
        functools.partial(share_sum_kernel, len(parts), slots),
        "share_sum",
        parts,
        [whole((rows, units))] * len(parts),
        [(shape, BF16)] * batch,
        [whole(shape)] * batch,
    )


def collect_kernel(places, at_ref, *refs):
    low_ref, first_ref = refs[-2:]
    rank = first_ref.shape[1]
    at = 0
    lows = len(refs) - 2 - len(places)
    for ref in refs[:lows]:
        for k in range(ref.shape[0]):
            low_ref[lax.bitwise_xor(at_ref[1], places[at])] = ref[k]
            at += 1
    for o, ref in zip(places, refs[lows:-2]):
        wide = ref.shape[1]
        for k in range(3):
            first_ref[o, :, pl.ds(k * wide, wide)] = ref[pl.ds(k * rank, rank), :]


def collect_call(order, places, lows, grads, feats):
    groups, (toks, wide) = len(grads), grads[0].shape
    rank = lows[0].shape[1] // 2
    extra = wide - feats
    low_shape, first_shape = (groups, 2 * rank, toks), (groups, rank, 3 * extra)
    return order.call(
        functools.partial(collect_kernel, places),
        "collect_blocks",
        [*lows, *[in_hbm(x) for x in grads]],
        [whole(b.shape) for b in lows]
        + [pl.BlockSpec((toks, extra), lambda i: (0, feats // extra))] * groups,
        [(low_shape, BF16), (first_shape, BF16)],
        [whole(low_shape), whole(first_shape)],
    )


def low_dense_kernel(at_ref, *refs):
    out_ref, sum_ref = refs[-2:]
    groups, both, _ = refs[0].shape
    rank = both // 2
    for o in range(groups):
        total = refs[0][lax.bitwise_xor(at_ref[1], o)].astype(F32)
        for ref in refs[1:-2]:
            total = total + ref[lax.bitwise_xor(at_ref[1], o)].astype(F32)
        for q in range(2):
            at = pl.ds((q * groups + o) * rank, rank)
            sum_ref[at, :] = total[q * rank : (q + 1) * rank]
    out_ref[...] = sum_ref[...].T


def low_dense_call(order, parts):
    groups, both, toks = parts[0].shape
    shape = (toks, groups * both)
    return order.call(
        low_dense_kernel,
        "low_dense",
        parts,
        [whole(parts[0].shape)] * len(parts),
        [(shape, F32)],
        [whole(shape)],
        scratch=[pltpu.VMEM((groups * both, toks), F32)],
    )[0]


def lowrank_hid_kernel(groups, at_ref, index_ref, hid_ref, *rest):
    firsts, out_ref = rest[:2], rest[2]
    top = index_ref.shape[1]
    rank = firsts[0].shape[0] // groups
    wide = jnp.concatenate([dot(hid_ref[...], ref[...], NT) for ref in firsts], axis=1)
    column = pair_column(relative(at_ref, index_ref[...], groups).astype(F32))
    wide = jnp.where(expert_mask(column, wide.shape[1], rank), wide, 0.0)
    out_ref[...] = wide.reshape(wide.shape[0] // top, top, wide.shape[1]).sum(axis=1)


def lowrank_hid_call(order, index, hid, firsts, groups):
    (toks, top), (pairs, units) = index.shape, hid.shape
    half = firsts[0].shape[0]
    steps = 4
    return order.call(
        functools.partial(lowrank_hid_kernel, groups),
        "lowrank_hid",
        [index, in_hbm(hid), *firsts],
        [
            pl.BlockSpec((toks // steps, top), lambda i: (i, 0)),
            pl.BlockSpec((pairs // steps, units), lambda i: (i, 0)),
        ]
        + [whole((half, units))] * 2,
        [((toks, 2 * half), F32)],
        [pl.BlockSpec((toks // steps, 2 * half), lambda i: (i, 0))],
        grid=(steps,),
    )[0]


def second_grad_kernel(places, units, at_ref, got_ref, *refs):
    grads, outs, first_ref = refs[:-3], refs[-3:-1], refs[-1]
    rank, tile = outs[0].shape
    toks = grads[0].shape[0]

    @pl.when(pl.program_id(0) == 0)
    def _():
        total = jnp.zeros((rank, units), F32)
        for source in range(got_ref.shape[0]):
            total = total + got_ref[source, :, pl.ds(0, units)].astype(F32)
        first_ref[...] = total

    totals = [jnp.zeros((rank, tile), F32) for _ in outs]
    for o, grad_ref in zip(places, grads):
        source = 2 * lax.bitwise_xor(at_ref[1], o) + at_ref[2]
        scaled = jnp.concatenate(
            [got_ref[source, :, pl.ds(units + q * toks, toks)] for q in range(2)], axis=0
        )
        value = dot(scaled, grad_ref[...], NN)
        totals = [total + value[q * rank : (q + 1) * rank] for q, total in enumerate(totals)]
    for total, out_ref in zip(totals, outs):
        out_ref[...] = adapter_scale * total


def second_grad_call(order, places, got, grads, units, feats):
    rank, toks = got.shape[1], grads[0].shape[0]
    steps = 4
    tile = feats // steps
    block = pl.BlockSpec((rank, tile), lambda i: (0, i))
    return order.call(
        functools.partial(second_grad_kernel, places, units),
        "second_grad",
        [got, *[in_hbm(x) for x in grads]],
        [whole(got.shape)] + [pl.BlockSpec((toks, tile), lambda i: (0, i))] * len(grads),
        [((rank, feats), F32)] * 2 + [((rank, units), F32)],
        [block] * 2 + [whole((rank, units))],
        grid=(steps,),
    )


def first_grad_kernel(groups, steps, parts, at_ref, index_ref, prob_ref, low_ref, hid_ref, *rest):
    index_all_ref, prob_all_ref, hids = rest[0], rest[1], rest[2 : 2 + parts]
    out_ref, sum_ref = rest[2 + parts :]
    step = pl.program_id(0)
    top = index_ref.shape[1]
    rank = out_ref.shape[1]
    units = sum_ref.shape[1]
    low = spread_pairs(low_ref[...], top)
    column = pair_column(relative(at_ref, index_ref[...], groups).astype(F32))
    keep = expert_mask(column, low.shape[1], rank)
    scaled = jnp.where(keep, low * pair_column(prob_ref[...].astype(F32)), 0.0).astype(BF16)
    part = adapter_scale * dot(scaled, hid_ref[...], TN)

    @pl.when(step == 0)
    def _():
        sum_ref[...] = part

    @pl.when(step > 0)
    def _():
        sum_ref[...] += part

    @pl.when(step == steps - 1)
    def _():
        total = hids[0][...]
        for ref in hids[1:]:
            total = total + ref[...]
        toks = total.shape[0]
        place = relative(at_ref, index_all_ref[...], groups)
        prob = prob_all_ref[...].astype(F32)
        expert = iota(total.shape, 1) // rank
        scale = jnp.zeros(total.shape, F32)
        for k in range(top):
            scale = jnp.where(expert == place[:, k : k + 1], prob[:, k : k + 1], scale)
        turned = (total * scale).T.astype(BF16)
        for o in range(groups):
            for q in range(2):
                at = (q * groups + o) * rank
                to = 2 * lax.bitwise_xor(at_ref[1], o) + lax.bitwise_xor(at_ref[2], q)
                out_ref[to, :, pl.ds(0, units)] = sum_ref[pl.ds(at, rank), :].astype(BF16)
                if q:
                    out_ref[to, :, pl.ds(units, 2 * toks)] = jnp.zeros((rank, 2 * toks), BF16)
                else:
                    for p in range(2):
                        rows = turned[(p * groups + o) * rank : (p * groups + o + 1) * rank]
                        out_ref[to, :, pl.ds(units + p * toks, toks)] = rows


def first_grad_call(order, index, prob, low, hid, hids, groups):
    (toks, top), (pairs, units) = index.shape, hid.shape
    width = low.shape[1]
    steps = 4
    shape = (2 * groups, width // groups // 2, units + 2 * toks)
    return order.call(
        functools.partial(first_grad_kernel, groups, steps, len(hids)),
        "first_grad",
        [index, prob, low, in_hbm(hid), index, prob, *hids],
        [
            pl.BlockSpec((toks // steps, top), lambda i: (i, 0)),
            pl.BlockSpec((toks // steps, top), lambda i: (i, 0)),
            pl.BlockSpec((toks // steps, width), lambda i: (i, 0)),
            pl.BlockSpec((pairs // steps, units), lambda i: (i, 0)),
            whole(index.shape),
            whole(prob.shape),
        ]
        + [whole(x.shape) for x in hids],
        [(shape, BF16)],
        [whole(shape)],
        grid=(steps,),
        scratch=[pltpu.VMEM((width, units), F32)],
    )[0]


def finish_kernel(count, slots, at_ref, index_all_ref, index_ref, prob_ref, low_ref, hid_ref, *rest):
    firsts, back = rest[:2], rest[2 : 2 + count]
    out_ref, sum_ref, all_ref, place_ref = rest[2 + count :]
    top = index_ref.shape[1]
    toks = index_all_ref.shape[0]
    experts = 2 * count

    @pl.when(pl.program_id(0) == 0)
    def _():
        for o, ref in enumerate(back):
            for q in range(2):
                all_ref[pl.ds((q * count + o) * slots, slots), :] = ref[pl.ds(q * slots, slots), :]
        experts_all = relative(at_ref, index_all_ref[...], count)
        hit = jnp.zeros((toks, experts), F32)
        for k in range(top):
            hit = jnp.where(iota((toks, experts), 1) == experts_all[:, k : k + 1], 1.0, hit)
        before = jnp.where(iota((toks, toks), 0) > iota((toks, toks), 1), 1.0, 0.0).astype(BF16)
        place_ref[...] = dot(before, hit.astype(BF16), NN)

    pairs = hid_ref.shape[0]
    some = index_ref.shape[0]
    column = pair_column(relative(at_ref, index_ref[...], count).astype(F32))
    place = spread_pairs(place_ref[pl.ds(pl.program_id(0) * some, some), :], top)
    mine = iota((pairs, experts), 1) == column.astype(jnp.int32)
    target = column * slots + jnp.sum(jnp.where(mine, place, 0.0), axis=1, keepdims=True)
    low = spread_pairs(low_ref[...], top)
    keep = expert_mask(column, low.shape[1], low.shape[1] // experts)
    low = jnp.where(keep, adapter_scale * low.astype(BF16).astype(F32), 0.0).astype(BF16)
    slot = iota((pairs, experts * slots), 1)
    pick = jnp.where(slot == target.astype(jnp.int32), 1.0, 0.0).astype(BF16)
    half = low.shape[1] // 2
    value = dot(pick, all_ref[...], NN)
    value = value + dot(low[:, :half], firsts[0][...], NN) + dot(low[:, half:], firsts[1][...], NN)
    value = value.astype(BF16).astype(F32)
    out_ref[...] = (value * pair_column(prob_ref[...].astype(F32))).astype(BF16)
    sums = jnp.sum(value * hid_ref[...].astype(F32), axis=1, keepdims=True)
    sums = jnp.where(diagonal(pairs, top), sums, 0.0)
    sum_ref[...] = sums.reshape(some, top, top).sum(axis=1)


def finish_call(order, index, prob, low, hid, firsts, back):
    (toks, top), (pairs, units) = index.shape, hid.shape
    width = low.shape[1]
    both = back[0].shape[0]
    steps = 4
    count = len(back)

    def rows(n, columns):
        return pl.BlockSpec((n // steps, columns), lambda i: (i, 0))

    return order.call(
        functools.partial(finish_kernel, count, both // 2),
        "finish",
        [index, index, prob, low, in_hbm(hid), *firsts, *[in_hbm(x) for x in back]],
        [whole(index.shape), rows(toks, top), rows(toks, top), rows(toks, width), rows(pairs, units)]
        + [whole(firsts[0].shape)] * 2
        + [whole((both, units))] * count,
        [((pairs, units), BF16), ((toks, top), F32)],
        [rows(pairs, units), rows(toks, top)],
        grid=(steps,),
        cost=LONG,
        scratch=[pltpu.VMEM((count * both, units), BF16), pltpu.VMEM((toks, 2 * count), F32)],
    )


def body(grad, hidden, index, weight, down, first, second):
    toks, top = index.shape
    exp_local, units_all, feats = down.shape
    units, rank = first.shape[1:]
    groups, cores, shares = lax.axis_size("ep"), lax.axis_size("sub"), lax.axis_size("rep")
    assert exp_local == 1 and cores == 2 and groups & (groups - 1) == 0
    cap = min(toks, 5 * toks * top // (4 * groups * cores))
    slots = -(-cap // 16) * 16
    pairs = toks * top
    at = jnp.stack([lax.axis_index(name).astype(jnp.int32) for name in ("rep", "ep", "sub")])
    order = Order(at)

    def turn(x, offset):
        return lax.ppermute(x, "rep", [(r, (r + offset) % shares) for r in range(shares)])

    def all_shares(x):
        return [x] + [turn(x, k) for k in range(1, shares)]

    def flip(x, mask):
        return lax.ppermute(x, "ep", [(i, i ^ mask) for i in range(groups)])

    def swap(x):
        return lax.ppermute(x, "sub", [(0, 1), (1, 0)])

    where = ("ep", "sub")

    def exchange(x, axes="ep"):
        return lax.all_to_all(x, axes, split_axis=0, concat_axis=0, tiled=True)

    blocks = {0: pack_call(order, grad, first[0].T, index.T)}

    def fetch(o):
        if o not in blocks:
            last = o & -o
            blocks[o] = flip(fetch(o ^ last), last)
        return blocks[o]

    own_down, own_second = load_call(order, down[0], second[0])
    downs = [own_down, swap(down[0])]
    seconds = [own_second, swap(own_second)]

    if groups == 8:
        batches = [(0, 1), (2, 4), (6, 5), (3, 7)]
    else:
        batches = [(o, o + 1) for o in range(0, groups, 2)]
    places = [o for batch in batches for o in batch]
    back, lows, waiting = {}, [], []

    def arrived(i):
        order.wait([back[o] for o in batches[i] if o])

    def send_back(batch, parts):
        for o, rows in zip(batch, share_sum_call(order, parts, 2, slots)):
            if batch in batches[-2:] and o > 1 and o % 2:
                back[o] = flip(flip(rows, 1), o - 1)
            else:
                back[o] = flip(rows, o) if o else rows

    for i, batch in enumerate(batches):
        if i > 1 and i == len(batches) - 1:
            for j in range(i - 1):
                arrived(j)
        *give, keep, low = expert_rows_call(
            order, [fetch(o) for o in batch], seconds, downs, shares, slots
        )
        lows.append(low)
        if i > 0:
            send_back(*waiting)
        waiting = (batch, [keep] + [turn(x, k + 1) for k, x in enumerate(give)])

    hid = hidden.reshape(pairs, units)
    grads = [blocks[o] for o in places]

    low_grad, first_own = collect_call(order, places, lows, grads, feats)
    firsts = [x.reshape(groups * rank, units) for x in (first_own, swap(first_own))]
    low_grad = all_shares(exchange(low_grad))
    low_hid = all_shares(lowrank_hid_call(order, index, hid, firsts, groups))
    order.wait([back[batches[-2][0]]])
    send_back(*waiting)

    low_grad = low_dense_call(order, low_grad)
    parts = first_grad_call(order, index, weight, low_grad, hid, low_hid, groups)

    order.wait([back[batches[-2][1]], back[batches[-1][0]], back[batches[-1][1]]])
    got = exchange(gate_call(order, [parts])[0], where)
    back = [back[o] for o in range(groups)]
    grad_hidden, sums = finish_call(order, index, weight, low_grad, hid, firsts, back)
    sums = sums + turn(sums, 1) if shares == 2 else lax.psum(sums, "rep")
    second_keep, second_give, first_grad = second_grad_call(
        order, places, got, grads, units, feats
    )
    second_grad = second_keep + swap(second_give)
    return (
        grad_hidden.reshape(toks, top, units),
        sums,
        first_grad.T[None],
        second_grad[None],
    )


def solution(mesh):
    return jax.shard_map(
        body,
        mesh=mesh,
        in_specs=(
            P(("grp", "ep", "sub"), "rep"),
            P(("grp", "ep", "sub"), None, "rep"),
            P(("grp", "ep", "sub"), None),
            P(("grp", "ep", "sub"), None),
            P(("ep", "sub"), None, "rep"),
            P(("grp", "ep", "sub"), "rep", None),
            P(("grp", "ep", "sub"), None, "rep"),
        ),
        out_specs=(
            P(("grp", "ep", "sub"), None, "rep"),
            P(("grp", "ep", "sub"), None),
            P(("grp", "ep", "sub"), "rep", None),
            P(("grp", "ep", "sub"), None, "rep"),
        ),
        check_vma=False,
    )
```

```python
import functools

import jax
import jax.numpy as jnp
from jax import lax
from jax.experimental import pallas as pl
from jax.experimental.pallas import tpu as pltpu
from jax.sharding import PartitionSpec as P

adapter_scale = 2.0
BF16 = jnp.bfloat16
F32 = jnp.float32
NT = (((1,), (1,)), ((), ()))
TN = (((0,), (0,)), ((), ()))
NN = (((1,), (0,)), ((), ()))
SMALL = pl.CostEstimate(flops=1, bytes_accessed=1, transcendentals=0)
LONG = pl.CostEstimate(flops=1, bytes_accessed=2 * 10**7, transcendentals=0)
ANY = pl.BlockSpec(memory_space=pl.ANY)
SMEM = pl.BlockSpec(memory_space=pltpu.SMEM)
VMEM = pl.BlockSpec(memory_space=pltpu.VMEM)


def dot(a, b, dims):
    return lax.dot_general(a, b, dims, preferred_element_type=F32)


def iota(shape, axis):
    return lax.broadcasted_iota(jnp.int32, shape, axis)


def whole(shape):
    return pl.BlockSpec(shape, lambda *_: (0,) * len(shape))


def in_hbm(x):
    return pltpu.with_memory_space_constraint(x, pltpu.HBM)


class Order:
    def __init__(self, at):
        self.at, self.last = at, []

    def wait(self, arrays):
        self.last = self.last + list(arrays)

    def call(self, kernel, name, arrays, in_specs, outs, out_specs, grid=(1,), scratch=(), mib=16, cost=SMALL, **more):
        count, last = 1 + len(arrays), len(self.last)

        def ordered(*refs):
            here = count + last + len(outs)
            kernel(*refs[:count], *refs[count + last : here], *refs[here + 1 :])

        *result, token = pl.pallas_call(
            ordered,
            grid=grid,
            in_specs=[SMEM, *in_specs] + [ANY] * last,
            out_specs=[*out_specs, ANY],
            scratch_shapes=scratch,
            out_shape=[jax.ShapeDtypeStruct(*o) if isinstance(o, tuple) else o for o in outs]
            + [pltpu.HBM((8, 128), F32)],
            compiler_params=pltpu.CompilerParams(vmem_limit_bytes=mib * 2**20),
            cost_estimate=cost,
            name=name,
            **more,
        )(self.at, *arrays, *self.last)
        self.last = [in_hbm(token)]
        return result


def relative(at_ref, index, groups):
    o = lax.bitwise_xor(lax.shift_right_logical(index, 1), at_ref[1])
    q = lax.bitwise_xor(lax.bitwise_and(index, 1), at_ref[2])
    return q * groups + o


def spread_pairs(dense, top):
    toks, width = dense.shape
    return jnp.broadcast_to(dense[:, None, :], (toks, top, width)).reshape(toks * top, width)


def diagonal(pairs, top):
    return iota((pairs, top), 1) == lax.bitwise_and(iota((pairs, top), 0), top - 1)


def pair_column(table):
    toks, top = table.shape
    wide = spread_pairs(table, top)
    return jnp.sum(jnp.where(diagonal(toks * top, top), wide, 0.0), axis=1, keepdims=True)


def expert_mask(column, width, rank):
    return iota((column.shape[0], width), 1) // rank == column.astype(jnp.int32)


def pack_kernel(at_ref, grad_ref, first_ref, index_ref, out_ref):
    toks, feats = grad_ref.shape
    rank = first_ref.shape[0]
    extra = out_ref.shape[1] - feats
    out_ref[:, pl.ds(0, feats)] = grad_ref[...]
    for k in range(3):
        piece = first_ref[:, pl.ds(k * extra, extra)]
        out_ref[pl.ds(k * rank, rank), pl.ds(feats, extra)] = piece
    top = index_ref.shape[0]
    out_ref[pl.ds(3 * rank, toks - 3 * rank), pl.ds(feats, extra)] = jnp.full(
        (toks - 3 * rank, extra), -1.0, BF16
    )
    routes = index_ref[...].astype(F32)
    routes = jnp.concatenate([routes, jnp.full((16 - top, toks), -1.0, F32)], axis=0)
    out_ref[pl.ds(3 * rank, 16), pl.ds(feats, toks)] = routes.astype(BF16)


def pack_call(order, grad, first, index):
    (toks, feats), (rank, units) = grad.shape, first.shape
    shape = (toks, feats + units // 3)
    return order.call(
        pack_kernel,
        "pack_block",
        [in_hbm(grad), first, index],
        [whole(grad.shape), whole(first.shape), whole(index.shape)],
        [(shape, BF16)],
        [whole(shape)],
    )[0]


def gate_kernel(at_ref, *refs):
    pass


def gate_call(order, arrays):
    return order.call(
        gate_kernel,
        "gate",
        arrays,
        [ANY] * len(arrays),
        [(x.shape, x.dtype) for x in arrays],
        [ANY] * len(arrays),
        input_output_aliases={1 + k: k for k in range(len(arrays))},
    )


def load_kernel(at_ref, down_ref, out_ref, sems):
    parts = sems.shape[0]
    rows = down_ref.shape[0] // parts
    copies = [
        pltpu.make_async_copy(
            down_ref.at[pl.ds(k * rows, rows), :], out_ref.at[pl.ds(k * rows, rows), :], sems.at[k]
        )
        for k in range(parts)
    ]
    for copy in copies:
        copy.start()
    for copy in copies:
        copy.wait()


def load_call(order, down):
    return order.call(
        load_kernel,
        "load_matrix",
        [in_hbm(down)],
        [ANY],
        [pltpu.VMEM(down.shape, down.dtype)],
        [VMEM],
        grid=(),
        scratch=[pltpu.SemaphoreType.DMA((4,))],
    )[0]


def expert_rows_kernel(slots, tiles, shares, batch, route_row, at_ref, *rest):
    grads, seconds, downs = rest[:batch], rest[batch : batch + 2], rest[batch + 2 : batch + 4]
    *outs, low_ref = rest[batch + 4 : batch + 5 + shares]
    block_ref, turned_ref, block_sems = rest[batch + 5 + shares :]
    tile = downs[0].shape[0] // shares // tiles
    feats = turned_ref.shape[1]
    toks = block_ref.shape[1]
    blocks = [
        pltpu.make_async_copy(ref, block_ref.at[k], block_sems.at[k]) for k, ref in enumerate(grads)
    ]
    for copy in blocks:
        copy.start()

    before = jnp.where(iota((toks, toks), 0) < iota((toks, toks), 1), 1.0, 0.0).astype(BF16)
    columns = turned_ref.shape[2]
    slot = iota((columns, batch * toks), 0).astype(F32)
    second = jnp.concatenate([ref[...] for ref in seconds], axis=0)
    routes = []
    for k in range(batch):
        blocks[k].wait()
        routes.append(block_ref[k, pl.ds(route_row, 16), pl.ds(feats, toks)].astype(F32))
    grad = block_ref[:, :, pl.ds(0, feats)].reshape(batch * toks, feats)
    for q in range(2):
        expert = at_ref[1] * 2 + lax.bitwise_xor(at_ref[2], q)
        targets = []
        for k in range(batch):
            hits = jnp.where(routes[k] == expert.astype(F32), 1.0, 0.0)
            mine = jnp.max(hits, axis=0, keepdims=True)
            pos = dot(jnp.broadcast_to(mine, (16, toks)).astype(BF16), before, NN)[:1]
            targets.append(jnp.where(mine > 0.0, pos + float(k * slots), -1.0))
        pick = jnp.where(slot == jnp.concatenate(targets, axis=1), 1.0, 0.0)
        turned_ref[q] = dot(grad, pick.T.astype(BF16), TN).astype(BF16)
    low = dot(second, grad, NT).astype(BF16)
    for k in range(batch):
        low_ref[k] = low[:, k * toks : (k + 1) * toks]

    rows = batch * slots
    for k in range(shares):
        share = lax.rem(at_ref[0] + k + 1, shares)
        for q in range(2):
            for t in range(tiles):
                row = pl.multiple_of((share * tiles + t) * tile, tile)
                value = dot(downs[q][pl.ds(row, tile), :], turned_ref[q], NN)
                outs[k][pl.ds(q * rows, rows), pl.ds(t * tile, tile)] = value.T[:rows].astype(BF16)


def expert_rows_call(order, grads, seconds, downs, shares, slots):
    batch, (toks, wide) = len(grads), grads[0].shape
    rank, feats = seconds[0].shape
    units = downs[0].shape[0] // shares
    rows = 2 * batch * slots
    return order.call(
        functools.partial(expert_rows_kernel, slots, 3, shares, batch, 3 * rank),
        "expert_rows",
        [*grads, *seconds, *[pltpu.with_memory_space_constraint(x, pltpu.VMEM) for x in downs]],
        [ANY] * batch + [VMEM] * 4,
        [((rows, units), BF16)] * shares + [((batch, 2 * rank, toks), BF16)],
        [VMEM] * (shares + 1),
        grid=(),
        scratch=[
            pltpu.VMEM((batch, toks, wide), BF16),
            pltpu.VMEM((2, feats, -(-batch * slots // 128) * 128), BF16),
            pltpu.SemaphoreType.DMA((batch,)),
        ],
    )


def share_sum_kernel(parts, slots, at_ref, *refs):
    outs = refs[parts:]
    for k, out_ref in enumerate(outs):
        for q in range(2):
            at = pl.ds((q * len(outs) + k) * slots, slots)
            total = refs[0][at, :].astype(F32)
            for part in refs[1:parts]:
                total = total + part[at, :].astype(F32)
            out_ref[pl.ds(q * slots, slots), :] = total.astype(BF16)


def share_sum_call(order, parts, batch, slots):
    rows, units = parts[0].shape
    shape = (2 * slots, units)
    return order.call(
        functools.partial(share_sum_kernel, len(parts), slots),
        "share_sum",
        parts,
        [whole((rows, units))] * len(parts),
        [(shape, BF16)] * batch,
        [whole(shape)] * batch,
    )


def collect_kernel(places, at_ref, *refs):
    low_ref, first_ref = refs[-2:]
    rank = first_ref.shape[1]
    at = 0
    lows = len(refs) - 2 - len(places)
    for ref in refs[:lows]:
        for k in range(ref.shape[0]):
            low_ref[lax.bitwise_xor(at_ref[1], places[at])] = ref[k]
            at += 1
    for o, ref in zip(places, refs[lows:-2]):
        wide = ref.shape[1]
        for k in range(3):
            first_ref[o, :, pl.ds(k * wide, wide)] = ref[pl.ds(k * rank, rank), :]


def collect_call(order, places, lows, grads, feats):
    groups, (toks, wide) = len(grads), grads[0].shape
    rank = lows[0].shape[1] // 2
    extra = wide - feats
    low_shape, first_shape = (groups, 2 * rank, toks), (groups, rank, 3 * extra)
    return order.call(
        functools.partial(collect_kernel, places),
        "collect_blocks",
        [*lows, *[in_hbm(x) for x in grads]],
        [whole(b.shape) for b in lows]
        + [pl.BlockSpec((toks, extra), lambda i: (0, feats // extra))] * groups,
        [(low_shape, BF16), (first_shape, BF16)],
        [whole(low_shape), whole(first_shape)],
    )


def low_dense_kernel(at_ref, *refs):
    out_ref, sum_ref = refs[-2:]
    groups, both, _ = refs[0].shape
    rank = both // 2
    for o in range(groups):
        total = refs[0][lax.bitwise_xor(at_ref[1], o)].astype(F32)
        for ref in refs[1:-2]:
            total = total + ref[lax.bitwise_xor(at_ref[1], o)].astype(F32)
        for q in range(2):
            at = pl.ds((q * groups + o) * rank, rank)
            sum_ref[at, :] = total[q * rank : (q + 1) * rank]
    out_ref[...] = sum_ref[...].T


def low_dense_call(order, parts):
    groups, both, toks = parts[0].shape
    shape = (toks, groups * both)
    return order.call(
        low_dense_kernel,
        "low_dense",
        parts,
        [whole(parts[0].shape)] * len(parts),
        [(shape, F32)],
        [whole(shape)],
        scratch=[pltpu.VMEM((groups * both, toks), F32)],
    )[0]


def lowrank_hid_kernel(groups, at_ref, index_ref, hid_ref, *rest):
    firsts, out_ref = rest[:2], rest[2]
    top = index_ref.shape[1]
    rank = firsts[0].shape[0] // groups
    wide = jnp.concatenate([dot(hid_ref[...], ref[...], NT) for ref in firsts], axis=1)
    column = pair_column(relative(at_ref, index_ref[...], groups).astype(F32))
    wide = jnp.where(expert_mask(column, wide.shape[1], rank), wide, 0.0)
    out_ref[...] = wide.reshape(wide.shape[0] // top, top, wide.shape[1]).sum(axis=1)


def lowrank_hid_call(order, index, hid, firsts, groups):
    (toks, top), (pairs, units) = index.shape, hid.shape
    half = firsts[0].shape[0]
    steps = 4
    return order.call(
        functools.partial(lowrank_hid_kernel, groups),
        "lowrank_hid",
        [index, in_hbm(hid), *firsts],
        [
            pl.BlockSpec((toks // steps, top), lambda i: (i, 0)),
            pl.BlockSpec((pairs // steps, units), lambda i: (i, 0)),
        ]
        + [whole((half, units))] * 2,
        [((toks, 2 * half), F32)],
        [pl.BlockSpec((toks // steps, 2 * half), lambda i: (i, 0))],
        grid=(steps,),
    )[0]


def second_grad_kernel(places, units, at_ref, got_ref, *refs):
    grads, outs, first_ref = refs[:-3], refs[-3:-1], refs[-1]
    rank, tile = outs[0].shape
    toks = grads[0].shape[0]

    @pl.when(pl.program_id(0) == 0)
    def _():
        total = jnp.zeros((rank, units), F32)
        for source in range(got_ref.shape[0]):
            total = total + got_ref[source, :, pl.ds(0, units)].astype(F32)
        first_ref[...] = total

    totals = [jnp.zeros((rank, tile), F32) for _ in outs]
    for o, grad_ref in zip(places, grads):
        source = lax.bitwise_xor(at_ref[1], o)
        scaled = jnp.concatenate(
            [got_ref[source, :, pl.ds(units + q * toks, toks)] for q in range(2)], axis=0
        )
        value = dot(scaled, grad_ref[...], NN)
        totals = [total + value[q * rank : (q + 1) * rank] for q, total in enumerate(totals)]
    for total, out_ref in zip(totals, outs):
        out_ref[...] = adapter_scale * total


def second_grad_call(order, places, got, grads, units, feats):
    rank, toks = got.shape[1], grads[0].shape[0]
    steps = 4
    tile = feats // steps
    block = pl.BlockSpec((rank, tile), lambda i: (0, i))
    return order.call(
        functools.partial(second_grad_kernel, places, units),
        "second_grad",
        [got, *[in_hbm(x) for x in grads]],
        [whole(got.shape)] + [pl.BlockSpec((toks, tile), lambda i: (0, i))] * len(grads),
        [((rank, feats), F32)] * 2 + [((rank, units), F32)],
        [block] * 2 + [whole((rank, units))],
        grid=(steps,),
    )


def first_grad_kernel(groups, steps, parts, at_ref, index_ref, prob_ref, low_ref, hid_ref, *rest):
    index_all_ref, prob_all_ref, hids = rest[0], rest[1], rest[2 : 2 + parts]
    keep_ref, give_ref, scaled_ref, sum_ref = rest[2 + parts :]
    step = pl.program_id(0)
    top = index_ref.shape[1]
    rank = keep_ref.shape[1]
    low = spread_pairs(low_ref[...], top)
    column = pair_column(relative(at_ref, index_ref[...], groups).astype(F32))
    keep = expert_mask(column, low.shape[1], rank)
    scaled = jnp.where(keep, low * pair_column(prob_ref[...].astype(F32)), 0.0).astype(BF16)
    part = adapter_scale * dot(scaled, hid_ref[...], TN)

    @pl.when(step == 0)
    def _():
        sum_ref[...] = part

    @pl.when(step > 0)
    def _():
        sum_ref[...] += part

    @pl.when(step == steps - 1)
    def _():
        total = hids[0][...]
        for ref in hids[1:]:
            total = total + ref[...]
        toks = total.shape[0]
        place = relative(at_ref, index_all_ref[...], groups)
        prob = prob_all_ref[...].astype(F32)
        expert = iota(total.shape, 1) // rank
        scale = jnp.zeros(total.shape, F32)
        for k in range(top):
            scale = jnp.where(expert == place[:, k : k + 1], prob[:, k : k + 1], scale)
        turned = (total * scale).T.astype(BF16)
        for o in range(groups):
            to = lax.bitwise_xor(at_ref[1], o)
            at, other = o * rank, (groups + o) * rank
            keep_ref[to] = sum_ref[pl.ds(at, rank), :]
            give_ref[to] = sum_ref[pl.ds(other, rank), :].astype(BF16)
            scaled_ref[to, :, pl.ds(0, toks)] = turned[at : at + rank]
            scaled_ref[to, :, pl.ds(toks, toks)] = turned[other : other + rank]


def first_grad_call(order, index, prob, low, hid, hids, groups):
    (toks, top), (pairs, units) = index.shape, hid.shape
    width = low.shape[1]
    steps = 4
    rank = width // groups // 2
    shape, scaled_shape = (groups, rank, units), (groups, rank, 2 * toks)
    return order.call(
        functools.partial(first_grad_kernel, groups, steps, len(hids)),
        "first_grad",
        [index, prob, low, in_hbm(hid), index, prob, *hids],
        [
            pl.BlockSpec((toks // steps, top), lambda i: (i, 0)),
            pl.BlockSpec((toks // steps, top), lambda i: (i, 0)),
            pl.BlockSpec((toks // steps, width), lambda i: (i, 0)),
            pl.BlockSpec((pairs // steps, units), lambda i: (i, 0)),
            whole(index.shape),
            whole(prob.shape),
        ]
        + [whole(x.shape) for x in hids],
        [(shape, F32), (shape, BF16), (scaled_shape, BF16)],
        [whole(shape), whole(shape), whole(scaled_shape)],
        grid=(steps,),
        scratch=[pltpu.VMEM((width, units), F32)],
    )


def first_sum_kernel(at_ref, keep_ref, got_ref, scaled_ref, out_ref):
    units = keep_ref.shape[2]
    out_ref[:, :, pl.ds(0, units)] = (keep_ref[...] + got_ref[...].astype(F32)).astype(BF16)
    out_ref[:, :, pl.ds(units, scaled_ref.shape[2])] = scaled_ref[...]


def first_sum_call(order, keep, got, scaled):
    shape = keep.shape[:2] + (keep.shape[2] + scaled.shape[2],)
    return order.call(
        first_sum_kernel,
        "first_sum",
        [keep, got, scaled],
        [whole(x.shape) for x in (keep, got, scaled)],
        [(shape, BF16)],
        [whole(shape)],
    )[0]


def finish_kernel(count, slots, at_ref, index_all_ref, index_ref, prob_ref, low_ref, hid_ref, *rest):
    firsts, back = rest[:2], rest[2 : 2 + count]
    out_ref, sum_ref, all_ref, place_ref = rest[2 + count :]
    top = index_ref.shape[1]
    toks = index_all_ref.shape[0]
    experts = 2 * count

    @pl.when(pl.program_id(0) == 0)
    def _():
        for o, ref in enumerate(back):
            for q in range(2):
                all_ref[pl.ds((q * count + o) * slots, slots), :] = ref[pl.ds(q * slots, slots), :]
        experts_all = relative(at_ref, index_all_ref[...], count)
        hit = jnp.zeros((toks, experts), F32)
        for k in range(top):
            hit = jnp.where(iota((toks, experts), 1) == experts_all[:, k : k + 1], 1.0, hit)
        before = jnp.where(iota((toks, toks), 0) > iota((toks, toks), 1), 1.0, 0.0).astype(BF16)
        place_ref[...] = dot(before, hit.astype(BF16), NN)

    pairs = hid_ref.shape[0]
    some = index_ref.shape[0]
    column = pair_column(relative(at_ref, index_ref[...], count).astype(F32))
    place = spread_pairs(place_ref[pl.ds(pl.program_id(0) * some, some), :], top)
    mine = iota((pairs, experts), 1) == column.astype(jnp.int32)
    target = column * slots + jnp.sum(jnp.where(mine, place, 0.0), axis=1, keepdims=True)
    low = spread_pairs(low_ref[...], top)
    keep = expert_mask(column, low.shape[1], low.shape[1] // experts)
    low = jnp.where(keep, adapter_scale * low.astype(BF16).astype(F32), 0.0).astype(BF16)
    slot = iota((pairs, experts * slots), 1)
    pick = jnp.where(slot == target.astype(jnp.int32), 1.0, 0.0).astype(BF16)
    half = low.shape[1] // 2
    value = dot(pick, all_ref[...], NN)
    value = value + dot(low[:, :half], firsts[0][...], NN) + dot(low[:, half:], firsts[1][...], NN)
    value = value.astype(BF16).astype(F32)
    out_ref[...] = (value * pair_column(prob_ref[...].astype(F32))).astype(BF16)
    sums = jnp.sum(value * hid_ref[...].astype(F32), axis=1, keepdims=True)
    sums = jnp.where(diagonal(pairs, top), sums, 0.0)
    sum_ref[...] = sums.reshape(some, top, top).sum(axis=1)


def finish_call(order, index, prob, low, hid, firsts, back):
    (toks, top), (pairs, units) = index.shape, hid.shape
    width = low.shape[1]
    both = back[0].shape[0]
    steps = 4
    count = len(back)

    def rows(n, columns):
        return pl.BlockSpec((n // steps, columns), lambda i: (i, 0))

    return order.call(
        functools.partial(finish_kernel, count, both // 2),
        "finish",
        [index, index, prob, low, in_hbm(hid), *firsts, *[in_hbm(x) for x in back]],
        [whole(index.shape), rows(toks, top), rows(toks, top), rows(toks, width), rows(pairs, units)]
        + [whole(firsts[0].shape)] * 2
        + [whole((both, units))] * count,
        [((pairs, units), BF16), ((toks, top), F32)],
        [rows(pairs, units), rows(toks, top)],
        grid=(steps,),
        cost=LONG,
        scratch=[pltpu.VMEM((count * both, units), BF16), pltpu.VMEM((toks, 2 * count), F32)],
    )


def body(grad, hidden, index, weight, down, first, second):
    toks, top = index.shape
    exp_local, units_all, feats = down.shape
    units, rank = first.shape[1:]
    groups, cores, shares = lax.axis_size("ep"), lax.axis_size("sub"), lax.axis_size("rep")
    assert exp_local == 1 and cores == 2 and groups & (groups - 1) == 0
    cap = min(toks, 5 * toks * top // (4 * groups * cores))
    slots = -(-cap // 16) * 16
    pairs = toks * top
    at = jnp.stack([lax.axis_index(name).astype(jnp.int32) for name in ("rep", "ep", "sub")])
    order = Order(at)

    def turn(x, offset):
        return lax.ppermute(x, "rep", [(r, (r + offset) % shares) for r in range(shares)])

    def all_shares(x):
        return [x] + [turn(x, k) for k in range(1, shares)]

    def flip(x, mask):
        return lax.ppermute(x, "ep", [(i, i ^ mask) for i in range(groups)])

    def swap(x):
        return lax.ppermute(x, "sub", [(0, 1), (1, 0)])

    where = ("ep", "sub")

    def exchange(x, axes="ep"):
        return lax.all_to_all(x, axes, split_axis=0, concat_axis=0, tiled=True)

    blocks = {0: pack_call(order, grad, first[0].T, index.T)}

    def fetch(o):
        if o not in blocks:
            last = o & -o
            blocks[o] = flip(fetch(o ^ last), last)
        return blocks[o]

    own_down = load_call(order, down[0])
    downs = [own_down, swap(down[0])]
    seconds = [second[0], swap(second[0])]

    if groups == 8:
        batches = [(0, 1), (2, 4), (6, 3), (5, 7)]
        steps = [("multiply", 0), ("gate", 4), ("multiply", 1), ("total", 0), ("total", 1)]
        steps += [("multiply", 2), ("multiply", 3), ("total", 2)]
        early = {("total", 0): 3, ("multiply", 2): 5}
    else:
        batches = [(o, o + 1) for o in range(0, groups, 2)]
        steps = [("multiply", 0)]
        for i in range(1, len(batches)):
            steps += [("multiply", i), ("total", i - 1)]
        early = {}
    last = len(batches) - 1
    places = [o for batch in batches for o in batch]
    back, lows, shared = {}, [], {}

    def arrived(i):
        order.wait([back[o] for o in batches[i] if o])

    def total(i):
        for o, rows in zip(batches[i], share_sum_call(order, shared[i], 2, slots)):
            masks = [o] if o else []
            if i >= last - 1 and o % 2:
                masks = [1 << k for k in range(o.bit_length()) if o >> k & 1]
            for mask in masks:
                rows = flip(rows, mask)
            back[o] = rows

    for kind, i in steps:
        if (kind, i) in early:
            order.wait([fetch(early[kind, i])])
        if kind == "gate":
            blocks[i] = gate_call(order, [fetch(i)])[0]
        elif kind == "total":
            total(i)
        else:
            if i == last and last > 2:
                for j in range(i - 1):
                    arrived(j)
            *give, keep, low = expert_rows_call(
                order, [fetch(o) for o in batches[i]], seconds, downs, shares, slots
            )
            lows.append(low)
            shared[i] = [keep] + [turn(x, k + 1) for k, x in enumerate(give)]

    hid = hidden.reshape(pairs, units)
    grads = [blocks[o] for o in places]

    low_grad, first_own = collect_call(order, places, lows, grads, feats)
    firsts = [x.reshape(groups * rank, units) for x in (first_own, swap(first_own))]
    low_grad = exchange(low_grad)
    low_hid = all_shares(lowrank_hid_call(order, index, hid, firsts, groups))
    order.wait([back[batches[-2][0]], low_grad])
    total(last)

    low_grad = low_dense_call(order, all_shares(low_grad))
    order.wait([back[batches[-1][0]]])
    keep, give, scaled = first_grad_call(order, index, weight, low_grad, hid, low_hid, groups)

    order.wait([back[batches[-2][1]], back[batches[-1][1]]])
    got = exchange(first_sum_call(order, keep, swap(give), scaled))
    back = [back[o] for o in range(groups)]
    grad_hidden, sums = finish_call(order, index, weight, low_grad, hid, firsts, back)
    if shares == 2:
        other_sums = turn(sums, 1)
        order.wait([other_sums])
        sums = sums + other_sums
    else:
        sums = lax.psum(sums, "rep")
    second_keep, second_give, first_grad = second_grad_call(
        order, places, got, grads, units, feats
    )
    second_grad = second_keep + swap(second_give)
    return (
        grad_hidden.reshape(toks, top, units),
        sums,
        first_grad.T[None],
        second_grad[None],
    )


def solution(mesh):
    return jax.shard_map(
        body,
        mesh=mesh,
        in_specs=(
            P(("grp", "ep", "sub"), "rep"),
            P(("grp", "ep", "sub"), None, "rep"),
            P(("grp", "ep", "sub"), None),
            P(("grp", "ep", "sub"), None),
            P(("ep", "sub"), None, "rep"),
            P(("grp", "ep", "sub"), "rep", None),
            P(("grp", "ep", "sub"), None, "rep"),
        ),
        out_specs=(
            P(("grp", "ep", "sub"), None, "rep"),
            P(("grp", "ep", "sub"), None),
            P(("grp", "ep", "sub"), "rep", None),
            P(("grp", "ep", "sub"), None, "rep"),
        ),
        check_vma=False,
    )
```

```python
import functools

import jax
import jax.numpy as jnp
from jax import lax
from jax.experimental import pallas as pl
from jax.experimental.pallas import tpu as pltpu
from jax.sharding import PartitionSpec as P

adapter_scale = 2.0
BF16 = jnp.bfloat16
F32 = jnp.float32
NT = (((1,), (1,)), ((), ()))
TN = (((0,), (0,)), ((), ()))
NN = (((1,), (0,)), ((), ()))
SMALL = pl.CostEstimate(flops=1, bytes_accessed=1, transcendentals=0)
LONG = pl.CostEstimate(flops=1, bytes_accessed=2 * 10**7, transcendentals=0)
ANY = pl.BlockSpec(memory_space=pl.ANY)
SMEM = pl.BlockSpec(memory_space=pltpu.SMEM)
VMEM = pl.BlockSpec(memory_space=pltpu.VMEM)


def dot(a, b, dims):
    return lax.dot_general(a, b, dims, preferred_element_type=F32)


def iota(shape, axis):
    return lax.broadcasted_iota(jnp.int32, shape, axis)


def whole(shape):
    return pl.BlockSpec(shape, lambda *_: (0,) * len(shape))


def in_hbm(x):
    return pltpu.with_memory_space_constraint(x, pltpu.HBM)


class Order:
    def __init__(self, at):
        self.at, self.last = at, []

    def wait(self, arrays):
        self.last = self.last + list(arrays)

    def call(self, kernel, name, arrays, in_specs, outs, out_specs, grid=(1,), scratch=(), mib=16, cost=SMALL, **more):
        count, last = 1 + len(arrays), len(self.last)

        def ordered(*refs):
            here = count + last + len(outs)
            kernel(*refs[:count], *refs[count + last : here], *refs[here + 1 :])

        *result, token = pl.pallas_call(
            ordered,
            grid=grid,
            in_specs=[SMEM, *in_specs] + [ANY] * last,
            out_specs=[*out_specs, ANY],
            scratch_shapes=scratch,
            out_shape=[jax.ShapeDtypeStruct(*o) if isinstance(o, tuple) else o for o in outs]
            + [pltpu.HBM((8, 128), F32)],
            compiler_params=pltpu.CompilerParams(vmem_limit_bytes=mib * 2**20),
            cost_estimate=cost,
            name=name,
            **more,
        )(self.at, *arrays, *self.last)
        self.last = [in_hbm(token)]
        return result


def relative(at_ref, index, groups):
    o = lax.bitwise_xor(lax.shift_right_logical(index, 1), at_ref[1])
    q = lax.bitwise_xor(lax.bitwise_and(index, 1), at_ref[2])
    return q * groups + o


def spread_pairs(dense, top):
    toks, width = dense.shape
    return jnp.broadcast_to(dense[:, None, :], (toks, top, width)).reshape(toks * top, width)


def diagonal(pairs, top):
    return iota((pairs, top), 1) == lax.bitwise_and(iota((pairs, top), 0), top - 1)


def pair_column(table):
    toks, top = table.shape
    wide = spread_pairs(table, top)
    return jnp.sum(jnp.where(diagonal(toks * top, top), wide, 0.0), axis=1, keepdims=True)


def expert_mask(column, width, rank):
    return iota((column.shape[0], width), 1) // rank == column.astype(jnp.int32)


def pack_kernel(at_ref, grad_ref, first_ref, index_ref, out_ref):
    toks, feats = grad_ref.shape
    rank = first_ref.shape[0]
    extra = out_ref.shape[1] - feats
    out_ref[:, pl.ds(0, feats)] = grad_ref[...]
    for k in range(3):
        piece = first_ref[:, pl.ds(k * extra, extra)]
        out_ref[pl.ds(k * rank, rank), pl.ds(feats, extra)] = piece
    top = index_ref.shape[0]
    out_ref[pl.ds(3 * rank, toks - 3 * rank), pl.ds(feats, extra)] = jnp.full(
        (toks - 3 * rank, extra), -1.0, BF16
    )
    routes = index_ref[...].astype(F32)
    routes = jnp.concatenate([routes, jnp.full((16 - top, toks), -1.0, F32)], axis=0)
    out_ref[pl.ds(3 * rank, 16), pl.ds(feats, toks)] = routes.astype(BF16)


def pack_call(order, grad, first, index):
    (toks, feats), (rank, units) = grad.shape, first.shape
    shape = (toks, feats + units // 3)
    return order.call(
        pack_kernel,
        "pack_block",
        [in_hbm(grad), first, index],
        [whole(grad.shape), whole(first.shape), whole(index.shape)],
        [(shape, BF16)],
        [whole(shape)],
    )[0]


def gate_kernel(at_ref, *refs):
    pass


def gate_call(order, arrays):
    return order.call(
        gate_kernel,
        "gate",
        arrays,
        [ANY] * len(arrays),
        [(x.shape, x.dtype) for x in arrays],
        [ANY] * len(arrays),
        input_output_aliases={1 + k: k for k in range(len(arrays))},
    )


def load_kernel(at_ref, down_ref, out_ref, sems):
    parts = sems.shape[0]
    rows = down_ref.shape[0] // parts
    copies = [
        pltpu.make_async_copy(
            down_ref.at[pl.ds(k * rows, rows), :], out_ref.at[pl.ds(k * rows, rows), :], sems.at[k]
        )
        for k in range(parts)
    ]
    for copy in copies:
        copy.start()
    for copy in copies:
        copy.wait()


def load_call(order, down):
    return order.call(
        load_kernel,
        "load_matrix",
        [in_hbm(down)],
        [ANY],
        [pltpu.VMEM(down.shape, down.dtype)],
        [VMEM],
        grid=(),
        scratch=[pltpu.SemaphoreType.DMA((4,))],
    )[0]


def expert_rows_kernel(slots, tiles, shares, batch, route_row, at_ref, *rest):
    grads, seconds, downs = rest[:batch], rest[batch : batch + 2], rest[batch + 2 : batch + 4]
    *outs, low_ref = rest[batch + 4 : batch + 5 + shares]
    block_ref, turned_ref, block_sems = rest[batch + 5 + shares :]
    tile = downs[0].shape[0] // shares // tiles
    feats = turned_ref.shape[1]
    toks = block_ref.shape[1]
    blocks = [
        pltpu.make_async_copy(ref, block_ref.at[k], block_sems.at[k]) for k, ref in enumerate(grads)
    ]
    for copy in blocks:
        copy.start()

    before = jnp.where(iota((toks, toks), 0) < iota((toks, toks), 1), 1.0, 0.0).astype(BF16)
    columns = turned_ref.shape[2]
    slot = iota((columns, batch * toks), 0).astype(F32)
    second = jnp.concatenate([ref[...] for ref in seconds], axis=0)
    routes = []
    for k in range(batch):
        blocks[k].wait()
        routes.append(block_ref[k, pl.ds(route_row, 16), pl.ds(feats, toks)].astype(F32))
    grad = block_ref[:, :, pl.ds(0, feats)].reshape(batch * toks, feats)
    for q in range(2):
        expert = at_ref[1] * 2 + lax.bitwise_xor(at_ref[2], q)
        targets = []
        for k in range(batch):
            hits = jnp.where(routes[k] == expert.astype(F32), 1.0, 0.0)
            mine = jnp.max(hits, axis=0, keepdims=True)
            pos = dot(jnp.broadcast_to(mine, (16, toks)).astype(BF16), before, NN)[:1]
            targets.append(jnp.where(mine > 0.0, pos + float(k * slots), -1.0))
        pick = jnp.where(slot == jnp.concatenate(targets, axis=1), 1.0, 0.0)
        turned_ref[q] = dot(grad, pick.T.astype(BF16), TN).astype(BF16)
    low = dot(second, grad, NT).astype(BF16)
    for k in range(batch):
        low_ref[k] = low[:, k * toks : (k + 1) * toks]

    rows = batch * slots
    for k in range(shares):
        share = lax.rem(at_ref[0] + k + 1, shares)
        for q in range(2):
            for t in range(tiles):
                row = pl.multiple_of((share * tiles + t) * tile, tile)
                value = dot(downs[q][pl.ds(row, tile), :], turned_ref[q], NN)
                outs[k][pl.ds(q * rows, rows), pl.ds(t * tile, tile)] = value.T[:rows].astype(BF16)


def expert_rows_call(order, grads, seconds, downs, shares, slots):
    batch, (toks, wide) = len(grads), grads[0].shape
    rank, feats = seconds[0].shape
    units = downs[0].shape[0] // shares
    rows = 2 * batch * slots
    return order.call(
        functools.partial(expert_rows_kernel, slots, 3, shares, batch, 3 * rank),
        "expert_rows",
        [*grads, *seconds, *[pltpu.with_memory_space_constraint(x, pltpu.VMEM) for x in downs]],
        [ANY] * batch + [VMEM] * 4,
        [((rows, units), BF16)] * shares + [((batch, 2 * rank, toks), BF16)],
        [VMEM] * (shares + 1),
        grid=(),
        scratch=[
            pltpu.VMEM((batch, toks, wide), BF16),
            pltpu.VMEM((2, feats, -(-batch * slots // 128) * 128), BF16),
            pltpu.SemaphoreType.DMA((batch,)),
        ],
    )


def share_sum_kernel(parts, slots, at_ref, *refs):
    outs = refs[parts:]
    for k, out_ref in enumerate(outs):
        for q in range(2):
            at = pl.ds((q * len(outs) + k) * slots, slots)
            total = refs[0][at, :].astype(F32)
            for part in refs[1:parts]:
                total = total + part[at, :].astype(F32)
            out_ref[pl.ds(q * slots, slots), :] = total.astype(BF16)


def share_sum_call(order, parts, batch, slots):
    rows, units = parts[0].shape
    shape = (2 * slots, units)
    return order.call(
        functools.partial(share_sum_kernel, len(parts), slots),
        "share_sum",
        parts,
        [whole((rows, units))] * len(parts),
        [(shape, BF16)] * batch,
        [whole(shape)] * batch,
    )


def collect_kernel(places, at_ref, *refs):
    low_ref, first_ref = refs[-2:]
    rank = first_ref.shape[1]
    at = 0
    lows = len(refs) - 2 - len(places)
    for ref in refs[:lows]:
        for k in range(ref.shape[0]):
            low_ref[lax.bitwise_xor(at_ref[1], places[at])] = ref[k]
            at += 1
    for o, ref in zip(places, refs[lows:-2]):
        wide = ref.shape[1]
        for k in range(3):
            first_ref[o, :, pl.ds(k * wide, wide)] = ref[pl.ds(k * rank, rank), :]


def collect_call(order, places, lows, grads, feats):
    groups, (toks, wide) = len(grads), grads[0].shape
    rank = lows[0].shape[1] // 2
    extra = wide - feats
    low_shape, first_shape = (groups, 2 * rank, toks), (groups, rank, 3 * extra)
    return order.call(
        functools.partial(collect_kernel, places),
        "collect_blocks",
        [*lows, *[in_hbm(x) for x in grads]],
        [whole(b.shape) for b in lows]
        + [pl.BlockSpec((toks, extra), lambda i: (0, feats // extra))] * groups,
        [(low_shape, BF16), (first_shape, BF16)],
        [whole(low_shape), whole(first_shape)],
    )


def low_dense_kernel(at_ref, *refs):
    out_ref, sum_ref = refs[-2:]
    groups, both, _ = refs[0].shape
    rank = both // 2
    for o in range(groups):
        total = refs[0][lax.bitwise_xor(at_ref[1], o)].astype(F32)
        for ref in refs[1:-2]:
            total = total + ref[lax.bitwise_xor(at_ref[1], o)].astype(F32)
        for q in range(2):
            at = pl.ds((q * groups + o) * rank, rank)
            sum_ref[at, :] = total[q * rank : (q + 1) * rank]
    out_ref[...] = sum_ref[...].T


def low_dense_call(order, parts):
    groups, both, toks = parts[0].shape
    shape = (toks, groups * both)
    return order.call(
        low_dense_kernel,
        "low_dense",
        parts,
        [whole(parts[0].shape)] * len(parts),
        [(shape, F32)],
        [whole(shape)],
        scratch=[pltpu.VMEM((groups * both, toks), F32)],
    )[0]


def lowrank_hid_kernel(groups, at_ref, index_ref, hid_ref, *rest):
    firsts, out_ref = rest[:2], rest[2]
    top = index_ref.shape[1]
    rank = firsts[0].shape[0] // groups
    wide = jnp.concatenate([dot(hid_ref[...], ref[...], NT) for ref in firsts], axis=1)
    column = pair_column(relative(at_ref, index_ref[...], groups).astype(F32))
    wide = jnp.where(expert_mask(column, wide.shape[1], rank), wide, 0.0)
    out_ref[...] = wide.reshape(wide.shape[0] // top, top, wide.shape[1]).sum(axis=1)


def lowrank_hid_call(order, index, hid, firsts, groups):
    (toks, top), (pairs, units) = index.shape, hid.shape
    half = firsts[0].shape[0]
    steps = 4
    return order.call(
        functools.partial(lowrank_hid_kernel, groups),
        "lowrank_hid",
        [index, in_hbm(hid), *firsts],
        [
            pl.BlockSpec((toks // steps, top), lambda i: (i, 0)),
            pl.BlockSpec((pairs // steps, units), lambda i: (i, 0)),
        ]
        + [whole((half, units))] * 2,
        [((toks, 2 * half), F32)],
        [pl.BlockSpec((toks // steps, 2 * half), lambda i: (i, 0))],
        grid=(steps,),
    )[0]


def second_grad_kernel(places, units, at_ref, got_ref, *refs):
    grads, outs, first_ref = refs[:-3], refs[-3:-1], refs[-1]
    rank, tile = outs[0].shape
    toks = grads[0].shape[0]

    @pl.when(pl.program_id(0) == 0)
    def _():
        total = jnp.zeros((rank, units), F32)
        for source in range(got_ref.shape[0]):
            total = total + got_ref[source, :, pl.ds(0, units)].astype(F32)
        first_ref[...] = total

    totals = [jnp.zeros((rank, tile), F32) for _ in outs]
    for o, grad_ref in zip(places, grads):
        source = lax.bitwise_xor(at_ref[1], o)
        scaled = jnp.concatenate(
            [got_ref[source, :, pl.ds(units + q * toks, toks)] for q in range(2)], axis=0
        )
        value = dot(scaled, grad_ref[...], NN)
        totals = [total + value[q * rank : (q + 1) * rank] for q, total in enumerate(totals)]
    for total, out_ref in zip(totals, outs):
        out_ref[...] = adapter_scale * total


def second_grad_call(order, places, got, grads, units, feats):
    rank, toks = got.shape[1], grads[0].shape[0]
    steps = 4
    tile = feats // steps
    block = pl.BlockSpec((rank, tile), lambda i: (0, i))
    return order.call(
        functools.partial(second_grad_kernel, places, units),
        "second_grad",
        [got, *[in_hbm(x) for x in grads]],
        [whole(got.shape)] + [pl.BlockSpec((toks, tile), lambda i: (0, i))] * len(grads),
        [((rank, feats), F32)] * 2 + [((rank, units), F32)],
        [block] * 2 + [whole((rank, units))],
        grid=(steps,),
    )


def first_grad_kernel(groups, steps, parts, at_ref, index_ref, prob_ref, low_ref, hid_ref, *rest):
    index_all_ref, prob_all_ref, hids = rest[0], rest[1], rest[2 : 2 + parts]
    keep_ref, give_ref, scaled_ref, sum_ref = rest[2 + parts :]
    step = pl.program_id(0)
    top = index_ref.shape[1]
    rank = keep_ref.shape[1]
    low = spread_pairs(low_ref[...], top)
    column = pair_column(relative(at_ref, index_ref[...], groups).astype(F32))
    keep = expert_mask(column, low.shape[1], rank)
    scaled = jnp.where(keep, low * pair_column(prob_ref[...].astype(F32)), 0.0).astype(BF16)
    part = adapter_scale * dot(scaled, hid_ref[...], TN)

    @pl.when(step == 0)
    def _():
        sum_ref[...] = part

    @pl.when(step > 0)
    def _():
        sum_ref[...] += part

    @pl.when(step == steps - 1)
    def _():
        total = hids[0][...]
        for ref in hids[1:]:
            total = total + ref[...]
        toks = total.shape[0]
        place = relative(at_ref, index_all_ref[...], groups)
        prob = prob_all_ref[...].astype(F32)
        expert = iota(total.shape, 1) // rank
        scale = jnp.zeros(total.shape, F32)
        for k in range(top):
            scale = jnp.where(expert == place[:, k : k + 1], prob[:, k : k + 1], scale)
        turned = (total * scale).T.astype(BF16)
        for o in range(groups):
            to = lax.bitwise_xor(at_ref[1], o)
            at, other = o * rank, (groups + o) * rank
            keep_ref[to] = sum_ref[pl.ds(at, rank), :]
            give_ref[to] = sum_ref[pl.ds(other, rank), :].astype(BF16)
            scaled_ref[to, :, pl.ds(0, toks)] = turned[at : at + rank]
            scaled_ref[to, :, pl.ds(toks, toks)] = turned[other : other + rank]


def first_grad_call(order, index, prob, low, hid, hids, groups):
    (toks, top), (pairs, units) = index.shape, hid.shape
    width = low.shape[1]
    steps = 4
    rank = width // groups // 2
    shape, scaled_shape = (groups, rank, units), (groups, rank, 2 * toks)
    return order.call(
        functools.partial(first_grad_kernel, groups, steps, len(hids)),
        "first_grad",
        [index, prob, low, in_hbm(hid), index, prob, *hids],
        [
            pl.BlockSpec((toks // steps, top), lambda i: (i, 0)),
            pl.BlockSpec((toks // steps, top), lambda i: (i, 0)),
            pl.BlockSpec((toks // steps, width), lambda i: (i, 0)),
            pl.BlockSpec((pairs // steps, units), lambda i: (i, 0)),
            whole(index.shape),
            whole(prob.shape),
        ]
        + [whole(x.shape) for x in hids],
        [(shape, F32), (shape, BF16), (scaled_shape, BF16)],
        [whole(shape), whole(shape), whole(scaled_shape)],
        grid=(steps,),
        scratch=[pltpu.VMEM((width, units), F32)],
    )


def first_sum_kernel(at_ref, keep_ref, got_ref, scaled_ref, out_ref):
    units = keep_ref.shape[2]
    out_ref[:, :, pl.ds(0, units)] = (keep_ref[...] + got_ref[...].astype(F32)).astype(BF16)
    out_ref[:, :, pl.ds(units, scaled_ref.shape[2])] = scaled_ref[...]


def first_sum_call(order, keep, got, scaled):
    shape = keep.shape[:2] + (keep.shape[2] + scaled.shape[2],)
    return order.call(
        first_sum_kernel,
        "first_sum",
        [keep, got, scaled],
        [whole(x.shape) for x in (keep, got, scaled)],
        [(shape, BF16)],
        [whole(shape)],
    )[0]


def finish_kernel(count, slots, at_ref, index_all_ref, index_ref, prob_ref, low_ref, hid_ref, *rest):
    firsts, back = rest[:2], rest[2 : 2 + count]
    out_ref, sum_ref, all_ref, place_ref = rest[2 + count :]
    top = index_ref.shape[1]
    toks = index_all_ref.shape[0]
    experts = 2 * count

    @pl.when(pl.program_id(0) == 0)
    def _():
        for o, ref in enumerate(back):
            for q in range(2):
                all_ref[pl.ds((q * count + o) * slots, slots), :] = ref[pl.ds(q * slots, slots), :]
        experts_all = relative(at_ref, index_all_ref[...], count)
        hit = jnp.zeros((toks, experts), F32)
        for k in range(top):
            hit = jnp.where(iota((toks, experts), 1) == experts_all[:, k : k + 1], 1.0, hit)
        before = jnp.where(iota((toks, toks), 0) > iota((toks, toks), 1), 1.0, 0.0).astype(BF16)
        place_ref[...] = dot(before, hit.astype(BF16), NN)

    pairs = hid_ref.shape[0]
    some = index_ref.shape[0]
    column = pair_column(relative(at_ref, index_ref[...], count).astype(F32))
    place = spread_pairs(place_ref[pl.ds(pl.program_id(0) * some, some), :], top)
    mine = iota((pairs, experts), 1) == column.astype(jnp.int32)
    target = column * slots + jnp.sum(jnp.where(mine, place, 0.0), axis=1, keepdims=True)
    low = spread_pairs(low_ref[...], top)
    keep = expert_mask(column, low.shape[1], low.shape[1] // experts)
    low = jnp.where(keep, adapter_scale * low.astype(BF16).astype(F32), 0.0).astype(BF16)
    slot = iota((pairs, experts * slots), 1)
    pick = jnp.where(slot == target.astype(jnp.int32), 1.0, 0.0).astype(BF16)
    half = low.shape[1] // 2
    value = dot(pick, all_ref[...], NN)
    value = value + dot(low[:, :half], firsts[0][...], NN) + dot(low[:, half:], firsts[1][...], NN)
    value = value.astype(BF16).astype(F32)
    out_ref[...] = (value * pair_column(prob_ref[...].astype(F32))).astype(BF16)
    sums = jnp.sum(value * hid_ref[...].astype(F32), axis=1, keepdims=True)
    sums = jnp.where(diagonal(pairs, top), sums, 0.0)
    sum_ref[...] = sums.reshape(some, top, top).sum(axis=1)


def finish_call(order, index, prob, low, hid, firsts, back):
    (toks, top), (pairs, units) = index.shape, hid.shape
    width = low.shape[1]
    both = back[0].shape[0]
    steps = 4
    count = len(back)

    def rows(n, columns):
        return pl.BlockSpec((n // steps, columns), lambda i: (i, 0))

    return order.call(
        functools.partial(finish_kernel, count, both // 2),
        "finish",
        [index, index, prob, low, in_hbm(hid), *firsts, *[in_hbm(x) for x in back]],
        [whole(index.shape), rows(toks, top), rows(toks, top), rows(toks, width), rows(pairs, units)]
        + [whole(firsts[0].shape)] * 2
        + [whole((both, units))] * count,
        [((pairs, units), BF16), ((toks, top), F32)],
        [rows(pairs, units), rows(toks, top)],
        grid=(steps,),
        cost=LONG,
        scratch=[pltpu.VMEM((count * both, units), BF16), pltpu.VMEM((toks, 2 * count), F32)],
    )


def body(grad, hidden, index, weight, down, first, second):
    toks, top = index.shape
    exp_local, units_all, feats = down.shape
    units, rank = first.shape[1:]
    groups, cores, shares = lax.axis_size("ep"), lax.axis_size("sub"), lax.axis_size("rep")
    assert exp_local == 1 and cores == 2 and groups & (groups - 1) == 0
    cap = min(toks, 5 * toks * top // (4 * groups * cores))
    slots = -(-cap // 16) * 16
    pairs = toks * top
    at = jnp.stack([lax.axis_index(name).astype(jnp.int32) for name in ("rep", "ep", "sub")])
    order = Order(at)

    def turn(x, offset):
        return lax.ppermute(x, "rep", [(r, (r + offset) % shares) for r in range(shares)])

    def all_shares(x):
        return [x] + [turn(x, k) for k in range(1, shares)]

    def flip(x, mask):
        return lax.ppermute(x, "ep", [(i, i ^ mask) for i in range(groups)])

    def swap(x):
        return lax.ppermute(x, "sub", [(0, 1), (1, 0)])

    where = ("ep", "sub")

    def exchange(x, axes="ep"):
        return lax.all_to_all(x, axes, split_axis=0, concat_axis=0, tiled=True)

    blocks = {0: pack_call(order, grad, first[0].T, index.T)}

    def fetch(o):
        if o not in blocks:
            last = o & -o
            blocks[o] = flip(fetch(o ^ last), last)
        return blocks[o]

    own_down = load_call(order, down[0])
    downs = [own_down, swap(down[0])]
    seconds = [second[0], swap(second[0])]

    if groups == 8:
        batches = [(0, 1), (2, 4), (6, 3), (5, 7)]
        steps = [("multiply", 0), ("gate", 4), ("multiply", 1), ("total", 0), ("total", 1)]
        steps += [("multiply", 2), ("multiply", 3), ("total", 2)]
        early = {("total", 0): 3, ("multiply", 2): 5}
    else:
        batches = [(o, o + 1) for o in range(0, groups, 2)]
        steps = [("multiply", 0)]
        for i in range(1, len(batches)):
            steps += [("multiply", i), ("total", i - 1)]
        early = {}
    last = len(batches) - 1
    places = [o for batch in batches for o in batch]
    back, lows, shared = {}, [], {}

    def total(i):
        for o, rows in zip(batches[i], share_sum_call(order, shared[i], 2, slots)):
            masks = [o] if o else []
            if i >= last - 1 and o % 2:
                masks = [1 << k for k in range(o.bit_length()) if o >> k & 1]
            elif o == 4 and groups == 8:
                masks = [2, 6]
            for mask in masks:
                rows = flip(rows, mask)
            back[o] = rows

    for kind, i in steps:
        if (kind, i) in early:
            order.wait([fetch(early[kind, i])])
        if kind == "gate":
            blocks[i] = gate_call(order, [fetch(i)])[0]
        elif kind == "total":
            total(i)
        else:
            if i == last and groups == 8:
                order.wait([back[4]])
            *give, keep, low = expert_rows_call(
                order, [fetch(o) for o in batches[i]], seconds, downs, shares, slots
            )
            lows.append(low)
            shared[i] = [keep] + [turn(x, k + 1) for k, x in enumerate(give)]

    hid = hidden.reshape(pairs, units)
    grads = [blocks[o] for o in places]

    low_grad, first_own = collect_call(order, places, lows, grads, feats)
    firsts = [x.reshape(groups * rank, units) for x in (first_own, swap(first_own))]
    low_grad = exchange(low_grad)
    order.wait([back[batches[-2][0]], back[1], back[2]])
    total(last)
    order.wait([low_grad])
    low_hid = all_shares(lowrank_hid_call(order, index, hid, firsts, groups))
    order.wait([back[batches[-2][1]]])

    low_grad = low_dense_call(order, all_shares(low_grad))
    order.wait([back[batches[-1][0]]])
    keep, give, scaled = first_grad_call(order, index, weight, low_grad, hid, low_hid, groups)

    order.wait([back[batches[-1][1]]])
    got = exchange(first_sum_call(order, keep, swap(give), scaled))
    back = [back[o] for o in range(groups)]
    grad_hidden, sums = finish_call(order, index, weight, low_grad, hid, firsts, back)
    if shares == 2:
        other_sums = turn(sums, 1)
        order.wait([other_sums])
        sums = sums + other_sums
    else:
        sums = lax.psum(sums, "rep")
    second_keep, second_give, first_grad = second_grad_call(
        order, places, got, grads, units, feats
    )
    second_grad = second_keep + swap(second_give)
    return (
        grad_hidden.reshape(toks, top, units),
        sums,
        first_grad.T[None],
        second_grad[None],
    )


def solution(mesh):
    return jax.shard_map(
        body,
        mesh=mesh,
        in_specs=(
            P(("grp", "ep", "sub"), "rep"),
            P(("grp", "ep", "sub"), None, "rep"),
            P(("grp", "ep", "sub"), None),
            P(("grp", "ep", "sub"), None),
            P(("ep", "sub"), None, "rep"),
            P(("grp", "ep", "sub"), "rep", None),
            P(("grp", "ep", "sub"), None, "rep"),
        ),
        out_specs=(
            P(("grp", "ep", "sub"), None, "rep"),
            P(("grp", "ep", "sub"), None),
            P(("grp", "ep", "sub"), "rep", None),
            P(("grp", "ep", "sub"), None, "rep"),
        ),
        check_vma=False,
    )
```

```python
import functools

import jax
import jax.numpy as jnp
from jax import lax
from jax.experimental import pallas as pl
from jax.experimental.pallas import tpu as pltpu
from jax.sharding import PartitionSpec as P

adapter_scale = 2.0
BF16 = jnp.bfloat16
F32 = jnp.float32
NT = (((1,), (1,)), ((), ()))
TN = (((0,), (0,)), ((), ()))
NN = (((1,), (0,)), ((), ()))
SMALL = pl.CostEstimate(flops=1, bytes_accessed=1, transcendentals=0)
LONG = pl.CostEstimate(flops=1, bytes_accessed=2 * 10**7, transcendentals=0)
ANY = pl.BlockSpec(memory_space=pl.ANY)
SMEM = pl.BlockSpec(memory_space=pltpu.SMEM)
VMEM = pl.BlockSpec(memory_space=pltpu.VMEM)


def dot(a, b, dims):
    return lax.dot_general(a, b, dims, preferred_element_type=F32)


def iota(shape, axis):
    return lax.broadcasted_iota(jnp.int32, shape, axis)


def whole(shape):
    return pl.BlockSpec(shape, lambda *_: (0,) * len(shape))


def in_hbm(x):
    return pltpu.with_memory_space_constraint(x, pltpu.HBM)


class Order:
    def __init__(self, at):
        self.at, self.last = at, []

    def wait(self, arrays):
        self.last = self.last + list(arrays)

    def call(self, kernel, name, arrays, in_specs, outs, out_specs, grid=(1,), scratch=(), mib=16, cost=SMALL, **more):
        count, last = 1 + len(arrays), len(self.last)

        def ordered(*refs):
            here = count + last + len(outs)
            kernel(*refs[:count], *refs[count + last : here], *refs[here + 1 :])

        *result, token = pl.pallas_call(
            ordered,
            grid=grid,
            in_specs=[SMEM, *in_specs] + [ANY] * last,
            out_specs=[*out_specs, ANY],
            scratch_shapes=scratch,
            out_shape=[jax.ShapeDtypeStruct(*o) if isinstance(o, tuple) else o for o in outs]
            + [pltpu.HBM((8, 128), F32)],
            compiler_params=pltpu.CompilerParams(vmem_limit_bytes=mib * 2**20),
            cost_estimate=cost,
            name=name,
            **more,
        )(self.at, *arrays, *self.last)
        self.last = [in_hbm(token)]
        return result


def relative(at_ref, index, groups):
    o = lax.bitwise_xor(lax.shift_right_logical(index, 1), at_ref[1])
    q = lax.bitwise_xor(lax.bitwise_and(index, 1), at_ref[2])
    return q * groups + o


def spread_pairs(dense, top):
    toks, width = dense.shape
    return jnp.broadcast_to(dense[:, None, :], (toks, top, width)).reshape(toks * top, width)


def diagonal(pairs, top):
    return iota((pairs, top), 1) == lax.bitwise_and(iota((pairs, top), 0), top - 1)


def pair_column(table):
    toks, top = table.shape
    wide = spread_pairs(table, top)
    return jnp.sum(jnp.where(diagonal(toks * top, top), wide, 0.0), axis=1, keepdims=True)


def expert_mask(column, width, rank):
    return iota((column.shape[0], width), 1) // rank == column.astype(jnp.int32)


def pack_kernel(at_ref, grad_ref, first_ref, index_ref, out_ref):
    toks, feats = grad_ref.shape
    rank = first_ref.shape[0]
    extra = out_ref.shape[1] - feats
    out_ref[:, pl.ds(0, feats)] = grad_ref[...]
    for k in range(3):
        piece = first_ref[:, pl.ds(k * extra, extra)]
        out_ref[pl.ds(k * rank, rank), pl.ds(feats, extra)] = piece
    top = index_ref.shape[0]
    out_ref[pl.ds(3 * rank, toks - 3 * rank), pl.ds(feats, extra)] = jnp.full(
        (toks - 3 * rank, extra), -1.0, BF16
    )
    routes = index_ref[...].astype(F32)
    routes = jnp.concatenate([routes, jnp.full((16 - top, toks), -1.0, F32)], axis=0)
    out_ref[pl.ds(3 * rank, 16), pl.ds(feats, toks)] = routes.astype(BF16)


def pack_call(order, grad, first, index):
    (toks, feats), (rank, units) = grad.shape, first.shape
    shape = (toks, feats + units // 3)
    return order.call(
        pack_kernel,
        "pack_block",
        [in_hbm(grad), first, index],
        [whole(grad.shape), whole(first.shape), whole(index.shape)],
        [(shape, BF16)],
        [whole(shape)],
    )[0]


def gate_kernel(at_ref, *refs):
    pass


def gate_call(order, arrays):
    return order.call(
        gate_kernel,
        "gate",
        arrays,
        [ANY] * len(arrays),
        [(x.shape, x.dtype) for x in arrays],
        [ANY] * len(arrays),
        input_output_aliases={1 + k: k for k in range(len(arrays))},
    )


def load_kernel(at_ref, down_ref, out_ref, sems):
    parts = sems.shape[0]
    rows = down_ref.shape[0] // parts
    copies = [
        pltpu.make_async_copy(
            down_ref.at[pl.ds(k * rows, rows), :], out_ref.at[pl.ds(k * rows, rows), :], sems.at[k]
        )
        for k in range(parts)
    ]
    for copy in copies:
        copy.start()
    for copy in copies:
        copy.wait()


def load_call(order, down):
    return order.call(
        load_kernel,
        "load_matrix",
        [in_hbm(down)],
        [ANY],
        [pltpu.VMEM(down.shape, down.dtype)],
        [VMEM],
        grid=(),
        scratch=[pltpu.SemaphoreType.DMA((4,))],
    )[0]


def expert_rows_kernel(slots, tiles, shares, batch, route_row, at_ref, *rest):
    grads, seconds, downs = rest[:batch], rest[batch : batch + 2], rest[batch + 2 : batch + 4]
    *outs, low_ref = rest[batch + 4 : batch + 5 + shares]
    block_ref, turned_ref, block_sems = rest[batch + 5 + shares :]
    tile = downs[0].shape[0] // shares // tiles
    feats = turned_ref.shape[1]
    toks = block_ref.shape[1]
    blocks = [
        pltpu.make_async_copy(ref, block_ref.at[k], block_sems.at[k]) for k, ref in enumerate(grads)
    ]
    for copy in blocks:
        copy.start()

    before = jnp.where(iota((toks, toks), 0) < iota((toks, toks), 1), 1.0, 0.0).astype(BF16)
    columns = turned_ref.shape[2]
    slot = iota((columns, batch * toks), 0).astype(F32)
    second = jnp.concatenate([ref[...] for ref in seconds], axis=0)
    routes = []
    for k in range(batch):
        blocks[k].wait()
        routes.append(block_ref[k, pl.ds(route_row, 16), pl.ds(feats, toks)].astype(F32))
    grad = block_ref[:, :, pl.ds(0, feats)].reshape(batch * toks, feats)
    for q in range(2):
        expert = at_ref[1] * 2 + lax.bitwise_xor(at_ref[2], q)
        targets = []
        for k in range(batch):
            hits = jnp.where(routes[k] == expert.astype(F32), 1.0, 0.0)
            mine = jnp.max(hits, axis=0, keepdims=True)
            pos = dot(jnp.broadcast_to(mine, (16, toks)).astype(BF16), before, NN)[:1]
            targets.append(jnp.where(mine > 0.0, pos + float(k * slots), -1.0))
        pick = jnp.where(slot == jnp.concatenate(targets, axis=1), 1.0, 0.0)
        turned_ref[q] = dot(grad, pick.T.astype(BF16), TN).astype(BF16)
    low = dot(second, grad, NT).astype(BF16)
    for k in range(batch):
        low_ref[k] = low[:, k * toks : (k + 1) * toks]

    rows = batch * slots
    for k in range(shares):
        share = lax.rem(at_ref[0] + k + 1, shares)
        for q in range(2):
            for t in range(tiles):
                row = pl.multiple_of((share * tiles + t) * tile, tile)
                value = dot(downs[q][pl.ds(row, tile), :], turned_ref[q], NN)
                outs[k][pl.ds(q * rows, rows), pl.ds(t * tile, tile)] = value.T[:rows].astype(BF16)


def expert_rows_call(order, grads, seconds, downs, shares, slots):
    batch, (toks, wide) = len(grads), grads[0].shape
    rank, feats = seconds[0].shape
    units = downs[0].shape[0] // shares
    rows = 2 * batch * slots
    return order.call(
        functools.partial(expert_rows_kernel, slots, 3, shares, batch, 3 * rank),
        "expert_rows",
        [*grads, *seconds, *[pltpu.with_memory_space_constraint(x, pltpu.VMEM) for x in downs]],
        [ANY] * batch + [VMEM] * 4,
        [((rows, units), BF16)] * shares + [((batch, 2 * rank, toks), BF16)],
        [VMEM] * (shares + 1),
        grid=(),
        scratch=[
            pltpu.VMEM((batch, toks, wide), BF16),
            pltpu.VMEM((2, feats, -(-batch * slots // 128) * 128), BF16),
            pltpu.SemaphoreType.DMA((batch,)),
        ],
    )


def share_sum_kernel(parts, slots, at_ref, *refs):
    outs = refs[parts:]
    for k, out_ref in enumerate(outs):
        for q in range(2):
            at = pl.ds((q * len(outs) + k) * slots, slots)
            total = refs[0][at, :].astype(F32)
            for part in refs[1:parts]:
                total = total + part[at, :].astype(F32)
            out_ref[pl.ds(q * slots, slots), :] = total.astype(BF16)


def share_sum_call(order, parts, batch, slots):
    rows, units = parts[0].shape
    shape = (2 * slots, units)
    return order.call(
        functools.partial(share_sum_kernel, len(parts), slots),
        "share_sum",
        parts,
        [whole((rows, units))] * len(parts),
        [(shape, BF16)] * batch,
        [whole(shape)] * batch,
    )


def collect_kernel(places, at_ref, *refs):
    low_ref, first_ref = refs[-2:]
    rank = first_ref.shape[1]
    at = 0
    lows = len(refs) - 2 - len(places)
    for ref in refs[:lows]:
        for k in range(ref.shape[0]):
            low_ref[lax.bitwise_xor(at_ref[1], places[at])] = ref[k]
            at += 1
    for o, ref in zip(places, refs[lows:-2]):
        wide = ref.shape[1]
        for k in range(3):
            first_ref[o, :, pl.ds(k * wide, wide)] = ref[pl.ds(k * rank, rank), :]


def collect_call(order, places, lows, grads, feats):
    groups, (toks, wide) = len(grads), grads[0].shape
    rank = lows[0].shape[1] // 2
    extra = wide - feats
    low_shape, first_shape = (groups, 2 * rank, toks), (groups, rank, 3 * extra)
    return order.call(
        functools.partial(collect_kernel, places),
        "collect_blocks",
        [*lows, *[in_hbm(x) for x in grads]],
        [whole(b.shape) for b in lows]
        + [pl.BlockSpec((toks, extra), lambda i: (0, feats // extra))] * groups,
        [(low_shape, BF16), (first_shape, BF16)],
        [whole(low_shape), whole(first_shape)],
    )


def low_dense_kernel(at_ref, *refs):
    out_ref, sum_ref = refs[-2:]
    groups, both, _ = refs[0].shape
    rank = both // 2
    for o in range(groups):
        total = refs[0][lax.bitwise_xor(at_ref[1], o)].astype(F32)
        for ref in refs[1:-2]:
            total = total + ref[lax.bitwise_xor(at_ref[1], o)].astype(F32)
        for q in range(2):
            at = pl.ds((q * groups + o) * rank, rank)
            sum_ref[at, :] = total[q * rank : (q + 1) * rank]
    out_ref[...] = sum_ref[...].T


def low_dense_call(order, parts):
    groups, both, toks = parts[0].shape
    shape = (toks, groups * both)
    return order.call(
        low_dense_kernel,
        "low_dense",
        parts,
        [whole(parts[0].shape)] * len(parts),
        [(shape, F32)],
        [whole(shape)],
        scratch=[pltpu.VMEM((groups * both, toks), F32)],
    )[0]


def lowrank_hid_kernel(groups, at_ref, index_ref, hid_ref, *rest):
    firsts, out_ref = rest[:2], rest[2]
    top = index_ref.shape[1]
    rank = firsts[0].shape[0] // groups
    wide = jnp.concatenate([dot(hid_ref[...], ref[...], NT) for ref in firsts], axis=1)
    column = pair_column(relative(at_ref, index_ref[...], groups).astype(F32))
    wide = jnp.where(expert_mask(column, wide.shape[1], rank), wide, 0.0)
    out_ref[...] = wide.reshape(wide.shape[0] // top, top, wide.shape[1]).sum(axis=1)


def lowrank_hid_call(order, index, hid, firsts, groups):
    (toks, top), (pairs, units) = index.shape, hid.shape
    half = firsts[0].shape[0]
    steps = 4
    return order.call(
        functools.partial(lowrank_hid_kernel, groups),
        "lowrank_hid",
        [index, in_hbm(hid), *firsts],
        [
            pl.BlockSpec((toks // steps, top), lambda i: (i, 0)),
            pl.BlockSpec((pairs // steps, units), lambda i: (i, 0)),
        ]
        + [whole((half, units))] * 2,
        [((toks, 2 * half), F32)],
        [pl.BlockSpec((toks // steps, 2 * half), lambda i: (i, 0))],
        grid=(steps,),
    )[0]


def second_grad_kernel(places, units, at_ref, got_ref, *refs):
    grads, outs, first_ref = refs[:-3], refs[-3:-1], refs[-1]
    rank, tile = outs[0].shape
    toks = grads[0].shape[0]

    @pl.when(pl.program_id(0) == 0)
    def _():
        total = jnp.zeros((rank, units), F32)
        for source in range(got_ref.shape[0]):
            total = total + got_ref[source, :, pl.ds(0, units)].astype(F32)
        first_ref[...] = total

    totals = [jnp.zeros((rank, tile), F32) for _ in outs]
    for o, grad_ref in zip(places, grads):
        source = lax.bitwise_xor(at_ref[1], o)
        scaled = jnp.concatenate(
            [got_ref[source, :, pl.ds(units + q * toks, toks)] for q in range(2)], axis=0
        )
        value = dot(scaled, grad_ref[...], NN)
        totals = [total + value[q * rank : (q + 1) * rank] for q, total in enumerate(totals)]
    for total, out_ref in zip(totals, outs):
        out_ref[...] = adapter_scale * total


def second_grad_call(order, places, got, grads, units, feats):
    rank, toks = got.shape[1], grads[0].shape[0]
    steps = 4
    tile = feats // steps
    block = pl.BlockSpec((rank, tile), lambda i: (0, i))
    return order.call(
        functools.partial(second_grad_kernel, places, units),
        "second_grad",
        [got, *[in_hbm(x) for x in grads]],
        [whole(got.shape)] + [pl.BlockSpec((toks, tile), lambda i: (0, i))] * len(grads),
        [((rank, feats), F32)] * 2 + [((rank, units), F32)],
        [block] * 2 + [whole((rank, units))],
        grid=(steps,),
    )


def first_grad_kernel(groups, steps, parts, at_ref, index_ref, prob_ref, low_ref, hid_ref, *rest):
    index_all_ref, prob_all_ref, hids = rest[0], rest[1], rest[2 : 2 + parts]
    keep_ref, give_ref, scaled_ref, sum_ref = rest[2 + parts :]
    step = pl.program_id(0)
    top = index_ref.shape[1]
    rank = keep_ref.shape[1]
    low = spread_pairs(low_ref[...], top)
    column = pair_column(relative(at_ref, index_ref[...], groups).astype(F32))
    keep = expert_mask(column, low.shape[1], rank)
    scaled = jnp.where(keep, low * pair_column(prob_ref[...].astype(F32)), 0.0).astype(BF16)
    part = adapter_scale * dot(scaled, hid_ref[...], TN)

    @pl.when(step == 0)
    def _():
        sum_ref[...] = part

    @pl.when(step > 0)
    def _():
        sum_ref[...] += part

    @pl.when(step == steps - 1)
    def _():
        total = hids[0][...]
        for ref in hids[1:]:
            total = total + ref[...]
        toks = total.shape[0]
        place = relative(at_ref, index_all_ref[...], groups)
        prob = prob_all_ref[...].astype(F32)
        expert = iota(total.shape, 1) // rank
        scale = jnp.zeros(total.shape, F32)
        for k in range(top):
            scale = jnp.where(expert == place[:, k : k + 1], prob[:, k : k + 1], scale)
        turned = (total * scale).T.astype(BF16)
        for o in range(groups):
            to = lax.bitwise_xor(at_ref[1], o)
            at, other = o * rank, (groups + o) * rank
            keep_ref[to] = sum_ref[pl.ds(at, rank), :]
            give_ref[to] = sum_ref[pl.ds(other, rank), :].astype(BF16)
            scaled_ref[to, :, pl.ds(0, toks)] = turned[at : at + rank]
            scaled_ref[to, :, pl.ds(toks, toks)] = turned[other : other + rank]


def first_grad_call(order, index, prob, low, hid, hids, groups):
    (toks, top), (pairs, units) = index.shape, hid.shape
    width = low.shape[1]
    steps = 4
    rank = width // groups // 2
    shape, scaled_shape = (groups, rank, units), (groups, rank, 2 * toks)
    return order.call(
        functools.partial(first_grad_kernel, groups, steps, len(hids)),
        "first_grad",
        [index, prob, low, in_hbm(hid), index, prob, *hids],
        [
            pl.BlockSpec((toks // steps, top), lambda i: (i, 0)),
            pl.BlockSpec((toks // steps, top), lambda i: (i, 0)),
            pl.BlockSpec((toks // steps, width), lambda i: (i, 0)),
            pl.BlockSpec((pairs // steps, units), lambda i: (i, 0)),
            whole(index.shape),
            whole(prob.shape),
        ]
        + [whole(x.shape) for x in hids],
        [(shape, F32), (shape, BF16), (scaled_shape, BF16)],
        [whole(shape), whole(shape), whole(scaled_shape)],
        grid=(steps,),
        scratch=[pltpu.VMEM((width, units), F32)],
    )


def first_sum_kernel(at_ref, keep_ref, got_ref, scaled_ref, out_ref):
    units = keep_ref.shape[2]
    out_ref[:, :, pl.ds(0, units)] = (keep_ref[...] + got_ref[...].astype(F32)).astype(BF16)
    out_ref[:, :, pl.ds(units, scaled_ref.shape[2])] = scaled_ref[...]


def first_sum_call(order, keep, got, scaled):
    shape = keep.shape[:2] + (keep.shape[2] + scaled.shape[2],)
    return order.call(
        first_sum_kernel,
        "first_sum",
        [keep, got, scaled],
        [whole(x.shape) for x in (keep, got, scaled)],
        [(shape, BF16)],
        [whole(shape)],
    )[0]


def finish_kernel(count, slots, at_ref, index_all_ref, index_ref, prob_ref, low_ref, hid_ref, *rest):
    firsts, back = rest[:2], rest[2 : 2 + count]
    out_ref, sum_ref, all_ref, place_ref = rest[2 + count :]
    top = index_ref.shape[1]
    toks = index_all_ref.shape[0]
    experts = 2 * count

    @pl.when(pl.program_id(0) == 0)
    def _():
        for o, ref in enumerate(back):
            for q in range(2):
                all_ref[pl.ds((q * count + o) * slots, slots), :] = ref[pl.ds(q * slots, slots), :]
        experts_all = relative(at_ref, index_all_ref[...], count)
        hit = jnp.zeros((toks, experts), F32)
        for k in range(top):
            hit = jnp.where(iota((toks, experts), 1) == experts_all[:, k : k + 1], 1.0, hit)
        before = jnp.where(iota((toks, toks), 0) > iota((toks, toks), 1), 1.0, 0.0).astype(BF16)
        place_ref[...] = dot(before, hit.astype(BF16), NN)

    pairs = hid_ref.shape[0]
    some = index_ref.shape[0]
    column = pair_column(relative(at_ref, index_ref[...], count).astype(F32))
    place = spread_pairs(place_ref[pl.ds(pl.program_id(0) * some, some), :], top)
    mine = iota((pairs, experts), 1) == column.astype(jnp.int32)
    target = column * slots + jnp.sum(jnp.where(mine, place, 0.0), axis=1, keepdims=True)
    low = spread_pairs(low_ref[...], top)
    keep = expert_mask(column, low.shape[1], low.shape[1] // experts)
    low = jnp.where(keep, adapter_scale * low.astype(BF16).astype(F32), 0.0).astype(BF16)
    slot = iota((pairs, experts * slots), 1)
    pick = jnp.where(slot == target.astype(jnp.int32), 1.0, 0.0).astype(BF16)
    half = low.shape[1] // 2
    value = dot(pick, all_ref[...], NN)
    value = value + dot(low[:, :half], firsts[0][...], NN) + dot(low[:, half:], firsts[1][...], NN)
    value = value.astype(BF16).astype(F32)
    out_ref[...] = (value * pair_column(prob_ref[...].astype(F32))).astype(BF16)
    sums = jnp.sum(value * hid_ref[...].astype(F32), axis=1, keepdims=True)
    sums = jnp.where(diagonal(pairs, top), sums, 0.0)
    sum_ref[...] = sums.reshape(some, top, top).sum(axis=1)


def finish_call(order, index, prob, low, hid, firsts, back):
    (toks, top), (pairs, units) = index.shape, hid.shape
    width = low.shape[1]
    both = back[0].shape[0]
    steps = 4
    count = len(back)

    def rows(n, columns):
        return pl.BlockSpec((n // steps, columns), lambda i: (i, 0))

    return order.call(
        functools.partial(finish_kernel, count, both // 2),
        "finish",
        [index, index, prob, low, in_hbm(hid), *firsts, *[in_hbm(x) for x in back]],
        [whole(index.shape), rows(toks, top), rows(toks, top), rows(toks, width), rows(pairs, units)]
        + [whole(firsts[0].shape)] * 2
        + [whole((both, units))] * count,
        [((pairs, units), BF16), ((toks, top), F32)],
        [rows(pairs, units), rows(toks, top)],
        grid=(steps,),
        cost=LONG,
        scratch=[pltpu.VMEM((count * both, units), BF16), pltpu.VMEM((toks, 2 * count), F32)],
    )


def body(grad, hidden, index, weight, down, first, second):
    toks, top = index.shape
    exp_local, units_all, feats = down.shape
    units, rank = first.shape[1:]
    groups, cores, shares = lax.axis_size("ep"), lax.axis_size("sub"), lax.axis_size("rep")
    assert exp_local == 1 and cores == 2 and groups & (groups - 1) == 0
    cap = min(toks, 5 * toks * top // (4 * groups * cores))
    slots = -(-cap // 16) * 16
    pairs = toks * top
    at = jnp.stack([lax.axis_index(name).astype(jnp.int32) for name in ("rep", "ep", "sub")])
    order = Order(at)

    def turn(x, offset):
        return lax.ppermute(x, "rep", [(r, (r + offset) % shares) for r in range(shares)])

    def all_shares(x):
        return [x] + [turn(x, k) for k in range(1, shares)]

    def flip(x, mask):
        return lax.ppermute(x, "ep", [(i, i ^ mask) for i in range(groups)])

    def swap(x):
        return lax.ppermute(x, "sub", [(0, 1), (1, 0)])

    where = ("ep", "sub")

    def exchange(x, axes="ep"):
        return lax.all_to_all(x, axes, split_axis=0, concat_axis=0, tiled=True)

    blocks = {0: pack_call(order, grad, first[0].T, index.T)}

    def fetch(o):
        if o not in blocks:
            last = o & -o
            blocks[o] = flip(fetch(o ^ last), last)
        return blocks[o]

    own_down = load_call(order, down[0])
    downs = [own_down, swap(down[0])]
    seconds = [second[0], swap(second[0])]

    if groups == 8:
        batches = [(0, 1), (2, 4), (6, 3), (5, 7)]
        steps = [("multiply", 0), ("gate", 4), ("multiply", 1), ("total", 0), ("total", 1)]
        steps += [("multiply", 2), ("multiply", 3), ("total", 2)]
        early = {("total", 0): 3, ("multiply", 2): 5}
    else:
        batches = [(o, o + 1) for o in range(0, groups, 2)]
        steps = [("multiply", 0)]
        for i in range(1, len(batches)):
            steps += [("multiply", i), ("total", i - 1)]
        early = {}
    last = len(batches) - 1
    places = [o for batch in batches for o in batch]
    back, lows, shared = {}, [], {}

    def total(i):
        for o, rows in zip(batches[i], share_sum_call(order, shared[i], 2, slots)):
            masks = [o] if o else []
            if i >= last - 1 and o % 2:
                masks = [o - 1, 1] if o > 1 else [1]
            elif o == 4 and groups == 8:
                masks = [2, 6]
            for mask in masks:
                rows = flip(rows, mask)
            back[o] = rows

    for kind, i in steps:
        if (kind, i) in early:
            order.wait([fetch(early[kind, i])])
        if kind == "gate":
            blocks[i] = gate_call(order, [fetch(i)])[0]
        elif kind == "total":
            total(i)
        else:
            *give, keep, low = expert_rows_call(
                order, [fetch(o) for o in batches[i]], seconds, downs, shares, slots
            )
            lows.append(low)
            shared[i] = [keep] + [turn(x, k + 1) for k, x in enumerate(give)]

    hid = hidden.reshape(pairs, units)
    grads = [blocks[o] for o in places]

    low_grad, first_own = collect_call(order, places, lows, grads, feats)
    firsts = [x.reshape(groups * rank, units) for x in (first_own, swap(first_own))]
    low_grad = exchange(low_grad)
    order.wait([back[batches[-2][0]], back[1], back[2]] + [back[4]] * (groups == 8))
    total(last)
    order.wait([low_grad])
    low_hid = all_shares(lowrank_hid_call(order, index, hid, firsts, groups))
    order.wait([back[batches[-2][1]]])

    low_grad = low_dense_call(order, all_shares(low_grad))
    order.wait([back[batches[-1][0]]])
    keep, give, scaled = first_grad_call(order, index, weight, low_grad, hid, low_hid, groups)

    order.wait([back[batches[-1][1]]])
    got = exchange(first_sum_call(order, keep, swap(give), scaled))
    back = [back[o] for o in range(groups)]
    grad_hidden, sums = finish_call(order, index, weight, low_grad, hid, firsts, back)
    if shares == 2:
        other_sums = turn(sums, 1)
        order.wait([other_sums])
        sums = sums + other_sums
    else:
        sums = lax.psum(sums, "rep")
    second_keep, second_give, first_grad = second_grad_call(
        order, places, got, grads, units, feats
    )
    second_grad = second_keep + swap(second_give)
    return (
        grad_hidden.reshape(toks, top, units),
        sums,
        first_grad.T[None],
        second_grad[None],
    )


def solution(mesh):
    return jax.shard_map(
        body,
        mesh=mesh,
        in_specs=(
            P(("grp", "ep", "sub"), "rep"),
            P(("grp", "ep", "sub"), None, "rep"),
            P(("grp", "ep", "sub"), None),
            P(("grp", "ep", "sub"), None),
            P(("ep", "sub"), None, "rep"),
            P(("grp", "ep", "sub"), "rep", None),
            P(("grp", "ep", "sub"), None, "rep"),
        ),
        out_specs=(
            P(("grp", "ep", "sub"), None, "rep"),
            P(("grp", "ep", "sub"), None),
            P(("grp", "ep", "sub"), "rep", None),
            P(("grp", "ep", "sub"), None, "rep"),
        ),
        check_vma=False,
    )
```

```python
import functools

import jax
import jax.numpy as jnp
from jax import lax
from jax.experimental import pallas as pl
from jax.experimental.pallas import tpu as pltpu
from jax.sharding import PartitionSpec as P

adapter_scale = 2.0
BF16 = jnp.bfloat16
F32 = jnp.float32
NT = (((1,), (1,)), ((), ()))
TN = (((0,), (0,)), ((), ()))
NN = (((1,), (0,)), ((), ()))
SMALL = pl.CostEstimate(flops=1, bytes_accessed=1, transcendentals=0)
LONG = pl.CostEstimate(flops=1, bytes_accessed=2 * 10**7, transcendentals=0)
ANY = pl.BlockSpec(memory_space=pl.ANY)
SMEM = pl.BlockSpec(memory_space=pltpu.SMEM)
VMEM = pl.BlockSpec(memory_space=pltpu.VMEM)


def dot(a, b, dims):
    return lax.dot_general(a, b, dims, preferred_element_type=F32)


def iota(shape, axis):
    return lax.broadcasted_iota(jnp.int32, shape, axis)


def whole(shape):
    return pl.BlockSpec(shape, lambda *_: (0,) * len(shape))


def in_hbm(x):
    return pltpu.with_memory_space_constraint(x, pltpu.HBM)


class Order:
    def __init__(self, at):
        self.at, self.last = at, []

    def wait(self, arrays):
        self.last = self.last + list(arrays)

    def call(self, kernel, name, arrays, in_specs, outs, out_specs, grid=(1,), scratch=(), mib=16, cost=SMALL, **more):
        count, last = 1 + len(arrays), len(self.last)

        def ordered(*refs):
            here = count + last + len(outs)
            kernel(*refs[:count], *refs[count + last : here], *refs[here + 1 :])

        *result, token = pl.pallas_call(
            ordered,
            grid=grid,
            in_specs=[SMEM, *in_specs] + [ANY] * last,
            out_specs=[*out_specs, ANY],
            scratch_shapes=scratch,
            out_shape=[jax.ShapeDtypeStruct(*o) if isinstance(o, tuple) else o for o in outs]
            + [pltpu.HBM((8, 128), F32)],
            compiler_params=pltpu.CompilerParams(vmem_limit_bytes=mib * 2**20),
            cost_estimate=cost,
            name=name,
            **more,
        )(self.at, *arrays, *self.last)
        self.last = [in_hbm(token)]
        return result


def relative(at_ref, index, groups):
    o = lax.bitwise_xor(lax.shift_right_logical(index, 1), at_ref[1])
    q = lax.bitwise_xor(lax.bitwise_and(index, 1), at_ref[2])
    return q * groups + o


def spread_pairs(dense, top):
    toks, width = dense.shape
    return jnp.broadcast_to(dense[:, None, :], (toks, top, width)).reshape(toks * top, width)


def diagonal(pairs, top):
    return iota((pairs, top), 1) == lax.bitwise_and(iota((pairs, top), 0), top - 1)


def pair_column(table):
    toks, top = table.shape
    wide = spread_pairs(table, top)
    return jnp.sum(jnp.where(diagonal(toks * top, top), wide, 0.0), axis=1, keepdims=True)


def expert_mask(column, width, rank):
    return iota((column.shape[0], width), 1) // rank == column.astype(jnp.int32)


def pack_kernel(at_ref, grad_ref, first_ref, index_ref, out_ref):
    toks, feats = grad_ref.shape
    rank = first_ref.shape[0]
    extra = out_ref.shape[1] - feats
    out_ref[:, pl.ds(0, feats)] = grad_ref[...]
    for k in range(3):
        piece = first_ref[:, pl.ds(k * extra, extra)]
        out_ref[pl.ds(k * rank, rank), pl.ds(feats, extra)] = piece
    top = index_ref.shape[0]
    out_ref[pl.ds(3 * rank, toks - 3 * rank), pl.ds(feats, extra)] = jnp.full(
        (toks - 3 * rank, extra), -1.0, BF16
    )
    routes = index_ref[...].astype(F32)
    routes = jnp.concatenate([routes, jnp.full((16 - top, toks), -1.0, F32)], axis=0)
    out_ref[pl.ds(3 * rank, 16), pl.ds(feats, toks)] = routes.astype(BF16)


def pack_call(order, grad, first, index):
    (toks, feats), (rank, units) = grad.shape, first.shape
    shape = (toks, feats + units // 3)
    return order.call(
        pack_kernel,
        "pack_block",
        [in_hbm(grad), first, index],
        [whole(grad.shape), whole(first.shape), whole(index.shape)],
        [(shape, BF16)],
        [whole(shape)],
    )[0]


def gate_kernel(at_ref, *refs):
    pass


def gate_call(order, arrays):
    return order.call(
        gate_kernel,
        "gate",
        arrays,
        [ANY] * len(arrays),
        [(x.shape, x.dtype) for x in arrays],
        [ANY] * len(arrays),
        input_output_aliases={1 + k: k for k in range(len(arrays))},
    )


def touch_kernel(block_ref, out_ref):
    out_ref[...] = jnp.zeros_like(out_ref)


def touch_call(block):
    return pl.pallas_call(
        touch_kernel,
        in_specs=[ANY],
        out_specs=VMEM,
        out_shape=jax.ShapeDtypeStruct((8, 128), F32),
        cost_estimate=SMALL,
        name="touch",
    )(block)


def load_kernel(at_ref, down_ref, out_ref, sems):
    parts = sems.shape[0]
    rows = down_ref.shape[0] // parts
    copies = [
        pltpu.make_async_copy(
            down_ref.at[pl.ds(k * rows, rows), :], out_ref.at[pl.ds(k * rows, rows), :], sems.at[k]
        )
        for k in range(parts)
    ]
    for copy in copies:
        copy.start()
    for copy in copies:
        copy.wait()


def load_call(order, down):
    return order.call(
        load_kernel,
        "load_matrix",
        [in_hbm(down)],
        [ANY],
        [pltpu.VMEM(down.shape, down.dtype)],
        [VMEM],
        grid=(),
        scratch=[pltpu.SemaphoreType.DMA((4,))],
    )[0]


def expert_rows_kernel(slots, tiles, shares, batch, route_row, at_ref, *rest):
    grads, seconds, downs = rest[:batch], rest[batch : batch + 2], rest[batch + 2 : batch + 4]
    *outs, low_ref = rest[batch + 4 : batch + 5 + shares]
    block_ref, turned_ref, block_sems = rest[batch + 5 + shares :]
    tile = downs[0].shape[0] // shares // tiles
    feats = turned_ref.shape[1]
    toks = block_ref.shape[1]
    blocks = [
        pltpu.make_async_copy(ref, block_ref.at[k], block_sems.at[k]) for k, ref in enumerate(grads)
    ]
    for copy in blocks:
        copy.start()

    before = jnp.where(iota((toks, toks), 0) < iota((toks, toks), 1), 1.0, 0.0).astype(BF16)
    columns = turned_ref.shape[2]
    slot = iota((columns, batch * toks), 0).astype(F32)
    second = jnp.concatenate([ref[...] for ref in seconds], axis=0)
    routes = []
    for k in range(batch):
        blocks[k].wait()
        routes.append(block_ref[k, pl.ds(route_row, 16), pl.ds(feats, toks)].astype(F32))
    grad = block_ref[:, :, pl.ds(0, feats)].reshape(batch * toks, feats)
    for q in range(2):
        expert = at_ref[1] * 2 + lax.bitwise_xor(at_ref[2], q)
        targets = []
        for k in range(batch):
            hits = jnp.where(routes[k] == expert.astype(F32), 1.0, 0.0)
            mine = jnp.max(hits, axis=0, keepdims=True)
            pos = dot(jnp.broadcast_to(mine, (16, toks)).astype(BF16), before, NN)[:1]
            targets.append(jnp.where(mine > 0.0, pos + float(k * slots), -1.0))
        pick = jnp.where(slot == jnp.concatenate(targets, axis=1), 1.0, 0.0)
        turned_ref[q] = dot(grad, pick.T.astype(BF16), TN).astype(BF16)
    low = dot(second, grad, NT).astype(BF16)
    for k in range(batch):
        low_ref[k] = low[:, k * toks : (k + 1) * toks]

    rows = batch * slots
    for k in range(shares):
        share = lax.rem(at_ref[0] + k + 1, shares)
        for q in range(2):
            for t in range(tiles):
                row = pl.multiple_of((share * tiles + t) * tile, tile)
                value = dot(downs[q][pl.ds(row, tile), :], turned_ref[q], NN)
                outs[k][pl.ds(q * rows, rows), pl.ds(t * tile, tile)] = value.T[:rows].astype(BF16)


def expert_rows_call(order, grads, seconds, downs, shares, slots):
    batch, (toks, wide) = len(grads), grads[0].shape
    rank, feats = seconds[0].shape
    units = downs[0].shape[0] // shares
    rows = 2 * batch * slots
    return order.call(
        functools.partial(expert_rows_kernel, slots, 3, shares, batch, 3 * rank),
        "expert_rows",
        [*grads, *seconds, *[pltpu.with_memory_space_constraint(x, pltpu.VMEM) for x in downs]],
        [ANY] * batch + [VMEM] * 4,
        [((rows, units), BF16)] * shares + [((batch, 2 * rank, toks), BF16)],
        [VMEM] * (shares + 1),
        grid=(),
        scratch=[
            pltpu.VMEM((batch, toks, wide), BF16),
            pltpu.VMEM((2, feats, -(-batch * slots // 128) * 128), BF16),
            pltpu.SemaphoreType.DMA((batch,)),
        ],
    )


def share_sum_kernel(parts, slots, at_ref, *refs):
    outs = refs[parts:]
    for k, out_ref in enumerate(outs):
        for q in range(2):
            at = pl.ds((q * len(outs) + k) * slots, slots)
            total = refs[0][at, :].astype(F32)
            for part in refs[1:parts]:
                total = total + part[at, :].astype(F32)
            out_ref[pl.ds(q * slots, slots), :] = total.astype(BF16)


def share_sum_call(order, parts, batch, slots):
    rows, units = parts[0].shape
    shape = (2 * slots, units)
    return order.call(
        functools.partial(share_sum_kernel, len(parts), slots),
        "share_sum",
        parts,
        [whole((rows, units))] * len(parts),
        [(shape, BF16)] * batch,
        [whole(shape)] * batch,
    )


def collect_kernel(places, at_ref, *refs):
    low_ref, first_ref = refs[-2:]
    rank = first_ref.shape[1]
    at = 0
    lows = len(refs) - 2 - len(places)
    for ref in refs[:lows]:
        for k in range(ref.shape[0]):
            low_ref[lax.bitwise_xor(at_ref[1], places[at])] = ref[k]
            at += 1
    for o, ref in zip(places, refs[lows:-2]):
        wide = ref.shape[1]
        for k in range(3):
            first_ref[o, :, pl.ds(k * wide, wide)] = ref[pl.ds(k * rank, rank), :]


def collect_call(order, places, lows, grads, feats):
    groups, (toks, wide) = len(grads), grads[0].shape
    rank = lows[0].shape[1] // 2
    extra = wide - feats
    low_shape, first_shape = (groups, 2 * rank, toks), (groups, rank, 3 * extra)
    return order.call(
        functools.partial(collect_kernel, places),
        "collect_blocks",
        [*lows, *[in_hbm(x) for x in grads]],
        [whole(b.shape) for b in lows]
        + [pl.BlockSpec((toks, extra), lambda i: (0, feats // extra))] * groups,
        [(low_shape, BF16), (first_shape, BF16)],
        [whole(low_shape), whole(first_shape)],
    )


def low_dense_kernel(at_ref, *refs):
    out_ref, sum_ref = refs[-2:]
    groups, both, _ = refs[0].shape
    rank = both // 2
    for o in range(groups):
        total = refs[0][lax.bitwise_xor(at_ref[1], o)].astype(F32)
        for ref in refs[1:-2]:
            total = total + ref[lax.bitwise_xor(at_ref[1], o)].astype(F32)
        for q in range(2):
            at = pl.ds((q * groups + o) * rank, rank)
            sum_ref[at, :] = total[q * rank : (q + 1) * rank]
    out_ref[...] = sum_ref[...].T


def low_dense_call(order, parts):
    groups, both, toks = parts[0].shape
    shape = (toks, groups * both)
    return order.call(
        low_dense_kernel,
        "low_dense",
        parts,
        [whole(parts[0].shape)] * len(parts),
        [(shape, F32)],
        [whole(shape)],
        scratch=[pltpu.VMEM((groups * both, toks), F32)],
    )[0]


def lowrank_hid_kernel(groups, at_ref, index_ref, hid_ref, *rest):
    firsts, out_ref = rest[:2], rest[2]
    top = index_ref.shape[1]
    rank = firsts[0].shape[0] // groups
    wide = jnp.concatenate([dot(hid_ref[...], ref[...], NT) for ref in firsts], axis=1)
    column = pair_column(relative(at_ref, index_ref[...], groups).astype(F32))
    wide = jnp.where(expert_mask(column, wide.shape[1], rank), wide, 0.0)
    out_ref[...] = wide.reshape(wide.shape[0] // top, top, wide.shape[1]).sum(axis=1)


def lowrank_hid_call(order, index, hid, firsts, groups):
    (toks, top), (pairs, units) = index.shape, hid.shape
    half = firsts[0].shape[0]
    steps = 4
    return order.call(
        functools.partial(lowrank_hid_kernel, groups),
        "lowrank_hid",
        [index, in_hbm(hid), *firsts],
        [
            pl.BlockSpec((toks // steps, top), lambda i: (i, 0)),
            pl.BlockSpec((pairs // steps, units), lambda i: (i, 0)),
        ]
        + [whole((half, units))] * 2,
        [((toks, 2 * half), F32)],
        [pl.BlockSpec((toks // steps, 2 * half), lambda i: (i, 0))],
        grid=(steps,),
    )[0]


def second_grad_kernel(places, units, at_ref, got_ref, *refs):
    grads, outs, first_ref = refs[:-3], refs[-3:-1], refs[-1]
    rank, tile = outs[0].shape
    toks = grads[0].shape[0]

    @pl.when(pl.program_id(0) == 0)
    def _():
        total = jnp.zeros((rank, units), F32)
        for source in range(got_ref.shape[0]):
            total = total + got_ref[source, :, pl.ds(0, units)].astype(F32)
        first_ref[...] = total

    totals = [jnp.zeros((rank, tile), F32) for _ in outs]
    for o, grad_ref in zip(places, grads):
        source = lax.bitwise_xor(at_ref[1], o)
        scaled = jnp.concatenate(
            [got_ref[source, :, pl.ds(units + q * toks, toks)] for q in range(2)], axis=0
        )
        value = dot(scaled, grad_ref[...], NN)
        totals = [total + value[q * rank : (q + 1) * rank] for q, total in enumerate(totals)]
    for total, out_ref in zip(totals, outs):
        out_ref[...] = adapter_scale * total


def second_grad_call(order, places, got, grads, units, feats):
    rank, toks = got.shape[1], grads[0].shape[0]
    steps = 4
    tile = feats // steps
    block = pl.BlockSpec((rank, tile), lambda i: (0, i))
    return order.call(
        functools.partial(second_grad_kernel, places, units),
        "second_grad",
        [got, *[in_hbm(x) for x in grads]],
        [whole(got.shape)] + [pl.BlockSpec((toks, tile), lambda i: (0, i))] * len(grads),
        [((rank, feats), F32)] * 2 + [((rank, units), F32)],
        [block] * 2 + [whole((rank, units))],
        grid=(steps,),
    )


def first_grad_kernel(groups, steps, parts, at_ref, index_ref, prob_ref, low_ref, hid_ref, *rest):
    index_all_ref, prob_all_ref, hids = rest[0], rest[1], rest[2 : 2 + parts]
    keep_ref, give_ref, scaled_ref, sum_ref = rest[2 + parts :]
    step = pl.program_id(0)
    top = index_ref.shape[1]
    rank = keep_ref.shape[1]
    low = spread_pairs(low_ref[...], top)
    column = pair_column(relative(at_ref, index_ref[...], groups).astype(F32))
    keep = expert_mask(column, low.shape[1], rank)
    scaled = jnp.where(keep, low * pair_column(prob_ref[...].astype(F32)), 0.0).astype(BF16)
    part = adapter_scale * dot(scaled, hid_ref[...], TN)

    @pl.when(step == 0)
    def _():
        sum_ref[...] = part

    @pl.when(step > 0)
    def _():
        sum_ref[...] += part

    @pl.when(step == steps - 1)
    def _():
        total = hids[0][...]
        for ref in hids[1:]:
            total = total + ref[...]
        toks = total.shape[0]
        place = relative(at_ref, index_all_ref[...], groups)
        prob = prob_all_ref[...].astype(F32)
        expert = iota(total.shape, 1) // rank
        scale = jnp.zeros(total.shape, F32)
        for k in range(top):
            scale = jnp.where(expert == place[:, k : k + 1], prob[:, k : k + 1], scale)
        turned = (total * scale).T.astype(BF16)
        for o in range(groups):
            to = lax.bitwise_xor(at_ref[1], o)
            at, other = o * rank, (groups + o) * rank
            keep_ref[to] = sum_ref[pl.ds(at, rank), :]
            give_ref[to] = sum_ref[pl.ds(other, rank), :].astype(BF16)
            scaled_ref[to, :, pl.ds(0, toks)] = turned[at : at + rank]
            scaled_ref[to, :, pl.ds(toks, toks)] = turned[other : other + rank]


def first_grad_call(order, index, prob, low, hid, hids, groups):
    (toks, top), (pairs, units) = index.shape, hid.shape
    width = low.shape[1]
    steps = 4
    rank = width // groups // 2
    shape, scaled_shape = (groups, rank, units), (groups, rank, 2 * toks)
    return order.call(
        functools.partial(first_grad_kernel, groups, steps, len(hids)),
        "first_grad",
        [index, prob, low, in_hbm(hid), index, prob, *hids],
        [
            pl.BlockSpec((toks // steps, top), lambda i: (i, 0)),
            pl.BlockSpec((toks // steps, top), lambda i: (i, 0)),
            pl.BlockSpec((toks // steps, width), lambda i: (i, 0)),
            pl.BlockSpec((pairs // steps, units), lambda i: (i, 0)),
            whole(index.shape),
            whole(prob.shape),
        ]
        + [whole(x.shape) for x in hids],
        [(shape, F32), (shape, BF16), (scaled_shape, BF16)],
        [whole(shape), whole(shape), whole(scaled_shape)],
        grid=(steps,),
        scratch=[pltpu.VMEM((width, units), F32)],
    )


def first_sum_kernel(at_ref, keep_ref, got_ref, scaled_ref, out_ref):
    units = keep_ref.shape[2]
    out_ref[:, :, pl.ds(0, units)] = (keep_ref[...] + got_ref[...].astype(F32)).astype(BF16)
    out_ref[:, :, pl.ds(units, scaled_ref.shape[2])] = scaled_ref[...]


def first_sum_call(order, keep, got, scaled):
    shape = keep.shape[:2] + (keep.shape[2] + scaled.shape[2],)
    return order.call(
        first_sum_kernel,
        "first_sum",
        [keep, got, scaled],
        [whole(x.shape) for x in (keep, got, scaled)],
        [(shape, BF16)],
        [whole(shape)],
    )[0]


def finish_kernel(count, slots, at_ref, index_all_ref, index_ref, prob_ref, low_ref, hid_ref, *rest):
    firsts, back = rest[:2], rest[2 : 2 + count]
    out_ref, sum_ref, all_ref, place_ref = rest[2 + count :]
    top = index_ref.shape[1]
    toks = index_all_ref.shape[0]
    experts = 2 * count

    @pl.when(pl.program_id(0) == 0)
    def _():
        for o, ref in enumerate(back):
            for q in range(2):
                all_ref[pl.ds((q * count + o) * slots, slots), :] = ref[pl.ds(q * slots, slots), :]
        experts_all = relative(at_ref, index_all_ref[...], count)
        hit = jnp.zeros((toks, experts), F32)
        for k in range(top):
            hit = jnp.where(iota((toks, experts), 1) == experts_all[:, k : k + 1], 1.0, hit)
        before = jnp.where(iota((toks, toks), 0) > iota((toks, toks), 1), 1.0, 0.0).astype(BF16)
        place_ref[...] = dot(before, hit.astype(BF16), NN)

    pairs = hid_ref.shape[0]
    some = index_ref.shape[0]
    column = pair_column(relative(at_ref, index_ref[...], count).astype(F32))
    place = spread_pairs(place_ref[pl.ds(pl.program_id(0) * some, some), :], top)
    mine = iota((pairs, experts), 1) == column.astype(jnp.int32)
    target = column * slots + jnp.sum(jnp.where(mine, place, 0.0), axis=1, keepdims=True)
    low = spread_pairs(low_ref[...], top)
    keep = expert_mask(column, low.shape[1], low.shape[1] // experts)
    low = jnp.where(keep, adapter_scale * low.astype(BF16).astype(F32), 0.0).astype(BF16)
    slot = iota((pairs, experts * slots), 1)
    pick = jnp.where(slot == target.astype(jnp.int32), 1.0, 0.0).astype(BF16)
    half = low.shape[1] // 2
    value = dot(pick, all_ref[...], NN)
    value = value + dot(low[:, :half], firsts[0][...], NN) + dot(low[:, half:], firsts[1][...], NN)
    value = value.astype(BF16).astype(F32)
    out_ref[...] = (value * pair_column(prob_ref[...].astype(F32))).astype(BF16)
    sums = jnp.sum(value * hid_ref[...].astype(F32), axis=1, keepdims=True)
    sums = jnp.where(diagonal(pairs, top), sums, 0.0)
    sum_ref[...] = sums.reshape(some, top, top).sum(axis=1)


def finish_call(order, index, prob, low, hid, firsts, back):
    (toks, top), (pairs, units) = index.shape, hid.shape
    width = low.shape[1]
    both = back[0].shape[0]
    steps = 4
    count = len(back)

    def rows(n, columns):
        return pl.BlockSpec((n // steps, columns), lambda i: (i, 0))

    return order.call(
        functools.partial(finish_kernel, count, both // 2),
        "finish",
        [index, index, prob, low, in_hbm(hid), *firsts, *[in_hbm(x) for x in back]],
        [whole(index.shape), rows(toks, top), rows(toks, top), rows(toks, width), rows(pairs, units)]
        + [whole(firsts[0].shape)] * 2
        + [whole((both, units))] * count,
        [((pairs, units), BF16), ((toks, top), F32)],
        [rows(pairs, units), rows(toks, top)],
        grid=(steps,),
        cost=LONG,
        scratch=[pltpu.VMEM((count * both, units), BF16), pltpu.VMEM((toks, 2 * count), F32)],
    )


def body(grad, hidden, index, weight, down, first, second):
    toks, top = index.shape
    exp_local, units_all, feats = down.shape
    units, rank = first.shape[1:]
    groups, cores, shares = lax.axis_size("ep"), lax.axis_size("sub"), lax.axis_size("rep")
    assert exp_local == 1 and cores == 2 and groups & (groups - 1) == 0
    cap = min(toks, 5 * toks * top // (4 * groups * cores))
    slots = -(-cap // 16) * 16
    pairs = toks * top
    at = jnp.stack([lax.axis_index(name).astype(jnp.int32) for name in ("rep", "ep", "sub")])
    order = Order(at)

    def turn(x, offset):
        return lax.ppermute(x, "rep", [(r, (r + offset) % shares) for r in range(shares)])

    def all_shares(x):
        return [x] + [turn(x, k) for k in range(1, shares)]

    def flip(x, mask):
        return lax.ppermute(x, "ep", [(i, i ^ mask) for i in range(groups)])

    def swap(x):
        return lax.ppermute(x, "sub", [(0, 1), (1, 0)])

    where = ("ep", "sub")

    def exchange(x, axes="ep"):
        return lax.all_to_all(x, axes, split_axis=0, concat_axis=0, tiled=True)

    blocks = {0: pack_call(order, grad, first[0].T, index.T)}

    def fetch(o):
        if o not in blocks:
            last = o & -o
            blocks[o] = flip(fetch(o ^ last), last)
        return blocks[o]

    own_down = load_call(order, down[0])
    downs = [own_down, swap(down[0])]
    seconds = [second[0], swap(second[0])]

    if groups == 8:
        batches = [(0, 1), (2, 4), (6, 3), (5, 7)]
        steps = [("multiply", 0), ("gate", 4), ("multiply", 1), ("total", 0), ("total", 1)]
        steps += [("multiply", 2), ("multiply", 3), ("total", 2)]
        early = {("total", 0): 3, ("multiply", 2): 5}
    else:
        batches = [(o, o + 1) for o in range(0, groups, 2)]
        steps = [("multiply", 0)]
        for i in range(1, len(batches)):
            steps += [("multiply", i), ("total", i - 1)]
        early = {}
    last = len(batches) - 1
    places = [o for batch in batches for o in batch]
    back, lows, shared = {}, [], {}

    def total(i):
        for o, rows in zip(batches[i], share_sum_call(order, shared[i], 2, slots)):
            masks = [o] if o else []
            if i >= last - 1 and o % 2:
                masks = [1 << k for k in reversed(range(o.bit_length())) if o >> k & 1]
            for mask in masks:
                rows = flip(rows, mask)
            back[o] = rows

    for kind, i in steps:
        if (kind, i) in early:
            order.wait([fetch(early[kind, i])])
        if kind == "gate":
            blocks[i] = gate_call(order, [fetch(i)])[0]
        elif kind == "total":
            total(i)
        else:
            *give, keep, low = expert_rows_call(
                order, [fetch(o) for o in batches[i]], seconds, downs, shares, slots
            )
            lows.append(low)
            shared[i] = [keep] + [turn(x, k + 1) for k, x in enumerate(give)]

    hid = hidden.reshape(pairs, units)
    grads = [blocks[o] for o in places]

    low_grad, first_own = collect_call(order, places, lows, grads, feats)
    firsts = [x.reshape(groups * rank, units) for x in (first_own, swap(first_own))]
    low_grad = exchange(low_grad)
    order.wait([back[batches[-2][0]], swap(touch_call(back[groups // 2]))])
    total(last)
    order.wait([low_grad, back[1], back[2]])
    low_hid = all_shares(lowrank_hid_call(order, index, hid, firsts, groups))
    order.wait([back[batches[-2][1]]])

    low_grad = low_dense_call(order, all_shares(low_grad))
    order.wait([back[batches[-1][0]]])
    keep, give, scaled = first_grad_call(order, index, weight, low_grad, hid, low_hid, groups)

    order.wait([back[batches[-1][1]]])
    got = exchange(first_sum_call(order, keep, swap(give), scaled))
    back = [back[o] for o in range(groups)]
    grad_hidden, sums = finish_call(order, index, weight, low_grad, hid, firsts, back)
    if shares == 2:
        other_sums = turn(sums, 1)
        order.wait([other_sums])
        sums = sums + other_sums
    else:
        sums = lax.psum(sums, "rep")
    second_keep, second_give, first_grad = second_grad_call(
        order, places, got, grads, units, feats
    )
    second_grad = second_keep + swap(second_give)
    return (
        grad_hidden.reshape(toks, top, units),
        sums,
        first_grad.T[None],
        second_grad[None],
    )


def solution(mesh):
    return jax.shard_map(
        body,
        mesh=mesh,
        in_specs=(
            P(("grp", "ep", "sub"), "rep"),
            P(("grp", "ep", "sub"), None, "rep"),
            P(("grp", "ep", "sub"), None),
            P(("grp", "ep", "sub"), None),
            P(("ep", "sub"), None, "rep"),
            P(("grp", "ep", "sub"), "rep", None),
            P(("grp", "ep", "sub"), None, "rep"),
        ),
        out_specs=(
            P(("grp", "ep", "sub"), None, "rep"),
            P(("grp", "ep", "sub"), None),
            P(("grp", "ep", "sub"), "rep", None),
            P(("grp", "ep", "sub"), None, "rep"),
        ),
        check_vma=False,
    )
```

```python
import functools

import jax
import jax.numpy as jnp
from jax import lax
from jax.experimental import pallas as pl
from jax.experimental.pallas import tpu as pltpu
from jax.sharding import PartitionSpec as P

adapter_scale = 2.0
BF16 = jnp.bfloat16
F32 = jnp.float32
NT = (((1,), (1,)), ((), ()))
TN = (((0,), (0,)), ((), ()))
NN = (((1,), (0,)), ((), ()))
SMALL = pl.CostEstimate(flops=1, bytes_accessed=1, transcendentals=0)
LONG = pl.CostEstimate(flops=1, bytes_accessed=2 * 10**7, transcendentals=0)
ANY = pl.BlockSpec(memory_space=pl.ANY)
SMEM = pl.BlockSpec(memory_space=pltpu.SMEM)
VMEM = pl.BlockSpec(memory_space=pltpu.VMEM)


def dot(a, b, dims):
    return lax.dot_general(a, b, dims, preferred_element_type=F32)


def iota(shape, axis):
    return lax.broadcasted_iota(jnp.int32, shape, axis)


def whole(shape):
    return pl.BlockSpec(shape, lambda *_: (0,) * len(shape))


def in_hbm(x):
    return pltpu.with_memory_space_constraint(x, pltpu.HBM)


class Order:
    def __init__(self, at):
        self.at, self.last = at, []

    def wait(self, arrays):
        self.last = self.last + list(arrays)

    def call(self, kernel, name, arrays, in_specs, outs, out_specs, grid=(1,), scratch=(), mib=16, cost=SMALL, **more):
        count, last = 1 + len(arrays), len(self.last)

        def ordered(*refs):
            here = count + last + len(outs)
            kernel(*refs[:count], *refs[count + last : here], *refs[here + 1 :])

        *result, token = pl.pallas_call(
            ordered,
            grid=grid,
            in_specs=[SMEM, *in_specs] + [ANY] * last,
            out_specs=[*out_specs, ANY],
            scratch_shapes=scratch,
            out_shape=[jax.ShapeDtypeStruct(*o) if isinstance(o, tuple) else o for o in outs]
            + [pltpu.HBM((8, 128), F32)],
            compiler_params=pltpu.CompilerParams(vmem_limit_bytes=mib * 2**20),
            cost_estimate=cost,
            name=name,
            **more,
        )(self.at, *arrays, *self.last)
        self.last = [in_hbm(token)]
        return result


def relative(at_ref, index, groups):
    o = lax.bitwise_xor(lax.shift_right_logical(index, 1), at_ref[1])
    q = lax.bitwise_xor(lax.bitwise_and(index, 1), at_ref[2])
    return q * groups + o


def spread_pairs(dense, top):
    toks, width = dense.shape
    return jnp.broadcast_to(dense[:, None, :], (toks, top, width)).reshape(toks * top, width)


def diagonal(pairs, top):
    return iota((pairs, top), 1) == lax.bitwise_and(iota((pairs, top), 0), top - 1)


def pair_column(table):
    toks, top = table.shape
    wide = spread_pairs(table, top)
    return jnp.sum(jnp.where(diagonal(toks * top, top), wide, 0.0), axis=1, keepdims=True)


def expert_mask(column, width, rank):
    return iota((column.shape[0], width), 1) // rank == column.astype(jnp.int32)


def pack_kernel(at_ref, grad_ref, first_ref, index_ref, out_ref):
    toks, feats = grad_ref.shape
    rank = first_ref.shape[0]
    extra = out_ref.shape[1] - feats
    out_ref[:, pl.ds(0, feats)] = grad_ref[...]
    for k in range(3):
        piece = first_ref[:, pl.ds(k * extra, extra)]
        out_ref[pl.ds(k * rank, rank), pl.ds(feats, extra)] = piece
    top = index_ref.shape[0]
    out_ref[pl.ds(3 * rank, toks - 3 * rank), pl.ds(feats, extra)] = jnp.full(
        (toks - 3 * rank, extra), -1.0, BF16
    )
    routes = index_ref[...].astype(F32)
    routes = jnp.concatenate([routes, jnp.full((16 - top, toks), -1.0, F32)], axis=0)
    out_ref[pl.ds(3 * rank, 16), pl.ds(feats, toks)] = routes.astype(BF16)


def pack_call(order, grad, first, index):
    (toks, feats), (rank, units) = grad.shape, first.shape
    shape = (toks, feats + units // 3)
    return order.call(
        pack_kernel,
        "pack_block",
        [in_hbm(grad), first, index],
        [whole(grad.shape), whole(first.shape), whole(index.shape)],
        [(shape, BF16)],
        [whole(shape)],
    )[0]


def gate_kernel(at_ref, *refs):
    pass


def gate_call(order, arrays):
    return order.call(
        gate_kernel,
        "gate",
        arrays,
        [ANY] * len(arrays),
        [(x.shape, x.dtype) for x in arrays],
        [ANY] * len(arrays),
        input_output_aliases={1 + k: k for k in range(len(arrays))},
    )


def load_kernel(at_ref, down_ref, out_ref, sems):
    parts = sems.shape[0]
    rows = down_ref.shape[0] // parts
    copies = [
        pltpu.make_async_copy(
            down_ref.at[pl.ds(k * rows, rows), :], out_ref.at[pl.ds(k * rows, rows), :], sems.at[k]
        )
        for k in range(parts)
    ]
    for copy in copies:
        copy.start()
    for copy in copies:
        copy.wait()


def load_call(order, down):
    return order.call(
        load_kernel,
        "load_matrix",
        [in_hbm(down)],
        [ANY],
        [pltpu.VMEM(down.shape, down.dtype)],
        [VMEM],
        grid=(),
        scratch=[pltpu.SemaphoreType.DMA((4,))],
    )[0]


def expert_rows_kernel(slots, tiles, shares, batch, route_row, at_ref, *rest):
    grads, seconds, downs = rest[:batch], rest[batch : batch + 2], rest[batch + 2 : batch + 4]
    *outs, low_ref = rest[batch + 4 : batch + 5 + shares]
    block_ref, turned_ref, block_sems = rest[batch + 5 + shares :]
    tile = downs[0].shape[0] // shares // tiles
    feats = turned_ref.shape[1]
    toks = block_ref.shape[1]
    blocks = [
        pltpu.make_async_copy(ref, block_ref.at[k], block_sems.at[k]) for k, ref in enumerate(grads)
    ]
    for copy in blocks:
        copy.start()

    before = jnp.where(iota((toks, toks), 0) < iota((toks, toks), 1), 1.0, 0.0).astype(BF16)
    columns = turned_ref.shape[2]
    slot = iota((columns, batch * toks), 0).astype(F32)
    second = jnp.concatenate([ref[...] for ref in seconds], axis=0)
    routes = []
    for k in range(batch):
        blocks[k].wait()
        routes.append(block_ref[k, pl.ds(route_row, 16), pl.ds(feats, toks)].astype(F32))
    grad = block_ref[:, :, pl.ds(0, feats)].reshape(batch * toks, feats)
    for q in range(2):
        expert = at_ref[1] * 2 + lax.bitwise_xor(at_ref[2], q)
        targets = []
        for k in range(batch):
            hits = jnp.where(routes[k] == expert.astype(F32), 1.0, 0.0)
            mine = jnp.max(hits, axis=0, keepdims=True)
            pos = dot(jnp.broadcast_to(mine, (16, toks)).astype(BF16), before, NN)[:1]
            targets.append(jnp.where(mine > 0.0, pos + float(k * slots), -1.0))
        pick = jnp.where(slot == jnp.concatenate(targets, axis=1), 1.0, 0.0)
        turned_ref[q] = dot(grad, pick.T.astype(BF16), TN).astype(BF16)
    low = dot(second, grad, NT).astype(BF16)
    for k in range(batch):
        low_ref[k] = low[:, k * toks : (k + 1) * toks]

    rows = batch * slots
    for k in range(shares):
        share = lax.rem(at_ref[0] + k + 1, shares)
        for q in range(2):
            for t in range(tiles):
                row = pl.multiple_of((share * tiles + t) * tile, tile)
                value = dot(downs[q][pl.ds(row, tile), :], turned_ref[q], NN)
                outs[k][pl.ds(q * rows, rows), pl.ds(t * tile, tile)] = value.T[:rows].astype(BF16)


def expert_rows_call(order, grads, seconds, downs, shares, slots):
    batch, (toks, wide) = len(grads), grads[0].shape
    rank, feats = seconds[0].shape
    units = downs[0].shape[0] // shares
    rows = 2 * batch * slots
    return order.call(
        functools.partial(expert_rows_kernel, slots, 3, shares, batch, 3 * rank),
        "expert_rows",
        [*grads, *seconds, *[pltpu.with_memory_space_constraint(x, pltpu.VMEM) for x in downs]],
        [ANY] * batch + [VMEM] * 4,
        [((rows, units), BF16)] * shares + [((batch, 2 * rank, toks), BF16)],
        [VMEM] * (shares + 1),
        grid=(),
        scratch=[
            pltpu.VMEM((batch, toks, wide), BF16),
            pltpu.VMEM((2, feats, -(-batch * slots // 128) * 128), BF16),
            pltpu.SemaphoreType.DMA((batch,)),
        ],
    )


def share_sum_kernel(parts, slots, at_ref, *refs):
    outs = refs[parts:]
    for k, out_ref in enumerate(outs):
        for q in range(2):
            at = pl.ds((q * len(outs) + k) * slots, slots)
            total = refs[0][at, :].astype(F32)
            for part in refs[1:parts]:
                total = total + part[at, :].astype(F32)
            out_ref[pl.ds(q * slots, slots), :] = total.astype(BF16)


def share_sum_call(order, parts, batch, slots):
    rows, units = parts[0].shape
    shape = (2 * slots, units)
    return order.call(
        functools.partial(share_sum_kernel, len(parts), slots),
        "share_sum",
        parts,
        [whole((rows, units))] * len(parts),
        [(shape, BF16)] * batch,
        [whole(shape)] * batch,
    )


def collect_kernel(places, at_ref, *refs):
    low_ref, first_ref = refs[-2:]
    rank = first_ref.shape[1]
    at = 0
    lows = len(refs) - 2 - len(places)
    for ref in refs[:lows]:
        for k in range(ref.shape[0]):
            low_ref[lax.bitwise_xor(at_ref[1], places[at])] = ref[k]
            at += 1
    for o, ref in zip(places, refs[lows:-2]):
        wide = ref.shape[1]
        for k in range(3):
            first_ref[o, :, pl.ds(k * wide, wide)] = ref[pl.ds(k * rank, rank), :]


def collect_call(order, places, lows, grads, feats):
    groups, (toks, wide) = len(grads), grads[0].shape
    rank = lows[0].shape[1] // 2
    extra = wide - feats
    low_shape, first_shape = (groups, 2 * rank, toks), (groups, rank, 3 * extra)
    return order.call(
        functools.partial(collect_kernel, places),
        "collect_blocks",
        [*lows, *[in_hbm(x) for x in grads]],
        [whole(b.shape) for b in lows]
        + [pl.BlockSpec((toks, extra), lambda i: (0, feats // extra))] * groups,
        [(low_shape, BF16), (first_shape, BF16)],
        [whole(low_shape), whole(first_shape)],
    )


def low_dense_kernel(at_ref, *refs):
    out_ref, sum_ref = refs[-2:]
    groups, both, _ = refs[0].shape
    rank = both // 2
    for o in range(groups):
        total = refs[0][lax.bitwise_xor(at_ref[1], o)].astype(F32)
        for ref in refs[1:-2]:
            total = total + ref[lax.bitwise_xor(at_ref[1], o)].astype(F32)
        for q in range(2):
            at = pl.ds((q * groups + o) * rank, rank)
            sum_ref[at, :] = total[q * rank : (q + 1) * rank]
    out_ref[...] = sum_ref[...].T


def low_dense_call(order, parts):
    groups, both, toks = parts[0].shape
    shape = (toks, groups * both)
    return order.call(
        low_dense_kernel,
        "low_dense",
        parts,
        [whole(parts[0].shape)] * len(parts),
        [(shape, F32)],
        [whole(shape)],
        scratch=[pltpu.VMEM((groups * both, toks), F32)],
    )[0]


def lowrank_hid_kernel(groups, at_ref, index_ref, hid_ref, *rest):
    firsts, out_ref = rest[:2], rest[2]
    top = index_ref.shape[1]
    rank = firsts[0].shape[0] // groups
    wide = jnp.concatenate([dot(hid_ref[...], ref[...], NT) for ref in firsts], axis=1)
    column = pair_column(relative(at_ref, index_ref[...], groups).astype(F32))
    wide = jnp.where(expert_mask(column, wide.shape[1], rank), wide, 0.0)
    out_ref[...] = wide.reshape(wide.shape[0] // top, top, wide.shape[1]).sum(axis=1)


def lowrank_hid_call(order, index, hid, firsts, groups):
    (toks, top), (pairs, units) = index.shape, hid.shape
    half = firsts[0].shape[0]
    steps = 4
    return order.call(
        functools.partial(lowrank_hid_kernel, groups),
        "lowrank_hid",
        [index, in_hbm(hid), *firsts],
        [
            pl.BlockSpec((toks // steps, top), lambda i: (i, 0)),
            pl.BlockSpec((pairs // steps, units), lambda i: (i, 0)),
        ]
        + [whole((half, units))] * 2,
        [((toks, 2 * half), F32)],
        [pl.BlockSpec((toks // steps, 2 * half), lambda i: (i, 0))],
        grid=(steps,),
    )[0]


def second_grad_kernel(places, units, at_ref, got_ref, *refs):
    grads, outs, first_ref = refs[:-3], refs[-3:-1], refs[-1]
    rank, tile = outs[0].shape
    toks = grads[0].shape[0]

    @pl.when(pl.program_id(0) == 0)
    def _():
        total = jnp.zeros((rank, units), F32)
        for source in range(got_ref.shape[0]):
            total = total + got_ref[source, :, pl.ds(0, units)].astype(F32)
        first_ref[...] = total

    totals = [jnp.zeros((rank, tile), F32) for _ in outs]
    for o, grad_ref in zip(places, grads):
        source = lax.bitwise_xor(at_ref[1], o)
        scaled = jnp.concatenate(
            [got_ref[source, :, pl.ds(units + q * toks, toks)] for q in range(2)], axis=0
        )
        value = dot(scaled, grad_ref[...], NN)
        totals = [total + value[q * rank : (q + 1) * rank] for q, total in enumerate(totals)]
    for total, out_ref in zip(totals, outs):
        out_ref[...] = adapter_scale * total


def second_grad_call(order, places, got, grads, units, feats):
    rank, toks = got.shape[1], grads[0].shape[0]
    steps = 4
    tile = feats // steps
    block = pl.BlockSpec((rank, tile), lambda i: (0, i))
    return order.call(
        functools.partial(second_grad_kernel, places, units),
        "second_grad",
        [got, *[in_hbm(x) for x in grads]],
        [whole(got.shape)] + [pl.BlockSpec((toks, tile), lambda i: (0, i))] * len(grads),
        [((rank, feats), F32)] * 2 + [((rank, units), F32)],
        [block] * 2 + [whole((rank, units))],
        grid=(steps,),
    )


def first_grad_kernel(groups, steps, parts, at_ref, index_ref, prob_ref, low_ref, hid_ref, *rest):
    index_all_ref, prob_all_ref, hids = rest[0], rest[1], rest[2 : 2 + parts]
    keep_ref, give_ref, scaled_ref, sum_ref = rest[2 + parts :]
    step = pl.program_id(0)
    top = index_ref.shape[1]
    rank = keep_ref.shape[1]
    low = spread_pairs(low_ref[...], top)
    column = pair_column(relative(at_ref, index_ref[...], groups).astype(F32))
    keep = expert_mask(column, low.shape[1], rank)
    scaled = jnp.where(keep, low * pair_column(prob_ref[...].astype(F32)), 0.0).astype(BF16)
    part = adapter_scale * dot(scaled, hid_ref[...], TN)

    @pl.when(step == 0)
    def _():
        sum_ref[...] = part

    @pl.when(step > 0)
    def _():
        sum_ref[...] += part

    @pl.when(step == steps - 1)
    def _():
        total = hids[0][...]
        for ref in hids[1:]:
            total = total + ref[...]
        toks = total.shape[0]
        place = relative(at_ref, index_all_ref[...], groups)
        prob = prob_all_ref[...].astype(F32)
        expert = iota(total.shape, 1) // rank
        scale = jnp.zeros(total.shape, F32)
        for k in range(top):
            scale = jnp.where(expert == place[:, k : k + 1], prob[:, k : k + 1], scale)
        turned = (total * scale).T.astype(BF16)
        for o in range(groups):
            to = lax.bitwise_xor(at_ref[1], o)
            at, other = o * rank, (groups + o) * rank
            keep_ref[to] = sum_ref[pl.ds(at, rank), :]
            give_ref[to] = sum_ref[pl.ds(other, rank), :].astype(BF16)
            scaled_ref[to, :, pl.ds(0, toks)] = turned[at : at + rank]
            scaled_ref[to, :, pl.ds(toks, toks)] = turned[other : other + rank]


def first_grad_call(order, index, prob, low, hid, hids, groups):
    (toks, top), (pairs, units) = index.shape, hid.shape
    width = low.shape[1]
    steps = 4
    rank = width // groups // 2
    shape, scaled_shape = (groups, rank, units), (groups, rank, 2 * toks)
    return order.call(
        functools.partial(first_grad_kernel, groups, steps, len(hids)),
        "first_grad",
        [index, prob, low, in_hbm(hid), index, prob, *hids],
        [
            pl.BlockSpec((toks // steps, top), lambda i: (i, 0)),
            pl.BlockSpec((toks // steps, top), lambda i: (i, 0)),
            pl.BlockSpec((toks // steps, width), lambda i: (i, 0)),
            pl.BlockSpec((pairs // steps, units), lambda i: (i, 0)),
            whole(index.shape),
            whole(prob.shape),
        ]
        + [whole(x.shape) for x in hids],
        [(shape, F32), (shape, BF16), (scaled_shape, BF16)],
        [whole(shape), whole(shape), whole(scaled_shape)],
        grid=(steps,),
        scratch=[pltpu.VMEM((width, units), F32)],
    )


def first_sum_kernel(at_ref, keep_ref, got_ref, scaled_ref, out_ref):
    units = keep_ref.shape[2]
    out_ref[:, :, pl.ds(0, units)] = (keep_ref[...] + got_ref[...].astype(F32)).astype(BF16)
    out_ref[:, :, pl.ds(units, scaled_ref.shape[2])] = scaled_ref[...]


def first_sum_call(order, keep, got, scaled):
    shape = keep.shape[:2] + (keep.shape[2] + scaled.shape[2],)
    return order.call(
        first_sum_kernel,
        "first_sum",
        [keep, got, scaled],
        [whole(x.shape) for x in (keep, got, scaled)],
        [(shape, BF16)],
        [whole(shape)],
    )[0]


def finish_kernel(count, slots, at_ref, index_all_ref, index_ref, prob_ref, low_ref, hid_ref, *rest):
    firsts, back = rest[:2], rest[2 : 2 + count]
    out_ref, sum_ref, all_ref, place_ref = rest[2 + count :]
    top = index_ref.shape[1]
    toks = index_all_ref.shape[0]
    experts = 2 * count

    @pl.when(pl.program_id(0) == 0)
    def _():
        for o, ref in enumerate(back):
            for q in range(2):
                all_ref[pl.ds((q * count + o) * slots, slots), :] = ref[pl.ds(q * slots, slots), :]
        experts_all = relative(at_ref, index_all_ref[...], count)
        hit = jnp.zeros((toks, experts), F32)
        for k in range(top):
            hit = jnp.where(iota((toks, experts), 1) == experts_all[:, k : k + 1], 1.0, hit)
        before = jnp.where(iota((toks, toks), 0) > iota((toks, toks), 1), 1.0, 0.0).astype(BF16)
        place_ref[...] = dot(before, hit.astype(BF16), NN)

    pairs = hid_ref.shape[0]
    some = index_ref.shape[0]
    column = pair_column(relative(at_ref, index_ref[...], count).astype(F32))
    place = spread_pairs(place_ref[pl.ds(pl.program_id(0) * some, some), :], top)
    mine = iota((pairs, experts), 1) == column.astype(jnp.int32)
    target = column * slots + jnp.sum(jnp.where(mine, place, 0.0), axis=1, keepdims=True)
    low = spread_pairs(low_ref[...], top)
    keep = expert_mask(column, low.shape[1], low.shape[1] // experts)
    low = jnp.where(keep, adapter_scale * low.astype(BF16).astype(F32), 0.0).astype(BF16)
    slot = iota((pairs, experts * slots), 1)
    pick = jnp.where(slot == target.astype(jnp.int32), 1.0, 0.0).astype(BF16)
    half = low.shape[1] // 2
    value = dot(pick, all_ref[...], NN)
    value = value + dot(low[:, :half], firsts[0][...], NN) + dot(low[:, half:], firsts[1][...], NN)
    value = value.astype(BF16).astype(F32)
    out_ref[...] = (value * pair_column(prob_ref[...].astype(F32))).astype(BF16)
    sums = jnp.sum(value * hid_ref[...].astype(F32), axis=1, keepdims=True)
    sums = jnp.where(diagonal(pairs, top), sums, 0.0)
    sum_ref[...] = sums.reshape(some, top, top).sum(axis=1)


def finish_call(order, index, prob, low, hid, firsts, back):
    (toks, top), (pairs, units) = index.shape, hid.shape
    width = low.shape[1]
    both = back[0].shape[0]
    steps = 4
    count = len(back)

    def rows(n, columns):
        return pl.BlockSpec((n // steps, columns), lambda i: (i, 0))

    return order.call(
        functools.partial(finish_kernel, count, both // 2),
        "finish",
        [index, index, prob, low, in_hbm(hid), *firsts, *[in_hbm(x) for x in back]],
        [whole(index.shape), rows(toks, top), rows(toks, top), rows(toks, width), rows(pairs, units)]
        + [whole(firsts[0].shape)] * 2
        + [whole((both, units))] * count,
        [((pairs, units), BF16), ((toks, top), F32)],
        [rows(pairs, units), rows(toks, top)],
        grid=(steps,),
        cost=LONG,
        scratch=[pltpu.VMEM((count * both, units), BF16), pltpu.VMEM((toks, 2 * count), F32)],
    )


def body(grad, hidden, index, weight, down, first, second):
    toks, top = index.shape
    exp_local, units_all, feats = down.shape
    units, rank = first.shape[1:]
    groups, cores, shares = lax.axis_size("ep"), lax.axis_size("sub"), lax.axis_size("rep")
    assert exp_local == 1 and cores == 2 and groups & (groups - 1) == 0
    cap = min(toks, 5 * toks * top // (4 * groups * cores))
    slots = -(-cap // 16) * 16
    pairs = toks * top
    at = jnp.stack([lax.axis_index(name).astype(jnp.int32) for name in ("rep", "ep", "sub")])
    order = Order(at)

    def turn(x, offset):
        return lax.ppermute(x, "rep", [(r, (r + offset) % shares) for r in range(shares)])

    def all_shares(x):
        return [x] + [turn(x, k) for k in range(1, shares)]

    def flip(x, mask):
        return lax.ppermute(x, "ep", [(i, i ^ mask) for i in range(groups)])

    def swap(x):
        return lax.ppermute(x, "sub", [(0, 1), (1, 0)])

    where = ("ep", "sub")

    def exchange(x, axes="ep"):
        return lax.all_to_all(x, axes, split_axis=0, concat_axis=0, tiled=True)

    blocks = {0: pack_call(order, grad, first[0].T, index.T)}

    def fetch(o):
        if o not in blocks:
            last = o & -o
            blocks[o] = flip(fetch(o ^ last), last)
        return blocks[o]

    own_down = load_call(order, down[0])
    downs = [own_down, swap(down[0])]
    seconds = [second[0], swap(second[0])]

    if groups == 8:
        batches = [(0, 1), (2, 4), (6, 3), (5, 7)]
        steps = [("multiply", 0), ("gate", 4), ("multiply", 1), ("total", 0), ("total", 1)]
        steps += [("multiply", 2), ("multiply", 3), ("total", 2)]
        early = {("total", 0): 3, ("multiply", 2): 5}
    else:
        batches = [(o, o + 1) for o in range(0, groups, 2)]
        steps = [("multiply", 0)]
        for i in range(1, len(batches)):
            steps += [("multiply", i), ("total", i - 1)]
        early = {}
    last = len(batches) - 1
    places = [o for batch in batches for o in batch]
    back, lows, shared = {}, [], {}

    def total(i):
        for o, rows in zip(batches[i], share_sum_call(order, shared[i], 2, slots)):
            masks = [o] if o else []
            if i >= last - 1 and o % 2:
                masks = [o - 1, 1] if o > 1 else [1]
            elif o == 4 and groups == 8:
                masks = [2, 6]
            for mask in masks:
                rows = flip(rows, mask)
            back[o] = rows

    for kind, i in steps:
        if (kind, i) in early:
            order.wait([fetch(early[kind, i])])
        if kind == "gate":
            blocks[i] = gate_call(order, [fetch(i)])[0]
        elif kind == "total":
            total(i)
        else:
            *give, keep, low = expert_rows_call(
                order, [fetch(o) for o in batches[i]], seconds, downs, shares, slots
            )
            lows.append(low)
            shared[i] = [keep] + [turn(x, k + 1) for k, x in enumerate(give)]

    hid = hidden.reshape(pairs, units)
    grads = [blocks[o] for o in places]

    low_grad, first_own = collect_call(order, places, lows, grads, feats)
    firsts = [x.reshape(groups * rank, units) for x in (first_own, swap(first_own))]
    low_grad = exchange(low_grad)
    order.wait([back[batches[-2][0]]] + [back[4]] * (groups == 8))
    total(last)
    order.wait([low_grad, back[1], back[2]])
    low_hid = all_shares(lowrank_hid_call(order, index, hid, firsts, groups))
    order.wait([back[batches[-2][1]]])

    low_grad = low_dense_call(order, all_shares(low_grad))
    order.wait([back[batches[-1][0]]])
    keep, give, scaled = first_grad_call(order, index, weight, low_grad, hid, low_hid, groups)

    order.wait([back[batches[-1][1]]])
    got = exchange(first_sum_call(order, keep, swap(give), scaled))
    back = [back[o] for o in range(groups)]
    grad_hidden, sums = finish_call(order, index, weight, low_grad, hid, firsts, back)
    if shares == 2:
        other_sums = turn(sums, 1)
        order.wait([other_sums])
        sums = sums + other_sums
    else:
        sums = lax.psum(sums, "rep")
    second_keep, second_give, first_grad = second_grad_call(
        order, places, got, grads, units, feats
    )
    second_grad = second_keep + swap(second_give)
    return (
        grad_hidden.reshape(toks, top, units),
        sums,
        first_grad.T[None],
        second_grad[None],
    )


def solution(mesh):
    return jax.shard_map(
        body,
        mesh=mesh,
        in_specs=(
            P(("grp", "ep", "sub"), "rep"),
            P(("grp", "ep", "sub"), None, "rep"),
            P(("grp", "ep", "sub"), None),
            P(("grp", "ep", "sub"), None),
            P(("ep", "sub"), None, "rep"),
            P(("grp", "ep", "sub"), "rep", None),
            P(("grp", "ep", "sub"), None, "rep"),
        ),
        out_specs=(
            P(("grp", "ep", "sub"), None, "rep"),
            P(("grp", "ep", "sub"), None),
            P(("grp", "ep", "sub"), "rep", None),
            P(("grp", "ep", "sub"), None, "rep"),
        ),
        check_vma=False,
    )
```

```python
import functools

import jax
import jax.numpy as jnp
from jax import lax
from jax.experimental import pallas as pl
from jax.experimental.pallas import tpu as pltpu
from jax.sharding import PartitionSpec as P

adapter_scale = 2.0
BF16 = jnp.bfloat16
F32 = jnp.float32
NT = (((1,), (1,)), ((), ()))
TN = (((0,), (0,)), ((), ()))
NN = (((1,), (0,)), ((), ()))
SMALL = pl.CostEstimate(flops=1, bytes_accessed=1, transcendentals=0)
LONG = pl.CostEstimate(flops=1, bytes_accessed=2 * 10**7, transcendentals=0)
ANY = pl.BlockSpec(memory_space=pl.ANY)
SMEM = pl.BlockSpec(memory_space=pltpu.SMEM)
VMEM = pl.BlockSpec(memory_space=pltpu.VMEM)


def dot(a, b, dims):
    return lax.dot_general(a, b, dims, preferred_element_type=F32)


def iota(shape, axis):
    return lax.broadcasted_iota(jnp.int32, shape, axis)


def whole(shape):
    return pl.BlockSpec(shape, lambda *_: (0,) * len(shape))


def in_hbm(x):
    return pltpu.with_memory_space_constraint(x, pltpu.HBM)


class Order:
    def __init__(self, at):
        self.at, self.last = at, []

    def wait(self, arrays):
        self.last = self.last + list(arrays)

    def call(self, kernel, name, arrays, in_specs, outs, out_specs, grid=(1,), scratch=(), mib=16, cost=SMALL, **more):
        count, last = 1 + len(arrays), len(self.last)

        def ordered(*refs):
            here = count + last + len(outs)
            kernel(*refs[:count], *refs[count + last : here], *refs[here + 1 :])

        *result, token = pl.pallas_call(
            ordered,
            grid=grid,
            in_specs=[SMEM, *in_specs] + [ANY] * last,
            out_specs=[*out_specs, ANY],
            scratch_shapes=scratch,
            out_shape=[jax.ShapeDtypeStruct(*o) if isinstance(o, tuple) else o for o in outs]
            + [pltpu.HBM((8, 128), F32)],
            compiler_params=pltpu.CompilerParams(vmem_limit_bytes=mib * 2**20),
            cost_estimate=cost,
            name=name,
            **more,
        )(self.at, *arrays, *self.last)
        self.last = [in_hbm(token)]
        return result


def relative(at_ref, index, groups):
    o = lax.bitwise_xor(lax.shift_right_logical(index, 1), at_ref[1])
    q = lax.bitwise_xor(lax.bitwise_and(index, 1), at_ref[2])
    return q * groups + o


def spread_pairs(dense, top):
    toks, width = dense.shape
    return jnp.broadcast_to(dense[:, None, :], (toks, top, width)).reshape(toks * top, width)


def diagonal(pairs, top):
    return iota((pairs, top), 1) == lax.bitwise_and(iota((pairs, top), 0), top - 1)


def pair_column(table):
    toks, top = table.shape
    wide = spread_pairs(table, top)
    return jnp.sum(jnp.where(diagonal(toks * top, top), wide, 0.0), axis=1, keepdims=True)


def expert_mask(column, width, rank):
    return iota((column.shape[0], width), 1) // rank == column.astype(jnp.int32)


def pack_kernel(at_ref, grad_ref, first_ref, index_ref, out_ref):
    toks, feats = grad_ref.shape
    rank = first_ref.shape[0]
    extra = out_ref.shape[1] - feats
    out_ref[:, pl.ds(0, feats)] = grad_ref[...]
    for k in range(3):
        piece = first_ref[:, pl.ds(k * extra, extra)]
        out_ref[pl.ds(k * rank, rank), pl.ds(feats, extra)] = piece
    top = index_ref.shape[0]
    out_ref[pl.ds(3 * rank, toks - 3 * rank), pl.ds(feats, extra)] = jnp.full(
        (toks - 3 * rank, extra), -1.0, BF16
    )
    routes = index_ref[...].astype(F32)
    routes = jnp.concatenate([routes, jnp.full((16 - top, toks), -1.0, F32)], axis=0)
    out_ref[pl.ds(3 * rank, 16), pl.ds(feats, toks)] = routes.astype(BF16)


def pack_call(order, grad, first, index):
    (toks, feats), (rank, units) = grad.shape, first.shape
    shape = (toks, feats + units // 3)
    return order.call(
        pack_kernel,
        "pack_block",
        [in_hbm(grad), first, index],
        [whole(grad.shape), whole(first.shape), whole(index.shape)],
        [(shape, BF16)],
        [whole(shape)],
    )[0]


def gate_kernel(at_ref, *refs):
    pass


def gate_call(order, arrays):
    return order.call(
        gate_kernel,
        "gate",
        arrays,
        [ANY] * len(arrays),
        [(x.shape, x.dtype) for x in arrays],
        [ANY] * len(arrays),
        input_output_aliases={1 + k: k for k in range(len(arrays))},
    )


def load_kernel(at_ref, down_ref, out_ref, sems):
    parts = sems.shape[0]
    rows = down_ref.shape[0] // parts
    copies = [
        pltpu.make_async_copy(
            down_ref.at[pl.ds(k * rows, rows), :], out_ref.at[pl.ds(k * rows, rows), :], sems.at[k]
        )
        for k in range(parts)
    ]
    for copy in copies:
        copy.start()
    for copy in copies:
        copy.wait()


def load_call(order, down):
    return order.call(
        load_kernel,
        "load_matrix",
        [in_hbm(down)],
        [ANY],
        [pltpu.VMEM(down.shape, down.dtype)],
        [VMEM],
        grid=(),
        scratch=[pltpu.SemaphoreType.DMA((4,))],
    )[0]


def expert_rows_kernel(slots, tiles, shares, batch, route_row, at_ref, *rest):
    grads, seconds, downs = rest[:batch], rest[batch : batch + 2], rest[batch + 2 : batch + 4]
    *outs, low_ref = rest[batch + 4 : batch + 5 + shares]
    block_ref, turned_ref, block_sems = rest[batch + 5 + shares :]
    tile = downs[0].shape[0] // shares // tiles
    feats = turned_ref.shape[1]
    toks = block_ref.shape[1]
    blocks = [
        pltpu.make_async_copy(ref, block_ref.at[k], block_sems.at[k]) for k, ref in enumerate(grads)
    ]
    for copy in blocks:
        copy.start()

    before = jnp.where(iota((toks, toks), 0) < iota((toks, toks), 1), 1.0, 0.0).astype(BF16)
    columns = turned_ref.shape[2]
    slot = iota((columns, batch * toks), 0).astype(F32)
    second = jnp.concatenate([ref[...] for ref in seconds], axis=0)
    routes = []
    for k in range(batch):
        blocks[k].wait()
        routes.append(block_ref[k, pl.ds(route_row, 16), pl.ds(feats, toks)].astype(F32))
    grad = block_ref[:, :, pl.ds(0, feats)].reshape(batch * toks, feats)
    for q in range(2):
        expert = at_ref[1] * 2 + lax.bitwise_xor(at_ref[2], q)
        targets = []
        for k in range(batch):
            hits = jnp.where(routes[k] == expert.astype(F32), 1.0, 0.0)
            mine = jnp.max(hits, axis=0, keepdims=True)
            pos = dot(jnp.broadcast_to(mine, (16, toks)).astype(BF16), before, NN)[:1]
            targets.append(jnp.where(mine > 0.0, pos + float(k * slots), -1.0))
        pick = jnp.where(slot == jnp.concatenate(targets, axis=1), 1.0, 0.0)
        turned_ref[q] = dot(grad, pick.T.astype(BF16), TN).astype(BF16)
    low = dot(second, grad, NT).astype(BF16)
    for k in range(batch):
        low_ref[k] = low[:, k * toks : (k + 1) * toks]

    rows = batch * slots
    for k in range(shares):
        share = lax.rem(at_ref[0] + k + 1, shares)
        for q in range(2):
            for t in range(tiles):
                row = pl.multiple_of((share * tiles + t) * tile, tile)
                value = dot(downs[q][pl.ds(row, tile), :], turned_ref[q], NN)
                outs[k][pl.ds(q * rows, rows), pl.ds(t * tile, tile)] = value.T[:rows].astype(BF16)


def expert_rows_call(order, grads, seconds, downs, shares, slots):
    batch, (toks, wide) = len(grads), grads[0].shape
    rank, feats = seconds[0].shape
    units = downs[0].shape[0] // shares
    rows = 2 * batch * slots
    return order.call(
        functools.partial(expert_rows_kernel, slots, 3, shares, batch, 3 * rank),
        "expert_rows",
        [*grads, *seconds, *[pltpu.with_memory_space_constraint(x, pltpu.VMEM) for x in downs]],
        [ANY] * batch + [VMEM] * 4,
        [((rows, units), BF16)] * shares + [((batch, 2 * rank, toks), BF16)],
        [VMEM] * (shares + 1),
        grid=(),
        scratch=[
            pltpu.VMEM((batch, toks, wide), BF16),
            pltpu.VMEM((2, feats, -(-batch * slots // 128) * 128), BF16),
            pltpu.SemaphoreType.DMA((batch,)),
        ],
    )


def share_sum_kernel(parts, slots, at_ref, *refs):
    outs = refs[parts:]
    for k, out_ref in enumerate(outs):
        for q in range(2):
            at = pl.ds((q * len(outs) + k) * slots, slots)
            total = refs[0][at, :].astype(F32)
            for part in refs[1:parts]:
                total = total + part[at, :].astype(F32)
            out_ref[pl.ds(q * slots, slots), :] = total.astype(BF16)


def share_sum_call(order, parts, batch, slots):
    rows, units = parts[0].shape
    shape = (2 * slots, units)
    return order.call(
        functools.partial(share_sum_kernel, len(parts), slots),
        "share_sum",
        parts,
        [whole((rows, units))] * len(parts),
        [(shape, BF16)] * batch,
        [whole(shape)] * batch,
    )


def collect_kernel(places, at_ref, *refs):
    low_ref, first_ref = refs[-2:]
    rank = first_ref.shape[1]
    at = 0
    lows = len(refs) - 2 - len(places)
    for ref in refs[:lows]:
        for k in range(ref.shape[0]):
            low_ref[lax.bitwise_xor(at_ref[1], places[at])] = ref[k]
            at += 1
    for o, ref in zip(places, refs[lows:-2]):
        wide = ref.shape[1]
        for k in range(3):
            first_ref[o, :, pl.ds(k * wide, wide)] = ref[pl.ds(k * rank, rank), :]


def collect_call(order, places, lows, grads, feats):
    groups, (toks, wide) = len(grads), grads[0].shape
    rank = lows[0].shape[1] // 2
    extra = wide - feats
    low_shape, first_shape = (groups, 2 * rank, toks), (groups, rank, 3 * extra)
    return order.call(
        functools.partial(collect_kernel, places),
        "collect_blocks",
        [*lows, *[in_hbm(x) for x in grads]],
        [whole(b.shape) for b in lows]
        + [pl.BlockSpec((toks, extra), lambda i: (0, feats // extra))] * groups,
        [(low_shape, BF16), (first_shape, BF16)],
        [whole(low_shape), whole(first_shape)],
    )


def low_dense_kernel(at_ref, *refs):
    out_ref, sum_ref = refs[-2:]
    groups, both, _ = refs[0].shape
    rank = both // 2
    for o in range(groups):
        total = refs[0][lax.bitwise_xor(at_ref[1], o)].astype(F32)
        for ref in refs[1:-2]:
            total = total + ref[lax.bitwise_xor(at_ref[1], o)].astype(F32)
        for q in range(2):
            at = pl.ds((q * groups + o) * rank, rank)
            sum_ref[at, :] = total[q * rank : (q + 1) * rank]
    out_ref[...] = sum_ref[...].T


def low_dense_call(order, parts):
    groups, both, toks = parts[0].shape
    shape = (toks, groups * both)
    return order.call(
        low_dense_kernel,
        "low_dense",
        parts,
        [whole(parts[0].shape)] * len(parts),
        [(shape, F32)],
        [whole(shape)],
        scratch=[pltpu.VMEM((groups * both, toks), F32)],
    )[0]


def lowrank_hid_kernel(groups, at_ref, index_ref, hid_ref, *rest):
    firsts, out_ref = rest[:2], rest[2]
    top = index_ref.shape[1]
    rank = firsts[0].shape[0] // groups
    wide = jnp.concatenate([dot(hid_ref[...], ref[...], NT) for ref in firsts], axis=1)
    column = pair_column(relative(at_ref, index_ref[...], groups).astype(F32))
    wide = jnp.where(expert_mask(column, wide.shape[1], rank), wide, 0.0)
    out_ref[...] = wide.reshape(wide.shape[0] // top, top, wide.shape[1]).sum(axis=1)


def lowrank_hid_call(order, index, hid, firsts, groups):
    (toks, top), (pairs, units) = index.shape, hid.shape
    half = firsts[0].shape[0]
    steps = 4
    return order.call(
        functools.partial(lowrank_hid_kernel, groups),
        "lowrank_hid",
        [index, in_hbm(hid), *firsts],
        [
            pl.BlockSpec((toks // steps, top), lambda i: (i, 0)),
            pl.BlockSpec((pairs // steps, units), lambda i: (i, 0)),
        ]
        + [whole((half, units))] * 2,
        [((toks, 2 * half), F32)],
        [pl.BlockSpec((toks // steps, 2 * half), lambda i: (i, 0))],
        grid=(steps,),
    )[0]


def second_grad_kernel(places, units, at_ref, got_ref, *refs):
    grads, outs, first_ref = refs[:-3], refs[-3:-1], refs[-1]
    rank, tile = outs[0].shape
    toks = grads[0].shape[0]

    @pl.when(pl.program_id(0) == 0)
    def _():
        total = jnp.zeros((rank, units), F32)
        for source in range(got_ref.shape[0]):
            total = total + got_ref[source, :, pl.ds(0, units)].astype(F32)
        first_ref[...] = total

    totals = [jnp.zeros((rank, tile), F32) for _ in outs]
    for o, grad_ref in zip(places, grads):
        source = lax.bitwise_xor(at_ref[1], o)
        scaled = jnp.concatenate(
            [got_ref[source, :, pl.ds(units + q * toks, toks)] for q in range(2)], axis=0
        )
        value = dot(scaled, grad_ref[...], NN)
        totals = [total + value[q * rank : (q + 1) * rank] for q, total in enumerate(totals)]
    for total, out_ref in zip(totals, outs):
        out_ref[...] = adapter_scale * total


def second_grad_call(order, places, got, grads, units, feats):
    rank, toks = got.shape[1], grads[0].shape[0]
    steps = 4
    tile = feats // steps
    block = pl.BlockSpec((rank, tile), lambda i: (0, i))
    return order.call(
        functools.partial(second_grad_kernel, places, units),
        "second_grad",
        [got, *[in_hbm(x) for x in grads]],
        [whole(got.shape)] + [pl.BlockSpec((toks, tile), lambda i: (0, i))] * len(grads),
        [((rank, feats), F32)] * 2 + [((rank, units), F32)],
        [block] * 2 + [whole((rank, units))],
        grid=(steps,),
    )


def first_grad_kernel(groups, steps, parts, at_ref, index_ref, prob_ref, low_ref, hid_ref, *rest):
    index_all_ref, prob_all_ref, hids = rest[0], rest[1], rest[2 : 2 + parts]
    keep_ref, give_ref, scaled_ref, sum_ref = rest[2 + parts :]
    step = pl.program_id(0)
    top = index_ref.shape[1]
    rank = keep_ref.shape[1]
    low = spread_pairs(low_ref[...], top)
    column = pair_column(relative(at_ref, index_ref[...], groups).astype(F32))
    keep = expert_mask(column, low.shape[1], rank)
    scaled = jnp.where(keep, low * pair_column(prob_ref[...].astype(F32)), 0.0).astype(BF16)
    part = adapter_scale * dot(scaled, hid_ref[...], TN)

    @pl.when(step == 0)
    def _():
        sum_ref[...] = part

    @pl.when(step > 0)
    def _():
        sum_ref[...] += part

    @pl.when(step == steps - 1)
    def _():
        total = hids[0][...]
        for ref in hids[1:]:
            total = total + ref[...]
        toks = total.shape[0]
        place = relative(at_ref, index_all_ref[...], groups)
        prob = prob_all_ref[...].astype(F32)
        expert = iota(total.shape, 1) // rank
        scale = jnp.zeros(total.shape, F32)
        for k in range(top):
            scale = jnp.where(expert == place[:, k : k + 1], prob[:, k : k + 1], scale)
        turned = (total * scale).T.astype(BF16)
        for o in range(groups):
            to = lax.bitwise_xor(at_ref[1], o)
            at, other = o * rank, (groups + o) * rank
            keep_ref[to] = sum_ref[pl.ds(at, rank), :]
            give_ref[to] = sum_ref[pl.ds(other, rank), :].astype(BF16)
            scaled_ref[to, :, pl.ds(0, toks)] = turned[at : at + rank]
            scaled_ref[to, :, pl.ds(toks, toks)] = turned[other : other + rank]


def first_grad_call(order, index, prob, low, hid, hids, groups):
    (toks, top), (pairs, units) = index.shape, hid.shape
    width = low.shape[1]
    steps = 4
    rank = width // groups // 2
    shape, scaled_shape = (groups, rank, units), (groups, rank, 2 * toks)
    return order.call(
        functools.partial(first_grad_kernel, groups, steps, len(hids)),
        "first_grad",
        [index, prob, low, in_hbm(hid), index, prob, *hids],
        [
            pl.BlockSpec((toks // steps, top), lambda i: (i, 0)),
            pl.BlockSpec((toks // steps, top), lambda i: (i, 0)),
            pl.BlockSpec((toks // steps, width), lambda i: (i, 0)),
            pl.BlockSpec((pairs // steps, units), lambda i: (i, 0)),
            whole(index.shape),
            whole(prob.shape),
        ]
        + [whole(x.shape) for x in hids],
        [(shape, F32), (shape, BF16), (scaled_shape, BF16)],
        [whole(shape), whole(shape), whole(scaled_shape)],
        grid=(steps,),
        scratch=[pltpu.VMEM((width, units), F32)],
    )


def first_sum_kernel(at_ref, keep_ref, got_ref, scaled_ref, out_ref):
    units = keep_ref.shape[2]
    out_ref[:, :, pl.ds(0, units)] = (keep_ref[...] + got_ref[...].astype(F32)).astype(BF16)
    out_ref[:, :, pl.ds(units, scaled_ref.shape[2])] = scaled_ref[...]


def first_sum_call(order, keep, got, scaled):
    shape = keep.shape[:2] + (keep.shape[2] + scaled.shape[2],)
    return order.call(
        first_sum_kernel,
        "first_sum",
        [keep, got, scaled],
        [whole(x.shape) for x in (keep, got, scaled)],
        [(shape, BF16)],
        [whole(shape)],
    )[0]


def finish_kernel(count, slots, at_ref, index_all_ref, index_ref, prob_ref, low_ref, hid_ref, *rest):
    firsts, back = rest[:2], rest[2 : 2 + count]
    out_ref, sum_ref, all_ref, place_ref = rest[2 + count :]
    top = index_ref.shape[1]
    toks = index_all_ref.shape[0]
    experts = 2 * count

    @pl.when(pl.program_id(0) == 0)
    def _():
        for o, ref in enumerate(back):
            for q in range(2):
                all_ref[pl.ds((q * count + o) * slots, slots), :] = ref[pl.ds(q * slots, slots), :]
        experts_all = relative(at_ref, index_all_ref[...], count)
        hit = jnp.zeros((toks, experts), F32)
        for k in range(top):
            hit = jnp.where(iota((toks, experts), 1) == experts_all[:, k : k + 1], 1.0, hit)
        before = jnp.where(iota((toks, toks), 0) > iota((toks, toks), 1), 1.0, 0.0).astype(BF16)
        place_ref[...] = dot(before, hit.astype(BF16), NN)

    pairs = hid_ref.shape[0]
    some = index_ref.shape[0]
    column = pair_column(relative(at_ref, index_ref[...], count).astype(F32))
    place = spread_pairs(place_ref[pl.ds(pl.program_id(0) * some, some), :], top)
    mine = iota((pairs, experts), 1) == column.astype(jnp.int32)
    target = column * slots + jnp.sum(jnp.where(mine, place, 0.0), axis=1, keepdims=True)
    low = spread_pairs(low_ref[...], top)
    keep = expert_mask(column, low.shape[1], low.shape[1] // experts)
    low = jnp.where(keep, adapter_scale * low.astype(BF16).astype(F32), 0.0).astype(BF16)
    slot = iota((pairs, experts * slots), 1)
    pick = jnp.where(slot == target.astype(jnp.int32), 1.0, 0.0).astype(BF16)
    half = low.shape[1] // 2
    value = dot(pick, all_ref[...], NN)
    value = value + dot(low[:, :half], firsts[0][...], NN) + dot(low[:, half:], firsts[1][...], NN)
    value = value.astype(BF16).astype(F32)
    out_ref[...] = (value * pair_column(prob_ref[...].astype(F32))).astype(BF16)
    sums = jnp.sum(value * hid_ref[...].astype(F32), axis=1, keepdims=True)
    sums = jnp.where(diagonal(pairs, top), sums, 0.0)
    sum_ref[...] = sums.reshape(some, top, top).sum(axis=1)


def finish_call(order, index, prob, low, hid, firsts, back):
    (toks, top), (pairs, units) = index.shape, hid.shape
    width = low.shape[1]
    both = back[0].shape[0]
    steps = 4
    count = len(back)

    def rows(n, columns):
        return pl.BlockSpec((n // steps, columns), lambda i: (i, 0))

    return order.call(
        functools.partial(finish_kernel, count, both // 2),
        "finish",
        [index, index, prob, low, in_hbm(hid), *firsts, *[in_hbm(x) for x in back]],
        [whole(index.shape), rows(toks, top), rows(toks, top), rows(toks, width), rows(pairs, units)]
        + [whole(firsts[0].shape)] * 2
        + [whole((both, units))] * count,
        [((pairs, units), BF16), ((toks, top), F32)],
        [rows(pairs, units), rows(toks, top)],
        grid=(steps,),
        cost=LONG,
        scratch=[pltpu.VMEM((count * both, units), BF16), pltpu.VMEM((toks, 2 * count), F32)],
    )


def body(grad, hidden, index, weight, down, first, second):
    toks, top = index.shape
    exp_local, units_all, feats = down.shape
    units, rank = first.shape[1:]
    groups, cores, shares = lax.axis_size("ep"), lax.axis_size("sub"), lax.axis_size("rep")
    assert exp_local == 1 and cores == 2 and groups & (groups - 1) == 0
    cap = min(toks, 5 * toks * top // (4 * groups * cores))
    slots = -(-cap // 16) * 16
    pairs = toks * top
    at = jnp.stack([lax.axis_index(name).astype(jnp.int32) for name in ("rep", "ep", "sub")])
    order = Order(at)

    def turn(x, offset):
        return lax.ppermute(x, "rep", [(r, (r + offset) % shares) for r in range(shares)])

    def all_shares(x):
        return [x] + [turn(x, k) for k in range(1, shares)]

    def flip(x, mask):
        return lax.ppermute(x, "ep", [(i, i ^ mask) for i in range(groups)])

    def swap(x):
        return lax.ppermute(x, "sub", [(0, 1), (1, 0)])

    where = ("ep", "sub")

    def exchange(x, axes="ep"):
        return lax.all_to_all(x, axes, split_axis=0, concat_axis=0, tiled=True)

    blocks = {0: pack_call(order, grad, first[0].T, index.T)}

    def fetch(o):
        if o not in blocks:
            last = o & -o
            blocks[o] = flip(fetch(o ^ last), last)
        return blocks[o]

    own_down = load_call(order, down[0])
    downs = [own_down, swap(down[0])]
    seconds = [second[0], swap(second[0])]

    if groups == 8:
        batches = [(0, 1), (2, 4), (6, 3), (5, 7)]
        steps = [("multiply", 0), ("gate", 4), ("multiply", 1), ("total", 0), ("total", 1)]
        steps += [("multiply", 2), ("multiply", 3), ("total", 2)]
        early = {("total", 0): 3, ("multiply", 2): 5}
    else:
        batches = [(o, o + 1) for o in range(0, groups, 2)]
        steps = [("multiply", 0)]
        for i in range(1, len(batches)):
            steps += [("multiply", i), ("total", i - 1)]
        early = {}
    last = len(batches) - 1
    places = [o for batch in batches for o in batch]
    back, lows, shared = {}, [], {}

    def total(i):
        for o, rows in zip(batches[i], share_sum_call(order, shared[i], 2, slots)):
            masks = [o] if o else []
            if i >= last - 1 and o % 2:
                masks = [o - 1, 1] if o > 1 else [1]
            for mask in masks:
                rows = flip(rows, mask)
            back[o] = rows

    for kind, i in steps:
        if (kind, i) in early:
            order.wait([fetch(early[kind, i])] + ([back[4]] if kind == "multiply" else []))
        if kind == "gate":
            blocks[i] = gate_call(order, [fetch(i)])[0]
        elif kind == "total":
            total(i)
        else:
            *give, keep, low = expert_rows_call(
                order, [fetch(o) for o in batches[i]], seconds, downs, shares, slots
            )
            lows.append(low)
            shared[i] = [keep] + [turn(x, k + 1) for k, x in enumerate(give)]

    hid = hidden.reshape(pairs, units)
    grads = [blocks[o] for o in places]

    low_grad, first_own = collect_call(order, places, lows, grads, feats)
    firsts = [x.reshape(groups * rank, units) for x in (first_own, swap(first_own))]
    low_grad = exchange(low_grad)
    order.wait([back[batches[-2][0]]])
    total(last)
    order.wait([low_grad, back[1], back[2]])
    low_hid = all_shares(lowrank_hid_call(order, index, hid, firsts, groups))
    order.wait([back[batches[-2][1]]])

    low_grad = low_dense_call(order, all_shares(low_grad))
    order.wait([back[batches[-1][0]]])
    keep, give, scaled = first_grad_call(order, index, weight, low_grad, hid, low_hid, groups)

    order.wait([back[batches[-1][1]]])
    got = exchange(first_sum_call(order, keep, swap(give), scaled))
    back = [back[o] for o in range(groups)]
    grad_hidden, sums = finish_call(order, index, weight, low_grad, hid, firsts, back)
    if shares == 2:
        other_sums = turn(sums, 1)
        order.wait([other_sums])
        sums = sums + other_sums
    else:
        sums = lax.psum(sums, "rep")
    second_keep, second_give, first_grad = second_grad_call(
        order, places, got, grads, units, feats
    )
    second_grad = second_keep + swap(second_give)
    return (
        grad_hidden.reshape(toks, top, units),
        sums,
        first_grad.T[None],
        second_grad[None],
    )


def solution(mesh):
    return jax.shard_map(
        body,
        mesh=mesh,
        in_specs=(
            P(("grp", "ep", "sub"), "rep"),
            P(("grp", "ep", "sub"), None, "rep"),
            P(("grp", "ep", "sub"), None),
            P(("grp", "ep", "sub"), None),
            P(("ep", "sub"), None, "rep"),
            P(("grp", "ep", "sub"), "rep", None),
            P(("grp", "ep", "sub"), None, "rep"),
        ),
        out_specs=(
            P(("grp", "ep", "sub"), None, "rep"),
            P(("grp", "ep", "sub"), None),
            P(("grp", "ep", "sub"), "rep", None),
            P(("grp", "ep", "sub"), None, "rep"),
        ),
        check_vma=False,
    )
```

```python
import functools

import jax
import jax.numpy as jnp
from jax import lax
from jax.experimental import pallas as pl
from jax.experimental.pallas import tpu as pltpu
from jax.sharding import PartitionSpec as P

adapter_scale = 2.0
BF16 = jnp.bfloat16
F32 = jnp.float32
NT = (((1,), (1,)), ((), ()))
TN = (((0,), (0,)), ((), ()))
NN = (((1,), (0,)), ((), ()))
SMALL = pl.CostEstimate(flops=1, bytes_accessed=1, transcendentals=0)
LONG = pl.CostEstimate(flops=1, bytes_accessed=2 * 10**7, transcendentals=0)
ANY = pl.BlockSpec(memory_space=pl.ANY)
SMEM = pl.BlockSpec(memory_space=pltpu.SMEM)
VMEM = pl.BlockSpec(memory_space=pltpu.VMEM)


def dot(a, b, dims):
    return lax.dot_general(a, b, dims, preferred_element_type=F32)


def iota(shape, axis):
    return lax.broadcasted_iota(jnp.int32, shape, axis)


def whole(shape):
    return pl.BlockSpec(shape, lambda *_: (0,) * len(shape))


def in_hbm(x):
    return pltpu.with_memory_space_constraint(x, pltpu.HBM)


class Order:
    def __init__(self, at):
        self.at, self.last = at, []

    def wait(self, arrays):
        self.last = self.last + list(arrays)

    def call(self, kernel, name, arrays, in_specs, outs, out_specs, grid=(1,), scratch=(), mib=16, cost=SMALL, **more):
        count, last = 1 + len(arrays), len(self.last)

        def ordered(*refs):
            here = count + last + len(outs)
            kernel(*refs[:count], *refs[count + last : here], *refs[here + 1 :])

        *result, token = pl.pallas_call(
            ordered,
            grid=grid,
            in_specs=[SMEM, *in_specs] + [ANY] * last,
            out_specs=[*out_specs, ANY],
            scratch_shapes=scratch,
            out_shape=[jax.ShapeDtypeStruct(*o) if isinstance(o, tuple) else o for o in outs]
            + [pltpu.HBM((8, 128), F32)],
            compiler_params=pltpu.CompilerParams(vmem_limit_bytes=mib * 2**20),
            cost_estimate=cost,
            name=name,
            **more,
        )(self.at, *arrays, *self.last)
        self.last = [in_hbm(token)]
        return result


def relative(at_ref, index, groups):
    o = lax.bitwise_xor(lax.shift_right_logical(index, 1), at_ref[1])
    q = lax.bitwise_xor(lax.bitwise_and(index, 1), at_ref[2])
    return q * groups + o


def spread_pairs(dense, top):
    toks, width = dense.shape
    return jnp.broadcast_to(dense[:, None, :], (toks, top, width)).reshape(toks * top, width)


def diagonal(pairs, top):
    return iota((pairs, top), 1) == lax.bitwise_and(iota((pairs, top), 0), top - 1)


def pair_column(table):
    toks, top = table.shape
    wide = spread_pairs(table, top)
    return jnp.sum(jnp.where(diagonal(toks * top, top), wide, 0.0), axis=1, keepdims=True)


def expert_mask(column, width, rank):
    return iota((column.shape[0], width), 1) // rank == column.astype(jnp.int32)


def pack_kernel(at_ref, grad_ref, first_ref, index_ref, out_ref):
    toks, feats = grad_ref.shape
    rank = first_ref.shape[0]
    extra = out_ref.shape[1] - feats
    out_ref[:, pl.ds(0, feats)] = grad_ref[...]
    for k in range(3):
        piece = first_ref[:, pl.ds(k * extra, extra)]
        out_ref[pl.ds(k * rank, rank), pl.ds(feats, extra)] = piece
    top = index_ref.shape[0]
    out_ref[pl.ds(3 * rank, toks - 3 * rank), pl.ds(feats, extra)] = jnp.full(
        (toks - 3 * rank, extra), -1.0, BF16
    )
    routes = index_ref[...].astype(F32)
    routes = jnp.concatenate([routes, jnp.full((16 - top, toks), -1.0, F32)], axis=0)
    out_ref[pl.ds(3 * rank, 16), pl.ds(feats, toks)] = routes.astype(BF16)


def pack_call(order, grad, first, index):
    (toks, feats), (rank, units) = grad.shape, first.shape
    shape = (toks, feats + units // 3)
    return order.call(
        pack_kernel,
        "pack_block",
        [in_hbm(grad), first, index],
        [whole(grad.shape), whole(first.shape), whole(index.shape)],
        [(shape, BF16)],
        [whole(shape)],
    )[0]


def gate_kernel(at_ref, *refs):
    pass


def gate_call(order, arrays):
    return order.call(
        gate_kernel,
        "gate",
        arrays,
        [ANY] * len(arrays),
        [(x.shape, x.dtype) for x in arrays],
        [ANY] * len(arrays),
        input_output_aliases={1 + k: k for k in range(len(arrays))},
    )


def load_kernel(at_ref, down_ref, out_ref, sems):
    parts = sems.shape[0]
    rows = down_ref.shape[0] // parts
    copies = [
        pltpu.make_async_copy(
            down_ref.at[pl.ds(k * rows, rows), :], out_ref.at[pl.ds(k * rows, rows), :], sems.at[k]
        )
        for k in range(parts)
    ]
    for copy in copies:
        copy.start()
    for copy in copies:
        copy.wait()


def load_call(order, down):
    return order.call(
        load_kernel,
        "load_matrix",
        [in_hbm(down)],
        [ANY],
        [pltpu.VMEM(down.shape, down.dtype)],
        [VMEM],
        grid=(),
        scratch=[pltpu.SemaphoreType.DMA((4,))],
    )[0]


def expert_rows_kernel(slots, tiles, shares, batch, route_row, at_ref, *rest):
    grads, seconds, downs = rest[:batch], rest[batch : batch + 2], rest[batch + 2 : batch + 4]
    *outs, low_ref = rest[batch + 4 : batch + 5 + shares]
    block_ref, turned_ref, block_sems = rest[batch + 5 + shares :]
    tile = downs[0].shape[0] // shares // tiles
    feats = turned_ref.shape[1]
    toks = block_ref.shape[1]
    blocks = [
        pltpu.make_async_copy(ref, block_ref.at[k], block_sems.at[k]) for k, ref in enumerate(grads)
    ]
    for copy in blocks:
        copy.start()

    before = jnp.where(iota((toks, toks), 0) < iota((toks, toks), 1), 1.0, 0.0).astype(BF16)
    columns = turned_ref.shape[2]
    slot = iota((columns, batch * toks), 0).astype(F32)
    second = jnp.concatenate([ref[...] for ref in seconds], axis=0)
    routes = []
    for k in range(batch):
        blocks[k].wait()
        routes.append(block_ref[k, pl.ds(route_row, 16), pl.ds(feats, toks)].astype(F32))
    grad = block_ref[:, :, pl.ds(0, feats)].reshape(batch * toks, feats)
    for q in range(2):
        expert = at_ref[1] * 2 + lax.bitwise_xor(at_ref[2], q)
        targets = []
        for k in range(batch):
            hits = jnp.where(routes[k] == expert.astype(F32), 1.0, 0.0)
            mine = jnp.max(hits, axis=0, keepdims=True)
            pos = dot(jnp.broadcast_to(mine, (16, toks)).astype(BF16), before, NN)[:1]
            targets.append(jnp.where(mine > 0.0, pos + float(k * slots), -1.0))
        pick = jnp.where(slot == jnp.concatenate(targets, axis=1), 1.0, 0.0)
        turned_ref[q] = dot(grad, pick.T.astype(BF16), TN).astype(BF16)
    low = dot(second, grad, NT).astype(BF16)
    for k in range(batch):
        low_ref[k] = low[:, k * toks : (k + 1) * toks]

    rows = batch * slots
    for k in range(shares):
        share = lax.rem(at_ref[0] + k + 1, shares)
        for q in range(2):
            for t in range(tiles):
                row = pl.multiple_of((share * tiles + t) * tile, tile)
                value = dot(downs[q][pl.ds(row, tile), :], turned_ref[q], NN)
                outs[k][pl.ds(q * rows, rows), pl.ds(t * tile, tile)] = value.T[:rows].astype(BF16)


def expert_rows_call(order, grads, seconds, downs, shares, slots):
    batch, (toks, wide) = len(grads), grads[0].shape
    rank, feats = seconds[0].shape
    units = downs[0].shape[0] // shares
    rows = 2 * batch * slots
    return order.call(
        functools.partial(expert_rows_kernel, slots, 3, shares, batch, 3 * rank),
        "expert_rows",
        [*grads, *seconds, *[pltpu.with_memory_space_constraint(x, pltpu.VMEM) for x in downs]],
        [ANY] * batch + [VMEM] * 4,
        [((rows, units), BF16)] * shares + [((batch, 2 * rank, toks), BF16)],
        [VMEM] * (shares + 1),
        grid=(),
        scratch=[
            pltpu.VMEM((batch, toks, wide), BF16),
            pltpu.VMEM((2, feats, -(-batch * slots // 128) * 128), BF16),
            pltpu.SemaphoreType.DMA((batch,)),
        ],
    )


def share_sum_kernel(parts, slots, at_ref, *refs):
    outs = refs[parts:]
    for k, out_ref in enumerate(outs):
        for q in range(2):
            at = pl.ds((q * len(outs) + k) * slots, slots)
            total = refs[0][at, :].astype(F32)
            for part in refs[1:parts]:
                total = total + part[at, :].astype(F32)
            out_ref[pl.ds(q * slots, slots), :] = total.astype(BF16)


def share_sum_call(order, parts, batch, slots):
    rows, units = parts[0].shape
    shape = (2 * slots, units)
    return order.call(
        functools.partial(share_sum_kernel, len(parts), slots),
        "share_sum",
        parts,
        [whole((rows, units))] * len(parts),
        [(shape, BF16)] * batch,
        [whole(shape)] * batch,
    )


def collect_kernel(places, at_ref, *refs):
    low_ref, first_ref = refs[-2:]
    rank = first_ref.shape[1]
    at = 0
    lows = len(refs) - 2 - len(places)
    for ref in refs[:lows]:
        for k in range(ref.shape[0]):
            low_ref[lax.bitwise_xor(at_ref[1], places[at])] = ref[k]
            at += 1
    for o, ref in zip(places, refs[lows:-2]):
        wide = ref.shape[1]
        for k in range(3):
            first_ref[o, :, pl.ds(k * wide, wide)] = ref[pl.ds(k * rank, rank), :]


def collect_call(order, places, lows, grads, feats):
    groups, (toks, wide) = len(grads), grads[0].shape
    rank = lows[0].shape[1] // 2
    extra = wide - feats
    low_shape, first_shape = (groups, 2 * rank, toks), (groups, rank, 3 * extra)
    return order.call(
        functools.partial(collect_kernel, places),
        "collect_blocks",
        [*lows, *[in_hbm(x) for x in grads]],
        [whole(b.shape) for b in lows]
        + [pl.BlockSpec((toks, extra), lambda i: (0, feats // extra))] * groups,
        [(low_shape, BF16), (first_shape, BF16)],
        [whole(low_shape), whole(first_shape)],
    )


def low_dense_kernel(at_ref, *refs):
    out_ref, sum_ref = refs[-2:]
    groups, both, _ = refs[0].shape
    rank = both // 2
    for o in range(groups):
        total = refs[0][lax.bitwise_xor(at_ref[1], o)].astype(F32)
        for ref in refs[1:-2]:
            total = total + ref[lax.bitwise_xor(at_ref[1], o)].astype(F32)
        for q in range(2):
            at = pl.ds((q * groups + o) * rank, rank)
            sum_ref[at, :] = total[q * rank : (q + 1) * rank]
    out_ref[...] = sum_ref[...].T


def low_dense_call(order, parts):
    groups, both, toks = parts[0].shape
    shape = (toks, groups * both)
    return order.call(
        low_dense_kernel,
        "low_dense",
        parts,
        [whole(parts[0].shape)] * len(parts),
        [(shape, F32)],
        [whole(shape)],
        scratch=[pltpu.VMEM((groups * both, toks), F32)],
    )[0]


def lowrank_hid_kernel(groups, at_ref, index_ref, hid_ref, *rest):
    firsts, out_ref = rest[:2], rest[2]
    top = index_ref.shape[1]
    rank = firsts[0].shape[0] // groups
    wide = jnp.concatenate([dot(hid_ref[...], ref[...], NT) for ref in firsts], axis=1)
    column = pair_column(relative(at_ref, index_ref[...], groups).astype(F32))
    wide = jnp.where(expert_mask(column, wide.shape[1], rank), wide, 0.0)
    out_ref[...] = wide.reshape(wide.shape[0] // top, top, wide.shape[1]).sum(axis=1)


def lowrank_hid_call(order, index, hid, firsts, groups):
    (toks, top), (pairs, units) = index.shape, hid.shape
    half = firsts[0].shape[0]
    steps = 4
    return order.call(
        functools.partial(lowrank_hid_kernel, groups),
        "lowrank_hid",
        [index, in_hbm(hid), *firsts],
        [
            pl.BlockSpec((toks // steps, top), lambda i: (i, 0)),
            pl.BlockSpec((pairs // steps, units), lambda i: (i, 0)),
        ]
        + [whole((half, units))] * 2,
        [((toks, 2 * half), F32)],
        [pl.BlockSpec((toks // steps, 2 * half), lambda i: (i, 0))],
        grid=(steps,),
    )[0]


def second_grad_kernel(places, units, at_ref, got_ref, *refs):
    grads, outs, first_ref = refs[:-3], refs[-3:-1], refs[-1]
    rank, tile = outs[0].shape
    toks = grads[0].shape[0]

    @pl.when(pl.program_id(0) == 0)
    def _():
        total = jnp.zeros((rank, units), F32)
        for source in range(got_ref.shape[0]):
            total = total + got_ref[source, :, pl.ds(0, units)].astype(F32)
        first_ref[...] = total

    totals = [jnp.zeros((rank, tile), F32) for _ in outs]
    for o, grad_ref in zip(places, grads):
        source = lax.bitwise_xor(at_ref[1], o)
        scaled = jnp.concatenate(
            [got_ref[source, :, pl.ds(units + q * toks, toks)] for q in range(2)], axis=0
        )
        value = dot(scaled, grad_ref[...], NN)
        totals = [total + value[q * rank : (q + 1) * rank] for q, total in enumerate(totals)]
    for total, out_ref in zip(totals, outs):
        out_ref[...] = adapter_scale * total


def second_grad_call(order, places, got, grads, units, feats):
    rank, toks = got.shape[1], grads[0].shape[0]
    steps = 4
    tile = feats // steps
    block = pl.BlockSpec((rank, tile), lambda i: (0, i))
    return order.call(
        functools.partial(second_grad_kernel, places, units),
        "second_grad",
        [got, *[in_hbm(x) for x in grads]],
        [whole(got.shape)] + [pl.BlockSpec((toks, tile), lambda i: (0, i))] * len(grads),
        [((rank, feats), F32)] * 2 + [((rank, units), F32)],
        [block] * 2 + [whole((rank, units))],
        grid=(steps,),
    )


def first_grad_kernel(groups, steps, parts, at_ref, index_ref, prob_ref, low_ref, hid_ref, *rest):
    index_all_ref, prob_all_ref, hids = rest[0], rest[1], rest[2 : 2 + parts]
    keep_ref, give_ref, scaled_ref, sum_ref = rest[2 + parts :]
    step = pl.program_id(0)
    top = index_ref.shape[1]
    rank = keep_ref.shape[1]
    low = spread_pairs(low_ref[...], top)
    column = pair_column(relative(at_ref, index_ref[...], groups).astype(F32))
    keep = expert_mask(column, low.shape[1], rank)
    scaled = jnp.where(keep, low * pair_column(prob_ref[...].astype(F32)), 0.0).astype(BF16)
    part = adapter_scale * dot(scaled, hid_ref[...], TN)

    @pl.when(step == 0)
    def _():
        sum_ref[...] = part

    @pl.when(step > 0)
    def _():
        sum_ref[...] += part

    @pl.when(step == steps - 1)
    def _():
        total = hids[0][...]
        for ref in hids[1:]:
            total = total + ref[...]
        toks = total.shape[0]
        place = relative(at_ref, index_all_ref[...], groups)
        prob = prob_all_ref[...].astype(F32)
        expert = iota(total.shape, 1) // rank
        scale = jnp.zeros(total.shape, F32)
        for k in range(top):
            scale = jnp.where(expert == place[:, k : k + 1], prob[:, k : k + 1], scale)
        turned = (total * scale).T.astype(BF16)
        for o in range(groups):
            to = lax.bitwise_xor(at_ref[1], o)
            at, other = o * rank, (groups + o) * rank
            keep_ref[to] = sum_ref[pl.ds(at, rank), :]
            give_ref[to] = sum_ref[pl.ds(other, rank), :].astype(BF16)
            scaled_ref[to, :, pl.ds(0, toks)] = turned[at : at + rank]
            scaled_ref[to, :, pl.ds(toks, toks)] = turned[other : other + rank]


def first_grad_call(order, index, prob, low, hid, hids, groups):
    (toks, top), (pairs, units) = index.shape, hid.shape
    width = low.shape[1]
    steps = 4
    rank = width // groups // 2
    shape, scaled_shape = (groups, rank, units), (groups, rank, 2 * toks)
    return order.call(
        functools.partial(first_grad_kernel, groups, steps, len(hids)),
        "first_grad",
        [index, prob, low, in_hbm(hid), index, prob, *hids],
        [
            pl.BlockSpec((toks // steps, top), lambda i: (i, 0)),
            pl.BlockSpec((toks // steps, top), lambda i: (i, 0)),
            pl.BlockSpec((toks // steps, width), lambda i: (i, 0)),
            pl.BlockSpec((pairs // steps, units), lambda i: (i, 0)),
            whole(index.shape),
            whole(prob.shape),
        ]
        + [whole(x.shape) for x in hids],
        [(shape, F32), (shape, BF16), (scaled_shape, BF16)],
        [whole(shape), whole(shape), whole(scaled_shape)],
        grid=(steps,),
        scratch=[pltpu.VMEM((width, units), F32)],
    )


def first_sum_kernel(at_ref, keep_ref, got_ref, scaled_ref, out_ref):
    units = keep_ref.shape[2]
    out_ref[:, :, pl.ds(0, units)] = (keep_ref[...] + got_ref[...].astype(F32)).astype(BF16)
    out_ref[:, :, pl.ds(units, scaled_ref.shape[2])] = scaled_ref[...]


def first_sum_call(order, keep, got, scaled):
    shape = keep.shape[:2] + (keep.shape[2] + scaled.shape[2],)
    return order.call(
        first_sum_kernel,
        "first_sum",
        [keep, got, scaled],
        [whole(x.shape) for x in (keep, got, scaled)],
        [(shape, BF16)],
        [whole(shape)],
    )[0]


def finish_kernel(count, slots, at_ref, index_all_ref, index_ref, prob_ref, low_ref, hid_ref, *rest):
    firsts, back = rest[:2], rest[2 : 2 + count]
    out_ref, sum_ref, all_ref, place_ref = rest[2 + count :]
    top = index_ref.shape[1]
    toks = index_all_ref.shape[0]
    experts = 2 * count

    @pl.when(pl.program_id(0) == 0)
    def _():
        for o, ref in enumerate(back):
            for q in range(2):
                all_ref[pl.ds((q * count + o) * slots, slots), :] = ref[pl.ds(q * slots, slots), :]
        experts_all = relative(at_ref, index_all_ref[...], count)
        hit = jnp.zeros((toks, experts), F32)
        for k in range(top):
            hit = jnp.where(iota((toks, experts), 1) == experts_all[:, k : k + 1], 1.0, hit)
        before = jnp.where(iota((toks, toks), 0) > iota((toks, toks), 1), 1.0, 0.0).astype(BF16)
        place_ref[...] = dot(before, hit.astype(BF16), NN)

    pairs = hid_ref.shape[0]
    some = index_ref.shape[0]
    column = pair_column(relative(at_ref, index_ref[...], count).astype(F32))
    place = spread_pairs(place_ref[pl.ds(pl.program_id(0) * some, some), :], top)
    mine = iota((pairs, experts), 1) == column.astype(jnp.int32)
    target = column * slots + jnp.sum(jnp.where(mine, place, 0.0), axis=1, keepdims=True)
    low = spread_pairs(low_ref[...], top)
    keep = expert_mask(column, low.shape[1], low.shape[1] // experts)
    low = jnp.where(keep, adapter_scale * low.astype(BF16).astype(F32), 0.0).astype(BF16)
    slot = iota((pairs, experts * slots), 1)
    pick = jnp.where(slot == target.astype(jnp.int32), 1.0, 0.0).astype(BF16)
    half = low.shape[1] // 2
    value = dot(pick, all_ref[...], NN)
    value = value + dot(low[:, :half], firsts[0][...], NN) + dot(low[:, half:], firsts[1][...], NN)
    value = value.astype(BF16).astype(F32)
    out_ref[...] = (value * pair_column(prob_ref[...].astype(F32))).astype(BF16)
    sums = jnp.sum(value * hid_ref[...].astype(F32), axis=1, keepdims=True)
    sums = jnp.where(diagonal(pairs, top), sums, 0.0)
    sum_ref[...] = sums.reshape(some, top, top).sum(axis=1)


def finish_call(order, index, prob, low, hid, firsts, back):
    (toks, top), (pairs, units) = index.shape, hid.shape
    width = low.shape[1]
    both = back[0].shape[0]
    steps = 4
    count = len(back)

    def rows(n, columns):
        return pl.BlockSpec((n // steps, columns), lambda i: (i, 0))

    return order.call(
        functools.partial(finish_kernel, count, both // 2),
        "finish",
        [index, index, prob, low, in_hbm(hid), *firsts, *[in_hbm(x) for x in back]],
        [whole(index.shape), rows(toks, top), rows(toks, top), rows(toks, width), rows(pairs, units)]
        + [whole(firsts[0].shape)] * 2
        + [whole((both, units))] * count,
        [((pairs, units), BF16), ((toks, top), F32)],
        [rows(pairs, units), rows(toks, top)],
        grid=(steps,),
        cost=LONG,
        scratch=[pltpu.VMEM((count * both, units), BF16), pltpu.VMEM((toks, 2 * count), F32)],
    )


def body(grad, hidden, index, weight, down, first, second):
    toks, top = index.shape
    exp_local, units_all, feats = down.shape
    units, rank = first.shape[1:]
    groups, cores, shares = lax.axis_size("ep"), lax.axis_size("sub"), lax.axis_size("rep")
    assert exp_local == 1 and cores == 2 and groups & (groups - 1) == 0
    cap = min(toks, 5 * toks * top // (4 * groups * cores))
    slots = -(-cap // 16) * 16
    pairs = toks * top
    at = jnp.stack([lax.axis_index(name).astype(jnp.int32) for name in ("rep", "ep", "sub")])
    order = Order(at)

    def turn(x, offset):
        return lax.ppermute(x, "rep", [(r, (r + offset) % shares) for r in range(shares)])

    def all_shares(x):
        return [x] + [turn(x, k) for k in range(1, shares)]

    def flip(x, mask):
        return lax.ppermute(x, "ep", [(i, i ^ mask) for i in range(groups)])

    def swap(x):
        return lax.ppermute(x, "sub", [(0, 1), (1, 0)])

    where = ("ep", "sub")

    def exchange(x, axes="ep"):
        return lax.all_to_all(x, axes, split_axis=0, concat_axis=0, tiled=True)

    blocks = {0: pack_call(order, grad, first[0].T, index.T)}

    def fetch(o):
        if o not in blocks:
            last = o & -o
            blocks[o] = flip(fetch(o ^ last), last)
        return blocks[o]

    own_down = load_call(order, down[0])
    downs = [own_down, swap(down[0])]
    seconds = [second[0], swap(second[0])]

    if groups == 8:
        batches = [(0, 1), (2, 4), (6, 5), (3, 7)]
        steps = [("multiply", 0), ("gate", 4), ("multiply", 1), ("total", 0), ("total", 1)]
        steps += [("multiply", 2), ("multiply", 3), ("total", 2)]
        early = {("total", 0): 5, ("multiply", 2): 3}
    else:
        batches = [(o, o + 1) for o in range(0, groups, 2)]
        steps = [("multiply", 0)]
        for i in range(1, len(batches)):
            steps += [("multiply", i), ("total", i - 1)]
        early = {}
    last = len(batches) - 1
    places = [o for batch in batches for o in batch]
    back, lows, shared = {}, [], {}

    def total(i):
        for o, rows in zip(batches[i], share_sum_call(order, shared[i], 2, slots)):
            masks = [o] if o else []
            if i >= last - 1 and o % 2:
                masks = [o - 1, 1] if o > 1 else [1]
            elif o == 4 and groups == 8:
                masks = [2, 6]
            for mask in masks:
                rows = flip(rows, mask)
            back[o] = rows

    for kind, i in steps:
        if (kind, i) in early:
            order.wait([fetch(early[kind, i])])
        if kind == "gate":
            blocks[i] = gate_call(order, [fetch(i)])[0]
        elif kind == "total":
            total(i)
        else:
            *give, keep, low = expert_rows_call(
                order, [fetch(o) for o in batches[i]], seconds, downs, shares, slots
            )
            lows.append(low)
            shared[i] = [keep] + [turn(x, k + 1) for k, x in enumerate(give)]

    hid = hidden.reshape(pairs, units)
    grads = [blocks[o] for o in places]

    low_grad, first_own = collect_call(order, places, lows, grads, feats)
    firsts = [x.reshape(groups * rank, units) for x in (first_own, swap(first_own))]
    low_grad = exchange(low_grad)
    order.wait([back[batches[-2][0]]] + [back[4]] * (groups == 8))
    total(last)
    order.wait([low_grad, back[1], back[2]])
    low_hid = all_shares(lowrank_hid_call(order, index, hid, firsts, groups))
    order.wait([back[batches[-2][1]]])

    low_grad = low_dense_call(order, all_shares(low_grad))
    order.wait([back[batches[-1][0]]])
    keep, give, scaled = first_grad_call(order, index, weight, low_grad, hid, low_hid, groups)

    order.wait([back[batches[-1][1]]])
    got = exchange(first_sum_call(order, keep, swap(give), scaled))
    back = [back[o] for o in range(groups)]
    grad_hidden, sums = finish_call(order, index, weight, low_grad, hid, firsts, back)
    if shares == 2:
        other_sums = turn(sums, 1)
        order.wait([other_sums])
        sums = sums + other_sums
    else:
        sums = lax.psum(sums, "rep")
    second_keep, second_give, first_grad = second_grad_call(
        order, places, got, grads, units, feats
    )
    second_grad = second_keep + swap(second_give)
    return (
        grad_hidden.reshape(toks, top, units),
        sums,
        first_grad.T[None],
        second_grad[None],
    )


def solution(mesh):
    return jax.shard_map(
        body,
        mesh=mesh,
        in_specs=(
            P(("grp", "ep", "sub"), "rep"),
            P(("grp", "ep", "sub"), None, "rep"),
            P(("grp", "ep", "sub"), None),
            P(("grp", "ep", "sub"), None),
            P(("ep", "sub"), None, "rep"),
            P(("grp", "ep", "sub"), "rep", None),
            P(("grp", "ep", "sub"), None, "rep"),
        ),
        out_specs=(
            P(("grp", "ep", "sub"), None, "rep"),
            P(("grp", "ep", "sub"), None),
            P(("grp", "ep", "sub"), "rep", None),
            P(("grp", "ep", "sub"), None, "rep"),
        ),
        check_vma=False,
    )
```

```python
import functools

import jax
import jax.numpy as jnp
from jax import lax
from jax.experimental import pallas as pl
from jax.experimental.pallas import tpu as pltpu
from jax.sharding import PartitionSpec as P

adapter_scale = 2.0
BF16 = jnp.bfloat16
F32 = jnp.float32
NT = (((1,), (1,)), ((), ()))
TN = (((0,), (0,)), ((), ()))
NN = (((1,), (0,)), ((), ()))
SMALL = pl.CostEstimate(flops=1, bytes_accessed=1, transcendentals=0)
LONG = pl.CostEstimate(flops=1, bytes_accessed=2 * 10**7, transcendentals=0)
ANY = pl.BlockSpec(memory_space=pl.ANY)
SMEM = pl.BlockSpec(memory_space=pltpu.SMEM)
VMEM = pl.BlockSpec(memory_space=pltpu.VMEM)


def dot(a, b, dims):
    return lax.dot_general(a, b, dims, preferred_element_type=F32)


def iota(shape, axis):
    return lax.broadcasted_iota(jnp.int32, shape, axis)


def whole(shape):
    return pl.BlockSpec(shape, lambda *_: (0,) * len(shape))


def in_hbm(x):
    return pltpu.with_memory_space_constraint(x, pltpu.HBM)


class Order:
    def __init__(self, at):
        self.at, self.last = at, []

    def wait(self, arrays):
        self.last = self.last + list(arrays)

    def call(self, kernel, name, arrays, in_specs, outs, out_specs, grid=(1,), scratch=(), mib=16, cost=SMALL, **more):
        count, last = 1 + len(arrays), len(self.last)

        def ordered(*refs):
            here = count + last + len(outs)
            kernel(*refs[:count], *refs[count + last : here], *refs[here + 1 :])

        *result, token = pl.pallas_call(
            ordered,
            grid=grid,
            in_specs=[SMEM, *in_specs] + [ANY] * last,
            out_specs=[*out_specs, ANY],
            scratch_shapes=scratch,
            out_shape=[jax.ShapeDtypeStruct(*o) if isinstance(o, tuple) else o for o in outs]
            + [pltpu.HBM((8, 128), F32)],
            compiler_params=pltpu.CompilerParams(vmem_limit_bytes=mib * 2**20),
            cost_estimate=cost,
            name=name,
            **more,
        )(self.at, *arrays, *self.last)
        self.last = [in_hbm(token)]
        return result


def relative(at_ref, index, groups):
    o = lax.bitwise_xor(lax.shift_right_logical(index, 1), at_ref[1])
    q = lax.bitwise_xor(lax.bitwise_and(index, 1), at_ref[2])
    return q * groups + o


def spread_pairs(dense, top):
    toks, width = dense.shape
    return jnp.broadcast_to(dense[:, None, :], (toks, top, width)).reshape(toks * top, width)


def diagonal(pairs, top):
    return iota((pairs, top), 1) == lax.bitwise_and(iota((pairs, top), 0), top - 1)


def pair_column(table):
    toks, top = table.shape
    wide = spread_pairs(table, top)
    return jnp.sum(jnp.where(diagonal(toks * top, top), wide, 0.0), axis=1, keepdims=True)


def expert_mask(column, width, rank):
    return iota((column.shape[0], width), 1) // rank == column.astype(jnp.int32)


def pack_kernel(at_ref, grad_ref, first_ref, index_ref, out_ref):
    toks, feats = grad_ref.shape
    rank = first_ref.shape[0]
    extra = out_ref.shape[1] - feats
    out_ref[:, pl.ds(0, feats)] = grad_ref[...]
    for k in range(3):
        piece = first_ref[:, pl.ds(k * extra, extra)]
        out_ref[pl.ds(k * rank, rank), pl.ds(feats, extra)] = piece
    top = index_ref.shape[0]
    out_ref[pl.ds(3 * rank, toks - 3 * rank), pl.ds(feats, extra)] = jnp.full(
        (toks - 3 * rank, extra), -1.0, BF16
    )
    routes = index_ref[...].astype(F32)
    routes = jnp.concatenate([routes, jnp.full((16 - top, toks), -1.0, F32)], axis=0)
    out_ref[pl.ds(3 * rank, 16), pl.ds(feats, toks)] = routes.astype(BF16)


def pack_call(order, grad, first, index):
    (toks, feats), (rank, units) = grad.shape, first.shape
    shape = (toks, feats + units // 3)
    return order.call(
        pack_kernel,
        "pack_block",
        [in_hbm(grad), first, index],
        [whole(grad.shape), whole(first.shape), whole(index.shape)],
        [(shape, BF16)],
        [whole(shape)],
    )[0]


def gate_kernel(at_ref, *refs):
    pass


def gate_call(order, arrays):
    return order.call(
        gate_kernel,
        "gate",
        arrays,
        [ANY] * len(arrays),
        [(x.shape, x.dtype) for x in arrays],
        [ANY] * len(arrays),
        input_output_aliases={1 + k: k for k in range(len(arrays))},
    )


def load_kernel(at_ref, down_ref, out_ref, sems):
    parts = sems.shape[0]
    rows = down_ref.shape[0] // parts
    copies = [
        pltpu.make_async_copy(
            down_ref.at[pl.ds(k * rows, rows), :], out_ref.at[pl.ds(k * rows, rows), :], sems.at[k]
        )
        for k in range(parts)
    ]
    for copy in copies:
        copy.start()
    for copy in copies:
        copy.wait()


def load_call(order, down):
    return order.call(
        load_kernel,
        "load_matrix",
        [in_hbm(down)],
        [ANY],
        [pltpu.VMEM(down.shape, down.dtype)],
        [VMEM],
        grid=(),
        scratch=[pltpu.SemaphoreType.DMA((4,))],
    )[0]


def expert_rows_kernel(slots, tiles, shares, batch, route_row, at_ref, *rest):
    grads, seconds, downs = rest[:batch], rest[batch : batch + 2], rest[batch + 2 : batch + 4]
    *outs, low_ref = rest[batch + 4 : batch + 5 + shares]
    block_ref, turned_ref, block_sems = rest[batch + 5 + shares :]
    tile = downs[0].shape[0] // shares // tiles
    feats = turned_ref.shape[1]
    toks = block_ref.shape[1]
    blocks = [
        pltpu.make_async_copy(ref, block_ref.at[k], block_sems.at[k]) for k, ref in enumerate(grads)
    ]
    for copy in blocks:
        copy.start()

    before = jnp.where(iota((toks, toks), 0) < iota((toks, toks), 1), 1.0, 0.0).astype(BF16)
    columns = turned_ref.shape[2]
    slot = iota((columns, batch * toks), 0).astype(F32)
    second = jnp.concatenate([ref[...] for ref in seconds], axis=0)
    routes = []
    for k in range(batch):
        blocks[k].wait()
        routes.append(block_ref[k, pl.ds(route_row, 16), pl.ds(feats, toks)].astype(F32))
    grad = block_ref[:, :, pl.ds(0, feats)].reshape(batch * toks, feats)
    for q in range(2):
        expert = at_ref[1] * 2 + lax.bitwise_xor(at_ref[2], q)
        targets = []
        for k in range(batch):
            hits = jnp.where(routes[k] == expert.astype(F32), 1.0, 0.0)
            mine = jnp.max(hits, axis=0, keepdims=True)
            pos = dot(jnp.broadcast_to(mine, (16, toks)).astype(BF16), before, NN)[:1]
            targets.append(jnp.where(mine > 0.0, pos + float(k * slots), -1.0))
        pick = jnp.where(slot == jnp.concatenate(targets, axis=1), 1.0, 0.0)
        turned_ref[q] = dot(grad, pick.T.astype(BF16), TN).astype(BF16)
    low = dot(second, grad, NT).astype(BF16)
    for k in range(batch):
        low_ref[k] = low[:, k * toks : (k + 1) * toks]

    rows = batch * slots
    for k in range(shares):
        share = lax.rem(at_ref[0] + k + 1, shares)
        for q in range(2):
            for t in range(tiles):
                row = pl.multiple_of((share * tiles + t) * tile, tile)
                value = dot(downs[q][pl.ds(row, tile), :], turned_ref[q], NN)
                outs[k][pl.ds(q * rows, rows), pl.ds(t * tile, tile)] = value.T[:rows].astype(BF16)


def expert_rows_call(order, grads, seconds, downs, shares, slots):
    batch, (toks, wide) = len(grads), grads[0].shape
    rank, feats = seconds[0].shape
    units = downs[0].shape[0] // shares
    rows = 2 * batch * slots
    return order.call(
        functools.partial(expert_rows_kernel, slots, 3, shares, batch, 3 * rank),
        "expert_rows",
        [*grads, *seconds, *[pltpu.with_memory_space_constraint(x, pltpu.VMEM) for x in downs]],
        [ANY] * batch + [VMEM] * 4,
        [((rows, units), BF16)] * shares + [((batch, 2 * rank, toks), BF16)],
        [VMEM] * (shares + 1),
        grid=(),
        scratch=[
            pltpu.VMEM((batch, toks, wide), BF16),
            pltpu.VMEM((2, feats, -(-batch * slots // 128) * 128), BF16),
            pltpu.SemaphoreType.DMA((batch,)),
        ],
    )


def share_sum_kernel(parts, slots, at_ref, *refs):
    outs = refs[parts:]
    for k, out_ref in enumerate(outs):
        for q in range(2):
            at = pl.ds((q * len(outs) + k) * slots, slots)
            total = refs[0][at, :].astype(F32)
            for part in refs[1:parts]:
                total = total + part[at, :].astype(F32)
            out_ref[pl.ds(q * slots, slots), :] = total.astype(BF16)


def share_sum_call(order, parts, batch, slots):
    rows, units = parts[0].shape
    shape = (2 * slots, units)
    return order.call(
        functools.partial(share_sum_kernel, len(parts), slots),
        "share_sum",
        parts,
        [whole((rows, units))] * len(parts),
        [(shape, BF16)] * batch,
        [whole(shape)] * batch,
    )


def collect_kernel(places, at_ref, *refs):
    low_ref, first_ref = refs[-2:]
    rank = first_ref.shape[1]
    at = 0
    lows = len(refs) - 2 - len(places)
    for ref in refs[:lows]:
        for k in range(ref.shape[0]):
            low_ref[lax.bitwise_xor(at_ref[1], places[at])] = ref[k]
            at += 1
    for o, ref in zip(places, refs[lows:-2]):
        wide = ref.shape[1]
        for k in range(3):
            first_ref[o, :, pl.ds(k * wide, wide)] = ref[pl.ds(k * rank, rank), :]


def collect_call(order, places, lows, grads, feats):
    groups, (toks, wide) = len(grads), grads[0].shape
    rank = lows[0].shape[1] // 2
    extra = wide - feats
    low_shape, first_shape = (groups, 2 * rank, toks), (groups, rank, 3 * extra)
    return order.call(
        functools.partial(collect_kernel, places),
        "collect_blocks",
        [*lows, *[in_hbm(x) for x in grads]],
        [whole(b.shape) for b in lows]
        + [pl.BlockSpec((toks, extra), lambda i: (0, feats // extra))] * groups,
        [(low_shape, BF16), (first_shape, BF16)],
        [whole(low_shape), whole(first_shape)],
    )


def low_dense_kernel(at_ref, *refs):
    out_ref, sum_ref = refs[-2:]
    groups, both, _ = refs[0].shape
    rank = both // 2
    for o in range(groups):
        total = refs[0][lax.bitwise_xor(at_ref[1], o)].astype(F32)
        for ref in refs[1:-2]:
            total = total + ref[lax.bitwise_xor(at_ref[1], o)].astype(F32)
        for q in range(2):
            at = pl.ds((q * groups + o) * rank, rank)
            sum_ref[at, :] = total[q * rank : (q + 1) * rank]
    out_ref[...] = sum_ref[...].T


def low_dense_call(order, parts):
    groups, both, toks = parts[0].shape
    shape = (toks, groups * both)
    return order.call(
        low_dense_kernel,
        "low_dense",
        parts,
        [whole(parts[0].shape)] * len(parts),
        [(shape, F32)],
        [whole(shape)],
        scratch=[pltpu.VMEM((groups * both, toks), F32)],
    )[0]


def lowrank_hid_kernel(groups, at_ref, index_ref, hid_ref, *rest):
    firsts, out_ref = rest[:2], rest[2]
    top = index_ref.shape[1]
    rank = firsts[0].shape[0] // groups
    wide = jnp.concatenate([dot(hid_ref[...], ref[...], NT) for ref in firsts], axis=1)
    column = pair_column(relative(at_ref, index_ref[...], groups).astype(F32))
    wide = jnp.where(expert_mask(column, wide.shape[1], rank), wide, 0.0)
    out_ref[...] = wide.reshape(wide.shape[0] // top, top, wide.shape[1]).sum(axis=1)


def lowrank_hid_call(order, index, hid, firsts, groups):
    (toks, top), (pairs, units) = index.shape, hid.shape
    half = firsts[0].shape[0]
    steps = 4
    return order.call(
        functools.partial(lowrank_hid_kernel, groups),
        "lowrank_hid",
        [index, in_hbm(hid), *firsts],
        [
            pl.BlockSpec((toks // steps, top), lambda i: (i, 0)),
            pl.BlockSpec((pairs // steps, units), lambda i: (i, 0)),
        ]
        + [whole((half, units))] * 2,
        [((toks, 2 * half), F32)],
        [pl.BlockSpec((toks // steps, 2 * half), lambda i: (i, 0))],
        grid=(steps,),
    )[0]


def second_grad_kernel(places, units, at_ref, got_ref, *refs):
    grads, outs, first_ref = refs[:-3], refs[-3:-1], refs[-1]
    rank, tile = outs[0].shape
    toks = grads[0].shape[0]

    @pl.when(pl.program_id(0) == 0)
    def _():
        total = jnp.zeros((rank, units), F32)
        for source in range(got_ref.shape[0]):
            total = total + got_ref[source, :, pl.ds(0, units)].astype(F32)
        first_ref[...] = total

    totals = [jnp.zeros((rank, tile), F32) for _ in outs]
    for o, grad_ref in zip(places, grads):
        source = lax.bitwise_xor(at_ref[1], o)
        scaled = jnp.concatenate(
            [got_ref[source, :, pl.ds(units + q * toks, toks)] for q in range(2)], axis=0
        )
        value = dot(scaled, grad_ref[...], NN)
        totals = [total + value[q * rank : (q + 1) * rank] for q, total in enumerate(totals)]
    for total, out_ref in zip(totals, outs):
        out_ref[...] = adapter_scale * total


def second_grad_call(order, places, got, grads, units, feats):
    rank, toks = got.shape[1], grads[0].shape[0]
    steps = 4
    tile = feats // steps
    block = pl.BlockSpec((rank, tile), lambda i: (0, i))
    return order.call(
        functools.partial(second_grad_kernel, places, units),
        "second_grad",
        [got, *[in_hbm(x) for x in grads]],
        [whole(got.shape)] + [pl.BlockSpec((toks, tile), lambda i: (0, i))] * len(grads),
        [((rank, feats), F32)] * 2 + [((rank, units), F32)],
        [block] * 2 + [whole((rank, units))],
        grid=(steps,),
    )


def first_grad_kernel(groups, steps, parts, at_ref, index_ref, prob_ref, low_ref, hid_ref, *rest):
    index_all_ref, prob_all_ref, hids = rest[0], rest[1], rest[2 : 2 + parts]
    keep_ref, give_ref, scaled_ref, sum_ref = rest[2 + parts :]
    step = pl.program_id(0)
    top = index_ref.shape[1]
    rank = keep_ref.shape[1]
    low = spread_pairs(low_ref[...], top)
    column = pair_column(relative(at_ref, index_ref[...], groups).astype(F32))
    keep = expert_mask(column, low.shape[1], rank)
    scaled = jnp.where(keep, low * pair_column(prob_ref[...].astype(F32)), 0.0).astype(BF16)
    part = adapter_scale * dot(scaled, hid_ref[...], TN)

    @pl.when(step == 0)
    def _():
        sum_ref[...] = part

    @pl.when(step > 0)
    def _():
        sum_ref[...] += part

    @pl.when(step == steps - 1)
    def _():
        total = hids[0][...]
        for ref in hids[1:]:
            total = total + ref[...]
        toks = total.shape[0]
        place = relative(at_ref, index_all_ref[...], groups)
        prob = prob_all_ref[...].astype(F32)
        expert = iota(total.shape, 1) // rank
        scale = jnp.zeros(total.shape, F32)
        for k in range(top):
            scale = jnp.where(expert == place[:, k : k + 1], prob[:, k : k + 1], scale)
        turned = (total * scale).T.astype(BF16)
        for o in range(groups):
            to = lax.bitwise_xor(at_ref[1], o)
            at, other = o * rank, (groups + o) * rank
            keep_ref[to] = sum_ref[pl.ds(at, rank), :]
            give_ref[to] = sum_ref[pl.ds(other, rank), :].astype(BF16)
            scaled_ref[to, :, pl.ds(0, toks)] = turned[at : at + rank]
            scaled_ref[to, :, pl.ds(toks, toks)] = turned[other : other + rank]


def first_grad_call(order, index, prob, low, hid, hids, groups):
    (toks, top), (pairs, units) = index.shape, hid.shape
    width = low.shape[1]
    steps = 4
    rank = width // groups // 2
    shape, scaled_shape = (groups, rank, units), (groups, rank, 2 * toks)
    return order.call(
        functools.partial(first_grad_kernel, groups, steps, len(hids)),
        "first_grad",
        [index, prob, low, in_hbm(hid), index, prob, *hids],
        [
            pl.BlockSpec((toks // steps, top), lambda i: (i, 0)),
            pl.BlockSpec((toks // steps, top), lambda i: (i, 0)),
            pl.BlockSpec((toks // steps, width), lambda i: (i, 0)),
            pl.BlockSpec((pairs // steps, units), lambda i: (i, 0)),
            whole(index.shape),
            whole(prob.shape),
        ]
        + [whole(x.shape) for x in hids],
        [(shape, F32), (shape, BF16), (scaled_shape, BF16)],
        [whole(shape), whole(shape), whole(scaled_shape)],
        grid=(steps,),
        scratch=[pltpu.VMEM((width, units), F32)],
    )


def first_sum_kernel(at_ref, keep_ref, got_ref, scaled_ref, out_ref):
    units = keep_ref.shape[2]
    out_ref[:, :, pl.ds(0, units)] = (keep_ref[...] + got_ref[...].astype(F32)).astype(BF16)
    out_ref[:, :, pl.ds(units, scaled_ref.shape[2])] = scaled_ref[...]


def first_sum_call(order, keep, got, scaled):
    shape = keep.shape[:2] + (keep.shape[2] + scaled.shape[2],)
    return order.call(
        first_sum_kernel,
        "first_sum",
        [keep, got, scaled],
        [whole(x.shape) for x in (keep, got, scaled)],
        [(shape, BF16)],
        [whole(shape)],
    )[0]


def finish_kernel(count, slots, at_ref, index_all_ref, index_ref, prob_ref, low_ref, hid_ref, *rest):
    firsts, back = rest[:2], rest[2 : 2 + count]
    out_ref, sum_ref, all_ref, place_ref = rest[2 + count :]
    top = index_ref.shape[1]
    toks = index_all_ref.shape[0]
    experts = 2 * count

    @pl.when(pl.program_id(0) == 0)
    def _():
        for o, ref in enumerate(back):
            for q in range(2):
                all_ref[pl.ds((q * count + o) * slots, slots), :] = ref[pl.ds(q * slots, slots), :]
        experts_all = relative(at_ref, index_all_ref[...], count)
        hit = jnp.zeros((toks, experts), F32)
        for k in range(top):
            hit = jnp.where(iota((toks, experts), 1) == experts_all[:, k : k + 1], 1.0, hit)
        before = jnp.where(iota((toks, toks), 0) > iota((toks, toks), 1), 1.0, 0.0).astype(BF16)
        place_ref[...] = dot(before, hit.astype(BF16), NN)

    pairs = hid_ref.shape[0]
    some = index_ref.shape[0]
    column = pair_column(relative(at_ref, index_ref[...], count).astype(F32))
    place = spread_pairs(place_ref[pl.ds(pl.program_id(0) * some, some), :], top)
    mine = iota((pairs, experts), 1) == column.astype(jnp.int32)
    target = column * slots + jnp.sum(jnp.where(mine, place, 0.0), axis=1, keepdims=True)
    low = spread_pairs(low_ref[...], top)
    keep = expert_mask(column, low.shape[1], low.shape[1] // experts)
    low = jnp.where(keep, adapter_scale * low.astype(BF16).astype(F32), 0.0).astype(BF16)
    slot = iota((pairs, experts * slots), 1)
    pick = jnp.where(slot == target.astype(jnp.int32), 1.0, 0.0).astype(BF16)
    half = low.shape[1] // 2
    value = dot(pick, all_ref[...], NN)
    value = value + dot(low[:, :half], firsts[0][...], NN) + dot(low[:, half:], firsts[1][...], NN)
    value = value.astype(BF16).astype(F32)
    out_ref[...] = (value * pair_column(prob_ref[...].astype(F32))).astype(BF16)
    sums = jnp.sum(value * hid_ref[...].astype(F32), axis=1, keepdims=True)
    sums = jnp.where(diagonal(pairs, top), sums, 0.0)
    sum_ref[...] = sums.reshape(some, top, top).sum(axis=1)


def finish_call(order, index, prob, low, hid, firsts, back):
    (toks, top), (pairs, units) = index.shape, hid.shape
    width = low.shape[1]
    both = back[0].shape[0]
    steps = 4
    count = len(back)

    def rows(n, columns):
        return pl.BlockSpec((n // steps, columns), lambda i: (i, 0))

    return order.call(
        functools.partial(finish_kernel, count, both // 2),
        "finish",
        [index, index, prob, low, in_hbm(hid), *firsts, *[in_hbm(x) for x in back]],
        [whole(index.shape), rows(toks, top), rows(toks, top), rows(toks, width), rows(pairs, units)]
        + [whole(firsts[0].shape)] * 2
        + [whole((both, units))] * count,
        [((pairs, units), BF16), ((toks, top), F32)],
        [rows(pairs, units), rows(toks, top)],
        grid=(steps,),
        cost=LONG,
        scratch=[pltpu.VMEM((count * both, units), BF16), pltpu.VMEM((toks, 2 * count), F32)],
    )


def body(grad, hidden, index, weight, down, first, second):
    toks, top = index.shape
    exp_local, units_all, feats = down.shape
    units, rank = first.shape[1:]
    groups, cores, shares = lax.axis_size("ep"), lax.axis_size("sub"), lax.axis_size("rep")
    assert exp_local == 1 and cores == 2 and groups & (groups - 1) == 0
    cap = min(toks, 5 * toks * top // (4 * groups * cores))
    slots = -(-cap // 16) * 16
    pairs = toks * top
    at = jnp.stack([lax.axis_index(name).astype(jnp.int32) for name in ("rep", "ep", "sub")])
    order = Order(at)

    def turn(x, offset):
        return lax.ppermute(x, "rep", [(r, (r + offset) % shares) for r in range(shares)])

    def all_shares(x):
        return [x] + [turn(x, k) for k in range(1, shares)]

    def flip(x, mask):
        return lax.ppermute(x, "ep", [(i, i ^ mask) for i in range(groups)])

    def swap(x):
        return lax.ppermute(x, "sub", [(0, 1), (1, 0)])

    where = ("ep", "sub")

    def exchange(x, axes="ep"):
        return lax.all_to_all(x, axes, split_axis=0, concat_axis=0, tiled=True)

    blocks = {0: pack_call(order, grad, first[0].T, index.T)}

    def fetch(o):
        if o not in blocks:
            last = o & -o
            blocks[o] = flip(fetch(o ^ last), last)
        return blocks[o]

    own_down = load_call(order, down[0])
    downs = [own_down, swap(down[0])]
    seconds = [second[0], swap(second[0])]

    if groups == 8:
        batches = [(0, 1), (2, 4), (6, 3), (5, 7)]
        steps = [("multiply", 0), ("gate", 4), ("multiply", 1), ("total", 0), ("total", 1)]
        steps += [("multiply", 2), ("multiply", 3), ("total", 2)]
        early = {("total", 0): 3, ("multiply", 2): 5}
    else:
        batches = [(o, o + 1) for o in range(0, groups, 2)]
        steps = [("multiply", 0)]
        for i in range(1, len(batches)):
            steps += [("multiply", i), ("total", i - 1)]
        early = {}
    last = len(batches) - 1
    places = [o for batch in batches for o in batch]
    back, lows, shared = {}, [], {}

    def total(i):
        for o, rows in zip(batches[i], share_sum_call(order, shared[i], 2, slots)):
            masks = [o] if o else []
            if i >= last - 1 and o % 2:
                masks = [o - 1, 1] if o > 1 else [1]
            elif o == 4 and groups == 8:
                masks = [2, 6]
            for mask in masks:
                rows = flip(rows, mask)
            back[o] = rows

    for kind, i in steps:
        if (kind, i) in early:
            order.wait([fetch(early[kind, i])])
        if kind == "gate":
            blocks[i] = gate_call(order, [fetch(i)])[0]
        elif kind == "total":
            total(i)
        else:
            *give, keep, low = expert_rows_call(
                order, [fetch(o) for o in batches[i]], seconds, downs, shares, slots
            )
            lows.append(low)
            shared[i] = [keep] + [turn(x, k + 1) for k, x in enumerate(give)]

    hid = hidden.reshape(pairs, units)
    grads = [blocks[o] for o in places]

    low_grad, first_own = collect_call(order, places, lows, grads, feats)
    firsts = [x.reshape(groups * rank, units) for x in (first_own, swap(first_own))]
    low_grad = exchange(low_grad)
    order.wait([back[batches[-2][0]]] + [back[4]] * (groups == 8))
    total(last)
    order.wait([low_grad, back[1], back[2]])
    low_hid = all_shares(lowrank_hid_call(order, index, hid, firsts, groups))
    order.wait([back[batches[-2][1]]])

    low_grad = low_dense_call(order, all_shares(low_grad))
    keep, give, scaled = first_grad_call(order, index, weight, low_grad, hid, low_hid, groups)

    order.wait([back[batches[-1][0]], back[batches[-1][1]]])
    got = exchange(first_sum_call(order, keep, swap(give), scaled))
    back = [back[o] for o in range(groups)]
    grad_hidden, sums = finish_call(order, index, weight, low_grad, hid, firsts, back)
    if shares == 2:
        other_sums = turn(sums, 1)
        order.wait([other_sums])
        sums = sums + other_sums
    else:
        sums = lax.psum(sums, "rep")
    second_keep, second_give, first_grad = second_grad_call(
        order, places, got, grads, units, feats
    )
    second_grad = second_keep + swap(second_give)
    return (
        grad_hidden.reshape(toks, top, units),
        sums,
        first_grad.T[None],
        second_grad[None],
    )


def solution(mesh):
    return jax.shard_map(
        body,
        mesh=mesh,
        in_specs=(
            P(("grp", "ep", "sub"), "rep"),
            P(("grp", "ep", "sub"), None, "rep"),
            P(("grp", "ep", "sub"), None),
            P(("grp", "ep", "sub"), None),
            P(("ep", "sub"), None, "rep"),
            P(("grp", "ep", "sub"), "rep", None),
            P(("grp", "ep", "sub"), None, "rep"),
        ),
        out_specs=(
            P(("grp", "ep", "sub"), None, "rep"),
            P(("grp", "ep", "sub"), None),
            P(("grp", "ep", "sub"), "rep", None),
            P(("grp", "ep", "sub"), None, "rep"),
        ),
        check_vma=False,
    )
```
